32 devices in a mesh: dp: 8 (over z, x), expert: 4 (over y, core).
Axes of the slice: x: 2, y: 2, z: 4, core: 2. Of those that a mesh axis runs over, the one named last changes fastest.
Arguments:
- tokens: bfloat16 [2, 16384, 768], P(None, ('dp', 'expert')), may hold values from -6 to 6
- routes: int32 [2, 16384, 2], P(None, ('dp', 'expert')), may hold values from 0 to 5, all different within a row
- lengths: int32 [2, 32, 4], P(None, ('dp', 'expert')), may hold values from 1 to 320, 512 in all within a row
- key_mask: int32 [2, 16384], P(None, ('dp', 'expert')), may hold values 0 or 1
- gain_one: float32 [768], replicated, may hold values from 0.5 to 1.5
- bias_one: float32 [768], replicated, may hold values from -1 to 1
- w_query: bfloat16 [768, 768], replicated, may hold values from -0.21875 to 0.21875
- w_key: bfloat16 [768, 768], replicated, may hold values from -0.21875 to 0.21875
- w_value: bfloat16 [768, 768], replicated, may hold values from -0.21875 to 0.21875
- w_output: bfloat16 [768, 768], replicated, may hold values from -0.625 to 0.625
- gain_two: float32 [768], replicated, may hold values from 0.5 to 1.5
- bias_two: float32 [768], replicated, may hold values from -1 to 1
- w_router: bfloat16 [768, 6], replicated, may hold values from -0.15625 to 0.15625
- frozen_in: bfloat16 [2, 768, 3072], replicated, may hold values from -0.21875 to 0.21875
- frozen_out: bfloat16 [2, 3072, 768], replicated, may hold values from -0.109375 to 0.109375
- new_in: float32 [4, 768, 3072], P('expert', None, 'dp'), may hold values from -0.21875 to 0.21875
- new_out: float32 [4, 3072, 768], P('expert', 'dp'), may hold values from -0.109375 to 0.109375
- cotangent: bfloat16 [2, 16384, 768], P(None, ('dp', 'expert')), may hold values from -6 to 6
Outputs:
- mixed: bfloat16 [2, 16384, 768], P(None, ('dp', 'expert'))
- input_grad: bfloat16 [2, 16384, 768], P(None, ('dp', 'expert'))
- gain_one_grad: float32 [768], P(('dp', 'expert'))
- bias_one_grad: float32 [768], P(('dp', 'expert'))
- query_grad: float32 [768, 768], P(('dp', 'expert'))
- key_grad: float32 [768, 768], P(('dp', 'expert'))
- value_grad: float32 [768, 768], P(('dp', 'expert'))
- output_grad: float32 [768, 768], P(('dp', 'expert'))
- gain_two_grad: float32 [768], P(('dp', 'expert'))
- bias_two_grad: float32 [768], P(('dp', 'expert'))
- router_grad: float32 [768, 6], P(('dp', 'expert'))
- new_in_grad: float32 [4, 768, 3072], P('expert', None, 'dp')
- new_out_grad: float32 [4, 3072, 768], P('expert', 'dp')
The draws below stay inside these ranges and needn't reach their ends.
Inputs may be any that keep to these rules, and one draw needn't show every extreme that they name: `routes`: the two picks of a row differ and every expert is named by some row; a block may name an expert more than 208 times. Each block's 4 lengths sum to 512, the largest exactly 320.
All inputs are finite; a program needn't handle non-finite values. No bound on the sum of `key_mask` on one device may be relied on, other than what follows from the above.
Results may differ from the reference program's by a relative error of at most 0.014.
Values may be sent and summed in bfloat16 or wider, within the bound.
A program may use at most 320 MiB of HBM per device.

```python
import math
import jax
import jax.numpy as jnp
import numpy as np
from jax import lax

D = 768
HEAD = 64
HEADS = 12
FF = 3072
FROZEN = 2
NEW_EXP = 4
EXPERTS = 6
MICRO = 2
TOK_MB = 512
TOKENS = 16384
DOCS = 4
DOC_MOST = 320
CAP = 208
N_DP = 8
N_EXPERT = 4


def set_ends(drawn, rng, low, top_value):
    shape = drawn.shape
    spot = [jax.random.randint(jax.random.fold_in(rng, axis), (), 0, shape[axis]) for axis in range(len(shape))]
    drawn = drawn.at[tuple(spot)].set(low)
    longest = shape.index(max(shape))
    spot[longest] = (spot[longest] + 1) % shape[longest]
    return drawn.at[tuple(spot)].set(top_value)


def levels(stream_key, shape, shards, low, top_value):
    def one(position, shards_of):
        draws = jax.random.uniform(jax.random.fold_in(jax.random.fold_in(stream_key, 6), position), (shards_of,), jnp.float32, low / len(shards), top_value / len(shards))
        return jnp.repeat(jnp.exp(draws), shape[position] // shards_of).reshape((-1,) + (1,) * (len(shape) - position - 1))

    level = one(*shards[0])
    for cut in shards[1:]:
        level = level * one(*cut)
    return level


def picks_of(stream_key, rows, amount, top, lift):
    ranking = jax.random.permutation(jax.random.fold_in(stream_key, 1), amount)
    favour = ranking
    for power in range(3):
        favour = favour * favour // amount
    favour = favour * lift // amount
    lots = jax.random.randint(jax.random.fold_in(stream_key, 2), (rows, amount), 0, 4096) + favour
    fixed_rows = jax.random.permutation(jax.random.fold_in(stream_key, 3), rows)[jnp.arange(amount) % rows]
    lots = jnp.where(jnp.arange(rows)[:, None] == fixed_rows[None, :], 1 << 14, lots)
    priority = lots * amount + jnp.arange(amount)
    return lax.top_k(priority.astype(jnp.int32), top)[1].astype(jnp.int32)


def length_profile(number_of, total, reach, slope):
    weights = [(1 << 20) // math.isqrt(rank ** slope) + 1 for rank in range(2, number_of + 1)]
    rest, given = total - reach - (number_of - 1), [1] * (number_of - 1)
    while rest > 0:
        candidates = [i for i in range(number_of - 1) if given[i] < reach]
        pool, remaining = sum([weights[i] for i in candidates]), rest
        for i in candidates:
            more = min(reach - given[i], max(1, remaining * weights[i] // pool), rest)
            given[i] = given[i] + more
            rest = rest - more
    return np.array([reach] + given)


def ragged_sizes(stream_key, number_of, total, limit, slope):
    if number_of == 2:
        one = jax.random.randint(stream_key, (), max(1, total - limit), min(limit, total - 1) + 1)
        return jnp.stack([one, total - one])
    sizes = jnp.asarray(length_profile(number_of, total, limit, slope), jnp.int32)
    couples = (number_of - 1) // 2
    source_of, taker = sizes[1:1 + 2 * couples:2], sizes[2:2 + 2 * couples:2]
    room = jnp.minimum(source_of - 1, limit - taker)
    passed = jax.random.randint(jax.random.fold_in(stream_key, 1), (couples,), 0, 1 << 20) % (room + 1)
    sizes = sizes.at[1:1 + 2 * couples:2].set(source_of - passed).at[2:2 + 2 * couples:2].set(taker + passed)
    return sizes[jax.random.permutation(jax.random.fold_in(stream_key, 2), number_of)]


def normal_values(key, dims, deviation, most, shards=(), kind=jnp.bfloat16):
    drawn = deviation * jax.random.normal(key, dims, jnp.float32)
    if shards:
        drawn = drawn * levels(key, dims, shards, -0.22, 0.18)
    return jnp.clip(drawn, -most, most).astype(kind)


def setup_inputs(seed: int = 0) -> dict:
    keys = jax.random.split(jax.random.key(seed), 19)
    tokens = normal_values(keys[0], (MICRO, TOKENS, D), 1.0, 6.0, ((1, 32),))
    routes = picks_of(keys[1], MICRO * TOKENS, EXPERTS, 2, 2730).reshape((MICRO, TOKENS, 2))
    lengths = jax.vmap(lambda own: ragged_sizes(own, DOCS, TOK_MB, DOC_MOST, 2))(jax.random.split(keys[2], MICRO * (N_DP * N_EXPERT))).reshape((MICRO, N_DP * N_EXPERT, DOCS)).astype(jnp.int32)
    key_mask = set_ends((jax.random.randint(keys[3], (MICRO, TOKENS), 0, 8) < 7).astype(jnp.int32), jax.random.fold_in(keys[3], 1), 0, 1)
    gain_one = jnp.clip(1.0 + 0.1 * jax.random.normal(keys[4], (D,), jnp.float32), 0.5, 1.5)
    bias_one = normal_values(keys[5], (D,), 0.2, 1.0, (), jnp.float32)
    w_query = normal_values(keys[6], (D, D), D ** -0.5, 0.21875)
    w_key = normal_values(keys[7], (D, D), D ** -0.5, 0.21875)
    w_value = normal_values(keys[8], (D, D), D ** -0.5, 0.21875)
    w_output = normal_values(keys[9], (D, D), (D // 8) ** -0.5, 0.625)
    gain_two = jnp.clip(1.0 + 0.1 * jax.random.normal(keys[10], (D,), jnp.float32), 0.5, 1.5)
    bias_two = normal_values(keys[11], (D,), 0.2, 1.0, (), jnp.float32)
    w_router = normal_values(keys[12], (D, EXPERTS), (2 * D) ** -0.5, 0.15625)
    frozen_in = normal_values(keys[13], (FROZEN, D, FF), D ** -0.5, 0.21875)
    frozen_out = normal_values(keys[14], (FROZEN, FF, D), FF ** -0.5, 0.109375)
    new_in = normal_values(keys[15], (NEW_EXP, D, FF), D ** -0.5, 0.21875, ((0, 4), (2, 8)), jnp.float32)
    new_out = normal_values(keys[16], (NEW_EXP, FF, D), FF ** -0.5, 0.109375, ((0, 4), (1, 8)), jnp.float32)
    cotangent = normal_values(keys[17], (MICRO, TOKENS, D), 1.0, 6.0, ((1, 32),))
    return dict(tokens=tokens, routes=routes, lengths=lengths, key_mask=key_mask, gain_one=gain_one, bias_one=bias_one, w_query=w_query, w_key=w_key, w_value=w_value, w_output=w_output, gain_two=gain_two, bias_two=bias_two, w_router=w_router, frozen_in=frozen_in, frozen_out=frozen_out, new_in=new_in, new_out=new_out, cotangent=cotangent)


@jax.custom_vjp
def low(v):
    return lax.optimization_barrier(v.astype(jnp.bfloat16)).astype(jnp.float32)

@jax.custom_vjp
def low_back(v):
    return v

def low_keep(v):
    return (low(v), None)

def low_pass(kept, grad):
    return (grad,)

def back_keep(v):
    return (v, None)

def back_low(kept, grad):
    return (low(grad),)
low.defvjp(low_keep, low_pass)
low_back.defvjp(back_keep, back_low)
highest = lax.Precision.HIGHEST

def layer_norm(values, gain, shift):
    center = values - lax.optimization_barrier(jnp.mean(values, -1, keepdims=True))
    scaled = center * lax.rsqrt(lax.optimization_barrier(jnp.mean(center * center, -1, keepdims=True)) + 1e-05)
    return scaled * gain + shift

def visible_mask(block_lengths, block_mask):
    places = jnp.arange(TOK_MB, dtype=jnp.int32)
    ends = jnp.cumsum(block_lengths).astype(jnp.int32)
    doc_ids = lax.optimization_barrier(jnp.sum((places[:, None] >= ends[None, :]).astype(jnp.int32), 1))
    same_doc = doc_ids[:, None] == doc_ids[None, :]
    causal = places[None, :] <= places[:, None]
    keep_key = (block_mask[None, :] == 1) | (places[None, :] == places[:, None])
    return same_doc & causal & keep_key

def slot_tables(route_rows):
    expert_ids = jnp.arange(EXPERTS, dtype=jnp.int32)
    pick_hot = [(route_rows[:, pick_no][:, None] == expert_ids[None, :]).astype(jnp.int32) for pick_no in range(2)]
    chosen_hot = pick_hot[0] + pick_hot[1]
    earlier = jnp.cumsum(chosen_hot, 0) - chosen_hot
    slot_ids = jnp.arange(CAP, dtype=jnp.int32)
    slot_match = earlier.T[:, None, :] == slot_ids[None, :, None]
    hots = [jnp.where(slot_match & (pick_hot[pick_no].T[:, None, :] == 1), 1.0, 0.0).astype(jnp.float32) for pick_no in range(2)]
    return ([table.astype(jnp.float32) for table in pick_hot], hots)

def block_forward(inner, expert_in, expert_out, inputs):
    gain_one, bias_one, w_query, w_key, w_value, w_output, gain_two, bias_two, w_router = inner
    values, route_rows, block_lengths, block_mask = inputs
    visible = visible_mask(block_lengths, block_mask)
    normed = low(layer_norm(values, gain_one, bias_one))
    queries = low(low_back(jnp.dot(normed, w_query, precision=highest))).reshape(TOK_MB, HEADS, HEAD)
    key_rows = low(low_back(jnp.dot(normed, w_key, precision=highest))).reshape(TOK_MB, HEADS, HEAD)
    value_rows = low(low_back(jnp.dot(normed, w_value, precision=highest))).reshape(TOK_MB, HEADS, HEAD)
    scores = low_back(jnp.einsum('thd,shd->hts', queries, key_rows, precision=highest) * HEAD ** (-0.5))
    scores = jnp.where(visible[None], scores, -1000000000.0)
    expo = jnp.exp(scores - lax.optimization_barrier(jnp.max(scores, -1, keepdims=True)))
    probs = low(expo / lax.optimization_barrier(jnp.sum(expo, -1, keepdims=True)))
    attended = low(low_back(jnp.einsum('hts,shd->thd', probs, value_rows, precision=highest).reshape(TOK_MB, D)))
    middle = values + low_back(jnp.dot(attended, w_output, precision=highest))
    second = low(layer_norm(middle, gain_two, bias_two))
    logits = low_back(jnp.dot(second, w_router, precision=highest))
    router_probs = jax.nn.softmax(logits, -1)
    pick_hot, hots = slot_tables(route_rows)
    chosen = [lax.optimization_barrier(jnp.sum(router_probs * pick_hot[pick_no], -1)) for pick_no in range(2)]
    chosen_total = chosen[0] + chosen[1]
    place = hots[0] + hots[1]
    buffers = low_back(jnp.einsum('ect,td->ecd', place, second, precision=highest))
    pre_act = low_back(jnp.einsum('ecd,edf->ecf', buffers, expert_in, precision=highest))
    hidden = low(jax.nn.gelu(pre_act))
    results = low(low_back(jnp.einsum('ecf,efd->ecd', hidden, expert_out, precision=highest)))
    mixed = middle
    for pick_no in range(2):
        picked = jnp.einsum('ect,ecd->td', hots[pick_no], results, precision=highest)
        mixed = mixed + (chosen[pick_no] / chosen_total)[:, None] * picked
    return mixed

def reference(tokens, routes, lengths, key_mask, gain_one, bias_one, w_query, w_key, w_value, w_output, gain_two, bias_two, w_router, frozen_in, frozen_out, new_in, new_out, cotangent):
    blocks = MICRO * N_DP * N_EXPERT
    frozen_a = frozen_in.astype(jnp.float32)
    frozen_b = frozen_out.astype(jnp.float32)
    weights = (gain_one, bias_one, w_query.astype(jnp.float32), w_key.astype(jnp.float32), w_value.astype(jnp.float32), w_output.astype(jnp.float32), gain_two, bias_two, w_router.astype(jnp.float32), new_in, new_out)
    route_blocks = routes.reshape(blocks, TOK_MB, 2)
    length_blocks = lengths.reshape(blocks, DOCS)
    mask_blocks = key_mask.reshape(blocks, TOK_MB)

    def forward(weights, values):
        expert_in = jnp.concatenate([frozen_a, low(weights[9])], 0)
        expert_out = jnp.concatenate([frozen_b, low(weights[10])], 0)
        inner = weights[:9]

        def one_block(inputs):
            return block_forward(inner, expert_in, expert_out, inputs)
        outs = lax.map(jax.checkpoint(one_block), (values.reshape(blocks, TOK_MB, D), route_blocks, length_blocks, mask_blocks))
        return outs.reshape(MICRO, TOKENS, D)
    mixed, pull = jax.vjp(forward, weights, tokens.astype(jnp.float32))
    grads, grad_values = pull(cotangent.astype(jnp.float32))
    return (mixed.astype(jnp.bfloat16), grad_values.astype(jnp.bfloat16), grads[0], grads[1], grads[2], grads[3], grads[4], grads[5], grads[6], grads[7], grads[8], grads[9], grads[10])
```

```python
import functools

import jax
import jax.numpy as jnp
from jax import lax
from jax.experimental import pallas as pl
from jax.experimental.pallas import tpu as pltpu
from jax.sharding import PartitionSpec as P

HEAD = 64
PAIR = 2 * HEAD
TILE = 256
EPS = 1e-05
HALF = jnp.bfloat16
SINGLE = jnp.float32
HIDDEN = -1000000000.0
GELU_C = 0.7978845608028654
GELU_A = 0.044715

NN = (((1,), (0,)), ((), ()))
NT = (((1,), (1,)), ((), ()))
TN = (((0,), (0,)), ((), ()))


def mm(a, b, dims=NN):
    return lax.dot_general(a, b, dims, preferred_element_type=SINGLE)


def norm_rows(values):
    center = values - jnp.mean(values, -1, keepdims=True)
    inverse = lax.rsqrt(jnp.mean(center * center, -1, keepdims=True) + EPS)
    return center * inverse, inverse


def norm_back(grad, unit_rows, inverse, gain):
    scaled = grad * gain
    return inverse * (
        scaled
        - jnp.mean(scaled, -1, keepdims=True)
        - unit_rows * jnp.mean(scaled * unit_rows, -1, keepdims=True)
    )


def doc_of(places, ends_ref):
    doc = jnp.zeros(places.shape, jnp.int32)
    for i in range(ends_ref.shape[0]):
        doc = doc + jnp.where(places >= ends_ref[i], 1, 0)
    return doc


def half_masks(rows):
    lane = lax.broadcasted_iota(jnp.int32, (rows, PAIR), 1)
    first = jnp.where(lane < HEAD, 1.0, 0.0).astype(HALF)
    second = jnp.where(lane < HEAD, 0.0, 1.0).astype(HALF)
    return lane < HEAD, (first, second)


def route_hots(routes_t_ref, rows, tokens):
    sub = lax.broadcasted_iota(jnp.int32, (rows, tokens), 0)
    return [sub == routes_t_ref[pick : pick + 1, :] for pick in range(2)]


def attend_kernel(
    capacity,
    experts,
    frozen,
    ends_ref,
    x_ref,
    dy_ref,
    routes_t_ref,
    mask_ref,
    norms_ref,
    wq_ref,
    wk_ref,
    wv_ref,
    wo_ref,
    wr_ref,
    a1_ref,
    q_ref,
    k_ref,
    v_ref,
    o_ref,
    x1_ref,
    a2_ref,
    lse_ref,
    info_ref,
    cols_ref,
    probs_ref,
    froz_ref,
    send_ref,
    bias_scr,
    lse_scr,
):
    tokens, width = x_ref.shape
    chunk = 128
    gain_one, bias_one = norms_ref[0:1, :], norms_ref[1:2, :]
    gain_two, bias_two = norms_ref[2:3, :], norms_ref[3:4, :]

    @pl.loop(0, tokens // chunk)
    def _(i):
        rows = pl.ds(pl.multiple_of(i * chunk, chunk), chunk)
        unit_rows, _ = norm_rows(x_ref[rows, :].astype(SINGLE))
        a1_ref[rows, :] = (unit_rows * gain_one + bias_one).astype(HALF)
        here = lax.broadcasted_iota(jnp.int32, (chunk, 1), 0) + i * chunk
        there = lax.broadcasted_iota(jnp.int32, (1, tokens), 1)
        same = doc_of(here, ends_ref) == doc_of(there, ends_ref)
        keep = (mask_ref[...] == 1) | (there == here)
        visible = same & (there <= here) & keep
        bias_scr[rows, :] = jnp.where(visible, 0.0, HIDDEN)

    @pl.loop(0, tokens // TILE)
    def _(i):
        rows = pl.ds(pl.multiple_of(i * TILE, TILE), TILE)
        a1 = a1_ref[rows, :]
        q_ref[rows, :] = (mm(a1, wq_ref[...]).astype(HALF) * HEAD ** (-0.5)).astype(HALF)
        k_ref[rows, :] = mm(a1, wk_ref[...]).astype(HALF)
        v_ref[rows, :] = mm(a1, wv_ref[...]).astype(HALF)

    lse_scr[...] = jnp.zeros_like(lse_scr)

    @pl.loop(0, width // PAIR)
    def _(i):
        cols = pl.ds(pl.multiple_of(i * PAIR, PAIR), PAIR)
        low, masks = half_masks(TILE)
        lane = lax.broadcasted_iota(jnp.int32, (TILE, 128), 1)
        for part in range(tokens // TILE):
            rows = slice(part * TILE, (part + 1) * TILE)
            keys = (part + 1) * TILE
            q_t = q_ref[rows, cols]
            k_t = k_ref[0:keys, cols]
            v_t = v_ref[0:keys, cols]
            results = []
            for h in range(2):
                scores = mm(q_t * masks[h], k_t, NT) + bias_scr[rows, 0:keys]
                top = jnp.max(scores, -1, keepdims=True)
                expo = jnp.exp(scores - top)
                total = jnp.sum(expo, -1, keepdims=True)
                results.append(mm(expo.astype(HALF), v_t) * (1.0 / total))
                log_total = top + jnp.log(total)
                lse_scr[rows, :] = jnp.where(lane == 2 * i + h, log_total, lse_scr[rows, :])
            o_ref[rows, cols] = jnp.where(low, results[0], results[1]).astype(HALF)

    lse_ref[...] = jnp.transpose(lse_scr[...])[0 : lse_ref.shape[0], :]

    @pl.loop(0, tokens // TILE)
    def _(i):
        rows = pl.ds(pl.multiple_of(i * TILE, TILE), TILE)
        x1 = x_ref[rows, :].astype(SINGLE) + mm(o_ref[rows, :], wo_ref[...])
        x1_ref[rows, :] = x1
        unit_rows, _ = norm_rows(x1)
        a2_ref[rows, :] = (unit_rows * gain_two + bias_two).astype(HALF)

    rows16 = wr_ref.shape[0]
    logits = mm(wr_ref[...], a2_ref[...], NT)
    sub = lax.broadcasted_iota(jnp.int32, (rows16, tokens), 0)
    logits = jnp.where(sub < experts, logits, -1e30)
    expo = jnp.exp(logits - jnp.max(logits, 0, keepdims=True))
    probs = expo / jnp.sum(expo, 0, keepdims=True)
    probs_ref[...] = probs
    hots = route_hots(routes_t_ref, rows16, tokens)
    chosen = [jnp.sum(jnp.where(hot, probs, 0.0), 0, keepdims=True) for hot in hots]
    chosen_total = chosen[0] + chosen[1]
    gates = [one / chosen_total for one in chosen]
    upper = jnp.where(
        lax.broadcasted_iota(jnp.int32, (tokens, tokens), 0)
        < lax.broadcasted_iota(jnp.int32, (tokens, tokens), 1),
        1.0,
        0.0,
    ).astype(HALF)
    both = jnp.where(hots[0] | hots[1], 1.0, 0.0).astype(HALF)
    earlier = mm(both, upper)
    places = []
    for pick in range(2):
        slot = jnp.sum(jnp.where(hots[pick], earlier, 0.0), 0, keepdims=True)
        first = routes_t_ref[pick : pick + 1, :].astype(SINGLE) * capacity
        places.append(jnp.where(slot < capacity, first + slot, -1.0))
    info = jnp.concatenate(
        places + gates + [mask_ref[...].astype(SINGLE), chosen_total, chosen_total, chosen_total], 0
    )
    info_ref[...] = info
    cols_ref[...] = jnp.transpose(
        jnp.concatenate([info, jnp.zeros((128 - info.shape[0], tokens), SINGLE)], 0)
    )
    spots = [one.astype(jnp.int32) for one in places]
    for e in range(experts):
        slots = lax.broadcasted_iota(jnp.int32, (capacity, tokens), 0) + e * capacity
        hit = [slots == spots[pick] for pick in range(2)]
        place = jnp.where(hit[0] | hit[1], 1.0, 0.0).astype(HALF)
        weight = jnp.sum(
            jnp.where(hit[0], gates[0], 0.0) + jnp.where(hit[1], gates[1], 0.0), 1, keepdims=True
        )
        target = froz_ref.at[e] if e < frozen else send_ref.at[e - frozen]
        target[0] = mm(place, a2_ref[...]).astype(HALF)
        target[1] = (mm(place, dy_ref[...]) * weight).astype(HALF)


def expert_step(x_scr, dy_scr, w_in, w_out, in_dims, acc_scr, h_scr, dp_scr, first, chunk):
    back_dims = NT if in_dims == NN else NN

    @pl.loop(0, x_scr.shape[0] // chunk)
    def _(i):
        rows = pl.ds(pl.multiple_of(i * chunk, 16), chunk)
        pre = mm(x_scr[rows, :], w_in, in_dims)
        grad = mm(dy_scr[rows, :], w_out, NT)
        square = pre * pre
        tanh = jnp.tanh(GELU_C * pre * (1.0 + GELU_A * square))
        plus = 0.5 * (1.0 + tanh)
        hidden = (pre * plus).astype(HALF)
        slope = plus + 0.5 * pre * (1.0 - tanh * tanh) * (GELU_C * (1.0 + 3.0 * GELU_A * square))
        grad_pre = (grad * slope).astype(HALF)
        if h_scr is not None:
            h_scr[rows, :] = hidden
            dp_scr[rows, :] = grad_pre
        out = mm(hidden, w_out)
        back = mm(grad_pre, w_in, back_dims)

        @pl.when(first)
        def _():
            acc_scr[0, rows, :] = out
            acc_scr[1, rows, :] = back

        @pl.when(jnp.logical_not(first))
        def _():
            acc_scr[0, rows, :] += out
            acc_scr[1, rows, :] += back


def frozen_kernel(
    r0_ref, r1_ref, win_ref, wout_ref, o0_ref, o1_ref, x_scr, dy_scr, acc_scr
):
    capacity = r0_ref.shape[2]
    step, last = pl.program_id(1), pl.num_programs(1) - 1

    @pl.when(step == 0)
    def _():
        for m, ref in enumerate((r0_ref, r1_ref)):
            x_scr[m * capacity : (m + 1) * capacity, :] = ref[0, 0]
            dy_scr[m * capacity : (m + 1) * capacity, :] = ref[0, 1]

    expert_step(
        x_scr, dy_scr, win_ref[0], wout_ref[0], NN, acc_scr, None, None, step == 0, capacity
    )

    @pl.when(step == last)
    def _():
        for m, ref in enumerate((o0_ref, o1_ref)):
            for part in range(2):
                ref[0, part] = acc_scr[part, m * capacity : (m + 1) * capacity, :].astype(HALF)


def owned_kernel(
    r0_ref,
    r1_ref,
    w_ref,
    o0_ref,
    o1_ref,
    dw_ref,
    x_scr,
    dy_scr,
    xt_scr,
    dyt_scr,
    acc_scr,
    h_scr,
    dp_scr,
):
    sources, _, capacity, width = r0_ref.shape
    group, _, shard, _ = w_ref.shape
    step, last = pl.program_id(0), pl.num_programs(0) - 1
    rows_all = x_scr.shape[0]

    @pl.when(step == 0)
    def _():
        for m, ref in enumerate((r0_ref, r1_ref)):
            for s in range(sources):
                at = (m * sources + s) * capacity
                x_scr[at : at + capacity, :] = ref[s, 0]
                dy_scr[at : at + capacity, :] = ref[s, 1]
        for at in range(0, width, 128):
            xt_scr[at : at + 128, :] = jnp.transpose(x_scr[:, at : at + 128])
            dyt_scr[at : at + 128, :] = jnp.transpose(dy_scr[:, at : at + 128])

    w_in = w_ref[:, 0].reshape(group * shard, width)
    w_out = w_ref[:, 1].reshape(group * shard, width)
    expert_step(
        x_scr, dy_scr, w_in, w_out, NT, acc_scr, h_scr, dp_scr, step == 0, 2 * capacity
    )

    @pl.loop(0, width // TILE)
    def _(i):
        rows = pl.ds(pl.multiple_of(i * TILE, TILE), TILE)
        for part, (left, right) in enumerate(((xt_scr, dp_scr), (dyt_scr, h_scr))):
            total = mm(left[rows, :], right[...]).astype(HALF)
            for g in range(group):
                dw_ref[g, part, rows, :] = total[:, g * shard : (g + 1) * shard]

    @pl.when(step == last)
    def _():
        for m, ref in enumerate((o0_ref, o1_ref)):
            for s in range(sources):
                at = (m * sources + s) * capacity
                for part in range(2):
                    ref[s, part] = acc_scr[part, at : at + capacity, :].astype(HALF)


def back_kernel(
    capacity,
    experts,
    ends_ref,
    x_ref,
    dy_ref,
    routes_t_ref,
    norms_ref,
    wq_ref,
    wk_ref,
    wv_ref,
    wo_ref,
    wr_ref,
    q_ref,
    k_ref,
    v_ref,
    o_ref,
    x1_ref,
    a2_ref,
    lse_ref,
    info_ref,
    cols_ref,
    probs_ref,
    froz_ref,
    back_ref,
    mixed_ref,
    xgrad_ref,
    dq_ref,
    dk_ref,
    dv_ref,
    db_ref,
    small_ref,
    out_scr,
    dbuf_scr,
    bias_scr,
    dx1_scr,
    do_scr,
    delta_scr,
):
    tokens, width = x_ref.shape
    frozen = froz_ref.shape[0]
    gain_one, gain_two = norms_ref[0:1, :], norms_ref[2:3, :]
    slots_all = experts * capacity
    for e in range(experts):
        source = froz_ref.at[e] if e < frozen else back_ref.at[e - frozen]
        out_scr[e * capacity : (e + 1) * capacity, :] = source[0]
        dbuf_scr[e * capacity : (e + 1) * capacity, :] = source[1]

    spots = [info_ref[pick : pick + 1, :].astype(jnp.int32) for pick in range(2)]
    gates = [info_ref[2 + pick : 3 + pick, :] for pick in range(2)]
    chosen_total = info_ref[5:6, :]

    def gate_part(e, carry):
        rows = pl.ds(pl.multiple_of(e * capacity, 16), capacity)
        overlap = mm(out_scr[rows, :], dy_ref[...], NT)
        slots = lax.broadcasted_iota(jnp.int32, (capacity, tokens), 0) + e * capacity
        return tuple(
            carry[pick]
            + jnp.sum(jnp.where(slots == spots[pick], overlap, 0.0), 0, keepdims=True)
            for pick in range(2)
        )

    zero_row = jnp.zeros((1, tokens), SINGLE)
    gate_grads = lax.fori_loop(0, experts, gate_part, (zero_row, zero_row))
    rows16 = wr_ref.shape[0]
    hots = route_hots(routes_t_ref, rows16, tokens)
    weighted = gate_grads[0] * gates[0] + gate_grads[1] * gates[1]
    grad_probs = jnp.where(hots[0], (gate_grads[0] - weighted) / chosen_total, 0.0)
    grad_probs = grad_probs + jnp.where(hots[1], (gate_grads[1] - weighted) / chosen_total, 0.0)
    probs = probs_ref[...]
    grad_logits = probs * (grad_probs - jnp.sum(grad_probs * probs, 0, keepdims=True))
    logits_low = grad_logits.astype(HALF)
    small_ref[0:rows16, :] = mm(logits_low, a2_ref[...])
    small_ref[rows16:, :] = jnp.zeros_like(small_ref[rows16:, :])

    @pl.loop(0, tokens // TILE)
    def _(i):
        rows = pl.ds(pl.multiple_of(i * TILE, TILE), TILE)
        slots = lax.broadcasted_iota(jnp.int32, (TILE, slots_all), 1)
        hit = [slots == cols_ref[rows, pick : pick + 1].astype(jnp.int32) for pick in range(2)]
        gated = jnp.where(hit[0], cols_ref[rows, 2:3], 0.0)
        gated = jnp.where(hit[1], cols_ref[rows, 3:4], gated).astype(HALF)
        place = jnp.where(hit[0] | hit[1], 1.0, 0.0).astype(HALF)
        x1 = x1_ref[rows, :]
        mixed_ref[rows, :] = (x1 + mm(gated, out_scr[...])).astype(HALF)
        dx1_scr[rows, :] = mm(place, dbuf_scr[...])

    logits_col = jnp.transpose(
        jnp.concatenate([grad_logits, jnp.zeros((128 - rows16, tokens), SINGLE)], 0)
    )
    delta_scr[...] = logits_col.astype(HALF).astype(SINGLE)
    router = jnp.concatenate([wr_ref[...], jnp.zeros((128 - rows16, width), HALF)], 0)

    @pl.loop(0, tokens // TILE)
    def _(i):
        rows = pl.ds(pl.multiple_of(i * TILE, TILE), TILE)
        unit_rows, inverse = norm_rows(x1_ref[rows, :])
        grad = dx1_scr[rows, :] + mm(delta_scr[rows, :].astype(HALF), router)
        small_ref[rows16 : rows16 + 1, :] += jnp.sum(grad * unit_rows, 0, keepdims=True)
        small_ref[rows16 + 1 : rows16 + 2, :] += jnp.sum(grad, 0, keepdims=True)
        dx1 = dy_ref[rows, :].astype(SINGLE) + norm_back(grad, unit_rows, inverse, gain_two)
        dx1_scr[rows, :] = dx1
        branch = dx1.astype(HALF)
        db_ref[rows, :] = branch
        do_scr[rows, :] = mm(branch, wo_ref[...], NT).astype(HALF)

    @pl.loop(0, tokens // 128)
    def _(i):
        rows = pl.ds(pl.multiple_of(i * 128, 128), 128)
        key = lax.broadcasted_iota(jnp.int32, (128, 1), 0) + i * 128
        query = lax.broadcasted_iota(jnp.int32, (1, tokens), 1)
        same = doc_of(key, ends_ref) == doc_of(query, ends_ref)
        keep = (cols_ref[rows, 4:5] > 0.5) | (query == key)
        visible = same & (key <= query) & keep
        bias_scr[rows, :] = jnp.where(visible, 0.0, HIDDEN)

    @pl.loop(0, width // PAIR)
    def _(i):
        cols = pl.ds(pl.multiple_of(i * PAIR, PAIR), PAIR)
        low, masks = half_masks(TILE)
        tiles = tokens // TILE
        half_sum = jnp.where(
            (lax.broadcasted_iota(jnp.int32, (8, PAIR), 1) // HEAD)
            == lax.broadcasted_iota(jnp.int32, (8, PAIR), 0),
            1.0,
            0.0,
        )
        overlap = do_scr[:, cols].astype(SINGLE) * o_ref[:, cols].astype(SINGLE)
        deltas = lax.dot_general(
            half_sum,
            overlap,
            NT,
            precision=lax.Precision.HIGHEST,
            preferred_element_type=SINGLE,
        )
        grad_q = [[None] * tiles for _ in range(2)]
        for part in range(tiles):
            keys = slice(part * TILE, (part + 1) * TILE)
            queries = slice(part * TILE, tokens)
            k_t, v_t = k_ref[keys, cols], v_ref[keys, cols]
            q_t, do_t = q_ref[queries, cols], do_scr[queries, cols]
            grad_k, grad_v = [], []
            for h in range(2):
                scores = mm(k_t * masks[h], q_t, NT) + bias_scr[keys, queries]
                log_total = lse_ref[pl.ds(2 * i + h, 1), queries]
                probs = jnp.exp(scores - log_total)
                grad_p = mm(v_t * masks[h], do_t, NT)
                grad_s = (probs * (grad_p - deltas[h : h + 1, queries])).astype(HALF)
                grad_v.append(mm(probs.astype(HALF), do_t))
                grad_k.append(mm(grad_s, q_t))
                step = mm(grad_s, k_t, TN)
                for t in range(part, tiles):
                    piece = step[(t - part) * TILE : (t - part + 1) * TILE, :]
                    grad_q[h][t] = piece if grad_q[h][t] is None else grad_q[h][t] + piece
            dv_ref[keys, cols] = jnp.where(low, grad_v[0], grad_v[1]).astype(HALF)
            dk_ref[keys, cols] = jnp.where(low, grad_k[0], grad_k[1]).astype(HALF)
        for t in range(tiles):
            both = jnp.where(low, grad_q[0][t], grad_q[1][t]) * HEAD ** (-0.5)
            dq_ref[t * TILE : (t + 1) * TILE, cols] = both.astype(HALF)

    @pl.loop(0, tokens // TILE)
    def _(i):
        rows = pl.ds(pl.multiple_of(i * TILE, TILE), TILE)
        unit_rows, inverse = norm_rows(x_ref[rows, :].astype(SINGLE))
        grad = mm(dq_ref[rows, :], wq_ref[...], NT)
        grad = grad + mm(dk_ref[rows, :], wk_ref[...], NT)
        grad = grad + mm(dv_ref[rows, :], wv_ref[...], NT)
        small_ref[rows16 + 2 : rows16 + 3, :] += jnp.sum(grad * unit_rows, 0, keepdims=True)
        small_ref[rows16 + 3 : rows16 + 4, :] += jnp.sum(grad, 0, keepdims=True)
        part = norm_back(grad, unit_rows, inverse, gain_one)
        xgrad_ref[rows, :] = (dx1_scr[rows, :] + part).astype(HALF)


def weights_kernel(*refs):
    ins, dw_ref = refs[:-1], refs[-1]
    micro = len(ins) // 6
    width = dw_ref.shape[-1]

    @pl.loop(0, width // TILE)
    def _(i):
        cols = pl.ds(pl.multiple_of(i * TILE, TILE), TILE)
        for part in range(4):
            total = None
            for m in range(micro):
                a1, o, dq, dk, dv, db = ins[6 * m : 6 * m + 6]
                left = o if part == 3 else a1
                right = (dq, dk, dv, db)[part]
                step = mm(left[:, cols], right[...], TN)
                total = step if total is None else total + step
            dw_ref[part, cols, :] = total.astype(HALF)


def vmem(count):
    return [pl.BlockSpec(memory_space=pltpu.VMEM)] * count


def params(mib, **more):
    return pltpu.CompilerParams(vmem_limit_bytes=mib << 20, **more)


def per_device(
    tokens,
    routes,
    lengths,
    key_mask,
    gain_one,
    bias_one,
    w_query,
    w_key,
    w_value,
    w_output,
    gain_two,
    bias_two,
    w_router,
    frozen_in,
    frozen_out,
    new_in,
    new_out,
    cotangent,
):
    micro, tok, width = tokens.shape
    owners = lax.axis_size("expert")
    dp = lax.axis_size("dp")
    frozen, _, ff = frozen_in.shape
    experts = frozen + owners
    capacity = 10 * tok // (4 * experts) // 8 * 8
    shard = new_in.shape[2]
    slots_all = experts * capacity
    shape = jax.ShapeDtypeStruct
    smem = pl.BlockSpec(memory_space=pltpu.SMEM)

    local_w = jnp.stack([new_in[0].T.astype(HALF), new_out[0].astype(HALF)], 0)
    all_w = lax.all_gather(local_w, "dp", axis=0, tiled=False)

    ends = jnp.cumsum(lengths[:, 0], axis=1).astype(jnp.int32)
    routes_t = jnp.swapaxes(routes, 1, 2)
    norms = jnp.stack([gain_one, bias_one, gain_two, bias_two], 0)
    rows16 = 16
    router_t = jnp.zeros((rows16, width), HALF).at[:experts].set(w_router.T)

    saved, froz_sent, arrived = [], [], []
    for m in range(micro):
        outs = pl.pallas_call(
            functools.partial(attend_kernel, capacity, experts, frozen),
            out_shape=[shape((tok, width), HALF)] * 5
            + [
                shape((tok, width), SINGLE),
                shape((tok, width), HALF),
                shape((16, tok), SINGLE),
                shape((8, tok), SINGLE),
                shape((tok, 128), SINGLE),
                shape((rows16, tok), SINGLE),
                shape((frozen, 2, capacity, width), HALF),
                shape((owners, 2, capacity, width), HALF),
            ],
            in_specs=[smem] + vmem(10),
            out_specs=vmem(13),
            scratch_shapes=[pltpu.VMEM((tok, tok), SINGLE), pltpu.VMEM((tok, 128), SINGLE)],
            compiler_params=params(56),
            cost_estimate=pl.CostEstimate(
                flops=8_000_000_000, bytes_accessed=20_000_000, transcendentals=3_000_000
            ),
            name="attend",
        )(
            ends[m],
            tokens[m],
            cotangent[m],
            routes_t[m],
            key_mask[m][None, :],
            norms,
            w_query,
            w_key,
            w_value,
            w_output,
            router_t,
        )
        saved.append(outs[:11])
        froz_sent.append(outs[11])
        arrived.append(
            lax.all_to_all(outs[12], "expert", split_axis=0, concat_axis=0, tiled=True)
        )

    block = min(768, ff)
    rows_spec = pl.BlockSpec((1, 2, capacity, width), lambda e, f: (e, 0, 0, 0))
    froz_back = pl.pallas_call(
        frozen_kernel,
        grid=(frozen, ff // block),
        out_shape=[shape((frozen, 2, capacity, width), HALF)] * 2,
        in_specs=[
            rows_spec,
            rows_spec,
            pl.BlockSpec((1, width, block), lambda e, f: (e, 0, f)),
            pl.BlockSpec((1, block, width), lambda e, f: (e, f, 0)),
        ],
        out_specs=[rows_spec, rows_spec],
        scratch_shapes=[
            pltpu.VMEM((2 * capacity, width), HALF),
            pltpu.VMEM((2 * capacity, width), HALF),
            pltpu.VMEM((2, 2 * capacity, width), SINGLE),
        ],
        compiler_params=params(50),
        cost_estimate=pl.CostEstimate(
            flops=16_000_000_000, bytes_accessed=25_000_000, transcendentals=2_500_000
        ),
        name="frozen",
    )(froz_sent[0], froz_sent[1], frozen_in, frozen_out)

    rows_all = micro * owners * capacity
    group = max(1, 768 // shard)
    whole = pl.BlockSpec((owners, 2, capacity, width), lambda f: (0, 0, 0, 0))
    done0, done1, grads_w = pl.pallas_call(
        owned_kernel,
        grid=(dp // group,),
        out_shape=[shape((owners, 2, capacity, width), HALF)] * 2
        + [shape((dp, 2, width, shard), HALF)],
        in_specs=[whole, whole, pl.BlockSpec((group, 2, shard, width), lambda f: (f, 0, 0, 0))],
        out_specs=[whole, whole, pl.BlockSpec((group, 2, width, shard), lambda f: (f, 0, 0, 0))],
        scratch_shapes=[
            pltpu.VMEM((rows_all, width), HALF),
            pltpu.VMEM((rows_all, width), HALF),
            pltpu.VMEM((width, rows_all), HALF),
            pltpu.VMEM((width, rows_all), HALF),
            pltpu.VMEM((2, rows_all, width), SINGLE),
            pltpu.VMEM((rows_all, group * shard), HALF),
            pltpu.VMEM((rows_all, group * shard), HALF),
        ],
        compiler_params=params(60),
        cost_estimate=pl.CostEstimate(
            flops=47_000_000_000, bytes_accessed=35_000_000, transcendentals=5_000_000
        ),
        name="owned",
    )(arrived[0], arrived[1], all_w)

    returned = [
        lax.all_to_all(one, "expert", split_axis=0, concat_axis=0, tiled=True)
        for one in (done0, done1)
    ]
    summed_w = lax.psum_scatter(grads_w, "dp", scatter_dimension=0, tiled=True)[0]

    mixed_list, xgrad_list, small_list, weight_ins = [], [], [], []
    for m in range(micro):
        a1, q, k, v, o, x1, a2, lse, info, cols, probs = saved[m]
        mixed, xgrad, dq, dk, dv, db, small = pl.pallas_call(
            functools.partial(back_kernel, capacity, experts),
            out_shape=[shape((tok, width), HALF)] * 6 + [shape((rows16 + 8, width), SINGLE)],
            in_specs=[smem] + vmem(21),
            out_specs=vmem(7),
            scratch_shapes=[
                pltpu.VMEM((slots_all, width), HALF),
                pltpu.VMEM((slots_all, width), HALF),
                pltpu.VMEM((tok, tok), SINGLE),
                pltpu.VMEM((tok, width), SINGLE),
                pltpu.VMEM((tok, width), HALF),
                pltpu.VMEM((tok, 128), SINGLE),
            ],
            compiler_params=params(56),
            cost_estimate=pl.CostEstimate(
                flops=16_000_000_000, bytes_accessed=25_000_000, transcendentals=3_000_000
            ),
            name="back",
        )(
            ends[m],
            tokens[m],
            cotangent[m],
            routes_t[m],
            norms,
            w_query,
            w_key,
            w_value,
            w_output,
            router_t,
            q,
            k,
            v,
            o,
            x1,
            a2,
            lse,
            info,
            cols,
            probs,
            froz_back[m],
            returned[m],
        )
        mixed_list.append(mixed)
        xgrad_list.append(xgrad)
        small_list.append(small)
        weight_ins += [a1, o, dq, dk, dv, db]

    grads = pl.pallas_call(
        weights_kernel,
        out_shape=shape((4, width, width), HALF),
        in_specs=vmem(len(weight_ins)),
        out_specs=vmem(1)[0],
        compiler_params=params(50),
        name="weights",
    )(*weight_ins)
    shared = lax.psum_scatter(grads, ("dp", "expert"), scatter_dimension=1, tiled=True)
    small = sum(small_list[1:], small_list[0])
    small = jnp.concatenate([small[:experts], small[rows16 : rows16 + 4]], 0).T
    small = lax.psum_scatter(small, ("dp", "expert"), scatter_dimension=0, tiled=True)
    shared = shared.astype(SINGLE)
    return (
        jnp.stack(mixed_list, 0),
        jnp.stack(xgrad_list, 0),
        small[:, experts + 2],
        small[:, experts + 3],
        shared[0],
        shared[1],
        shared[2],
        shared[3],
        small[:, experts],
        small[:, experts + 1],
        small[:, :experts],
        summed_w[0].astype(SINGLE)[None],
        summed_w[1].astype(SINGLE).T[None],
    )


def solution(mesh):
    both = ("dp", "expert")
    return jax.shard_map(
        per_device,
        mesh=mesh,
        in_specs=(
            P(None, both, None),
            P(None, both, None),
            P(None, both, None),
            P(None, both),
        )
        + (P(),) * 11
        + (P("expert", None, "dp"), P("expert", "dp", None), P(None, both, None)),
        out_specs=(P(None, both, None), P(None, both, None), P(both), P(both))
        + (P(both, None),) * 4
        + (P(both), P(both), P(both, None), P("expert", None, "dp"), P("expert", "dp", None)),
        check_vma=False,
    )
```

```python
import functools

import jax
import jax.numpy as jnp
from jax import lax
from jax.experimental import pallas as pl
from jax.experimental.pallas import tpu as pltpu
from jax.sharding import PartitionSpec as P

HEAD = 64
PAIR = 2 * HEAD
TILE = 256
EPS = 1e-05
HALF = jnp.bfloat16
SINGLE = jnp.float32
HIDDEN = -1000000000.0
GELU_C = 0.7978845608028654
GELU_A = 0.044715

NN = (((1,), (0,)), ((), ()))
NT = (((1,), (1,)), ((), ()))
TN = (((0,), (0,)), ((), ()))


def mm(a, b, dims=NN):
    return lax.dot_general(a, b, dims, preferred_element_type=SINGLE)


def norm_rows(values):
    center = values - jnp.mean(values, -1, keepdims=True)
    inverse = lax.rsqrt(jnp.mean(center * center, -1, keepdims=True) + EPS)
    return center * inverse, inverse


def norm_back(grad, unit_rows, inverse, gain):
    scaled = grad * gain
    return inverse * (
        scaled
        - jnp.mean(scaled, -1, keepdims=True)
        - unit_rows * jnp.mean(scaled * unit_rows, -1, keepdims=True)
    )


def doc_of(places, ends_ref):
    doc = jnp.zeros(places.shape, jnp.int32)
    for i in range(ends_ref.shape[0]):
        doc = doc + jnp.where(places >= ends_ref[i], 1, 0)
    return doc


def half_masks(rows):
    lane = lax.broadcasted_iota(jnp.int32, (rows, PAIR), 1)
    first = jnp.where(lane < HEAD, 1.0, 0.0).astype(HALF)
    second = jnp.where(lane < HEAD, 0.0, 1.0).astype(HALF)
    return lane < HEAD, (first, second)


def route_hots(routes_t_ref, rows, tokens):
    sub = lax.broadcasted_iota(jnp.int32, (rows, tokens), 0)
    return [sub == routes_t_ref[pick : pick + 1, :] for pick in range(2)]


def attend_kernel(
    capacity,
    experts,
    frozen,
    ends_ref,
    x_ref,
    dy_ref,
    routes_t_ref,
    mask_ref,
    norms_ref,
    wq_ref,
    wk_ref,
    wv_ref,
    wo_ref,
    wr_ref,
    a1_ref,
    q_ref,
    k_ref,
    v_ref,
    o_ref,
    x1_ref,
    a2_ref,
    lse_ref,
    info_ref,
    cols_ref,
    probs_ref,
    froz_ref,
    send_ref,
    bias_scr,
    lse_scr,
):
    tokens, width = x_ref.shape
    chunk = 128
    gain_one, bias_one = norms_ref[0:1, :], norms_ref[1:2, :]
    gain_two, bias_two = norms_ref[2:3, :], norms_ref[3:4, :]

    @pl.loop(0, tokens // chunk)
    def _(i):
        rows = pl.ds(pl.multiple_of(i * chunk, chunk), chunk)
        unit_rows, _ = norm_rows(x_ref[rows, :].astype(SINGLE))
        a1_ref[rows, :] = (unit_rows * gain_one + bias_one).astype(HALF)
        here = lax.broadcasted_iota(jnp.int32, (chunk, 1), 0) + i * chunk
        there = lax.broadcasted_iota(jnp.int32, (1, tokens), 1)
        same = doc_of(here, ends_ref) == doc_of(there, ends_ref)
        keep = (mask_ref[...] == 1) | (there == here)
        visible = same & (there <= here) & keep
        bias_scr[rows, :] = jnp.where(visible, 0.0, HIDDEN)

    @pl.loop(0, tokens // TILE)
    def _(i):
        rows = pl.ds(pl.multiple_of(i * TILE, TILE), TILE)
        a1 = a1_ref[rows, :]
        q_ref[rows, :] = (mm(a1, wq_ref[...]).astype(HALF) * HEAD ** (-0.5)).astype(HALF)
        k_ref[rows, :] = mm(a1, wk_ref[...]).astype(HALF)
        v_ref[rows, :] = mm(a1, wv_ref[...]).astype(HALF)

    lse_scr[...] = jnp.zeros_like(lse_scr)

    @pl.loop(0, width // PAIR)
    def _(i):
        cols = pl.ds(pl.multiple_of(i * PAIR, PAIR), PAIR)
        low, masks = half_masks(TILE)
        lane = lax.broadcasted_iota(jnp.int32, (TILE, 128), 1)
        for part in range(tokens // TILE):
            rows = slice(part * TILE, (part + 1) * TILE)
            keys = (part + 1) * TILE
            q_t = q_ref[rows, cols]
            k_t = k_ref[0:keys, cols]
            v_t = v_ref[0:keys, cols]
            results = []
            for h in range(2):
                scores = mm(q_t * masks[h], k_t, NT) + bias_scr[rows, 0:keys]
                top = jnp.max(scores, -1, keepdims=True)
                expo = jnp.exp(scores - top)
                total = jnp.sum(expo, -1, keepdims=True)
                results.append(mm(expo.astype(HALF), v_t) * (1.0 / total))
                log_total = top + jnp.log(total)
                lse_scr[rows, :] = jnp.where(lane == 2 * i + h, log_total, lse_scr[rows, :])
            o_ref[rows, cols] = jnp.where(low, results[0], results[1]).astype(HALF)

    lse_ref[...] = jnp.transpose(lse_scr[...])[0 : lse_ref.shape[0], :]

    @pl.loop(0, tokens // TILE)
    def _(i):
        rows = pl.ds(pl.multiple_of(i * TILE, TILE), TILE)
        x1 = x_ref[rows, :].astype(SINGLE) + mm(o_ref[rows, :], wo_ref[...])
        x1_ref[rows, :] = x1
        unit_rows, _ = norm_rows(x1)
        a2_ref[rows, :] = (unit_rows * gain_two + bias_two).astype(HALF)

    rows16 = wr_ref.shape[0]
    logits = mm(wr_ref[...], a2_ref[...], NT)
    sub = lax.broadcasted_iota(jnp.int32, (rows16, tokens), 0)
    logits = jnp.where(sub < experts, logits, -1e30)
    expo = jnp.exp(logits - jnp.max(logits, 0, keepdims=True))
    probs = expo / jnp.sum(expo, 0, keepdims=True)
    probs_ref[...] = probs
    hots = route_hots(routes_t_ref, rows16, tokens)
    chosen = [jnp.sum(jnp.where(hot, probs, 0.0), 0, keepdims=True) for hot in hots]
    chosen_total = chosen[0] + chosen[1]
    gates = [one / chosen_total for one in chosen]
    upper = jnp.where(
        lax.broadcasted_iota(jnp.int32, (tokens, tokens), 0)
        < lax.broadcasted_iota(jnp.int32, (tokens, tokens), 1),
        1.0,
        0.0,
    ).astype(HALF)
    both = jnp.where(hots[0] | hots[1], 1.0, 0.0).astype(HALF)
    earlier = mm(both, upper)
    places = []
    for pick in range(2):
        slot = jnp.sum(jnp.where(hots[pick], earlier, 0.0), 0, keepdims=True)
        first = routes_t_ref[pick : pick + 1, :].astype(SINGLE) * capacity
        places.append(jnp.where(slot < capacity, first + slot, -1.0))
    info = jnp.concatenate(
        places + gates + [mask_ref[...].astype(SINGLE), chosen_total, chosen_total, chosen_total], 0
    )
    info_ref[...] = info
    cols_ref[...] = jnp.transpose(
        jnp.concatenate([info, jnp.zeros((128 - info.shape[0], tokens), SINGLE)], 0)
    )
    spots = [one.astype(jnp.int32) for one in places]
    for e in range(experts):
        slots = lax.broadcasted_iota(jnp.int32, (capacity, tokens), 0) + e * capacity
        hit = [slots == spots[pick] for pick in range(2)]
        place = jnp.where(hit[0] | hit[1], 1.0, 0.0).astype(HALF)
        weight = jnp.sum(
            jnp.where(hit[0], gates[0], 0.0) + jnp.where(hit[1], gates[1], 0.0), 1, keepdims=True
        )
        target = froz_ref.at[e] if e < frozen else send_ref.at[e - frozen]
        target[0] = mm(place, a2_ref[...]).astype(HALF)
        target[1] = (mm(place, dy_ref[...]) * weight).astype(HALF)


def expert_step(x_scr, dy_scr, w_in, w_out, in_dims, acc_scr, h_scr, dp_scr, first, chunk):
    back_dims = NT if in_dims == NN else NN

    @pl.loop(0, x_scr.shape[0] // chunk)
    def _(i):
        rows = pl.ds(pl.multiple_of(i * chunk, 16), chunk)
        pre = mm(x_scr[rows, :], w_in, in_dims)
        grad = mm(dy_scr[rows, :], w_out, NT)
        square = pre * pre
        tanh = jnp.tanh(GELU_C * pre * (1.0 + GELU_A * square))
        plus = 0.5 * (1.0 + tanh)
        hidden = (pre * plus).astype(HALF)
        slope = plus + 0.5 * pre * (1.0 - tanh * tanh) * (GELU_C * (1.0 + 3.0 * GELU_A * square))
        grad_pre = (grad * slope).astype(HALF)
        if h_scr is not None:
            h_scr[rows, :] = hidden
            dp_scr[rows, :] = grad_pre
        out = mm(hidden, w_out)
        back = mm(grad_pre, w_in, back_dims)

        @pl.when(first)
        def _():
            acc_scr[0, rows, :] = out
            acc_scr[1, rows, :] = back

        @pl.when(jnp.logical_not(first))
        def _():
            acc_scr[0, rows, :] += out
            acc_scr[1, rows, :] += back


def frozen_kernel(
    r0_ref, r1_ref, win_ref, wout_ref, o0_ref, o1_ref, x_scr, dy_scr, acc_scr
):
    capacity = r0_ref.shape[2]
    step, last = pl.program_id(1), pl.num_programs(1) - 1

    @pl.when(step == 0)
    def _():
        for m, ref in enumerate((r0_ref, r1_ref)):
            x_scr[m * capacity : (m + 1) * capacity, :] = ref[0, 0]
            dy_scr[m * capacity : (m + 1) * capacity, :] = ref[0, 1]

    expert_step(
        x_scr, dy_scr, win_ref[0], wout_ref[0], NN, acc_scr, None, None, step == 0, capacity
    )

    @pl.when(step == last)
    def _():
        for m, ref in enumerate((o0_ref, o1_ref)):
            for part in range(2):
                ref[0, part] = acc_scr[part, m * capacity : (m + 1) * capacity, :].astype(HALF)


def owned_kernel(
    r0_ref,
    r1_ref,
    w_ref,
    o0_ref,
    o1_ref,
    dw_ref,
    x_scr,
    dy_scr,
    xt_scr,
    dyt_scr,
    acc_scr,
    h_scr,
    dp_scr,
):
    sources, _, capacity, width = r0_ref.shape
    group, _, shard, _ = w_ref.shape
    step, last = pl.program_id(0), pl.num_programs(0) - 1
    rows_all = x_scr.shape[0]

    @pl.when(step == 0)
    def _():
        for m, ref in enumerate((r0_ref, r1_ref)):
            for s in range(sources):
                at = (m * sources + s) * capacity
                x_scr[at : at + capacity, :] = ref[s, 0]
                dy_scr[at : at + capacity, :] = ref[s, 1]
        for at in range(0, width, 128):
            xt_scr[at : at + 128, :] = jnp.transpose(x_scr[:, at : at + 128])
            dyt_scr[at : at + 128, :] = jnp.transpose(dy_scr[:, at : at + 128])

    w_in = w_ref[:, 0].reshape(group * shard, width)
    w_out = w_ref[:, 1].reshape(group * shard, width)
    expert_step(
        x_scr, dy_scr, w_in, w_out, NT, acc_scr, h_scr, dp_scr, step == 0, 2 * capacity
    )

    @pl.loop(0, width // TILE)
    def _(i):
        rows = pl.ds(pl.multiple_of(i * TILE, TILE), TILE)
        for part, (left, right) in enumerate(((xt_scr, dp_scr), (dyt_scr, h_scr))):
            total = mm(left[rows, :], right[...]).astype(HALF)
            for g in range(group):
                dw_ref[g, part, rows, :] = total[:, g * shard : (g + 1) * shard]

    @pl.when(step == last)
    def _():
        for m, ref in enumerate((o0_ref, o1_ref)):
            for s in range(sources):
                at = (m * sources + s) * capacity
                for part in range(2):
                    ref[s, part] = acc_scr[part, at : at + capacity, :].astype(HALF)


def back_kernel(
    capacity,
    experts,
    ends_ref,
    x_ref,
    dy_ref,
    routes_t_ref,
    norms_ref,
    wq_ref,
    wk_ref,
    wv_ref,
    wo_ref,
    wr_ref,
    q_ref,
    k_ref,
    v_ref,
    o_ref,
    x1_ref,
    a2_ref,
    lse_ref,
    info_ref,
    cols_ref,
    probs_ref,
    froz_ref,
    back_ref,
    mixed_ref,
    xgrad_ref,
    dq_ref,
    dk_ref,
    dv_ref,
    db_ref,
    small_ref,
    out_scr,
    dbuf_scr,
    bias_scr,
    dx1_scr,
    do_scr,
    delta_scr,
):
    tokens, width = x_ref.shape
    frozen = froz_ref.shape[0]
    gain_one, gain_two = norms_ref[0:1, :], norms_ref[2:3, :]
    slots_all = experts * capacity
    for e in range(experts):
        source = froz_ref.at[e] if e < frozen else back_ref.at[e - frozen]
        out_scr[e * capacity : (e + 1) * capacity, :] = source[0]
        dbuf_scr[e * capacity : (e + 1) * capacity, :] = source[1]

    spots = [info_ref[pick : pick + 1, :].astype(jnp.int32) for pick in range(2)]
    gates = [info_ref[2 + pick : 3 + pick, :] for pick in range(2)]
    chosen_total = info_ref[5:6, :]

    def gate_part(e, carry):
        rows = pl.ds(pl.multiple_of(e * capacity, 16), capacity)
        overlap = mm(out_scr[rows, :], dy_ref[...], NT)
        slots = lax.broadcasted_iota(jnp.int32, (capacity, tokens), 0) + e * capacity
        return tuple(
            carry[pick]
            + jnp.sum(jnp.where(slots == spots[pick], overlap, 0.0), 0, keepdims=True)
            for pick in range(2)
        )

    zero_row = jnp.zeros((1, tokens), SINGLE)
    gate_grads = lax.fori_loop(0, experts, gate_part, (zero_row, zero_row))
    rows16 = wr_ref.shape[0]
    hots = route_hots(routes_t_ref, rows16, tokens)
    weighted = gate_grads[0] * gates[0] + gate_grads[1] * gates[1]
    grad_probs = jnp.where(hots[0], (gate_grads[0] - weighted) / chosen_total, 0.0)
    grad_probs = grad_probs + jnp.where(hots[1], (gate_grads[1] - weighted) / chosen_total, 0.0)
    probs = probs_ref[...]
    grad_logits = probs * (grad_probs - jnp.sum(grad_probs * probs, 0, keepdims=True))
    logits_low = grad_logits.astype(HALF)
    small_ref[0:rows16, :] = mm(logits_low, a2_ref[...])
    small_ref[rows16:, :] = jnp.zeros_like(small_ref[rows16:, :])

    @pl.loop(0, tokens // TILE)
    def _(i):
        rows = pl.ds(pl.multiple_of(i * TILE, TILE), TILE)
        slots = lax.broadcasted_iota(jnp.int32, (TILE, slots_all), 1)
        hit = [slots == cols_ref[rows, pick : pick + 1].astype(jnp.int32) for pick in range(2)]
        gated = jnp.where(hit[0], cols_ref[rows, 2:3], 0.0)
        gated = jnp.where(hit[1], cols_ref[rows, 3:4], gated).astype(HALF)
        place = jnp.where(hit[0] | hit[1], 1.0, 0.0).astype(HALF)
        x1 = x1_ref[rows, :]
        mixed_ref[rows, :] = (x1 + mm(gated, out_scr[...])).astype(HALF)
        dx1_scr[rows, :] = mm(place, dbuf_scr[...])

    logits_col = jnp.transpose(
        jnp.concatenate([grad_logits, jnp.zeros((128 - rows16, tokens), SINGLE)], 0)
    )
    delta_scr[...] = logits_col.astype(HALF).astype(SINGLE)
    router = jnp.concatenate([wr_ref[...], jnp.zeros((128 - rows16, width), HALF)], 0)

    @pl.loop(0, tokens // TILE)
    def _(i):
        rows = pl.ds(pl.multiple_of(i * TILE, TILE), TILE)
        unit_rows, inverse = norm_rows(x1_ref[rows, :])
        grad = dx1_scr[rows, :] + mm(delta_scr[rows, :].astype(HALF), router)
        small_ref[rows16 : rows16 + 1, :] += jnp.sum(grad * unit_rows, 0, keepdims=True)
        small_ref[rows16 + 1 : rows16 + 2, :] += jnp.sum(grad, 0, keepdims=True)
        dx1 = dy_ref[rows, :].astype(SINGLE) + norm_back(grad, unit_rows, inverse, gain_two)
        dx1_scr[rows, :] = dx1
        branch = dx1.astype(HALF)
        db_ref[rows, :] = branch
        do_scr[rows, :] = mm(branch, wo_ref[...], NT).astype(HALF)

    @pl.loop(0, tokens // 128)
    def _(i):
        rows = pl.ds(pl.multiple_of(i * 128, 128), 128)
        key = lax.broadcasted_iota(jnp.int32, (128, 1), 0) + i * 128
        query = lax.broadcasted_iota(jnp.int32, (1, tokens), 1)
        same = doc_of(key, ends_ref) == doc_of(query, ends_ref)
        keep = (cols_ref[rows, 4:5] > 0.5) | (query == key)
        visible = same & (key <= query) & keep
        bias_scr[rows, :] = jnp.where(visible, 0.0, HIDDEN)

    @pl.loop(0, width // PAIR)
    def _(i):
        cols = pl.ds(pl.multiple_of(i * PAIR, PAIR), PAIR)
        low, masks = half_masks(TILE)
        tiles = tokens // TILE
        half_sum = jnp.where(
            (lax.broadcasted_iota(jnp.int32, (8, PAIR), 1) // HEAD)
            == lax.broadcasted_iota(jnp.int32, (8, PAIR), 0),
            1.0,
            0.0,
        )
        overlap = do_scr[:, cols].astype(SINGLE) * o_ref[:, cols].astype(SINGLE)
        deltas = lax.dot_general(
            half_sum,
            overlap,
            NT,
            precision=lax.Precision.HIGHEST,
            preferred_element_type=SINGLE,
        )
        grad_q = [[None] * tiles for _ in range(2)]
        for part in range(tiles):
            keys = slice(part * TILE, (part + 1) * TILE)
            queries = slice(part * TILE, tokens)
            k_t, v_t = k_ref[keys, cols], v_ref[keys, cols]
            q_t, do_t = q_ref[queries, cols], do_scr[queries, cols]
            grad_k, grad_v = [], []
            for h in range(2):
                scores = mm(k_t * masks[h], q_t, NT) + bias_scr[keys, queries]
                log_total = lse_ref[pl.ds(2 * i + h, 1), queries]
                probs = jnp.exp(scores - log_total)
                grad_p = mm(v_t * masks[h], do_t, NT)
                grad_s = (probs * (grad_p - deltas[h : h + 1, queries])).astype(HALF)
                grad_v.append(mm(probs.astype(HALF), do_t))
                grad_k.append(mm(grad_s, q_t))
                step = mm(grad_s, k_t, TN)
                for t in range(part, tiles):
                    piece = step[(t - part) * TILE : (t - part + 1) * TILE, :]
                    grad_q[h][t] = piece if grad_q[h][t] is None else grad_q[h][t] + piece
            dv_ref[keys, cols] = jnp.where(low, grad_v[0], grad_v[1]).astype(HALF)
            dk_ref[keys, cols] = jnp.where(low, grad_k[0], grad_k[1]).astype(HALF)
        for t in range(tiles):
            both = jnp.where(low, grad_q[0][t], grad_q[1][t]) * HEAD ** (-0.5)
            dq_ref[t * TILE : (t + 1) * TILE, cols] = both.astype(HALF)

    @pl.loop(0, tokens // TILE)
    def _(i):
        rows = pl.ds(pl.multiple_of(i * TILE, TILE), TILE)
        unit_rows, inverse = norm_rows(x_ref[rows, :].astype(SINGLE))
        grad = mm(dq_ref[rows, :], wq_ref[...], NT)
        grad = grad + mm(dk_ref[rows, :], wk_ref[...], NT)
        grad = grad + mm(dv_ref[rows, :], wv_ref[...], NT)
        small_ref[rows16 + 2 : rows16 + 3, :] += jnp.sum(grad * unit_rows, 0, keepdims=True)
        small_ref[rows16 + 3 : rows16 + 4, :] += jnp.sum(grad, 0, keepdims=True)
        part = norm_back(grad, unit_rows, inverse, gain_one)
        xgrad_ref[rows, :] = (dx1_scr[rows, :] + part).astype(HALF)


def weights_kernel(*refs):
    ins, dw_ref = refs[:-1], refs[-1]
    micro = len(ins) // 6
    width = dw_ref.shape[-1]

    @pl.loop(0, width // TILE)
    def _(i):
        cols = pl.ds(pl.multiple_of(i * TILE, TILE), TILE)
        for part in range(4):
            total = weight_grad(ins, micro, part, cols)
            dw_ref[part, cols, :] = total.astype(HALF)


def weight_grad(ins, micro, part, cols):
    total = None
    for m in range(micro):
        a1, o, dq, dk, dv, db = ins[6 * m : 6 * m + 6]
        left = o if part == 3 else a1
        right = (dq, dk, dv, db)[part]
        step = mm(left[:, cols], right[...], TN)
        total = step if total is None else total + step
    return total


def reduce_kernel(micro, *refs):
    ins, smalls = refs[: 6 * micro], refs[6 * micro : 7 * micro]
    out_ref, tiny_ref, pay, got, tiny, tiny_got, send_sem, recv_sem = refs[7 * micro :]
    zs, xs, ys, cs, rows_all, width = pay.shape
    rows = rows_all // 4
    pair = 2 * rows
    dp, ex = lax.axis_index("dp"), lax.axis_index("expert")
    z, x, y, c = dp // xs, dp % xs, ex // cs, ex % cs

    def device(zz, xx, yy, cc):
        return (zz * xs + xx, yy * cs + cc)

    others = [(z + step) % zs for step in range(1, zs)]
    core = device(z, x, y, 1 - c)
    side = device(z, 1 - x, y, c)
    deep = device(z, x, 1 - y, c)
    column = [device(zz, x, y, c) for zz in others]
    peers = [core, side, deep] + column
    barrier = pltpu.get_barrier_semaphore()
    for peer in peers:
        pl.semaphore_signal(barrier, inc=1, device_id=peer, device_id_type=pl.DeviceIdType.MESH)
    pl.semaphore_wait(barrier, len(peers))

    count = [0]

    def send(source, target, peer):
        copy = pltpu.make_async_remote_copy(
            src_ref=source,
            dst_ref=target,
            send_sem=send_sem.at[count[0]],
            recv_sem=recv_sem.at[count[0]],
            device_id=peer,
            device_id_type=pl.DeviceIdType.MESH,
        )
        count[0] += 1
        copy.start()
        return copy

    def produce(parts, base):
        tile = 16 * rows
        for j in range(width // tile):
            cols = slice(j * tile, (j + 1) * tile)
            for at, part in enumerate(parts):
                total = weight_grad(ins, micro, part, cols).astype(HALF)
                for i in range(16):
                    number = 16 * j + i
                    place = (
                        number // (ys * cs) // xs,
                        number // (ys * cs) % xs,
                        number % (ys * cs) // cs,
                        number % cs,
                    )
                    pay[place + (slice(base + at * rows, base + (at + 1) * rows),)] = total[
                        i * rows : (i + 1) * rows, :
                    ]

    def add(place, band, held):
        pay[place + (band,)] = (
            pay[place + (band,)].astype(SINGLE) + held[...].astype(SINGLE)
        ).astype(HALF)

    top, low = pl.ds(0, pair), pl.ds(pair, pair)
    core_a, core_b, deep_a, side_b, side_a, col_b, col_a, deep_b = got
    total = smalls[0][...]
    for ref in smalls[1:]:
        total = total + ref[...]
    tiny[...] = total

    produce((3, 2), 0)
    first = send(pay.at[:, :, :, 1 - c, top], core_a, core)
    tiny_core = send(tiny, tiny_got.at[0], core)
    produce((0, 1), pair)
    second = send(pay.at[:, :, :, 1 - c, low], core_b, core)

    first.wait()

    @pl.loop(0, zs)
    def _(i):
        for xx in range(xs):
            for yy in range(ys):
                add((i, xx, yy, c), top, core_a.at[i, xx, yy])

    third = send(pay.at[:, :, 1 - y, c, top], deep_a, deep)
    tiny_core.wait()
    tiny[...] += tiny_got[0]
    tiny_deep = send(tiny, tiny_got.at[1], deep)
    second.wait()

    @pl.loop(0, zs)
    def _(i):
        for xx in range(xs):
            for yy in range(ys):
                add((i, xx, yy, c), low, core_b.at[i, xx, yy])

    fourth = send(pay.at[:, 1 - x, :, c, low], side_b, side)
    tiny_deep.wait()
    tiny[...] += tiny_got[1]
    tiny_side = send(tiny, tiny_got.at[2], side)

    third.wait()

    @pl.loop(0, zs)
    def _(i):
        for xx in range(xs):
            add((i, xx, y, c), top, deep_a.at[i, xx])

    fifth = send(pay.at[:, 1 - x, y, c, top], side_a, side)
    tiny_side.wait()
    tiny[...] += tiny_got[2]
    tiny_col = [send(tiny, tiny_got.at[3 + i], peer) for i, peer in enumerate(column)]

    fourth.wait()

    @pl.loop(0, zs)
    def _(i):
        for yy in range(ys):
            add((i, x, yy, c), low, side_b.at[i, yy])

    sixth = [
        send(pay.at[zz, x, :, c, low], col_b.at[i], peer)
        for i, (zz, peer) in enumerate(zip(others, column))
    ]
    fifth.wait()

    @pl.loop(0, zs)
    def _(i):
        add((i, x, y, c), top, side_a.at[i])

    seventh = [
        send(pay.at[zz, x, y, c, top], col_a.at[i], peer)
        for i, (zz, peer) in enumerate(zip(others, column))
    ]
    for copy in sixth:
        copy.wait()
    for yy in range(ys):
        place = (z, x, yy, c, low)
        total = pay[place].astype(SINGLE)
        for i in range(zs - 1):
            total = total + col_b[i, yy].astype(SINGLE)
        pay[place] = total.astype(HALF)
    eighth = send(pay.at[z, x, 1 - y, c, low], deep_b, deep)
    for copy in seventh:
        copy.wait()
    total = pay[z, x, y, c, 0:pair].astype(SINGLE)
    for i in range(zs - 1):
        total = total + col_a[i].astype(SINGLE)
    out_ref[3] = total[0:rows]
    out_ref[2] = total[rows:pair]
    for copy in tiny_col:
        copy.wait()
    total = tiny[...]
    for i in range(zs - 1):
        total = total + tiny_got[3 + i]
    tiny_ref[...] = total
    eighth.wait()
    total = pay[z, x, y, c, pair : 2 * pair].astype(SINGLE) + deep_b[...].astype(SINGLE)
    out_ref[0] = total[0:rows]
    out_ref[1] = total[rows:pair]


def vmem(count):
    return [pl.BlockSpec(memory_space=pltpu.VMEM)] * count


def params(mib, **more):
    return pltpu.CompilerParams(vmem_limit_bytes=mib << 20, **more)


def per_device(
    tokens,
    routes,
    lengths,
    key_mask,
    gain_one,
    bias_one,
    w_query,
    w_key,
    w_value,
    w_output,
    gain_two,
    bias_two,
    w_router,
    frozen_in,
    frozen_out,
    new_in,
    new_out,
    cotangent,
):
    micro, tok, width = tokens.shape
    owners = lax.axis_size("expert")
    dp = lax.axis_size("dp")
    frozen, _, ff = frozen_in.shape
    experts = frozen + owners
    capacity = 10 * tok // (4 * experts) // 8 * 8
    shard = new_in.shape[2]
    slots_all = experts * capacity
    shape = jax.ShapeDtypeStruct
    smem = pl.BlockSpec(memory_space=pltpu.SMEM)

    local_w = jnp.stack([new_in[0].T.astype(HALF), new_out[0].astype(HALF)], 0)
    all_w = lax.all_gather(local_w, "dp", axis=0, tiled=False)

    ends = jnp.cumsum(lengths[:, 0], axis=1).astype(jnp.int32)
    routes_t = jnp.swapaxes(routes, 1, 2)
    norms = jnp.stack([gain_one, bias_one, gain_two, bias_two], 0)
    rows16 = 16
    router_t = jnp.zeros((rows16, width), HALF).at[:experts].set(w_router.T)

    saved, froz_sent, arrived = [], [], []
    for m in range(micro):
        outs = pl.pallas_call(
            functools.partial(attend_kernel, capacity, experts, frozen),
            out_shape=[shape((tok, width), HALF)] * 5
            + [
                shape((tok, width), SINGLE),
                shape((tok, width), HALF),
                shape((16, tok), SINGLE),
                shape((8, tok), SINGLE),
                shape((tok, 128), SINGLE),
                shape((rows16, tok), SINGLE),
                shape((frozen, 2, capacity, width), HALF),
                shape((owners, 2, capacity, width), HALF),
            ],
            in_specs=[smem] + vmem(10),
            out_specs=vmem(13),
            scratch_shapes=[pltpu.VMEM((tok, tok), SINGLE), pltpu.VMEM((tok, 128), SINGLE)],
            compiler_params=params(56),
            cost_estimate=pl.CostEstimate(
                flops=8_000_000_000, bytes_accessed=20_000_000, transcendentals=3_000_000
            ),
            name="attend",
        )(
            ends[m],
            tokens[m],
            cotangent[m],
            routes_t[m],
            key_mask[m][None, :],
            norms,
            w_query,
            w_key,
            w_value,
            w_output,
            router_t,
        )
        saved.append(outs[:11])
        froz_sent.append(outs[11])
        arrived.append(
            lax.all_to_all(outs[12], "expert", split_axis=0, concat_axis=0, tiled=True)
        )

    block = min(768, ff)
    rows_spec = pl.BlockSpec((1, 2, capacity, width), lambda e, f: (e, 0, 0, 0))
    froz_back = pl.pallas_call(
        frozen_kernel,
        grid=(frozen, ff // block),
        out_shape=[shape((frozen, 2, capacity, width), HALF)] * 2,
        in_specs=[
            rows_spec,
            rows_spec,
            pl.BlockSpec((1, width, block), lambda e, f: (e, 0, f)),
            pl.BlockSpec((1, block, width), lambda e, f: (e, f, 0)),
        ],
        out_specs=[rows_spec, rows_spec],
        scratch_shapes=[
            pltpu.VMEM((2 * capacity, width), HALF),
            pltpu.VMEM((2 * capacity, width), HALF),
            pltpu.VMEM((2, 2 * capacity, width), SINGLE),
        ],
        compiler_params=params(50),
        cost_estimate=pl.CostEstimate(
            flops=16_000_000_000, bytes_accessed=25_000_000, transcendentals=2_500_000
        ),
        name="frozen",
    )(froz_sent[0], froz_sent[1], frozen_in, frozen_out)

    rows_all = micro * owners * capacity
    group = max(1, 768 // shard)
    whole = pl.BlockSpec((owners, 2, capacity, width), lambda f: (0, 0, 0, 0))
    done0, done1, grads_w = pl.pallas_call(
        owned_kernel,
        grid=(dp // group,),
        out_shape=[shape((owners, 2, capacity, width), HALF)] * 2
        + [shape((dp, 2, width, shard), HALF)],
        in_specs=[whole, whole, pl.BlockSpec((group, 2, shard, width), lambda f: (f, 0, 0, 0))],
        out_specs=[whole, whole, pl.BlockSpec((group, 2, width, shard), lambda f: (f, 0, 0, 0))],
        scratch_shapes=[
            pltpu.VMEM((rows_all, width), HALF),
            pltpu.VMEM((rows_all, width), HALF),
            pltpu.VMEM((width, rows_all), HALF),
            pltpu.VMEM((width, rows_all), HALF),
            pltpu.VMEM((2, rows_all, width), SINGLE),
            pltpu.VMEM((rows_all, group * shard), HALF),
            pltpu.VMEM((rows_all, group * shard), HALF),
        ],
        compiler_params=params(60),
        cost_estimate=pl.CostEstimate(
            flops=47_000_000_000, bytes_accessed=35_000_000, transcendentals=5_000_000
        ),
        name="owned",
    )(arrived[0], arrived[1], all_w)

    returned = [
        lax.all_to_all(one, "expert", split_axis=0, concat_axis=0, tiled=True)
        for one in (done0, done1)
    ]
    summed_w = lax.psum_scatter(grads_w, "dp", scatter_dimension=0, tiled=True)[0]

    mixed_list, xgrad_list, small_list, weight_ins = [], [], [], []
    for m in range(micro):
        a1, q, k, v, o, x1, a2, lse, info, cols, probs = saved[m]
        mixed, xgrad, dq, dk, dv, db, small = pl.pallas_call(
            functools.partial(back_kernel, capacity, experts),
            out_shape=[shape((tok, width), HALF)] * 6 + [shape((rows16 + 8, width), SINGLE)],
            in_specs=[smem] + vmem(21),
            out_specs=vmem(7),
            scratch_shapes=[
                pltpu.VMEM((slots_all, width), HALF),
                pltpu.VMEM((slots_all, width), HALF),
                pltpu.VMEM((tok, tok), SINGLE),
                pltpu.VMEM((tok, width), SINGLE),
                pltpu.VMEM((tok, width), HALF),
                pltpu.VMEM((tok, 128), SINGLE),
            ],
            compiler_params=params(56),
            cost_estimate=pl.CostEstimate(
                flops=16_000_000_000, bytes_accessed=25_000_000, transcendentals=3_000_000
            ),
            name="back",
        )(
            ends[m],
            tokens[m],
            cotangent[m],
            routes_t[m],
            norms,
            w_query,
            w_key,
            w_value,
            w_output,
            router_t,
            q,
            k,
            v,
            o,
            x1,
            a2,
            lse,
            info,
            cols,
            probs,
            froz_back[m],
            returned[m],
        )
        mixed_list.append(mixed)
        xgrad_list.append(xgrad)
        small_list.append(small)
        weight_ins += [a1, o, dq, dk, dv, db]

    pieces = dp * owners
    if dp == 8 and owners == 4:
        zs, xs, ys, cs = 4, 2, 2, 2
        rows = width // pieces
        pair = 2 * rows
        landing = [
            (zs, xs, ys),
            (zs, xs, ys),
            (zs, xs),
            (zs, ys),
            (zs,),
            (zs - 1, ys),
            (zs - 1,),
            (),
        ]
        small_rows = small_list[0].shape[0]
        shared, small = pl.pallas_call(
            functools.partial(reduce_kernel, micro),
            out_shape=[shape((4, rows, width), SINGLE), shape((small_rows, width), SINGLE)],
            in_specs=vmem(7 * micro),
            out_specs=vmem(2),
            scratch_shapes=[
                pltpu.VMEM((zs, xs, ys, cs, 4 * rows, width), HALF),
                [pltpu.VMEM(lead + (pair, width), HALF) for lead in landing],
                pltpu.VMEM((small_rows, width), SINGLE),
                pltpu.VMEM((zs + 2, small_rows, width), SINGLE),
                pltpu.SemaphoreType.DMA((18,)),
                pltpu.SemaphoreType.DMA((18,)),
            ],
            compiler_params=params(56, collective_id=1, has_side_effects=True),
            name="reduce",
        )(*weight_ins, *small_list)
        small = jnp.concatenate([small[:experts], small[rows16 : rows16 + 4]], 0)
        at = (lax.axis_index("dp") * owners + lax.axis_index("expert")) * rows
        small = lax.dynamic_slice_in_dim(small, at, rows, 1).T
    else:
        grads = pl.pallas_call(
            weights_kernel,
            out_shape=shape((4, width, width), HALF),
            in_specs=vmem(len(weight_ins)),
            out_specs=vmem(1)[0],
            compiler_params=params(50),
            name="weights",
        )(*weight_ins)
        shared = lax.psum_scatter(grads, ("dp", "expert"), scatter_dimension=1, tiled=True)
        shared = shared.astype(SINGLE)
        small = sum(small_list[1:], small_list[0])
        small = jnp.concatenate([small[:experts], small[rows16 : rows16 + 4]], 0).T
        small = lax.psum_scatter(small, ("dp", "expert"), scatter_dimension=0, tiled=True)
    return (
        jnp.stack(mixed_list, 0),
        jnp.stack(xgrad_list, 0),
        small[:, experts + 2],
        small[:, experts + 3],
        shared[0],
        shared[1],
        shared[2],
        shared[3],
        small[:, experts],
        small[:, experts + 1],
        small[:, :experts],
        summed_w[0].astype(SINGLE)[None],
        summed_w[1].astype(SINGLE).T[None],
    )


def solution(mesh):
    both = ("dp", "expert")
    return jax.shard_map(
        per_device,
        mesh=mesh,
        in_specs=(
            P(None, both, None),
            P(None, both, None),
            P(None, both, None),
            P(None, both),
        )
        + (P(),) * 11
        + (P("expert", None, "dp"), P("expert", "dp", None), P(None, both, None)),
        out_specs=(P(None, both, None), P(None, both, None), P(both), P(both))
        + (P(both, None),) * 4
        + (P(both), P(both), P(both, None), P("expert", None, "dp"), P("expert", "dp", None)),
        check_vma=False,
    )
```

```python
import functools

import jax
import jax.numpy as jnp
from jax import lax
from jax.experimental import pallas as pl
from jax.experimental.pallas import tpu as pltpu
from jax.sharding import PartitionSpec as P

HEAD = 64
PAIR = 2 * HEAD
TILE = 256
EPS = 1e-05
HALF = jnp.bfloat16
SINGLE = jnp.float32
HIDDEN = -1000000000.0
GELU_C = 0.7978845608028654
GELU_A = 0.044715

NN = (((1,), (0,)), ((), ()))
NT = (((1,), (1,)), ((), ()))
TN = (((0,), (0,)), ((), ()))


def mm(a, b, dims=NN):
    return lax.dot_general(a, b, dims, preferred_element_type=SINGLE)


def norm_rows(values):
    center = values - jnp.mean(values, -1, keepdims=True)
    inverse = lax.rsqrt(jnp.mean(center * center, -1, keepdims=True) + EPS)
    return center * inverse, inverse


def norm_back(grad, unit_rows, inverse, gain):
    scaled = grad * gain
    return inverse * (
        scaled
        - jnp.mean(scaled, -1, keepdims=True)
        - unit_rows * jnp.mean(scaled * unit_rows, -1, keepdims=True)
    )


def doc_of(places, ends_ref):
    doc = jnp.zeros(places.shape, jnp.int32)
    for i in range(ends_ref.shape[0]):
        doc = doc + jnp.where(places >= ends_ref[i], 1, 0)
    return doc


def half_masks(rows):
    lane = lax.broadcasted_iota(jnp.int32, (rows, PAIR), 1)
    first = jnp.where(lane < HEAD, 1.0, 0.0).astype(HALF)
    second = jnp.where(lane < HEAD, 0.0, 1.0).astype(HALF)
    return lane < HEAD, (first, second)


def route_hots(routes_t_ref, rows, tokens):
    sub = lax.broadcasted_iota(jnp.int32, (rows, tokens), 0)
    return [sub == routes_t_ref[pick : pick + 1, :] for pick in range(2)]


def attend_kernel(capacity, experts, frozen, *refs):
    froz_ref, send_ref, bias_scr, lse_scr = refs[-4:]

    def target(e, part):
        return froz_ref.at[e, part] if e < frozen else send_ref.at[e - frozen, part]

    attend_body(capacity, experts, target, *refs[:-4], bias_scr, lse_scr)


def attend_body(
    capacity,
    experts,
    target,
    ends_ref,
    x_ref,
    dy_ref,
    routes_t_ref,
    mask_ref,
    norms_ref,
    wq_ref,
    wk_ref,
    wv_ref,
    wo_ref,
    wr_ref,
    a1_ref,
    q_ref,
    k_ref,
    v_ref,
    o_ref,
    x1_ref,
    a2_ref,
    lse_ref,
    info_ref,
    cols_ref,
    probs_ref,
    bias_scr,
    lse_scr,
):
    tokens, width = x_ref.shape
    chunk = 128
    gain_one, bias_one = norms_ref[0:1, :], norms_ref[1:2, :]
    gain_two, bias_two = norms_ref[2:3, :], norms_ref[3:4, :]

    @pl.loop(0, tokens // chunk)
    def _(i):
        rows = pl.ds(pl.multiple_of(i * chunk, chunk), chunk)
        unit_rows, _ = norm_rows(x_ref[rows, :].astype(SINGLE))
        a1_ref[rows, :] = (unit_rows * gain_one + bias_one).astype(HALF)
        here = lax.broadcasted_iota(jnp.int32, (chunk, 1), 0) + i * chunk
        there = lax.broadcasted_iota(jnp.int32, (1, tokens), 1)
        same = doc_of(here, ends_ref) == doc_of(there, ends_ref)
        keep = (mask_ref[...] == 1) | (there == here)
        visible = same & (there <= here) & keep
        bias_scr[rows, :] = jnp.where(visible, 0.0, HIDDEN)

    @pl.loop(0, tokens // TILE)
    def _(i):
        rows = pl.ds(pl.multiple_of(i * TILE, TILE), TILE)
        a1 = a1_ref[rows, :]
        q_ref[rows, :] = (mm(a1, wq_ref[...]).astype(HALF) * HEAD ** (-0.5)).astype(HALF)
        k_ref[rows, :] = mm(a1, wk_ref[...]).astype(HALF)
        v_ref[rows, :] = mm(a1, wv_ref[...]).astype(HALF)

    lse_scr[...] = jnp.zeros_like(lse_scr)

    @pl.loop(0, width // PAIR)
    def _(i):
        cols = pl.ds(pl.multiple_of(i * PAIR, PAIR), PAIR)
        low, masks = half_masks(TILE)
        lane = lax.broadcasted_iota(jnp.int32, (TILE, 128), 1)
        for part in range(tokens // TILE):
            rows = slice(part * TILE, (part + 1) * TILE)
            keys = (part + 1) * TILE
            q_t = q_ref[rows, cols]
            k_t = k_ref[0:keys, cols]
            v_t = v_ref[0:keys, cols]
            results = []
            for h in range(2):
                scores = mm(q_t * masks[h], k_t, NT) + bias_scr[rows, 0:keys]
                top = jnp.max(scores, -1, keepdims=True)
                expo = jnp.exp(scores - top)
                total = jnp.sum(expo, -1, keepdims=True)
                results.append(mm(expo.astype(HALF), v_t) * (1.0 / total))
                log_total = top + jnp.log(total)
                lse_scr[rows, :] = jnp.where(lane == 2 * i + h, log_total, lse_scr[rows, :])
            o_ref[rows, cols] = jnp.where(low, results[0], results[1]).astype(HALF)

    lse_ref[...] = jnp.transpose(lse_scr[...])[0 : lse_ref.shape[0], :]

    @pl.loop(0, tokens // TILE)
    def _(i):
        rows = pl.ds(pl.multiple_of(i * TILE, TILE), TILE)
        x1 = x_ref[rows, :].astype(SINGLE) + mm(o_ref[rows, :], wo_ref[...])
        x1_ref[rows, :] = x1
        unit_rows, _ = norm_rows(x1)
        a2_ref[rows, :] = (unit_rows * gain_two + bias_two).astype(HALF)

    rows16 = wr_ref.shape[0]
    logits = mm(wr_ref[...], a2_ref[...], NT)
    sub = lax.broadcasted_iota(jnp.int32, (rows16, tokens), 0)
    logits = jnp.where(sub < experts, logits, -1e30)
    expo = jnp.exp(logits - jnp.max(logits, 0, keepdims=True))
    probs = expo / jnp.sum(expo, 0, keepdims=True)
    probs_ref[...] = probs
    hots = route_hots(routes_t_ref, rows16, tokens)
    chosen = [jnp.sum(jnp.where(hot, probs, 0.0), 0, keepdims=True) for hot in hots]
    chosen_total = chosen[0] + chosen[1]
    gates = [one / chosen_total for one in chosen]
    upper = jnp.where(
        lax.broadcasted_iota(jnp.int32, (tokens, tokens), 0)
        < lax.broadcasted_iota(jnp.int32, (tokens, tokens), 1),
        1.0,
        0.0,
    ).astype(HALF)
    both = jnp.where(hots[0] | hots[1], 1.0, 0.0).astype(HALF)
    earlier = mm(both, upper)
    places = []
    for pick in range(2):
        slot = jnp.sum(jnp.where(hots[pick], earlier, 0.0), 0, keepdims=True)
        first = routes_t_ref[pick : pick + 1, :].astype(SINGLE) * capacity
        places.append(jnp.where(slot < capacity, first + slot, -1.0))
    info = jnp.concatenate(
        places + gates + [mask_ref[...].astype(SINGLE), chosen_total, chosen_total, chosen_total], 0
    )
    info_ref[...] = info
    cols_ref[...] = jnp.transpose(
        jnp.concatenate([info, jnp.zeros((128 - info.shape[0], tokens), SINGLE)], 0)
    )
    spots = [one.astype(jnp.int32) for one in places]
    for e in range(experts):
        slots = lax.broadcasted_iota(jnp.int32, (capacity, tokens), 0) + e * capacity
        hit = [slots == spots[pick] for pick in range(2)]
        place = jnp.where(hit[0] | hit[1], 1.0, 0.0).astype(HALF)
        weight = jnp.sum(
            jnp.where(hit[0], gates[0], 0.0) + jnp.where(hit[1], gates[1], 0.0), 1, keepdims=True
        )
        target(e, 0)[...] = mm(place, a2_ref[...]).astype(HALF)
        target(e, 1)[...] = (mm(place, dy_ref[...]) * weight).astype(HALF)


def expert_step(x_of, dy_of, total, w_in, w_out, in_dims, acc_scr, held, first, chunk):
    back_dims = NT if in_dims == NN else NN

    @pl.loop(0, total // chunk)
    def _(i):
        rows = pl.ds(pl.multiple_of(i * chunk, 16), chunk)
        pre = mm(x_of(i), w_in, in_dims)
        grad = mm(dy_of(i), w_out, NT)
        square = pre * pre
        tanh = jnp.tanh(GELU_C * pre * (1.0 + GELU_A * square))
        plus = 0.5 * (1.0 + tanh)
        hidden = (pre * plus).astype(HALF)
        slope = plus + 0.5 * pre * (1.0 - tanh * tanh) * (GELU_C * (1.0 + 3.0 * GELU_A * square))
        grad_pre = (grad * slope).astype(HALF)
        if held is not None:
            held[0, rows, :] = hidden
            held[1, rows, :] = grad_pre
        out = mm(hidden, w_out)
        back = mm(grad_pre, w_in, back_dims)
        if first is True:
            acc_scr[0, rows, :] = out
            acc_scr[1, rows, :] = back
        elif first is False:
            acc_scr[0, rows, :] += out
            acc_scr[1, rows, :] += back
        else:

            @pl.when(first)
            def _():
                acc_scr[0, rows, :] = out
                acc_scr[1, rows, :] = back

            @pl.when(jnp.logical_not(first))
            def _():
                acc_scr[0, rows, :] += out
                acc_scr[1, rows, :] += back


def frozen_kernel(
    r0_ref, r1_ref, win_ref, wout_ref, o0_ref, o1_ref, x_scr, dy_scr, acc_scr
):
    capacity = r0_ref.shape[2]
    step, last = pl.program_id(1), pl.num_programs(1) - 1

    @pl.when(step == 0)
    def _():
        for m, ref in enumerate((r0_ref, r1_ref)):
            x_scr[m * capacity : (m + 1) * capacity, :] = ref[0, 0]
            dy_scr[m * capacity : (m + 1) * capacity, :] = ref[0, 1]

    expert_step(
        lambda i: x_scr[...],
        lambda i: dy_scr[...],
        2 * capacity,
        win_ref[0],
        wout_ref[0],
        NN,
        acc_scr,
        None,
        step == 0,
        2 * capacity,
    )

    @pl.when(step == last)
    def _():
        for m, ref in enumerate((o0_ref, o1_ref)):
            for part in range(2):
                ref[0, part] = acc_scr[part, m * capacity : (m + 1) * capacity, :].astype(HALF)


def owned_kernel(
    r0_ref,
    r1_ref,
    w_ref,
    o0_ref,
    o1_ref,
    dw_ref,
    x_scr,
    dy_scr,
    xt_scr,
    dyt_scr,
    acc_scr,
    held_scr,
):
    sources, _, capacity, width = r0_ref.shape
    group, _, shard, _ = w_ref.shape
    step, last = pl.program_id(0), pl.num_programs(0) - 1
    rows_all = x_scr.shape[0]

    @pl.when(step == 0)
    def _():
        for m, ref in enumerate((r0_ref, r1_ref)):
            for s in range(sources):
                at = (m * sources + s) * capacity
                x_scr[at : at + capacity, :] = ref[s, 0]
                dy_scr[at : at + capacity, :] = ref[s, 1]
        for at in range(0, width, 128):
            xt_scr[at : at + 128, :] = jnp.transpose(x_scr[:, at : at + 128])
            dyt_scr[at : at + 128, :] = jnp.transpose(dy_scr[:, at : at + 128])

    w_in = w_ref[:, 0].reshape(group * shard, width)
    w_out = w_ref[:, 1].reshape(group * shard, width)
    chunk = 2 * capacity
    expert_step(
        lambda i: x_scr[pl.ds(pl.multiple_of(i * chunk, 16), chunk), :],
        lambda i: dy_scr[pl.ds(pl.multiple_of(i * chunk, 16), chunk), :],
        rows_all,
        w_in,
        w_out,
        NT,
        acc_scr,
        held_scr,
        step == 0,
        chunk,
    )

    @pl.loop(0, width // TILE)
    def _(i):
        rows = pl.ds(pl.multiple_of(i * TILE, TILE), TILE)
        for part, (left, right) in enumerate(((xt_scr, held_scr.at[1]), (dyt_scr, held_scr.at[0]))):
            total = mm(left[rows, :], right[...]).astype(HALF)
            for g in range(group):
                dw_ref[g, part, rows, :] = total[:, g * shard : (g + 1) * shard]

    @pl.when(step == last)
    def _():
        for m, ref in enumerate((o0_ref, o1_ref)):
            for s in range(sources):
                at = (m * sources + s) * capacity
                for part in range(2):
                    ref[s, part] = acc_scr[part, at : at + capacity, :].astype(HALF)


def back_kernel(capacity, experts, *refs):
    froz_ref, back_ref = refs[20:22]
    mixed_ref, xgrad_ref, dq_ref, dk_ref, dv_ref, db_ref, small_ref = refs[22:29]
    out_scr, dbuf_scr = refs[29:31]
    frozen = froz_ref.shape[0]
    for e in range(experts):
        source = froz_ref.at[e] if e < frozen else back_ref.at[e - frozen]
        out_scr[e * capacity : (e + 1) * capacity, :] = source[0]
        dbuf_scr[e * capacity : (e + 1) * capacity, :] = source[1]
    back_body(capacity, experts, None, *refs[:20], *refs[22:])


def flat(ref):
    rows = ref[...]
    return rows if rows.ndim == 2 else rows.reshape(-1, rows.shape[-1])


def block_of(ref, e, rows):
    return ref[rows, :] if len(ref.shape) == 2 else ref[e]


def back_body(
    capacity,
    experts,
    middle,
    ends_ref,
    x_ref,
    dy_ref,
    routes_t_ref,
    norms_ref,
    wq_ref,
    wk_ref,
    wv_ref,
    wo_ref,
    wr_ref,
    q_ref,
    k_ref,
    v_ref,
    o_ref,
    x1_ref,
    a2_ref,
    lse_ref,
    info_ref,
    cols_ref,
    probs_ref,
    mixed_ref,
    xgrad_ref,
    dq_ref,
    dk_ref,
    dv_ref,
    db_ref,
    small_ref,
    out_scr,
    dbuf_scr,
    bias_scr,
    dx1_scr,
    do_scr,
    delta_scr,
):
    tokens, width = x_ref.shape
    gain_one, gain_two = norms_ref[0:1, :], norms_ref[2:3, :]
    slots_all = experts * capacity

    spots = [info_ref[pick : pick + 1, :].astype(jnp.int32) for pick in range(2)]
    gates = [info_ref[2 + pick : 3 + pick, :] for pick in range(2)]
    chosen_total = info_ref[5:6, :]

    def gate_part(e, carry):
        rows = pl.ds(pl.multiple_of(e * capacity, 16), capacity)
        overlap = mm(block_of(out_scr, e, rows), dy_ref[...], NT)
        slots = lax.broadcasted_iota(jnp.int32, (capacity, tokens), 0) + e * capacity
        return tuple(
            carry[pick]
            + jnp.sum(jnp.where(slots == spots[pick], overlap, 0.0), 0, keepdims=True)
            for pick in range(2)
        )

    zero_row = jnp.zeros((1, tokens), SINGLE)
    gate_grads = lax.fori_loop(0, experts, gate_part, (zero_row, zero_row))
    rows16 = wr_ref.shape[0]
    hots = route_hots(routes_t_ref, rows16, tokens)
    weighted = gate_grads[0] * gates[0] + gate_grads[1] * gates[1]
    grad_probs = jnp.where(hots[0], (gate_grads[0] - weighted) / chosen_total, 0.0)
    grad_probs = grad_probs + jnp.where(hots[1], (gate_grads[1] - weighted) / chosen_total, 0.0)
    probs = probs_ref[...]
    grad_logits = probs * (grad_probs - jnp.sum(grad_probs * probs, 0, keepdims=True))
    logits_low = grad_logits.astype(HALF)
    small_ref[0:rows16, :] = mm(logits_low, a2_ref[...])
    small_ref[rows16:, :] = jnp.zeros_like(small_ref[rows16:, :])

    @pl.loop(0, tokens // TILE)
    def _(i):
        rows = pl.ds(pl.multiple_of(i * TILE, TILE), TILE)
        slots = lax.broadcasted_iota(jnp.int32, (TILE, slots_all), 1)
        hit = [slots == cols_ref[rows, pick : pick + 1].astype(jnp.int32) for pick in range(2)]
        gated = jnp.where(hit[0], cols_ref[rows, 2:3], 0.0)
        gated = jnp.where(hit[1], cols_ref[rows, 3:4], gated).astype(HALF)
        place = jnp.where(hit[0] | hit[1], 1.0, 0.0).astype(HALF)
        x1 = x1_ref[rows, :]
        mixed_ref[rows, :] = (x1 + mm(gated, flat(out_scr))).astype(HALF)
        dx1_scr[rows, :] = mm(place, flat(dbuf_scr))

    logits_col = jnp.transpose(
        jnp.concatenate([grad_logits, jnp.zeros((128 - rows16, tokens), SINGLE)], 0)
    )
    delta_scr[...] = logits_col.astype(HALF).astype(SINGLE)
    router = jnp.concatenate([wr_ref[...], jnp.zeros((128 - rows16, width), HALF)], 0)

    @pl.loop(0, tokens // TILE)
    def _(i):
        rows = pl.ds(pl.multiple_of(i * TILE, TILE), TILE)
        unit_rows, inverse = norm_rows(x1_ref[rows, :])
        grad = dx1_scr[rows, :] + mm(delta_scr[rows, :].astype(HALF), router)
        small_ref[rows16 : rows16 + 1, :] += jnp.sum(grad * unit_rows, 0, keepdims=True)
        small_ref[rows16 + 1 : rows16 + 2, :] += jnp.sum(grad, 0, keepdims=True)
        dx1 = dy_ref[rows, :].astype(SINGLE) + norm_back(grad, unit_rows, inverse, gain_two)
        dx1_scr[rows, :] = dx1
        branch = dx1.astype(HALF)
        db_ref[rows, :] = branch
        do_scr[rows, :] = mm(branch, wo_ref[...], NT).astype(HALF)

    if middle is not None:
        middle()

    @pl.loop(0, tokens // 128)
    def _(i):
        rows = pl.ds(pl.multiple_of(i * 128, 128), 128)
        key = lax.broadcasted_iota(jnp.int32, (128, 1), 0) + i * 128
        query = lax.broadcasted_iota(jnp.int32, (1, tokens), 1)
        same = doc_of(key, ends_ref) == doc_of(query, ends_ref)
        keep = (cols_ref[rows, 4:5] > 0.5) | (query == key)
        visible = same & (key <= query) & keep
        bias_scr[rows, :] = jnp.where(visible, 0.0, HIDDEN)

    @pl.loop(0, width // PAIR)
    def _(i):
        cols = pl.ds(pl.multiple_of(i * PAIR, PAIR), PAIR)
        low, masks = half_masks(TILE)
        tiles = tokens // TILE
        half_sum = jnp.where(
            (lax.broadcasted_iota(jnp.int32, (8, PAIR), 1) // HEAD)
            == lax.broadcasted_iota(jnp.int32, (8, PAIR), 0),
            1.0,
            0.0,
        )
        overlap = do_scr[:, cols].astype(SINGLE) * o_ref[:, cols].astype(SINGLE)
        deltas = lax.dot_general(
            half_sum,
            overlap,
            NT,
            precision=lax.Precision.HIGHEST,
            preferred_element_type=SINGLE,
        )
        grad_q = [[None] * tiles for _ in range(2)]
        for part in range(tiles):
            keys = slice(part * TILE, (part + 1) * TILE)
            queries = slice(part * TILE, tokens)
            k_t, v_t = k_ref[keys, cols], v_ref[keys, cols]
            q_t, do_t = q_ref[queries, cols], do_scr[queries, cols]
            grad_k, grad_v = [], []
            for h in range(2):
                scores = mm(k_t * masks[h], q_t, NT) + bias_scr[keys, queries]
                log_total = lse_ref[pl.ds(2 * i + h, 1), queries]
                probs = jnp.exp(scores - log_total)
                grad_p = mm(v_t * masks[h], do_t, NT)
                grad_s = (probs * (grad_p - deltas[h : h + 1, queries])).astype(HALF)
                grad_v.append(mm(probs.astype(HALF), do_t))
                grad_k.append(mm(grad_s, q_t))
                step = mm(grad_s, k_t, TN)
                for t in range(part, tiles):
                    piece = step[(t - part) * TILE : (t - part + 1) * TILE, :]
                    grad_q[h][t] = piece if grad_q[h][t] is None else grad_q[h][t] + piece
            dv_ref[keys, cols] = jnp.where(low, grad_v[0], grad_v[1]).astype(HALF)
            dk_ref[keys, cols] = jnp.where(low, grad_k[0], grad_k[1]).astype(HALF)
        for t in range(tiles):
            both = jnp.where(low, grad_q[0][t], grad_q[1][t]) * HEAD ** (-0.5)
            dq_ref[t * TILE : (t + 1) * TILE, cols] = both.astype(HALF)

    @pl.loop(0, tokens // TILE)
    def _(i):
        rows = pl.ds(pl.multiple_of(i * TILE, TILE), TILE)
        unit_rows, inverse = norm_rows(x_ref[rows, :].astype(SINGLE))
        grad = mm(dq_ref[rows, :], wq_ref[...], NT)
        grad = grad + mm(dk_ref[rows, :], wk_ref[...], NT)
        grad = grad + mm(dv_ref[rows, :], wv_ref[...], NT)
        small_ref[rows16 + 2 : rows16 + 3, :] += jnp.sum(grad * unit_rows, 0, keepdims=True)
        small_ref[rows16 + 3 : rows16 + 4, :] += jnp.sum(grad, 0, keepdims=True)
        part = norm_back(grad, unit_rows, inverse, gain_one)
        xgrad_ref[rows, :] = (dx1_scr[rows, :] + part).astype(HALF)


def weights_kernel(*refs):
    ins, dw_ref = refs[:-1], refs[-1]
    micro = len(ins) // 6
    width = dw_ref.shape[-1]

    @pl.loop(0, width // TILE)
    def _(i):
        cols = pl.ds(pl.multiple_of(i * TILE, TILE), TILE)
        for part in range(4):
            total = weight_grad(ins, micro, part, cols)
            dw_ref[part, cols, :] = total.astype(HALF)


def weight_grad(ins, micro, part, cols):
    total = None
    for m in range(micro):
        a1, o, dq, dk, dv, db = ins[6 * m : 6 * m + 6]
        left = o if part == 3 else a1
        right = (dq, dk, dv, db)[part]
        step = mm(left[:, cols], right[...], TN)
        total = step if total is None else total + step
    return total


def meet(peers):
    barrier = pltpu.get_barrier_semaphore()
    for peer in peers:
        pl.semaphore_signal(barrier, inc=1, device_id=peer, device_id_type=pl.DeviceIdType.MESH)
    return barrier


def remote(source, target, peer, send_sem, recv_sem, at):
    return pltpu.make_async_remote_copy(
        src_ref=source,
        dst_ref=target,
        send_sem=send_sem.at[at],
        recv_sem=recv_sem.at[at],
        device_id=peer,
        device_id_type=pl.DeviceIdType.MESH,
    )


def reduce_peers(z, x, y, c, zs, xs, cs):
    places = [(z, x, y, 1 - c), (z, 1 - x, y, c), (z, x, 1 - y, c)]
    places += [((z + step) % zs, x, y, c) for step in range(1, zs)]
    return [(zz * xs + xx, yy * cs + cc) for zz, xx, yy, cc in places]


def reduce_body(
    micro, ins, smalls, out_ref, tiny_ref, pay, got, tiny, tiny_got, send_sem, recv_sem, middle=None
):
    zs, xs, ys, cs, rows_all, width = pay.shape
    rows = rows_all // 4
    pair = 2 * rows
    dp, ex = lax.axis_index("dp"), lax.axis_index("expert")
    z, x, y, c = dp // xs, dp % xs, ex // cs, ex % cs

    def device(zz, xx, yy, cc):
        return (zz * xs + xx, yy * cs + cc)

    others = [(z + step) % zs for step in range(1, zs)]
    core = device(z, x, y, 1 - c)
    side = device(z, 1 - x, y, c)
    deep = device(z, x, 1 - y, c)
    column = [device(zz, x, y, c) for zz in others]
    count = [0]

    def send(source, target, peer):
        copy = remote(source, target, peer, send_sem, recv_sem, count[0])
        count[0] += 1
        copy.start()
        return copy

    def produce(parts, base):
        tile = 16 * rows
        for j in range(width // tile):
            cols = slice(j * tile, (j + 1) * tile)
            for at, part in enumerate(parts):
                total = weight_grad(ins, micro, part, cols).astype(HALF)
                for i in range(16):
                    number = 16 * j + i
                    place = (
                        number // (ys * cs) // xs,
                        number // (ys * cs) % xs,
                        number % (ys * cs) // cs,
                        number % cs,
                    )
                    pay[place + (slice(base + at * rows, base + (at + 1) * rows),)] = total[
                        i * rows : (i + 1) * rows, :
                    ]

    def add(place, band, held):
        pay[place + (band,)] = (
            pay[place + (band,)].astype(SINGLE) + held[...].astype(SINGLE)
        ).astype(HALF)

    top, low = pl.ds(0, pair), pl.ds(pair, pair)
    core_a, core_b, deep_a, side_b, side_a, col_b, col_a, deep_b = got
    total = smalls[0][...]
    for ref in smalls[1:]:
        total = total + ref[...]
    tiny[...] = total

    produce((3, 2), 0)
    first = send(pay.at[:, :, :, 1 - c, top], core_a, core)
    tiny_core = send(tiny, tiny_got.at[0], core)
    produce((0, 1), pair)
    second = send(pay.at[:, :, :, 1 - c, low], core_b, core)
    if middle is not None:
        middle()

    first.wait()

    @pl.loop(0, zs)
    def _(i):
        for xx in range(xs):
            for yy in range(ys):
                add((i, xx, yy, c), top, core_a.at[i, xx, yy])

    third = send(pay.at[:, :, 1 - y, c, top], deep_a, deep)
    tiny_core.wait()
    tiny[...] += tiny_got[0]
    tiny_deep = send(tiny, tiny_got.at[1], deep)
    second.wait()

    @pl.loop(0, zs)
    def _(i):
        for xx in range(xs):
            for yy in range(ys):
                add((i, xx, yy, c), low, core_b.at[i, xx, yy])

    fourth = send(pay.at[:, 1 - x, :, c, low], side_b, side)
    tiny_deep.wait()
    tiny[...] += tiny_got[1]
    tiny_side = send(tiny, tiny_got.at[2], side)

    third.wait()

    @pl.loop(0, zs)
    def _(i):
        for xx in range(xs):
            add((i, xx, y, c), top, deep_a.at[i, xx])

    fifth = send(pay.at[:, 1 - x, y, c, top], side_a, side)
    tiny_side.wait()
    tiny[...] += tiny_got[2]
    tiny_col = [send(tiny, tiny_got.at[3 + i], peer) for i, peer in enumerate(column)]

    fourth.wait()

    @pl.loop(0, zs)
    def _(i):
        for yy in range(ys):
            add((i, x, yy, c), low, side_b.at[i, yy])

    sixth = [
        send(pay.at[zz, x, :, c, low], col_b.at[i], peer)
        for i, (zz, peer) in enumerate(zip(others, column))
    ]
    fifth.wait()

    @pl.loop(0, zs)
    def _(i):
        add((i, x, y, c), top, side_a.at[i])

    seventh = [
        send(pay.at[zz, x, y, c, top], col_a.at[i], peer)
        for i, (zz, peer) in enumerate(zip(others, column))
    ]
    for copy in sixth:
        copy.wait()
    for yy in range(ys):
        place = (z, x, yy, c, low)
        total = pay[place].astype(SINGLE)
        for i in range(zs - 1):
            total = total + col_b[i, yy].astype(SINGLE)
        pay[place] = total.astype(HALF)
    eighth = send(pay.at[z, x, 1 - y, c, low], deep_b, deep)
    for copy in seventh:
        copy.wait()
    total = pay[z, x, y, c, 0:pair].astype(SINGLE)
    for i in range(zs - 1):
        total = total + col_a[i].astype(SINGLE)
    out_ref[3] = total[0:rows]
    out_ref[2] = total[rows:pair]
    for copy in tiny_col:
        copy.wait()
    total = tiny[...]
    for i in range(zs - 1):
        total = total + tiny_got[3 + i]
    tiny_ref[...] = total
    eighth.wait()
    total = pay[z, x, y, c, pair : 2 * pair].astype(SINGLE) + deep_b[...].astype(SINGLE)
    out_ref[0] = total[0:rows]
    out_ref[1] = total[rows:pair]


def front_kernel(
    capacity,
    experts,
    frozen,
    ends_ref,
    routes_t_ref,
    mask_ref,
    norms_ref,
    wr_ref,
    tokens_ref,
    cot_ref,
    wq_any,
    wk_any,
    wv_any,
    wo_any,
    fin_any,
    fout_any,
    nin_any,
    nout_any,
    a1_any,
    q_any,
    k_any,
    v_any,
    o_any,
    x1_any,
    a2_any,
    lse_ref,
    info_ref,
    cols_ref,
    probs_ref,
    froz_any,
    ret_any,
    done_any,
    dw_any,
    all_w,
    local_w,
    stage,
    arrived,
    ret_stage,
    send_sem,
    recv_sem,
    own_sem,
):
    micro, tok, width = tokens_ref.shape
    zs, xs, cs = 4, 2, 2
    shard = nin_any.shape[2]
    dp, ex = lax.axis_index("dp"), lax.axis_index("expert")
    z, x, y, c = dp // xs, dp % xs, ex // cs, ex % cs
    me = y * xs + x
    owners = experts - frozen

    def device(zz, xx, yy, cc):
        return (zz * xs + xx, yy * cs + cc)

    def near(step):
        return z + 1 - 2 * (z % 2) if step == 1 else (zs - 1 - z if step == 3 else (z + 2) % zs)

    core = device(z, x, y, 1 - c)
    swapped = device(z, c, y, x)
    one, three = device(near(1), c, y, x), device(near(3), c, y, x)
    straight = device(near(1), x, y, c)
    others = [(x + (d & 1)) % 2 + xs * ((y + (d >> 1)) % 2) for d in (3, 2, 1)]
    row_peers = [device(z, other % xs, other // xs, c) for other in others]
    fourth = device(z + (near(1) - z) * ((x + c + 1) % 2), c, y, x)
    peers = [core, one, three, straight, fourth] + row_peers
    pl.semaphore_wait(meet(peers), len(peers))

    def link(source, target, peer, at):
        return remote(source, target, peer, send_sem, recv_sem, at)

    spread = [
        link(local_w, all_w.at[dp], swapped, 0),
        link(local_w, all_w.at[dp], one, 1),
        link(local_w, all_w.at[dp], three, 2),
    ]
    keep_own = pltpu.make_async_copy(local_w, all_w.at[dp], own_sem.at[0])
    far = near(3) * xs + c
    onward = link(all_w.at[far], all_w.at[far], straight, 3)
    order = [z, near(1), near(3), near(2)]
    across = [
        link(all_w.at[zz * xs + c], all_w.at[zz * xs + c], core, 4 + i)
        for i, zz in enumerate(order)
    ]
    rows_out = [
        [
            link(
                stage.at[:, m * owners + other],
                arrived.at[:, m * owners + me],
                peer,
                8 + 3 * m + i,
            )
            for i, (other, peer) in enumerate(zip(others, row_peers))
        ]
        for m in range(micro)
    ]
    rows_own = [
        pltpu.make_async_copy(
            stage.at[:, m * owners + me], arrived.at[:, m * owners + me], own_sem.at[1 + m]
        )
        for m in range(micro)
    ]
    results_out = [
        link(ret_stage.at[other], ret_any.at[me], peer, 14 + i)
        for i, (other, peer) in enumerate(zip(others, row_peers))
    ]
    results_own = pltpu.make_async_copy(ret_stage.at[me], ret_any.at[me], own_sem.at[3])

    def first_half(
        w_scr,
        x_scr,
        dy_scr,
        a1_scr,
        q_scr,
        k_scr,
        v_scr,
        o_scr,
        x1_scr,
        a2_scr,
        bias_scr,
        lse_scr,
        froz_rows,
        win_scr,
        wout_scr,
        acc_scr,
        nin_scr,
        in_sem,
        out_sem,
        stream_sem,
    ):
        def load(source, target, at):
            copy = pltpu.make_async_copy(source, target, in_sem.at[at])
            copy.start()
            return copy

        nout_scr = x1_scr.at[1, pl.ds(0, shard)]
        new_loads = [load(nin_any.at[0], nin_scr, 0), load(nout_any.at[0], nout_scr, 1)]
        row_loads = [
            [
                load(tokens_ref.at[m], x_scr.at[m], 2 + 2 * m),
                load(cot_ref.at[m], dy_scr.at[m], 3 + 2 * m),
            ]
            for m in range(micro)
        ]
        weight_loads = [
            load(ref, w_scr.at[i], 2 + 2 * micro + i)
            for i, ref in enumerate((wq_any, wk_any, wv_any, wo_any))
        ]
        for copy in new_loads:
            copy.wait()
        local_w[0] = jnp.transpose(nin_scr[...]).astype(HALF)
        local_w[1] = nout_scr[...].astype(HALF)
        spread[1].start()
        spread[2].start()

        @pl.when(x != c)
        def _():
            spread[0].start()

        @pl.when(x == c)
        def _():
            keep_own.start()

        blocks = fin_any.shape[2] // width

        def stream(step, slot):
            e, f = step // blocks, step % blocks
            at = pl.ds(pl.multiple_of(f * width, width), width)
            return (
                pltpu.make_async_copy(
                    fin_any.at[e, :, at], win_scr.at[slot], stream_sem.at[0, slot]
                ),
                pltpu.make_async_copy(
                    fout_any.at[e, at, :], wout_scr.at[slot], stream_sem.at[1, slot]
                ),
            )

        for copy in stream(0, 0):
            copy.start()
        for copy in weight_loads + row_loads[0]:
            copy.wait()
        saves = []
        for m in range(micro):
            if m:
                for copy in row_loads[m]:
                    copy.wait()

            def target(e, part, m=m):
                if e < frozen:
                    return froz_rows.at[part, e, m]
                return stage.at[part, m * owners + e - frozen]

            attend_body(
                capacity,
                experts,
                target,
                ends_ref.at[m],
                x_scr.at[m],
                dy_scr.at[m],
                routes_t_ref.at[m],
                mask_ref.at[m],
                norms_ref,
                w_scr.at[0],
                w_scr.at[1],
                w_scr.at[2],
                w_scr.at[3],
                wr_ref,
                a1_scr.at[m],
                q_scr.at[m],
                k_scr.at[m],
                v_scr.at[m],
                o_scr.at[m],
                x1_scr.at[m],
                a2_scr.at[m],
                lse_ref.at[m],
                info_ref.at[m],
                cols_ref.at[m],
                probs_ref.at[m],
                bias_scr,
                lse_scr,
            )
            for copy in rows_out[m]:
                copy.start()
            rows_own[m].start()
            for i, (source, target_any) in enumerate(
                (
                    (a1_scr, a1_any),
                    (q_scr, q_any),
                    (k_scr, k_any),
                    (v_scr, v_any),
                    (o_scr, o_any),
                    (x1_scr, x1_any),
                    (a2_scr, a2_any),
                )
            ):
                copy = pltpu.make_async_copy(
                    source.at[m], target_any.at[m], out_sem.at[7 * m + i]
                )
                copy.start()
                saves.append(copy)
            if m == 0:

                @pl.when(x != c)
                def _():
                    spread[0].wait_recv()

                @pl.when(x == c)
                def _():
                    keep_own.wait()

                across[0].start()

        steps = frozen * blocks

        @pl.loop(0, steps)
        def _(step):
            slot = step % 2
            e = step // blocks

            @pl.when(step + 1 < steps)
            def _():
                for copy in stream(step + 1, 1 - slot):
                    copy.start()

            for copy in stream(step, slot):
                copy.wait()
            expert_step(
                lambda rows: froz_rows[0, e].reshape(micro * capacity, width)[...],
                lambda rows: froz_rows[1, e].reshape(micro * capacity, width)[...],
                micro * capacity,
                win_scr[slot],
                wout_scr[slot],
                NN,
                acc_scr,
                None,
                step % blocks == 0,
                micro * capacity,
            )

            @pl.when(step % blocks == blocks - 1)
            def _():
                for m in range(micro):
                    for part in range(2):
                        froz_rows[part, e, m] = acc_scr[
                            part, m * capacity : (m + 1) * capacity, :
                        ].astype(HALF)

            @pl.when(step == steps // 2)
            def _():
                spread[1].wait_recv()
                spread[2].wait_recv()
                onward.start()
                across[1].start()
                across[2].start()

        last = pltpu.make_async_copy(froz_rows, froz_any, out_sem.at[7 * micro])
        last.start()
        for copy in saves:
            copy.wait()
        last.wait()

    pl.run_scoped(
        first_half,
        pltpu.VMEM((4, width, width), HALF),
        pltpu.VMEM((micro, tok, width), HALF),
        pltpu.VMEM((micro, tok, width), HALF),
        pltpu.VMEM((micro, tok, width), HALF),
        pltpu.VMEM((micro, tok, width), HALF),
        pltpu.VMEM((micro, tok, width), HALF),
        pltpu.VMEM((micro, tok, width), HALF),
        pltpu.VMEM((micro, tok, width), HALF),
        pltpu.VMEM((micro, tok, width), SINGLE),
        pltpu.VMEM((micro, tok, width), HALF),
        pltpu.VMEM((tok, tok), SINGLE),
        pltpu.VMEM((tok, 128), SINGLE),
        pltpu.VMEM((2, frozen, micro, capacity, width), HALF),
        pltpu.VMEM((2, width, width), HALF),
        pltpu.VMEM((2, width, width), HALF),
        pltpu.VMEM((2, micro * capacity, width), SINGLE),
        pltpu.VMEM((width, shard), SINGLE),
        pltpu.SemaphoreType.DMA((2 + 2 * micro + 4,)),
        pltpu.SemaphoreType.DMA((7 * micro + 1,)),
        pltpu.SemaphoreType.DMA((2, 2)),
    )

    rows_one = owners * capacity
    rows_all = micro * rows_one

    def second_half(xt_scr, dyt_scr, acc_scr, held, current, dw_stage, held_sem, dw_sem):
        def rows_of(part, m):
            def get(rows):
                return arrived[part, pl.ds(m * owners + 2 * rows, 2)].reshape(2 * capacity, width)

            return get

        def weights(i):
            two = all_w.at[pl.ds(order[i] * xs, xs)]
            return (
                two[:, 0].reshape(xs * shard, width),
                two[:, 1].reshape(xs * shard, width),
            )

        rows_own[0].wait()
        for copy in rows_out[0]:
            copy.wait_recv()
        for i in range(zs):
            if i < 3:
                across[i].wait_recv()
            else:
                across[3].wait_recv()
            w_in, w_out = weights(i)
            expert_step(
                rows_of(0, 0),
                rows_of(1, 0),
                rows_one,
                w_in,
                w_out,
                NT,
                acc_scr,
                held.at[:, i],
                i == 0,
                2 * capacity,
            )
            if i == 1:
                onward.wait_recv()
                across[3].start()
        for other in range(owners):
            for part in range(2):
                ret_stage[other, part] = acc_scr[
                    part, other * capacity : (other + 1) * capacity, :
                ].astype(HALF)
        for copy in results_out:
            copy.start()
        results_own.start()

        rows_own[1].wait()
        for copy in rows_out[1]:
            copy.wait_recv()
        for at in range(0, width, 128):
            for part, scr in enumerate((xt_scr, dyt_scr)):
                scr[at : at + 128, :] = jnp.transpose(
                    arrived[part, :, :, at : at + 128].reshape(rows_all, 128)
                )
        dw_copies = []
        for i in range(zs):
            slot = i % 2
            fetch = [
                pltpu.make_async_copy(
                    held.at[part, i], current.at[part, pl.ds(0, rows_one)], held_sem.at[part]
                )
                for part in range(2)
            ]
            for copy in fetch:
                copy.start()
            w_in, w_out = weights(i)
            expert_step(
                rows_of(0, 1),
                rows_of(1, 1),
                rows_one,
                w_in,
                w_out,
                NT,
                acc_scr,
                current.at[:, pl.ds(rows_one, rows_one)],
                i == 0,
                2 * capacity,
            )
            for copy in fetch:
                copy.wait()
            if i >= 2:
                dw_copies[i - 2].wait()

            @pl.loop(0, width // TILE)
            def _(r):
                rows = pl.ds(pl.multiple_of(r * TILE, TILE), TILE)
                for part, left in enumerate((xt_scr, dyt_scr)):
                    total = mm(left[rows, :], current[1 - part]).astype(HALF)
                    for g in range(xs):
                        dw_stage[slot, g, part, rows, :] = total[:, g * shard : (g + 1) * shard]

            copy = pltpu.make_async_copy(
                dw_stage.at[slot], dw_any.at[pl.ds(order[i] * xs, xs)], dw_sem.at[slot]
            )
            copy.start()
            dw_copies.append(copy)
        for copy in results_out:
            copy.wait_send()
        results_own.wait()
        for other in range(owners):
            for part in range(2):
                ret_stage[other, part] = acc_scr[
                    part, other * capacity : (other + 1) * capacity, :
                ].astype(HALF)
        final = pltpu.make_async_copy(ret_stage, done_any, held_sem.at[0])
        final.start()
        dw_copies[zs - 2].wait()
        dw_copies[zs - 1].wait()
        final.wait()

    pl.run_scoped(
        second_half,
        pltpu.VMEM((width, rows_all), HALF),
        pltpu.VMEM((width, rows_all), HALF),
        pltpu.VMEM((2, rows_one, width), SINGLE),
        pltpu.VMEM((2, zs, rows_one, xs * shard), HALF),
        pltpu.VMEM((2, rows_all, xs * shard), HALF),
        pltpu.VMEM((2, xs, 2, width, shard), HALF),
        pltpu.SemaphoreType.DMA((2,)),
        pltpu.SemaphoreType.DMA((2,)),
    )

    @pl.when(x != c)
    def _():
        spread[0].wait_send()

    spread[1].wait_send()
    spread[2].wait_send()
    onward.wait_send()
    for copy in across:
        copy.wait_send()
    for m in range(micro):
        for copy in rows_out[m]:
            copy.wait_send()
    for copy in results_out:
        copy.wait_recv()


def tail_kernel(
    capacity,
    experts,
    frozen,
    ends_ref,
    routes_t_ref,
    norms_ref,
    wr_ref,
    lse_ref,
    info_ref,
    cols_ref,
    probs_ref,
    tokens_ref,
    cot_ref,
    wq_any,
    wk_any,
    wv_any,
    wo_any,
    a1_any,
    q_any,
    k_any,
    v_any,
    o_any,
    x1_any,
    a2_any,
    froz_any,
    ret_any,
    done_any,
    dw_any,
    mixed_any,
    xgrad_any,
    shared_ref,
    tiny_ref,
    wgrad_any,
    w_scr,
    rows_scr,
    x1_scr,
    db_scr,
    comb,
    small_scr,
    bias_scr,
    dx1_scr,
    do_scr,
    delta_scr,
    part_w,
    land_core,
    land_near,
    land_far,
    land_side,
    wgrad_scr,
    pay,
    got,
    tiny,
    tiny_got,
    send_sem,
    recv_sem,
    red_send,
    red_recv,
    in_sem,
    out_sem,
):
    micro, tok, width = tokens_ref.shape
    zs, xs, ys, cs = 4, 2, 2, 2
    dp, ex = lax.axis_index("dp"), lax.axis_index("expert")
    z, x, y, c = dp // xs, dp % xs, ex // cs, ex % cs
    me = y * xs + x
    owners = experts - frozen

    def device(zz, xx, yy, cc):
        return (zz * xs + xx, yy * cs + cc)

    z1, z2, z3 = z + 1 - 2 * (z % 2), (z + 2) % zs, zs - 1 - z
    others = [(x + (d & 1)) % 2 + xs * ((y + (d >> 1)) % 2) for d in (3, 2, 1)]
    row_peers = [device(z, other % xs, other // xs, c) for other in others]
    core = device(z, x, y, 1 - c)
    straight = device(z1, x, y, c)
    swapped, crossed = device(z, c, y, x), device(z3, c, y, x)
    fourth = device(z + (z1 - z) * ((x + c + 1) % 2), c, y, x)
    peers = row_peers + [crossed, fourth] + reduce_peers(z, x, y, c, zs, xs, cs)
    pl.semaphore_wait(meet(peers), len(peers))

    def link(source, target, peer, at):
        return remote(source, target, peer, send_sem, recv_sem, at)

    results_out = [
        link(done_any.at[other], comb.at[1, :, frozen + me], peer, i)
        for i, (other, peer) in enumerate(zip(others, row_peers))
    ]
    halves = link(dw_any.at[:, 1 - c], land_core, core, 3)
    near_far = link(part_w.at[z2], land_near.at[1], straight, 4)
    near_own = link(part_w.at[z1], land_near.at[0], straight, 5)
    far_sum = link(part_w.at[z3], land_far, crossed, 6)
    side_sum = link(part_w.at[z], land_side, swapped, 7)

    for copy in results_out:
        copy.start()
    halves.start()

    def load(source, target, at):
        copy = pltpu.make_async_copy(source, target, in_sem.at[at])
        copy.start()
        return copy

    loads = []
    for m in range(micro):
        group = []
        for i, source in enumerate(
            (tokens_ref, cot_ref, q_any, k_any, v_any, o_any, a2_any, a1_any)
        ):
            group.append(load(source.at[m], rows_scr.at[i, m], 16 * m + i))
        group.append(load(x1_any.at[m], x1_scr.at[m], 16 * m + 8))
        group.append(load(froz_any.at[:, :, m], comb.at[m, :, pl.ds(0, frozen)], 16 * m + 9))
        if m == 0:
            for e in range(owners):
                group.append(load(ret_any.at[e], comb.at[0, :, frozen + e], 10 + e))
            for i, source in enumerate((wq_any, wk_any, wv_any, wo_any)):
                group.append(load(source, w_scr.at[i], 32 + i))
            mine = load(dw_any.at[:, c], part_w, 14)
        else:
            group.append(load(done_any.at[me], comb.at[1, :, frozen + me], 16 * m + 10))
        loads.append(group)

    def add_rows(target, source):
        @pl.loop(0, target.shape[0])
        def _(part):
            @pl.loop(0, target.shape[1] // 128)
            def _(i):
                rows = pl.ds(pl.multiple_of(i * 128, 128), 128)
                target[part, rows, :] = (
                    target[part, rows, :].astype(SINGLE) + source[part, rows, :].astype(SINGLE)
                ).astype(HALF)

    def after_core():
        mine.wait()
        halves.wait()
        for zz in (z2, z1, z3, z):
            add_rows(part_w.at[zz], land_core.at[zz])
        near_far.start()
        near_own.start()

    def after_near():
        near_far.wait()
        add_rows(part_w.at[z3], land_near.at[1])
        far_sum.start()

    def after_own():
        near_own.wait()
        add_rows(part_w.at[z], land_near.at[0])

        @pl.when(x != c)
        def _():
            side_sum.start()

    outs = []
    for m in range(micro):
        for copy in loads[m]:
            copy.wait()
        if m == 1:
            for copy in results_out:
                copy.wait()
        x_ref, dy_ref, q_ref, k_ref, v_ref, o_ref, a2_ref, a1_ref = [
            rows_scr.at[i, m] for i in range(8)
        ]
        back_body(
            capacity,
            experts,
            after_core if m == 0 else after_near,
            ends_ref.at[m],
            x_ref,
            dy_ref,
            routes_t_ref.at[m],
            norms_ref,
            w_scr.at[0],
            w_scr.at[1],
            w_scr.at[2],
            w_scr.at[3],
            wr_ref,
            q_ref,
            k_ref,
            v_ref,
            o_ref,
            x1_scr.at[m],
            a2_ref,
            lse_ref.at[m],
            info_ref.at[m],
            cols_ref.at[m],
            probs_ref.at[m],
            a2_ref,
            x_ref,
            q_ref,
            k_ref,
            v_ref,
            db_scr.at[m],
            small_scr.at[m],
            comb.at[m, 0],
            comb.at[m, 1],
            bias_scr,
            dx1_scr,
            do_scr,
            delta_scr,
        )
        for i, (source, target) in enumerate(((a2_ref, mixed_any), (x_ref, xgrad_any))):
            copy = pltpu.make_async_copy(source, target.at[m], out_sem.at[2 * m + i])
            copy.start()
            outs.append(copy)

    ins = []
    for m in range(micro):
        ins += [rows_scr.at[i, m] for i in (7, 5, 2, 3, 4)] + [db_scr.at[m]]
    reduce_body(
        micro,
        ins,
        [small_scr.at[m] for m in range(micro)],
        shared_ref,
        tiny_ref,
        pay,
        got,
        tiny,
        tiny_got,
        red_send,
        red_recv,
        after_own,
    )

    for copy in outs:
        copy.wait()
    far_sum.wait()

    @pl.when(x != c)
    def _():
        side_sum.wait()

    @pl.loop(0, 2)
    def _(part):
        @pl.loop(0, width // 128)
        def _(i):
            rows = pl.ds(pl.multiple_of(i * 128, 128), 128)
            base = land_far[part, rows, :].astype(SINGLE)

            @pl.when(x != c)
            def _():
                wgrad_scr[part, rows, :] = base + land_side[part, rows, :].astype(SINGLE)

            @pl.when(x == c)
            def _():
                wgrad_scr[part, rows, :] = base + part_w[z, part, rows, :].astype(SINGLE)

    done = pltpu.make_async_copy(wgrad_scr, wgrad_any, out_sem.at[2 * micro])
    done.start()
    done.wait()


def vmem(count):
    return [pl.BlockSpec(memory_space=pltpu.VMEM)] * count


def params(mib, **more):
    return pltpu.CompilerParams(vmem_limit_bytes=mib << 20, **more)


def general(
    tokens,
    routes,
    lengths,
    key_mask,
    gain_one,
    bias_one,
    w_query,
    w_key,
    w_value,
    w_output,
    gain_two,
    bias_two,
    w_router,
    frozen_in,
    frozen_out,
    new_in,
    new_out,
    cotangent,
):
    micro, tok, width = tokens.shape
    owners = lax.axis_size("expert")
    dp = lax.axis_size("dp")
    frozen, _, ff = frozen_in.shape
    experts = frozen + owners
    capacity = 10 * tok // (4 * experts) // 8 * 8
    shard = new_in.shape[2]
    slots_all = experts * capacity
    shape = jax.ShapeDtypeStruct
    smem = pl.BlockSpec(memory_space=pltpu.SMEM)

    local_w = jnp.stack([new_in[0].T.astype(HALF), new_out[0].astype(HALF)], 0)
    all_w = lax.all_gather(local_w, "dp", axis=0, tiled=False)

    ends = jnp.cumsum(lengths[:, 0], axis=1).astype(jnp.int32)
    routes_t = jnp.swapaxes(routes, 1, 2)
    norms = jnp.stack([gain_one, bias_one, gain_two, bias_two], 0)
    rows16 = 16
    router_t = jnp.zeros((rows16, width), HALF).at[:experts].set(w_router.T)

    saved, froz_sent, arrived = [], [], []
    for m in range(micro):
        outs = pl.pallas_call(
            functools.partial(attend_kernel, capacity, experts, frozen),
            out_shape=[shape((tok, width), HALF)] * 5
            + [
                shape((tok, width), SINGLE),
                shape((tok, width), HALF),
                shape((16, tok), SINGLE),
                shape((8, tok), SINGLE),
                shape((tok, 128), SINGLE),
                shape((rows16, tok), SINGLE),
                shape((frozen, 2, capacity, width), HALF),
                shape((owners, 2, capacity, width), HALF),
            ],
            in_specs=[smem] + vmem(10),
            out_specs=vmem(13),
            scratch_shapes=[pltpu.VMEM((tok, tok), SINGLE), pltpu.VMEM((tok, 128), SINGLE)],
            compiler_params=params(56),
            cost_estimate=pl.CostEstimate(
                flops=8_000_000_000, bytes_accessed=20_000_000, transcendentals=3_000_000
            ),
            name="attend",
        )(
            ends[m],
            tokens[m],
            cotangent[m],
            routes_t[m],
            key_mask[m][None, :],
            norms,
            w_query,
            w_key,
            w_value,
            w_output,
            router_t,
        )
        saved.append(outs[:11])
        froz_sent.append(outs[11])
        arrived.append(
            lax.all_to_all(outs[12], "expert", split_axis=0, concat_axis=0, tiled=True)
        )

    block = min(768, ff)
    rows_spec = pl.BlockSpec((1, 2, capacity, width), lambda e, f: (e, 0, 0, 0))
    froz_back = pl.pallas_call(
        frozen_kernel,
        grid=(frozen, ff // block),
        out_shape=[shape((frozen, 2, capacity, width), HALF)] * 2,
        in_specs=[
            rows_spec,
            rows_spec,
            pl.BlockSpec((1, width, block), lambda e, f: (e, 0, f)),
            pl.BlockSpec((1, block, width), lambda e, f: (e, f, 0)),
        ],
        out_specs=[rows_spec, rows_spec],
        scratch_shapes=[
            pltpu.VMEM((2 * capacity, width), HALF),
            pltpu.VMEM((2 * capacity, width), HALF),
            pltpu.VMEM((2, 2 * capacity, width), SINGLE),
        ],
        compiler_params=params(50),
        cost_estimate=pl.CostEstimate(
            flops=16_000_000_000, bytes_accessed=25_000_000, transcendentals=2_500_000
        ),
        name="frozen",
    )(froz_sent[0], froz_sent[1], frozen_in, frozen_out)

    rows_all = micro * owners * capacity
    group = max(1, 768 // shard)
    whole = pl.BlockSpec((owners, 2, capacity, width), lambda f: (0, 0, 0, 0))
    done0, done1, grads_w = pl.pallas_call(
        owned_kernel,
        grid=(dp // group,),
        out_shape=[shape((owners, 2, capacity, width), HALF)] * 2
        + [shape((dp, 2, width, shard), HALF)],
        in_specs=[whole, whole, pl.BlockSpec((group, 2, shard, width), lambda f: (f, 0, 0, 0))],
        out_specs=[whole, whole, pl.BlockSpec((group, 2, width, shard), lambda f: (f, 0, 0, 0))],
        scratch_shapes=[
            pltpu.VMEM((rows_all, width), HALF),
            pltpu.VMEM((rows_all, width), HALF),
            pltpu.VMEM((width, rows_all), HALF),
            pltpu.VMEM((width, rows_all), HALF),
            pltpu.VMEM((2, rows_all, width), SINGLE),
            pltpu.VMEM((2, rows_all, group * shard), HALF),
        ],
        compiler_params=params(60),
        cost_estimate=pl.CostEstimate(
            flops=47_000_000_000, bytes_accessed=35_000_000, transcendentals=5_000_000
        ),
        name="owned",
    )(arrived[0], arrived[1], all_w)

    returned = [
        lax.all_to_all(one, "expert", split_axis=0, concat_axis=0, tiled=True)
        for one in (done0, done1)
    ]
    summed_w = lax.psum_scatter(grads_w, "dp", scatter_dimension=0, tiled=True)[0]

    mixed_list, xgrad_list, small_list, weight_ins = [], [], [], []
    for m in range(micro):
        a1, q, k, v, o, x1, a2, lse, info, cols, probs = saved[m]
        mixed, xgrad, dq, dk, dv, db, small = pl.pallas_call(
            functools.partial(back_kernel, capacity, experts),
            out_shape=[shape((tok, width), HALF)] * 6 + [shape((rows16 + 8, width), SINGLE)],
            in_specs=[smem] + vmem(21),
            out_specs=vmem(7),
            scratch_shapes=[
                pltpu.VMEM((slots_all, width), HALF),
                pltpu.VMEM((slots_all, width), HALF),
                pltpu.VMEM((tok, tok), SINGLE),
                pltpu.VMEM((tok, width), SINGLE),
                pltpu.VMEM((tok, width), HALF),
                pltpu.VMEM((tok, 128), SINGLE),
            ],
            compiler_params=params(56),
            cost_estimate=pl.CostEstimate(
                flops=16_000_000_000, bytes_accessed=25_000_000, transcendentals=3_000_000
            ),
            name="back",
        )(
            ends[m],
            tokens[m],
            cotangent[m],
            routes_t[m],
            norms,
            w_query,
            w_key,
            w_value,
            w_output,
            router_t,
            q,
            k,
            v,
            o,
            x1,
            a2,
            lse,
            info,
            cols,
            probs,
            froz_back[m],
            returned[m],
        )
        mixed_list.append(mixed)
        xgrad_list.append(xgrad)
        small_list.append(small)
        weight_ins += [a1, o, dq, dk, dv, db]

    grads = pl.pallas_call(
        weights_kernel,
        out_shape=shape((4, width, width), HALF),
        in_specs=vmem(len(weight_ins)),
        out_specs=vmem(1)[0],
        compiler_params=params(50),
        name="weights",
    )(*weight_ins)
    shared = lax.psum_scatter(grads, ("dp", "expert"), scatter_dimension=1, tiled=True)
    shared = shared.astype(SINGLE)
    small = sum(small_list[1:], small_list[0])
    small = jnp.concatenate([small[:experts], small[rows16 : rows16 + 4]], 0).T
    small = lax.psum_scatter(small, ("dp", "expert"), scatter_dimension=0, tiled=True)
    return (
        jnp.stack(mixed_list, 0),
        jnp.stack(xgrad_list, 0),
        small[:, experts + 2],
        small[:, experts + 3],
        shared[0],
        shared[1],
        shared[2],
        shared[3],
        small[:, experts],
        small[:, experts + 1],
        small[:, :experts],
        summed_w[0].astype(SINGLE)[None],
        summed_w[1].astype(SINGLE).T[None],
    )


def fused(
    tokens,
    routes,
    lengths,
    key_mask,
    gain_one,
    bias_one,
    w_query,
    w_key,
    w_value,
    w_output,
    gain_two,
    bias_two,
    w_router,
    frozen_in,
    frozen_out,
    new_in,
    new_out,
    cotangent,
):
    micro, tok, width = tokens.shape
    owners = lax.axis_size("expert")
    dp = lax.axis_size("dp")
    frozen = frozen_in.shape[0]
    experts = frozen + owners
    capacity = 10 * tok // (4 * experts) // 8 * 8
    shard = new_in.shape[2]
    zs, xs, ys, cs = 4, 2, 2, 2
    shape = jax.ShapeDtypeStruct
    smem = pl.BlockSpec(memory_space=pltpu.SMEM)

    def anywhere(count):
        return [pl.BlockSpec(memory_space=pl.ANY)] * count

    ends = jnp.cumsum(lengths[:, 0], axis=1).astype(jnp.int32)
    routes_t = jnp.swapaxes(routes, 1, 2)
    norms = jnp.stack([gain_one, bias_one, gain_two, bias_two], 0)
    rows16 = 16
    router_t = jnp.zeros((rows16, width), HALF).at[:experts].set(w_router.T)
    dma = pltpu.SemaphoreType.DMA

    outs = pl.pallas_call(
        functools.partial(front_kernel, capacity, experts, frozen),
        out_shape=[shape((micro, tok, width), HALF)] * 5
        + [
            shape((micro, tok, width), SINGLE),
            shape((micro, tok, width), HALF),
            shape((micro, 16, tok), SINGLE),
            shape((micro, 8, tok), SINGLE),
            shape((micro, tok, 128), SINGLE),
            shape((micro, rows16, tok), SINGLE),
            shape((2, frozen, micro, capacity, width), HALF),
            shape((owners, 2, capacity, width), HALF),
            shape((owners, 2, capacity, width), HALF),
            shape((dp, 2, width, shard), HALF),
        ],
        in_specs=[smem] + vmem(4) + anywhere(10),
        out_specs=anywhere(7) + vmem(4) + anywhere(4),
        scratch_shapes=[
            pltpu.VMEM((dp, 2, shard, width), HALF),
            pltpu.VMEM((2, shard, width), HALF),
            pltpu.VMEM((2, micro * owners, capacity, width), HALF),
            pltpu.VMEM((2, micro * owners, capacity, width), HALF),
            pltpu.VMEM((owners, 2, capacity, width), HALF),
            dma((17,)),
            dma((17,)),
            dma((4,)),
        ],
        compiler_params=params(63, collective_id=1, has_side_effects=True),
        name="front",
    )(
        ends,
        routes_t,
        key_mask[:, None, :],
        norms,
        router_t,
        tokens,
        cotangent,
        w_query,
        w_key,
        w_value,
        w_output,
        frozen_in,
        frozen_out,
        new_in,
        new_out,
    )
    a1, q, k, v, o, x1, a2, lse, info, cols, probs, froz, ret, done, dw = outs
    rows = width // (dp * owners)
    pair = 2 * rows
    landing = [(zs, xs, ys), (zs, xs, ys), (zs, xs), (zs, ys), (zs,), (zs - 1, ys), (zs - 1,), ()]
    mixed, xgrad, shared, small, wgrad = pl.pallas_call(
        functools.partial(tail_kernel, capacity, experts, frozen),
        out_shape=[
            shape((micro, tok, width), HALF),
            shape((micro, tok, width), HALF),
            shape((4, rows, width), SINGLE),
            shape((rows16 + 8, width), SINGLE),
            shape((2, width, shard), SINGLE),
        ],
        in_specs=[smem] + vmem(7) + anywhere(17),
        out_specs=anywhere(2) + vmem(2) + anywhere(1),
        scratch_shapes=[
            pltpu.VMEM((4, width, width), HALF),
            pltpu.VMEM((8, micro, tok, width), HALF),
            pltpu.VMEM((micro, tok, width), SINGLE),
            pltpu.VMEM((micro, tok, width), HALF),
            pltpu.VMEM((micro, 2, experts, capacity, width), HALF),
            pltpu.VMEM((micro, rows16 + 8, width), SINGLE),
            pltpu.VMEM((tok, tok), SINGLE),
            pltpu.VMEM((tok, width), SINGLE),
            pltpu.VMEM((tok, width), HALF),
            pltpu.VMEM((tok, 128), SINGLE),
            pltpu.VMEM((zs, 2, width, shard), HALF),
            pltpu.VMEM((zs, 2, width, shard), HALF),
            pltpu.VMEM((2, 2, width, shard), HALF),
            pltpu.VMEM((2, width, shard), HALF),
            pltpu.VMEM((2, width, shard), HALF),
            pltpu.VMEM((2, width, shard), SINGLE),
            pltpu.VMEM((zs, xs, ys, cs, 4 * rows, width), HALF),
            [pltpu.VMEM(lead + (pair, width), HALF) for lead in landing],
            pltpu.VMEM((rows16 + 8, width), SINGLE),
            pltpu.VMEM((zs + 2, rows16 + 8, width), SINGLE),
            dma((8,)),
            dma((8,)),
            dma((18,)),
            dma((18,)),
            dma((36,)),
            dma((2 * micro + 1,)),
        ],
        compiler_params=params(63, collective_id=2, has_side_effects=True),
        name="tail",
    )(
        ends,
        routes_t,
        norms,
        router_t,
        lse,
        info,
        cols,
        probs,
        tokens,
        cotangent,
        w_query,
        w_key,
        w_value,
        w_output,
        a1,
        q,
        k,
        v,
        o,
        x1,
        a2,
        froz,
        ret,
        done,
        dw.reshape(zs, xs, 2, width, shard),
    )
    at = (lax.axis_index("dp") * owners + lax.axis_index("expert")) * rows
    small = lax.dynamic_slice_in_dim(small, at, rows, 1)
    return (
        mixed,
        xgrad,
        small[rows16 + 2],
        small[rows16 + 3],
        shared[0],
        shared[1],
        shared[2],
        shared[3],
        small[rows16],
        small[rows16 + 1],
        small[:experts].T,
        wgrad[0][None],
        wgrad[1].T[None],
    )


def solution(mesh):
    both = ("dp", "expert")
    small_slice = mesh.shape["dp"] == 8 and mesh.shape["expert"] == 4
    return jax.shard_map(
        fused if small_slice else general,
        mesh=mesh,
        in_specs=(
            P(None, both, None),
            P(None, both, None),
            P(None, both, None),
            P(None, both),
        )
        + (P(),) * 11
        + (P("expert", None, "dp"), P("expert", "dp", None), P(None, both, None)),
        out_specs=(P(None, both, None), P(None, both, None), P(both), P(both))
        + (P(both, None),) * 4
        + (P(both), P(both), P(both, None), P("expert", None, "dp"), P("expert", "dp", None)),
        check_vma=False,
    )
```

```python
import functools

import jax
import jax.numpy as jnp
from jax import lax
from jax.experimental import pallas as pl
from jax.experimental.pallas import tpu as pltpu
from jax.sharding import PartitionSpec as P

HEAD = 64
PAIR = 2 * HEAD
TILE = 256
EPS = 1e-05
HALF = jnp.bfloat16
SINGLE = jnp.float32
HIDDEN = -1000000000.0
GELU_C = 0.7978845608028654
GELU_A = 0.044715

NN = (((1,), (0,)), ((), ()))
NT = (((1,), (1,)), ((), ()))
TN = (((0,), (0,)), ((), ()))


def mm(a, b, dims=NN):
    return lax.dot_general(a, b, dims, preferred_element_type=SINGLE)


def norm_rows(values):
    center = values - jnp.mean(values, -1, keepdims=True)
    inverse = lax.rsqrt(jnp.mean(center * center, -1, keepdims=True) + EPS)
    return center * inverse, inverse


def norm_back(grad, unit_rows, inverse, gain):
    scaled = grad * gain
    return inverse * (
        scaled
        - jnp.mean(scaled, -1, keepdims=True)
        - unit_rows * jnp.mean(scaled * unit_rows, -1, keepdims=True)
    )


def doc_of(places, lengths_ref):
    doc = jnp.zeros(places.shape, jnp.int32)
    end = 0
    for i in range(lengths_ref.shape[0]):
        end = end + lengths_ref[i]
        doc = doc + jnp.where(places >= end, 1, 0)
    return doc


def half_masks(rows):
    lane = lax.broadcasted_iota(jnp.int32, (rows, PAIR), 1)
    first = jnp.where(lane < HEAD, 1.0, 0.0).astype(HALF)
    second = jnp.where(lane < HEAD, 0.0, 1.0).astype(HALF)
    return lane < HEAD, (first, second)


def route_hots(routes_t_ref, rows, tokens):
    sub = lax.broadcasted_iota(jnp.int32, (rows, tokens), 0)
    return [sub == routes_t_ref[pick : pick + 1, :] for pick in range(2)]


def attend_kernel(capacity, experts, frozen, *refs):
    froz_ref, send_ref, bias_scr, lse_scr = refs[-4:]

    def target(e, part):
        return froz_ref.at[e, part] if e < frozen else send_ref.at[e - frozen, part]

    attend_body(capacity, experts, target, *refs[:-4], bias_scr, lse_scr)


def attend_body(
    capacity,
    experts,
    target,
    lengths_ref,
    x_ref,
    dy_ref,
    routes_t_ref,
    mask_ref,
    norms_ref,
    wq_ref,
    wk_ref,
    wv_ref,
    wo_ref,
    wr_ref,
    a1_ref,
    q_ref,
    k_ref,
    v_ref,
    o_ref,
    x1_ref,
    a2_ref,
    lse_ref,
    info_ref,
    cols_ref,
    probs_ref,
    bias_scr,
    lse_scr,
):
    tokens, width = x_ref.shape
    chunk = 128
    gain_one, bias_one = norms_ref[0:1, :], norms_ref[1:2, :]
    gain_two, bias_two = norms_ref[2:3, :], norms_ref[3:4, :]

    @pl.loop(0, tokens // chunk)
    def _(i):
        rows = pl.ds(pl.multiple_of(i * chunk, chunk), chunk)
        unit_rows, _ = norm_rows(x_ref[rows, :].astype(SINGLE))
        a1_ref[rows, :] = (unit_rows * gain_one + bias_one).astype(HALF)
        here = lax.broadcasted_iota(jnp.int32, (chunk, 1), 0) + i * chunk
        there = lax.broadcasted_iota(jnp.int32, (1, tokens), 1)
        same = doc_of(here, lengths_ref) == doc_of(there, lengths_ref)
        keep = (mask_ref[...] == 1) | (there == here)
        visible = same & (there <= here) & keep
        bias_scr[rows, :] = jnp.where(visible, 0.0, HIDDEN)

    @pl.loop(0, tokens // TILE)
    def _(i):
        rows = pl.ds(pl.multiple_of(i * TILE, TILE), TILE)
        a1 = a1_ref[rows, :]
        q_ref[rows, :] = (mm(a1, wq_ref[...]).astype(HALF) * HEAD ** (-0.5)).astype(HALF)
        k_ref[rows, :] = mm(a1, wk_ref[...]).astype(HALF)
        v_ref[rows, :] = mm(a1, wv_ref[...]).astype(HALF)

    lse_scr[...] = jnp.zeros_like(lse_scr)

    @pl.loop(0, width // PAIR)
    def _(i):
        cols = pl.ds(pl.multiple_of(i * PAIR, PAIR), PAIR)
        low, masks = half_masks(TILE)
        lane = lax.broadcasted_iota(jnp.int32, (TILE, 128), 1)
        for part in range(tokens // TILE):
            rows = slice(part * TILE, (part + 1) * TILE)
            keys = (part + 1) * TILE
            q_t = q_ref[rows, cols]
            k_t = k_ref[0:keys, cols]
            v_t = v_ref[0:keys, cols]
            results = []
            for h in range(2):
                scores = mm(q_t * masks[h], k_t, NT) + bias_scr[rows, 0:keys]
                top = jnp.max(scores, -1, keepdims=True)
                expo = jnp.exp(scores - top)
                total = jnp.sum(expo, -1, keepdims=True)
                results.append(mm(expo.astype(HALF), v_t) * (1.0 / total))
                log_total = top + jnp.log(total)
                lse_scr[rows, :] = jnp.where(lane == 2 * i + h, log_total, lse_scr[rows, :])
            o_ref[rows, cols] = jnp.where(low, results[0], results[1]).astype(HALF)

    lse_ref[...] = jnp.transpose(lse_scr[...])[0 : lse_ref.shape[0], :]

    @pl.loop(0, tokens // TILE)
    def _(i):
        rows = pl.ds(pl.multiple_of(i * TILE, TILE), TILE)
        x1 = x_ref[rows, :].astype(SINGLE) + mm(o_ref[rows, :], wo_ref[...])
        x1_ref[rows, :] = x1
        unit_rows, _ = norm_rows(x1)
        a2_ref[rows, :] = (unit_rows * gain_two + bias_two).astype(HALF)

    rows16 = wr_ref.shape[0]
    logits = mm(wr_ref[...], a2_ref[...], NT)
    sub = lax.broadcasted_iota(jnp.int32, (rows16, tokens), 0)
    logits = jnp.where(sub < experts, logits, -1e30)
    expo = jnp.exp(logits - jnp.max(logits, 0, keepdims=True))
    probs = expo / jnp.sum(expo, 0, keepdims=True)
    probs_ref[...] = probs
    hots = route_hots(routes_t_ref, rows16, tokens)
    chosen = [jnp.sum(jnp.where(hot, probs, 0.0), 0, keepdims=True) for hot in hots]
    chosen_total = chosen[0] + chosen[1]
    gates = [one / chosen_total for one in chosen]
    upper = jnp.where(
        lax.broadcasted_iota(jnp.int32, (tokens, tokens), 0)
        < lax.broadcasted_iota(jnp.int32, (tokens, tokens), 1),
        1.0,
        0.0,
    ).astype(HALF)
    both = jnp.where(hots[0] | hots[1], 1.0, 0.0).astype(HALF)
    earlier = mm(both, upper)
    places = []
    for pick in range(2):
        slot = jnp.sum(jnp.where(hots[pick], earlier, 0.0), 0, keepdims=True)
        first = routes_t_ref[pick : pick + 1, :].astype(SINGLE) * capacity
        places.append(jnp.where(slot < capacity, first + slot, -1.0))
    info = jnp.concatenate(
        places + gates + [mask_ref[...].astype(SINGLE), chosen_total, chosen_total, chosen_total], 0
    )
    info_ref[...] = info
    cols_ref[...] = jnp.transpose(
        jnp.concatenate([info, jnp.zeros((128 - info.shape[0], tokens), SINGLE)], 0)
    )
    spots = [one.astype(jnp.int32) for one in places]
    for e in range(experts):
        slots = lax.broadcasted_iota(jnp.int32, (capacity, tokens), 0) + e * capacity
        hit = [slots == spots[pick] for pick in range(2)]
        place = jnp.where(hit[0] | hit[1], 1.0, 0.0).astype(HALF)
        weight = jnp.sum(
            jnp.where(hit[0], gates[0], 0.0) + jnp.where(hit[1], gates[1], 0.0), 1, keepdims=True
        )
        target(e, 0)[...] = mm(place, a2_ref[...]).astype(HALF)
        target(e, 1)[...] = (mm(place, dy_ref[...]) * weight).astype(HALF)


def expert_step(x_of, dy_of, total, w_in, w_out, in_dims, acc_scr, held, first, chunk):
    back_dims = NT if in_dims == NN else NN

    @pl.loop(0, total // chunk)
    def _(i):
        rows = pl.ds(pl.multiple_of(i * chunk, 16), chunk)
        pre = mm(x_of(i), w_in, in_dims)
        grad = mm(dy_of(i), w_out, NT)
        square = pre * pre
        tanh = jnp.tanh(GELU_C * pre * (1.0 + GELU_A * square))
        plus = 0.5 * (1.0 + tanh)
        hidden = (pre * plus).astype(HALF)
        slope = plus + 0.5 * pre * (1.0 - tanh * tanh) * (GELU_C * (1.0 + 3.0 * GELU_A * square))
        grad_pre = (grad * slope).astype(HALF)
        if held is not None:
            held[0, rows, :] = hidden
            held[1, rows, :] = grad_pre
        out = mm(hidden, w_out)
        back = mm(grad_pre, w_in, back_dims)
        if first is True:
            acc_scr[0, rows, :] = out
            acc_scr[1, rows, :] = back
        elif first is False:
            acc_scr[0, rows, :] += out
            acc_scr[1, rows, :] += back
        else:

            @pl.when(first)
            def _():
                acc_scr[0, rows, :] = out
                acc_scr[1, rows, :] = back

            @pl.when(jnp.logical_not(first))
            def _():
                acc_scr[0, rows, :] += out
                acc_scr[1, rows, :] += back


def frozen_kernel(
    r0_ref, r1_ref, win_ref, wout_ref, o0_ref, o1_ref, x_scr, dy_scr, acc_scr
):
    capacity = r0_ref.shape[2]
    step, last = pl.program_id(1), pl.num_programs(1) - 1

    @pl.when(step == 0)
    def _():
        for m, ref in enumerate((r0_ref, r1_ref)):
            x_scr[m * capacity : (m + 1) * capacity, :] = ref[0, 0]
            dy_scr[m * capacity : (m + 1) * capacity, :] = ref[0, 1]

    expert_step(
        lambda i: x_scr[...],
        lambda i: dy_scr[...],
        2 * capacity,
        win_ref[0],
        wout_ref[0],
        NN,
        acc_scr,
        None,
        step == 0,
        2 * capacity,
    )

    @pl.when(step == last)
    def _():
        for m, ref in enumerate((o0_ref, o1_ref)):
            for part in range(2):
                ref[0, part] = acc_scr[part, m * capacity : (m + 1) * capacity, :].astype(HALF)


def owned_kernel(
    r0_ref,
    r1_ref,
    w_ref,
    o0_ref,
    o1_ref,
    dw_ref,
    x_scr,
    dy_scr,
    xt_scr,
    dyt_scr,
    acc_scr,
    held_scr,
):
    sources, _, capacity, width = r0_ref.shape
    group, _, shard, _ = w_ref.shape
    step, last = pl.program_id(0), pl.num_programs(0) - 1
    rows_all = x_scr.shape[0]

    @pl.when(step == 0)
    def _():
        for m, ref in enumerate((r0_ref, r1_ref)):
            for s in range(sources):
                at = (m * sources + s) * capacity
                x_scr[at : at + capacity, :] = ref[s, 0]
                dy_scr[at : at + capacity, :] = ref[s, 1]
        for at in range(0, width, 128):
            xt_scr[at : at + 128, :] = jnp.transpose(x_scr[:, at : at + 128])
            dyt_scr[at : at + 128, :] = jnp.transpose(dy_scr[:, at : at + 128])

    w_in = w_ref[:, 0].reshape(group * shard, width)
    w_out = w_ref[:, 1].reshape(group * shard, width)
    chunk = 2 * capacity
    expert_step(
        lambda i: x_scr[pl.ds(pl.multiple_of(i * chunk, 16), chunk), :],
        lambda i: dy_scr[pl.ds(pl.multiple_of(i * chunk, 16), chunk), :],
        rows_all,
        w_in,
        w_out,
        NT,
        acc_scr,
        held_scr,
        step == 0,
        chunk,
    )

    @pl.loop(0, width // TILE)
    def _(i):
        rows = pl.ds(pl.multiple_of(i * TILE, TILE), TILE)
        for part, (left, right) in enumerate(((xt_scr, held_scr.at[1]), (dyt_scr, held_scr.at[0]))):
            total = mm(left[rows, :], right[...]).astype(HALF)
            for g in range(group):
                dw_ref[g, part, rows, :] = total[:, g * shard : (g + 1) * shard]

    @pl.when(step == last)
    def _():
        for m, ref in enumerate((o0_ref, o1_ref)):
            for s in range(sources):
                at = (m * sources + s) * capacity
                for part in range(2):
                    ref[s, part] = acc_scr[part, at : at + capacity, :].astype(HALF)


def back_kernel(capacity, experts, *refs):
    froz_ref, back_ref = refs[20:22]
    mixed_ref, xgrad_ref, dq_ref, dk_ref, dv_ref, db_ref, small_ref = refs[22:29]
    out_scr, dbuf_scr = refs[29:31]
    frozen = froz_ref.shape[0]
    for e in range(experts):
        source = froz_ref.at[e] if e < frozen else back_ref.at[e - frozen]
        out_scr[e * capacity : (e + 1) * capacity, :] = source[0]
        dbuf_scr[e * capacity : (e + 1) * capacity, :] = source[1]
    dx1_scr = refs[32]
    back_body(capacity, experts, None, *refs[:20], mixed_ref, dx1_scr, *refs[24:])
    finish_body(
        refs[1],
        refs[4],
        *refs[5:8],
        dx1_scr,
        xgrad_ref,
        dq_ref,
        dk_ref,
        dv_ref,
        small_ref,
        refs[9].shape[0],
    )


def flat(ref):
    rows = ref[...]
    return rows if rows.ndim == 2 else rows.reshape(-1, rows.shape[-1])


def block_of(ref, e, rows):
    return ref[rows, :] if len(ref.shape) == 2 else ref[e]


def back_body(
    capacity,
    experts,
    middle,
    lengths_ref,
    x_ref,
    dy_ref,
    routes_t_ref,
    norms_ref,
    wq_ref,
    wk_ref,
    wv_ref,
    wo_ref,
    wr_ref,
    q_ref,
    k_ref,
    v_ref,
    o_ref,
    x1_ref,
    a2_ref,
    lse_ref,
    info_ref,
    cols_ref,
    probs_ref,
    mixed_ref,
    dx1_ref,
    dq_ref,
    dk_ref,
    dv_ref,
    db_ref,
    small_ref,
    out_scr,
    dbuf_scr,
    bias_scr,
    dx1_scr,
    do_scr,
    delta_scr,
):
    tokens, width = x_ref.shape
    gain_two = norms_ref[2:3, :]
    slots_all = experts * capacity

    spots = [info_ref[pick : pick + 1, :].astype(jnp.int32) for pick in range(2)]
    gates = [info_ref[2 + pick : 3 + pick, :] for pick in range(2)]
    chosen_total = info_ref[5:6, :]

    def gate_part(e, carry):
        rows = pl.ds(pl.multiple_of(e * capacity, 16), capacity)
        overlap = mm(block_of(out_scr, e, rows), dy_ref[...], NT)
        slots = lax.broadcasted_iota(jnp.int32, (capacity, tokens), 0) + e * capacity
        return tuple(
            carry[pick]
            + jnp.sum(jnp.where(slots == spots[pick], overlap, 0.0), 0, keepdims=True)
            for pick in range(2)
        )

    zero_row = jnp.zeros((1, tokens), SINGLE)
    gate_grads = lax.fori_loop(0, experts, gate_part, (zero_row, zero_row))
    rows16 = wr_ref.shape[0]
    hots = route_hots(routes_t_ref, rows16, tokens)
    weighted = gate_grads[0] * gates[0] + gate_grads[1] * gates[1]
    grad_probs = jnp.where(hots[0], (gate_grads[0] - weighted) / chosen_total, 0.0)
    grad_probs = grad_probs + jnp.where(hots[1], (gate_grads[1] - weighted) / chosen_total, 0.0)
    probs = probs_ref[...]
    grad_logits = probs * (grad_probs - jnp.sum(grad_probs * probs, 0, keepdims=True))
    logits_low = grad_logits.astype(HALF)
    small_ref[0:rows16, :] = mm(logits_low, a2_ref[...])
    small_ref[rows16:, :] = jnp.zeros_like(small_ref[rows16:, :])

    @pl.loop(0, tokens // TILE)
    def _(i):
        rows = pl.ds(pl.multiple_of(i * TILE, TILE), TILE)
        slots = lax.broadcasted_iota(jnp.int32, (TILE, slots_all), 1)
        hit = [slots == cols_ref[rows, pick : pick + 1].astype(jnp.int32) for pick in range(2)]
        gated = jnp.where(hit[0], cols_ref[rows, 2:3], 0.0)
        gated = jnp.where(hit[1], cols_ref[rows, 3:4], gated).astype(HALF)
        place = jnp.where(hit[0] | hit[1], 1.0, 0.0).astype(HALF)
        x1 = x1_ref[rows, :]
        mixed_ref[rows, :] = (x1 + mm(gated, flat(out_scr))).astype(HALF)
        dx1_scr[rows, :] = mm(place, flat(dbuf_scr))

    logits_col = jnp.transpose(
        jnp.concatenate([grad_logits, jnp.zeros((128 - rows16, tokens), SINGLE)], 0)
    )
    delta_scr[...] = logits_col.astype(HALF).astype(SINGLE)
    router = jnp.concatenate([wr_ref[...], jnp.zeros((128 - rows16, width), HALF)], 0)

    @pl.loop(0, tokens // TILE)
    def _(i):
        rows = pl.ds(pl.multiple_of(i * TILE, TILE), TILE)
        unit_rows, inverse = norm_rows(x1_ref[rows, :])
        grad = dx1_scr[rows, :] + mm(delta_scr[rows, :].astype(HALF), router)
        small_ref[rows16 : rows16 + 1, :] += jnp.sum(grad * unit_rows, 0, keepdims=True)
        small_ref[rows16 + 1 : rows16 + 2, :] += jnp.sum(grad, 0, keepdims=True)
        dx1 = dy_ref[rows, :].astype(SINGLE) + norm_back(grad, unit_rows, inverse, gain_two)
        dx1_ref[rows, :] = dx1
        branch = dx1.astype(HALF)
        db_ref[rows, :] = branch
        do_scr[rows, :] = mm(branch, wo_ref[...], NT).astype(HALF)

    if middle is not None:
        middle()

    @pl.loop(0, tokens // 128)
    def _(i):
        rows = pl.ds(pl.multiple_of(i * 128, 128), 128)
        key = lax.broadcasted_iota(jnp.int32, (128, 1), 0) + i * 128
        query = lax.broadcasted_iota(jnp.int32, (1, tokens), 1)
        same = doc_of(key, lengths_ref) == doc_of(query, lengths_ref)
        keep = (cols_ref[rows, 4:5] > 0.5) | (query == key)
        visible = same & (key <= query) & keep
        bias_scr[rows, :] = jnp.where(visible, 0.0, HIDDEN)

    @pl.loop(0, width // PAIR)
    def _(i):
        cols = pl.ds(pl.multiple_of(i * PAIR, PAIR), PAIR)
        low, masks = half_masks(TILE)
        tiles = tokens // TILE
        half_sum = jnp.where(
            (lax.broadcasted_iota(jnp.int32, (8, PAIR), 1) // HEAD)
            == lax.broadcasted_iota(jnp.int32, (8, PAIR), 0),
            1.0,
            0.0,
        )
        overlap = do_scr[:, cols].astype(SINGLE) * o_ref[:, cols].astype(SINGLE)
        deltas = lax.dot_general(
            half_sum,
            overlap,
            NT,
            precision=lax.Precision.HIGHEST,
            preferred_element_type=SINGLE,
        )
        grad_q = [[None] * tiles for _ in range(2)]
        for part in range(tiles):
            keys = slice(part * TILE, (part + 1) * TILE)
            queries = slice(part * TILE, tokens)
            k_t, v_t = k_ref[keys, cols], v_ref[keys, cols]
            q_t, do_t = q_ref[queries, cols], do_scr[queries, cols]
            grad_k, grad_v = [], []
            for h in range(2):
                scores = mm(k_t * masks[h], q_t, NT) + bias_scr[keys, queries]
                log_total = lse_ref[pl.ds(2 * i + h, 1), queries]
                probs = jnp.exp(scores - log_total)
                grad_p = mm(v_t * masks[h], do_t, NT)
                grad_s = (probs * (grad_p - deltas[h : h + 1, queries])).astype(HALF)
                grad_v.append(mm(probs.astype(HALF), do_t))
                grad_k.append(mm(grad_s, q_t))
                step = mm(grad_s, k_t, TN)
                for t in range(part, tiles):
                    piece = step[(t - part) * TILE : (t - part + 1) * TILE, :]
                    grad_q[h][t] = piece if grad_q[h][t] is None else grad_q[h][t] + piece
            dv_ref[keys, cols] = jnp.where(low, grad_v[0], grad_v[1]).astype(HALF)
            dk_ref[keys, cols] = jnp.where(low, grad_k[0], grad_k[1]).astype(HALF)
        for t in range(tiles):
            both = jnp.where(low, grad_q[0][t], grad_q[1][t]) * HEAD ** (-0.5)
            dq_ref[t * TILE : (t + 1) * TILE, cols] = both.astype(HALF)


def finish_body(
    x_ref, norms_ref, wq_ref, wk_ref, wv_ref, dx1_ref, xgrad_ref, dq_ref, dk_ref, dv_ref, small_ref, rows16
):
    tokens = x_ref.shape[0]
    gain_one = norms_ref[0:1, :]

    @pl.loop(0, tokens // TILE)
    def _(i):
        rows = pl.ds(pl.multiple_of(i * TILE, TILE), TILE)
        unit_rows, inverse = norm_rows(x_ref[rows, :].astype(SINGLE))
        grad = mm(dq_ref[rows, :], wq_ref[...], NT)
        grad = grad + mm(dk_ref[rows, :], wk_ref[...], NT)
        grad = grad + mm(dv_ref[rows, :], wv_ref[...], NT)
        small_ref[rows16 + 2 : rows16 + 3, :] += jnp.sum(grad * unit_rows, 0, keepdims=True)
        small_ref[rows16 + 3 : rows16 + 4, :] += jnp.sum(grad, 0, keepdims=True)
        part = norm_back(grad, unit_rows, inverse, gain_one)
        xgrad_ref[rows, :] = (dx1_ref[rows, :] + part).astype(HALF)


def weights_kernel(*refs):
    ins, dw_ref = refs[:-1], refs[-1]
    micro = len(ins) // 6
    width = dw_ref.shape[-1]

    @pl.loop(0, width // TILE)
    def _(i):
        cols = pl.ds(pl.multiple_of(i * TILE, TILE), TILE)
        for part in range(4):
            total = weight_grad(ins, micro, part, cols)
            dw_ref[part, cols, :] = total.astype(HALF)


def weight_grad(ins, micro, part, cols):
    total = None
    for m in range(micro):
        a1, o, dq, dk, dv, db = ins[6 * m : 6 * m + 6]
        left = o if part == 3 else a1
        right = (dq, dk, dv, db)[part]
        step = mm(left[:, cols], right[...], TN)
        total = step if total is None else total + step
    return total


def meet(peers):
    barrier = pltpu.get_barrier_semaphore()
    for peer in peers:
        pl.semaphore_signal(barrier, inc=1, device_id=peer, device_id_type=pl.DeviceIdType.MESH)
    return barrier


def remote(source, target, peer, send_sem, recv_sem, at):
    return pltpu.make_async_remote_copy(
        src_ref=source,
        dst_ref=target,
        send_sem=send_sem.at[at],
        recv_sem=recv_sem.at[at],
        device_id=peer,
        device_id_type=pl.DeviceIdType.MESH,
    )


def reduce_peers(z, x, y, c, zs, xs, cs):
    places = [(z, x, y, 1 - c), (z, 1 - x, y, c), (z, x, 1 - y, c)]
    places += [((z + step) % zs, x, y, c) for step in range(1, zs)]
    return [(zz * xs + xx, yy * cs + cc) for zz, xx, yy, cc in places]


def reduce_body(
    micro,
    ins,
    smalls,
    out_ref,
    tiny_ref,
    pay,
    got,
    tiny,
    tiny_got,
    send_sem,
    recv_sem,
    finish,
    after_own,
):
    zs, xs, ys, cs, rows_all, width = pay.shape
    rows = rows_all // 4
    pair = 2 * rows
    dp, ex = lax.axis_index("dp"), lax.axis_index("expert")
    z, x, y, c = dp // xs, dp % xs, ex // cs, ex % cs

    def device(zz, xx, yy, cc):
        return (zz * xs + xx, yy * cs + cc)

    others = [(z + step) % zs for step in range(1, zs)]
    core = device(z, x, y, 1 - c)
    side = device(z, 1 - x, y, c)
    deep = device(z, x, 1 - y, c)
    column = [device(zz, x, y, c) for zz in others]
    count = [0]

    def send(source, target, peer):
        copy = remote(source, target, peer, send_sem, recv_sem, count[0])
        count[0] += 1
        copy.start()
        return copy

    def produce(parts, base):
        tile = 16 * rows
        for j in range(width // tile):
            cols = slice(j * tile, (j + 1) * tile)
            for at, part in enumerate(parts):
                total = weight_grad(ins, micro, part, cols).astype(HALF)
                for i in range(16):
                    number = 16 * j + i
                    place = (
                        number // (ys * cs) // xs,
                        number // (ys * cs) % xs,
                        number % (ys * cs) // cs,
                        number % cs,
                    )
                    pay[place + (slice(base + at * rows, base + (at + 1) * rows),)] = total[
                        i * rows : (i + 1) * rows, :
                    ]

    def add(place, band, held):
        pay[place + (band,)] = (
            pay[place + (band,)].astype(SINGLE) + held[...].astype(SINGLE)
        ).astype(HALF)

    top, low = pl.ds(0, pair), pl.ds(pair, pair)
    core_a, core_b, deep_a, side_b, side_a, col_b, col_a, deep_b = got
    def add_all(count, places):
        @pl.loop(0, count)
        def _(i):
            for place, band, held in places(i):
                add(place, band, held)

    produce((3, 2), 0)
    first = send(pay.at[:, :, :, 1 - c, top], core_a, core)
    produce((0, 1), pair)
    second = send(pay.at[:, :, :, 1 - c, low], core_b, core)

    first.wait()
    add_all(
        zs,
        lambda i: [
            ((i, xx, yy, c), top, core_a.at[i, xx, yy]) for xx in range(xs) for yy in range(ys)
        ],
    )
    third = send(pay.at[:, :, 1 - y, c, top], deep_a, deep)
    second.wait()
    add_all(
        zs,
        lambda i: [
            ((i, xx, yy, c), low, core_b.at[i, xx, yy]) for xx in range(xs) for yy in range(ys)
        ],
    )
    fourth = send(pay.at[:, 1 - x, :, c, low], side_b, side)
    finish(0)

    third.wait()
    add_all(zs, lambda i: [((i, xx, y, c), top, deep_a.at[i, xx]) for xx in range(xs)])
    fifth = send(pay.at[:, 1 - x, y, c, top], side_a, side)
    fourth.wait()
    add_all(zs, lambda i: [((i, x, yy, c), low, side_b.at[i, yy]) for yy in range(ys)])
    sixth = [
        send(pay.at[zz, x, :, c, low], col_b.at[i], peer)
        for i, (zz, peer) in enumerate(zip(others, column))
    ]
    for m in range(1, micro):
        finish(m)
    total = smalls[0][...]
    for ref in smalls[1:]:
        total = total + ref[...]
    tiny[...] = total
    tiny_core = send(tiny, tiny_got.at[0], core)

    fifth.wait()
    add_all(zs, lambda i: [((i, x, y, c), top, side_a.at[i])])
    seventh = [
        send(pay.at[zz, x, y, c, top], col_a.at[i], peer)
        for i, (zz, peer) in enumerate(zip(others, column))
    ]
    tiny_core.wait()
    tiny[...] += tiny_got[0]
    tiny_deep = send(tiny, tiny_got.at[1], deep)
    after_own()
    tiny_deep.wait()
    tiny[...] += tiny_got[1]
    tiny_side = send(tiny, tiny_got.at[2], side)
    for copy in sixth:
        copy.wait()
    for yy in range(ys):
        place = (z, x, yy, c, low)
        total = pay[place].astype(SINGLE)
        for i in range(zs - 1):
            total = total + col_b[i, yy].astype(SINGLE)
        pay[place] = total.astype(HALF)
    eighth = send(pay.at[z, x, 1 - y, c, low], deep_b, deep)
    tiny_side.wait()
    tiny[...] += tiny_got[2]
    tiny_col = [send(tiny, tiny_got.at[3 + i], peer) for i, peer in enumerate(column)]
    for copy in seventh:
        copy.wait()
    total = pay[z, x, y, c, 0:pair].astype(SINGLE)
    for i in range(zs - 1):
        total = total + col_a[i].astype(SINGLE)
    out_ref[3] = total[0:rows]
    out_ref[2] = total[rows:pair]
    eighth.wait()
    total = pay[z, x, y, c, pair : 2 * pair].astype(SINGLE) + deep_b[...].astype(SINGLE)
    out_ref[0] = total[0:rows]
    out_ref[1] = total[rows:pair]
    for copy in tiny_col:
        copy.wait()
    total = tiny[...]
    for i in range(zs - 1):
        total = total + tiny_got[3 + i]
    tiny_ref[...] = total


def front_kernel(
    capacity,
    experts,
    frozen,
    lengths_ref,
    routes_t_ref,
    mask_ref,
    norms_ref,
    wr_ref,
    tokens_ref,
    cot_ref,
    wq_any,
    wk_any,
    wv_any,
    wo_any,
    fin_any,
    fout_any,
    nin_any,
    nout_any,
    a1_any,
    q_any,
    k_any,
    v_any,
    o_any,
    x1_any,
    a2_any,
    lse_ref,
    info_ref,
    cols_ref,
    probs_ref,
    froz_any,
    ret_any,
    done_any,
    dw_any,
    core_any,
    near_any,
    all_w,
    local_w,
    stage,
    arrived,
    ret_stage,
    send_sem,
    recv_sem,
    own_sem,
):
    micro, tok, width = tokens_ref.shape
    zs, xs, cs = 4, 2, 2
    shard = nin_any.shape[2]
    dp, ex = lax.axis_index("dp"), lax.axis_index("expert")
    z, x, y, c = dp // xs, dp % xs, ex // cs, ex % cs
    me = y * xs + x
    owners = experts - frozen

    def device(zz, xx, yy, cc):
        return (zz * xs + xx, yy * cs + cc)

    def near(step):
        return z + 1 - 2 * (z % 2) if step == 1 else (zs - 1 - z if step == 3 else (z + 2) % zs)

    core = device(z, x, y, 1 - c)
    swapped = device(z, c, y, x)
    straight, distant = device(near(1), x, y, c), device(near(3), x, y, c)
    others = [(x + (d & 1)) % 2 + xs * ((y + (d >> 1)) % 2) for d in (3, 2, 1)]
    row_peers = [device(z, other % xs, other // xs, c) for other in others]
    fourth = device(z + (near(1) - z) * ((x + c + 1) % 2), c, y, x)
    peers = [core, straight, distant, fourth] + row_peers
    pl.semaphore_wait(meet(peers), len(peers))

    def link(source, target, peer, at):
        return remote(source, target, peer, send_sem, recv_sem, at)

    held_w = all_w.at[z * xs + c]
    exchange = link(local_w, all_w.at[dp], swapped, 0)
    spread = [link(held_w, held_w, straight, 1), link(held_w, held_w, distant, 2)]
    spread_own = [link(local_w, held_w, straight, 1), link(local_w, held_w, distant, 2)]
    keep_own = pltpu.make_async_copy(local_w, all_w.at[dp], own_sem.at[0])
    far = near(3) * xs + c
    onward = link(all_w.at[far], all_w.at[far], straight, 3)
    order = [z, near(1), near(3), near(2)]
    across = [
        link(all_w.at[zz * xs + c], all_w.at[zz * xs + c], core, 4 + i)
        for i, zz in enumerate(order)
    ]
    rows_out = [
        [
            link(
                stage.at[:, m * owners + other],
                arrived.at[:, m * owners + me],
                peer,
                8 + 3 * m + i,
            )
            for i, (other, peer) in enumerate(zip(others, row_peers))
        ]
        for m in range(micro)
    ]
    rows_own = [
        pltpu.make_async_copy(
            stage.at[:, m * owners + me], arrived.at[:, m * owners + me], own_sem.at[1 + m]
        )
        for m in range(micro)
    ]
    results_out = [
        link(ret_stage.at[other], ret_any.at[me], peer, 14 + i)
        for i, (other, peer) in enumerate(zip(others, row_peers))
    ]
    results_own = pltpu.make_async_copy(ret_stage.at[me], ret_any.at[me], own_sem.at[3])
    near_half = link(dw_any.at[near(2), 0], near_any, straight, 21)

    def first_half(
        w_scr,
        x_scr,
        dy_scr,
        a1_scr,
        q_scr,
        k_scr,
        v_scr,
        o_scr,
        x1_scr,
        a2_scr,
        bias_scr,
        lse_scr,
        froz_rows,
        win_scr,
        wout_scr,
        acc_scr,
        nin_scr,
        in_sem,
        out_sem,
        stream_sem,
    ):
        def load(source, target, at):
            copy = pltpu.make_async_copy(source, target, in_sem.at[at])
            copy.start()
            return copy

        nout_scr = x1_scr.at[1, pl.ds(0, shard)]
        new_loads = [load(nin_any.at[0], nin_scr, 0), load(nout_any.at[0], nout_scr, 1)]
        row_loads = [
            [
                load(tokens_ref.at[m], x_scr.at[m], 2 + 2 * m),
                load(cot_ref.at[m], dy_scr.at[m], 3 + 2 * m),
            ]
            for m in range(micro)
        ]
        weight_loads = [
            load(ref, w_scr.at[i], 2 + 2 * micro + i)
            for i, ref in enumerate((wq_any, wk_any, wv_any, wo_any))
        ]
        for copy in new_loads:
            copy.wait()
        local_w[0] = jnp.transpose(nin_scr[...]).astype(HALF)
        local_w[1] = nout_scr[...].astype(HALF)

        @pl.when(x != c)
        def _():
            exchange.start()

        @pl.when(x == c)
        def _():
            keep_own.start()
            spread_own[1].start()
            spread_own[0].start()

        blocks = fin_any.shape[2] // width

        def stream(step, slot):
            e, f = step // blocks, step % blocks
            at = pl.ds(pl.multiple_of(f * width, width), width)
            return (
                pltpu.make_async_copy(
                    fin_any.at[e, :, at], win_scr.at[slot], stream_sem.at[0, slot]
                ),
                pltpu.make_async_copy(
                    fout_any.at[e, at, :], wout_scr.at[slot], stream_sem.at[1, slot]
                ),
            )

        for copy in stream(0, 0):
            copy.start()
        for copy in weight_loads + row_loads[0]:
            copy.wait()
        saves = []
        for m in range(micro):
            if m:
                for copy in row_loads[m]:
                    copy.wait()

            def target(e, part, m=m):
                if e < frozen:
                    return froz_rows.at[part, e, m]
                return stage.at[part, m * owners + e - frozen]

            attend_body(
                capacity,
                experts,
                target,
                lengths_ref.at[m],
                x_scr.at[m],
                dy_scr.at[m],
                routes_t_ref.at[m],
                mask_ref.at[pl.ds(m, 1)],
                norms_ref,
                w_scr.at[0],
                w_scr.at[1],
                w_scr.at[2],
                w_scr.at[3],
                wr_ref,
                a1_scr.at[m],
                q_scr.at[m],
                k_scr.at[m],
                v_scr.at[m],
                o_scr.at[m],
                x1_scr.at[m],
                a2_scr.at[m],
                lse_ref.at[m],
                info_ref.at[m],
                cols_ref.at[m],
                probs_ref.at[m],
                bias_scr,
                lse_scr,
            )
            for copy in rows_out[m]:
                copy.start()
            rows_own[m].start()
            for i, (source, target_any) in enumerate(
                (
                    (a1_scr, a1_any),
                    (q_scr, q_any),
                    (k_scr, k_any),
                    (v_scr, v_any),
                    (o_scr, o_any),
                    (x1_scr, x1_any),
                    (a2_scr, a2_any),
                )
            ):
                copy = pltpu.make_async_copy(
                    source.at[m], target_any.at[m], out_sem.at[7 * m + i]
                )
                copy.start()
                saves.append(copy)
            if m == 0:

                @pl.when(x != c)
                def _():
                    exchange.wait_recv()
                    spread[1].start()
                    spread[0].start()

                @pl.when(x == c)
                def _():
                    keep_own.wait()

                across[0].start()


        steps = frozen * blocks

        @pl.loop(0, steps)
        def _(step):
            slot = step % 2
            e = step // blocks

            @pl.when(step + 1 < steps)
            def _():
                for copy in stream(step + 1, 1 - slot):
                    copy.start()

            for copy in stream(step, slot):
                copy.wait()
            expert_step(
                lambda rows: froz_rows[0, e].reshape(micro * capacity, width)[...],
                lambda rows: froz_rows[1, e].reshape(micro * capacity, width)[...],
                micro * capacity,
                win_scr[slot],
                wout_scr[slot],
                NN,
                acc_scr,
                None,
                step % blocks == 0,
                micro * capacity,
            )

            @pl.when(step % blocks == blocks - 1)
            def _():
                for m in range(micro):
                    for part in range(2):
                        froz_rows[part, e, m] = acc_scr[
                            part, m * capacity : (m + 1) * capacity, :
                        ].astype(HALF)

            @pl.when(step == steps // 2)
            def _():
                spread[1].wait_recv()
                onward.start()
                across[2].start()

            @pl.when(step == steps // 2 + 1)
            def _():
                spread[0].wait_recv()
                across[1].start()

        last = pltpu.make_async_copy(froz_rows, froz_any, out_sem.at[7 * micro])
        last.start()
        for copy in saves:
            copy.wait()
        last.wait()

    pl.run_scoped(
        first_half,
        pltpu.VMEM((4, width, width), HALF),
        pltpu.VMEM((micro, tok, width), HALF),
        pltpu.VMEM((micro, tok, width), HALF),
        pltpu.VMEM((micro, tok, width), HALF),
        pltpu.VMEM((micro, tok, width), HALF),
        pltpu.VMEM((micro, tok, width), HALF),
        pltpu.VMEM((micro, tok, width), HALF),
        pltpu.VMEM((micro, tok, width), HALF),
        pltpu.VMEM((micro, tok, width), SINGLE),
        pltpu.VMEM((micro, tok, width), HALF),
        pltpu.VMEM((tok, tok), SINGLE),
        pltpu.VMEM((tok, 128), SINGLE),
        pltpu.VMEM((2, frozen, micro, capacity, width), HALF),
        pltpu.VMEM((2, width, width), HALF),
        pltpu.VMEM((2, width, width), HALF),
        pltpu.VMEM((2, micro * capacity, width), SINGLE),
        pltpu.VMEM((width, shard), SINGLE),
        pltpu.SemaphoreType.DMA((2 + 2 * micro + 4,)),
        pltpu.SemaphoreType.DMA((7 * micro + 1,)),
        pltpu.SemaphoreType.DMA((2, 2)),
    )

    rows_one = owners * capacity
    rows_all = micro * rows_one

    def second_half(
        xt_scr, dyt_scr, acc_scr, held, current, dw_stage, core_scr, held_sem, dw_sem, core_sem
    ):
        def rows_of(part, m):
            def get(rows):
                return arrived[part, pl.ds(m * owners + 2 * rows, 2)].reshape(2 * capacity, width)

            return get

        def weights(zz):
            two = all_w.at[pl.ds(zz * xs, xs)]
            return (
                two[:, 0].reshape(xs * shard, width),
                two[:, 1].reshape(xs * shard, width),
            )

        rows_own[0].wait()
        for copy in rows_out[0]:
            copy.wait_recv()
        for i in range(zs):
            if i < 3:
                across[i].wait_recv()
            else:
                across[3].wait_recv()
            w_in, w_out = weights(order[i])
            expert_step(
                rows_of(0, 0),
                rows_of(1, 0),
                rows_one,
                w_in,
                w_out,
                NT,
                acc_scr,
                held.at[:, i],
                i == 0,
                2 * capacity,
            )
            if i == 1:
                onward.wait_recv()
                across[3].start()
        for other in range(owners):
            for part in range(2):
                ret_stage[other, part] = acc_scr[
                    part, other * capacity : (other + 1) * capacity, :
                ].astype(HALF)
        for copy in results_out:
            copy.start()
        results_own.start()

        rows_own[1].wait()
        for copy in rows_out[1]:
            copy.wait_recv()
        for at in range(0, width, 128):
            for part, scr in enumerate((xt_scr, dyt_scr)):
                scr[at : at + 128, :] = jnp.transpose(
                    arrived[part, :, :, at : at + 128].reshape(rows_all, 128)
                )
        turn = [3, 1, 2, 0]
        halves = [
            link(dw_stage.at[i % 2, 1 - c], core_any.at[i], core, 17 + i) for i in range(zs)
        ]
        fetches = [
            pltpu.make_async_copy(core_any.at[i], core_scr, core_sem) for i in range(zs)
        ]
        writes = [
            pltpu.make_async_copy(
                dw_stage.at[i % 2, c], dw_any.at[order[turn[i]]], dw_sem.at[i % 2]
            )
            for i in range(zs)
        ]

        def add_core(i):
            fetches[i].wait()
            for part in range(2):

                @pl.loop(0, width // 128)
                def _(r):
                    rows = pl.ds(pl.multiple_of(r * 128, 128), 128)
                    dw_stage[i % 2, c, part, rows, :] = (
                        dw_stage[i % 2, c, part, rows, :].astype(SINGLE)
                        + core_scr[part, rows, :].astype(SINGLE)
                    ).astype(HALF)

            writes[i].start()

        for i in range(zs):
            slot = i % 2
            fetch = [
                pltpu.make_async_copy(
                    held.at[part, turn[i]], current.at[part, pl.ds(0, rows_one)], held_sem.at[part]
                )
                for part in range(2)
            ]
            for copy in fetch:
                copy.start()
            w_in, w_out = weights(order[turn[i]])
            expert_step(
                rows_of(0, 1),
                rows_of(1, 1),
                rows_one,
                w_in,
                w_out,
                NT,
                acc_scr,
                current.at[:, pl.ds(rows_one, rows_one)],
                i == 0,
                2 * capacity,
            )
            for copy in fetch:
                copy.wait()
            if i >= 1:
                halves[i - 1].wait_recv()
                fetches[i - 1].start()
            if i >= 2:
                halves[i - 2].wait_send()
                if i > 2:
                    writes[i - 2].wait()

            @pl.loop(0, width // TILE)
            def _(r):
                rows = pl.ds(pl.multiple_of(r * TILE, TILE), TILE)
                for part, left in enumerate((xt_scr, dyt_scr)):
                    total = mm(left[rows, :], current[1 - part]).astype(HALF)
                    for g in range(xs):
                        dw_stage[slot, g, part, rows, :] = total[:, g * shard : (g + 1) * shard]

            halves[i].start()
            if i >= 1:
                add_core(i - 1)
            if i == 1:
                writes[0].wait()
                near_half.start()
        for copy in results_out:
            copy.wait_send()
        results_own.wait()
        for other in range(owners):
            for part in range(2):
                ret_stage[other, part] = acc_scr[
                    part, other * capacity : (other + 1) * capacity, :
                ].astype(HALF)
        final = pltpu.make_async_copy(ret_stage, done_any, held_sem.at[0])
        final.start()
        halves[zs - 1].wait_recv()
        fetches[zs - 1].start()
        add_core(zs - 1)
        halves[zs - 2].wait_send()
        halves[zs - 1].wait_send()
        writes[zs - 2].wait()
        writes[zs - 1].wait()
        final.wait()

    pl.run_scoped(
        second_half,
        pltpu.VMEM((width, rows_all), HALF),
        pltpu.VMEM((width, rows_all), HALF),
        pltpu.VMEM((2, rows_one, width), SINGLE),
        pltpu.VMEM((2, zs, rows_one, xs * shard), HALF),
        pltpu.VMEM((2, rows_all, xs * shard), HALF),
        pltpu.VMEM((2, xs, 2, width, shard), HALF),
        pltpu.VMEM((2, width, shard), HALF),
        pltpu.SemaphoreType.DMA((2,)),
        pltpu.SemaphoreType.DMA((2,)),
        pltpu.SemaphoreType.DMA,
    )

    @pl.when(x != c)
    def _():
        exchange.wait_send()

    spread[0].wait_send()
    spread[1].wait_send()
    onward.wait_send()
    for copy in across:
        copy.wait_send()
    for m in range(micro):
        for copy in rows_out[m]:
            copy.wait_send()
    for copy in results_out:
        copy.wait_recv()
    near_half.wait()


def tail_kernel(
    capacity,
    experts,
    frozen,
    lengths_ref,
    routes_t_ref,
    norms_ref,
    wr_ref,
    lse_ref,
    info_ref,
    cols_ref,
    probs_ref,
    tokens_ref,
    cot_ref,
    wq_any,
    wk_any,
    wv_any,
    wo_any,
    a1_any,
    q_any,
    k_any,
    v_any,
    o_any,
    x1_any,
    a2_any,
    froz_any,
    ret_any,
    done_any,
    dw_any,
    near_any,
    mixed_any,
    xgrad_any,
    shared_ref,
    tiny_ref,
    gin_any,
    gout_any,
    w_scr,
    rows_scr,
    x1_scr,
    db_scr,
    comb,
    small_scr,
    bias_scr,
    dx1_scr,
    do_scr,
    delta_scr,
    part_w,
    near_scr,
    land_near,
    land_own,
    land_far,
    land_side,
    gin_scr,
    gout_scr,
    pay,
    got,
    tiny,
    tiny_got,
    send_sem,
    recv_sem,
    red_send,
    red_recv,
    in_sem,
    out_sem,
):
    micro, tok, width = tokens_ref.shape
    zs, xs, ys, cs = 4, 2, 2, 2
    dp, ex = lax.axis_index("dp"), lax.axis_index("expert")
    z, x, y, c = dp // xs, dp % xs, ex // cs, ex % cs
    me = y * xs + x
    owners = experts - frozen

    def device(zz, xx, yy, cc):
        return (zz * xs + xx, yy * cs + cc)

    z1, z2, z3 = z + 1 - 2 * (z % 2), (z + 2) % zs, zs - 1 - z
    others = [(x + (d & 1)) % 2 + xs * ((y + (d >> 1)) % 2) for d in (3, 2, 1)]
    row_peers = [device(z, other % xs, other // xs, c) for other in others]
    core = device(z, x, y, 1 - c)
    straight = device(z1, x, y, c)
    swapped, crossed = device(z, c, y, x), device(z3, c, y, x)
    fourth = device(z + (z1 - z) * ((x + c + 1) % 2), c, y, x)
    peers = row_peers + [crossed, fourth] + reduce_peers(z, x, y, c, zs, xs, cs)
    pl.semaphore_wait(meet(peers), len(peers))

    def link(source, target, peer, at):
        return remote(source, target, peer, send_sem, recv_sem, at)

    results_out = [
        link(done_any.at[other], comb.at[1, :, frozen + me], peer, i)
        for i, (other, peer) in enumerate(zip(others, row_peers))
    ]
    near_far = link(dw_any.at[z2, 1], land_near, straight, 3)
    near_own = link(dw_any.at[z1], land_own, straight, 4)
    far_sum = [link(part_w.at[0, i], land_far.at[i], crossed, 5 + i) for i in range(2)]
    side_sum = link(part_w.at[1], land_side, swapped, 7)

    near_far.start()
    for copy in results_out:
        copy.start()

    def load(source, target, at):
        copy = pltpu.make_async_copy(source, target, in_sem.at[at])
        copy.start()
        return copy

    loads = []
    for m in range(micro):
        group = []
        for i, source in enumerate(
            (tokens_ref, cot_ref, q_any, k_any, v_any, o_any, a2_any, a1_any)
        ):
            group.append(load(source.at[m], rows_scr.at[i, m], 16 * m + i))
        group.append(load(x1_any.at[m], x1_scr.at[m], 16 * m + 8))
        group.append(load(froz_any.at[:, :, m], comb.at[m, :, pl.ds(0, frozen)], 16 * m + 9))
        if m == 0:
            for e in range(owners):
                group.append(load(ret_any.at[e], comb.at[0, :, frozen + e], 10 + e))
            for i, source in enumerate((wq_any, wk_any, wv_any, wo_any)):
                group.append(load(source, w_scr.at[i], 32 + i))
            mine = [load(dw_any.at[z3], part_w.at[0], 14), load(near_any, near_scr, 15)]
            mine_last = load(dw_any.at[z], part_w.at[1], 36)
        else:
            group.append(load(done_any.at[me], comb.at[1, :, frozen + me], 16 * m + 10))
        loads.append(group)

    def add_rows(target, source):
        @pl.loop(0, width // 128)
        def _(i):
            rows = pl.ds(pl.multiple_of(i * 128, 128), 128)
            target[rows, :] = (
                target[rows, :].astype(SINGLE) + source[rows, :].astype(SINGLE)
            ).astype(HALF)

    def after_near():
        near_far.wait()
        add_rows(part_w.at[0, 1], land_near)
        far_sum[1].start()

    def after_own():
        near_own.wait()
        mine_last.wait()
        for i in range(2):
            add_rows(part_w.at[1, i], land_own.at[i])

        @pl.when(x != c)
        def _():
            side_sum.start()

    for copy in mine:
        copy.wait()
    add_rows(part_w.at[0, 0], near_scr)
    far_sum[0].start()
    outs = []
    for m in range(micro):
        for copy in loads[m]:
            copy.wait()
        if m == 1:
            for copy in results_out:
                copy.wait()
        x_ref, dy_ref, q_ref, k_ref, v_ref, o_ref, a2_ref, a1_ref = [
            rows_scr.at[i, m] for i in range(8)
        ]
        back_body(
            capacity,
            experts,
            near_own.start if m == 0 else None,
            lengths_ref.at[m],
            x_ref,
            dy_ref,
            routes_t_ref.at[m],
            norms_ref,
            w_scr.at[0],
            w_scr.at[1],
            w_scr.at[2],
            w_scr.at[3],
            wr_ref,
            q_ref,
            k_ref,
            v_ref,
            o_ref,
            x1_scr.at[m],
            a2_ref,
            lse_ref.at[m],
            info_ref.at[m],
            cols_ref.at[m],
            probs_ref.at[m],
            a2_ref,
            x1_scr.at[m],
            q_ref,
            k_ref,
            v_ref,
            db_scr.at[m],
            small_scr.at[m],
            comb.at[m, 0],
            comb.at[m, 1],
            bias_scr,
            dx1_scr,
            do_scr,
            delta_scr,
        )
        copy = pltpu.make_async_copy(a2_ref, mixed_any.at[m], out_sem.at[2 * m])
        copy.start()
        outs.append(copy)
        if m == 0:
            after_near()

    def finish(m):
        x_ref = rows_scr.at[0, m]
        finish_body(
            x_ref,
            norms_ref,
            w_scr.at[0],
            w_scr.at[1],
            w_scr.at[2],
            x1_scr.at[m],
            x_ref,
            rows_scr.at[2, m],
            rows_scr.at[3, m],
            rows_scr.at[4, m],
            small_scr.at[m],
            wr_ref.shape[0],
        )
        copy = pltpu.make_async_copy(x_ref, xgrad_any.at[m], out_sem.at[2 * m + 1])
        copy.start()
        outs.append(copy)

    ins = []
    for m in range(micro):
        ins += [rows_scr.at[i, m] for i in (7, 5, 2, 3, 4)] + [db_scr.at[m]]
    reduce_body(
        micro,
        ins,
        [small_scr.at[m] for m in range(micro)],
        shared_ref,
        tiny_ref,
        pay,
        got,
        tiny,
        tiny_got,
        red_send,
        red_recv,
        finish,
        after_own,
    )

    for copy in outs:
        copy.wait()
    for copy in far_sum:
        copy.wait()

    @pl.when(x != c)
    def _():
        side_sum.wait()

    def total_of(part, rows):
        base = land_far[part, rows, :].astype(SINGLE)
        own = part_w[1, part, rows, :].astype(SINGLE)
        other = land_side[part, rows, :].astype(SINGLE)
        return base + jnp.where(x == c, own, other)

    for i in range(0, width, 128):
        gin_scr[i : i + 128, :] = total_of(0, slice(i, i + 128))
        gout_scr[:, i : i + 128] = jnp.transpose(total_of(1, slice(i, i + 128)))
    done = [
        pltpu.make_async_copy(gin_scr, gin_any.at[0], out_sem.at[2 * micro]),
        pltpu.make_async_copy(gout_scr, gout_any.at[0], out_sem.at[2 * micro + 1]),
    ]
    for copy in done:
        copy.start()
    for copy in done:
        copy.wait()


def vmem(count):
    return [pl.BlockSpec(memory_space=pltpu.VMEM)] * count


def params(mib, **more):
    return pltpu.CompilerParams(vmem_limit_bytes=mib << 20, **more)


def general(
    tokens,
    routes,
    lengths,
    key_mask,
    gain_one,
    bias_one,
    w_query,
    w_key,
    w_value,
    w_output,
    gain_two,
    bias_two,
    w_router,
    frozen_in,
    frozen_out,
    new_in,
    new_out,
    cotangent,
):
    micro, tok, width = tokens.shape
    owners = lax.axis_size("expert")
    dp = lax.axis_size("dp")
    frozen, _, ff = frozen_in.shape
    experts = frozen + owners
    capacity = 10 * tok // (4 * experts) // 8 * 8
    shard = new_in.shape[2]
    slots_all = experts * capacity
    shape = jax.ShapeDtypeStruct
    smem = pl.BlockSpec(memory_space=pltpu.SMEM)

    local_w = jnp.stack([new_in[0].T.astype(HALF), new_out[0].astype(HALF)], 0)
    all_w = lax.all_gather(local_w, "dp", axis=0, tiled=False)

    routes_t = jnp.swapaxes(routes, 1, 2)
    norms = jnp.concatenate([gain_one, bias_one, gain_two, bias_two]).reshape(4, width)
    rows16 = 16
    router_t = jnp.pad(w_router.T, ((0, rows16 - experts), (0, 0)))

    saved, froz_sent, arrived = [], [], []
    for m in range(micro):
        outs = pl.pallas_call(
            functools.partial(attend_kernel, capacity, experts, frozen),
            out_shape=[shape((tok, width), HALF)] * 5
            + [
                shape((tok, width), SINGLE),
                shape((tok, width), HALF),
                shape((16, tok), SINGLE),
                shape((8, tok), SINGLE),
                shape((tok, 128), SINGLE),
                shape((rows16, tok), SINGLE),
                shape((frozen, 2, capacity, width), HALF),
                shape((owners, 2, capacity, width), HALF),
            ],
            in_specs=[smem] + vmem(10),
            out_specs=vmem(13),
            scratch_shapes=[pltpu.VMEM((tok, tok), SINGLE), pltpu.VMEM((tok, 128), SINGLE)],
            compiler_params=params(56),
            cost_estimate=pl.CostEstimate(
                flops=8_000_000_000, bytes_accessed=20_000_000, transcendentals=3_000_000
            ),
            name="attend",
        )(
            lengths[m, 0],
            tokens[m],
            cotangent[m],
            routes_t[m],
            key_mask[m][None, :],
            norms,
            w_query,
            w_key,
            w_value,
            w_output,
            router_t,
        )
        saved.append(outs[:11])
        froz_sent.append(outs[11])
        arrived.append(
            lax.all_to_all(outs[12], "expert", split_axis=0, concat_axis=0, tiled=True)
        )

    block = min(768, ff)
    rows_spec = pl.BlockSpec((1, 2, capacity, width), lambda e, f: (e, 0, 0, 0))
    froz_back = pl.pallas_call(
        frozen_kernel,
        grid=(frozen, ff // block),
        out_shape=[shape((frozen, 2, capacity, width), HALF)] * 2,
        in_specs=[
            rows_spec,
            rows_spec,
            pl.BlockSpec((1, width, block), lambda e, f: (e, 0, f)),
            pl.BlockSpec((1, block, width), lambda e, f: (e, f, 0)),
        ],
        out_specs=[rows_spec, rows_spec],
        scratch_shapes=[
            pltpu.VMEM((2 * capacity, width), HALF),
            pltpu.VMEM((2 * capacity, width), HALF),
            pltpu.VMEM((2, 2 * capacity, width), SINGLE),
        ],
        compiler_params=params(50),
        cost_estimate=pl.CostEstimate(
            flops=16_000_000_000, bytes_accessed=25_000_000, transcendentals=2_500_000
        ),
        name="frozen",
    )(froz_sent[0], froz_sent[1], frozen_in, frozen_out)

    rows_all = micro * owners * capacity
    group = max(1, 768 // shard)
    whole = pl.BlockSpec((owners, 2, capacity, width), lambda f: (0, 0, 0, 0))
    done0, done1, grads_w = pl.pallas_call(
        owned_kernel,
        grid=(dp // group,),
        out_shape=[shape((owners, 2, capacity, width), HALF)] * 2
        + [shape((dp, 2, width, shard), HALF)],
        in_specs=[whole, whole, pl.BlockSpec((group, 2, shard, width), lambda f: (f, 0, 0, 0))],
        out_specs=[whole, whole, pl.BlockSpec((group, 2, width, shard), lambda f: (f, 0, 0, 0))],
        scratch_shapes=[
            pltpu.VMEM((rows_all, width), HALF),
            pltpu.VMEM((rows_all, width), HALF),
            pltpu.VMEM((width, rows_all), HALF),
            pltpu.VMEM((width, rows_all), HALF),
            pltpu.VMEM((2, rows_all, width), SINGLE),
            pltpu.VMEM((2, rows_all, group * shard), HALF),
        ],
        compiler_params=params(60),
        cost_estimate=pl.CostEstimate(
            flops=47_000_000_000, bytes_accessed=35_000_000, transcendentals=5_000_000
        ),
        name="owned",
    )(arrived[0], arrived[1], all_w)

    returned = [
        lax.all_to_all(one, "expert", split_axis=0, concat_axis=0, tiled=True)
        for one in (done0, done1)
    ]
    summed_w = lax.psum_scatter(grads_w, "dp", scatter_dimension=0, tiled=True)[0]

    mixed_list, xgrad_list, small_list, weight_ins = [], [], [], []
    for m in range(micro):
        a1, q, k, v, o, x1, a2, lse, info, cols, probs = saved[m]
        mixed, xgrad, dq, dk, dv, db, small = pl.pallas_call(
            functools.partial(back_kernel, capacity, experts),
            out_shape=[shape((tok, width), HALF)] * 6 + [shape((rows16 + 8, width), SINGLE)],
            in_specs=[smem] + vmem(21),
            out_specs=vmem(7),
            scratch_shapes=[
                pltpu.VMEM((slots_all, width), HALF),
                pltpu.VMEM((slots_all, width), HALF),
                pltpu.VMEM((tok, tok), SINGLE),
                pltpu.VMEM((tok, width), SINGLE),
                pltpu.VMEM((tok, width), HALF),
                pltpu.VMEM((tok, 128), SINGLE),
            ],
            compiler_params=params(56),
            cost_estimate=pl.CostEstimate(
                flops=16_000_000_000, bytes_accessed=25_000_000, transcendentals=3_000_000
            ),
            name="back",
        )(
            lengths[m, 0],
            tokens[m],
            cotangent[m],
            routes_t[m],
            norms,
            w_query,
            w_key,
            w_value,
            w_output,
            router_t,
            q,
            k,
            v,
            o,
            x1,
            a2,
            lse,
            info,
            cols,
            probs,
            froz_back[m],
            returned[m],
        )
        mixed_list.append(mixed)
        xgrad_list.append(xgrad)
        small_list.append(small)
        weight_ins += [a1, o, dq, dk, dv, db]

    grads = pl.pallas_call(
        weights_kernel,
        out_shape=shape((4, width, width), HALF),
        in_specs=vmem(len(weight_ins)),
        out_specs=vmem(1)[0],
        compiler_params=params(50),
        name="weights",
    )(*weight_ins)
    shared = lax.psum_scatter(grads, ("dp", "expert"), scatter_dimension=1, tiled=True)
    shared = shared.astype(SINGLE)
    small = sum(small_list[1:], small_list[0])
    small = jnp.concatenate([small[:experts], small[rows16 : rows16 + 4]], 0).T
    small = lax.psum_scatter(small, ("dp", "expert"), scatter_dimension=0, tiled=True)
    return (
        jnp.stack(mixed_list, 0),
        jnp.stack(xgrad_list, 0),
        small[:, experts + 2],
        small[:, experts + 3],
        shared[0],
        shared[1],
        shared[2],
        shared[3],
        small[:, experts],
        small[:, experts + 1],
        small[:, :experts],
        summed_w[0].astype(SINGLE)[None],
        summed_w[1].astype(SINGLE).T[None],
    )


def fused(
    tokens,
    routes,
    lengths,
    key_mask,
    gain_one,
    bias_one,
    w_query,
    w_key,
    w_value,
    w_output,
    gain_two,
    bias_two,
    w_router,
    frozen_in,
    frozen_out,
    new_in,
    new_out,
    cotangent,
):
    micro, tok, width = tokens.shape
    owners = lax.axis_size("expert")
    dp = lax.axis_size("dp")
    frozen = frozen_in.shape[0]
    experts = frozen + owners
    capacity = 10 * tok // (4 * experts) // 8 * 8
    shard = new_in.shape[2]
    zs, xs, ys, cs = 4, 2, 2, 2
    shape = jax.ShapeDtypeStruct
    smem = pl.BlockSpec(memory_space=pltpu.SMEM)

    def anywhere(count):
        return [pl.BlockSpec(memory_space=pl.ANY)] * count

    routes_t = jnp.swapaxes(routes, 1, 2)
    norms = jnp.concatenate([gain_one, bias_one, gain_two, bias_two]).reshape(4, width)
    rows16 = 16
    router_t = jnp.pad(w_router.T, ((0, rows16 - experts), (0, 0)))
    dma = pltpu.SemaphoreType.DMA

    outs = pl.pallas_call(
        functools.partial(front_kernel, capacity, experts, frozen),
        out_shape=[shape((micro, tok, width), HALF)] * 5
        + [
            shape((micro, tok, width), SINGLE),
            shape((micro, tok, width), HALF),
            shape((micro, 16, tok), SINGLE),
            shape((micro, 8, tok), SINGLE),
            shape((micro, tok, 128), SINGLE),
            shape((micro, rows16, tok), SINGLE),
            shape((2, frozen, micro, capacity, width), HALF),
            shape((owners, 2, capacity, width), HALF),
            shape((owners, 2, capacity, width), HALF),
            shape((zs, 2, width, shard), HALF),
            shape((zs, 2, width, shard), HALF),
            shape((width, shard), HALF),
        ],
        in_specs=[smem] + vmem(4) + anywhere(10),
        out_specs=anywhere(7) + vmem(4) + anywhere(6),
        scratch_shapes=[
            pltpu.VMEM((dp, 2, shard, width), HALF),
            pltpu.VMEM((2, shard, width), HALF),
            pltpu.VMEM((2, micro * owners, capacity, width), HALF),
            pltpu.VMEM((2, micro * owners, capacity, width), HALF),
            pltpu.VMEM((owners, 2, capacity, width), HALF),
            dma((22,)),
            dma((22,)),
            dma((4,)),
        ],
        compiler_params=params(63, collective_id=1, has_side_effects=True),
        name="front",
    )(
        lengths[:, 0],
        routes_t,
        key_mask,
        norms,
        router_t,
        tokens,
        cotangent,
        w_query,
        w_key,
        w_value,
        w_output,
        frozen_in,
        frozen_out,
        new_in,
        new_out,
    )
    a1, q, k, v, o, x1, a2, lse, info, cols, probs, froz, ret, done, dw, _, near = outs
    rows = width // (dp * owners)
    pair = 2 * rows
    landing = [(zs, xs, ys), (zs, xs, ys), (zs, xs), (zs, ys), (zs,), (zs - 1, ys), (zs - 1,), ()]
    mixed, xgrad, shared, small, grad_in, grad_out = pl.pallas_call(
        functools.partial(tail_kernel, capacity, experts, frozen),
        out_shape=[
            shape((micro, tok, width), HALF),
            shape((micro, tok, width), HALF),
            shape((4, rows, width), SINGLE),
            shape((rows16 + 8, width), SINGLE),
            shape((1, width, shard), SINGLE),
            shape((1, shard, width), SINGLE),
        ],
        in_specs=[smem] + vmem(7) + anywhere(18),
        out_specs=anywhere(2) + vmem(2) + anywhere(2),
        scratch_shapes=[
            pltpu.VMEM((4, width, width), HALF),
            pltpu.VMEM((8, micro, tok, width), HALF),
            pltpu.VMEM((micro, tok, width), SINGLE),
            pltpu.VMEM((micro, tok, width), HALF),
            pltpu.VMEM((micro, 2, experts, capacity, width), HALF),
            pltpu.VMEM((micro, rows16 + 8, width), SINGLE),
            pltpu.VMEM((tok, tok), SINGLE),
            pltpu.VMEM((tok, width), SINGLE),
            pltpu.VMEM((tok, width), HALF),
            pltpu.VMEM((tok, 128), SINGLE),
            pltpu.VMEM((2, 2, width, shard), HALF),
            pltpu.VMEM((width, shard), HALF),
            pltpu.VMEM((width, shard), HALF),
            pltpu.VMEM((2, width, shard), HALF),
            pltpu.VMEM((2, width, shard), HALF),
            pltpu.VMEM((2, width, shard), HALF),
            pltpu.VMEM((width, shard), SINGLE),
            pltpu.VMEM((shard, width), SINGLE),
            pltpu.VMEM((zs, xs, ys, cs, 4 * rows, width), HALF),
            [pltpu.VMEM(lead + (pair, width), HALF) for lead in landing],
            pltpu.VMEM((rows16 + 8, width), SINGLE),
            pltpu.VMEM((zs + 2, rows16 + 8, width), SINGLE),
            dma((8,)),
            dma((8,)),
            dma((18,)),
            dma((18,)),
            dma((37,)),
            dma((2 * micro + 2,)),
        ],
        compiler_params=params(63, collective_id=2, has_side_effects=True),
        name="tail",
    )(
        lengths[:, 0],
        routes_t,
        norms,
        router_t,
        lse,
        info,
        cols,
        probs,
        tokens,
        cotangent,
        w_query,
        w_key,
        w_value,
        w_output,
        a1,
        q,
        k,
        v,
        o,
        x1,
        a2,
        froz,
        ret,
        done,
        dw,
        near,
    )
    at = (lax.axis_index("dp") * owners + lax.axis_index("expert")) * rows
    small = lax.dynamic_slice_in_dim(small, at, rows, 1)
    return (
        mixed,
        xgrad,
        small[rows16 + 2],
        small[rows16 + 3],
        shared[0],
        shared[1],
        shared[2],
        shared[3],
        small[rows16],
        small[rows16 + 1],
        small[:experts].T,
        grad_in,
        grad_out,
    )


def solution(mesh):
    both = ("dp", "expert")
    small_slice = mesh.shape["dp"] == 8 and mesh.shape["expert"] == 4
    return jax.shard_map(
        fused if small_slice else general,
        mesh=mesh,
        in_specs=(
            P(None, both, None),
            P(None, both, None),
            P(None, both, None),
            P(None, both),
        )
        + (P(),) * 11
        + (P("expert", None, "dp"), P("expert", "dp", None), P(None, both, None)),
        out_specs=(P(None, both, None), P(None, both, None), P(both), P(both))
        + (P(both, None),) * 4
        + (P(both), P(both), P(both, None), P("expert", None, "dp"), P("expert", "dp", None)),
        check_vma=False,
    )
```

```python
import functools

import jax
import jax.numpy as jnp
from jax import lax
from jax.experimental import pallas as pl
from jax.experimental.pallas import tpu as pltpu
from jax.sharding import PartitionSpec as P

HEAD = 64
PAIR = 2 * HEAD
TILE = 256
EPS = 1e-05
HALF = jnp.bfloat16
SINGLE = jnp.float32
HIDDEN = -1000000000.0
GELU_C = 0.7978845608028654
GELU_A = 0.044715

NN = (((1,), (0,)), ((), ()))
NT = (((1,), (1,)), ((), ()))
TN = (((0,), (0,)), ((), ()))


def mm(a, b, dims=NN):
    return lax.dot_general(a, b, dims, preferred_element_type=SINGLE)


def norm_rows(values):
    center = values - jnp.mean(values, -1, keepdims=True)
    inverse = lax.rsqrt(jnp.mean(center * center, -1, keepdims=True) + EPS)
    return center * inverse, inverse


def norm_back(grad, unit_rows, inverse, gain):
    scaled = grad * gain
    return inverse * (
        scaled
        - jnp.mean(scaled, -1, keepdims=True)
        - unit_rows * jnp.mean(scaled * unit_rows, -1, keepdims=True)
    )


def doc_of(places, lengths_ref):
    doc = jnp.zeros(places.shape, jnp.int32)
    end = 0
    for i in range(lengths_ref.shape[0]):
        end = end + lengths_ref[i]
        doc = doc + jnp.where(places >= end, 1, 0)
    return doc


def half_masks(rows):
    lane = lax.broadcasted_iota(jnp.int32, (rows, PAIR), 1)
    first = jnp.where(lane < HEAD, 1.0, 0.0).astype(HALF)
    second = jnp.where(lane < HEAD, 0.0, 1.0).astype(HALF)
    return lane < HEAD, (first, second)


def route_hots(routes_t_ref, rows, tokens):
    sub = lax.broadcasted_iota(jnp.int32, (rows, tokens), 0)
    return [sub == routes_t_ref[pick : pick + 1, :] for pick in range(2)]


def attend_kernel(capacity, experts, frozen, *refs):
    froz_ref, send_ref, bias_scr, lse_scr = refs[-4:]

    def target(e, part):
        return froz_ref.at[e, part] if e < frozen else send_ref.at[e - frozen, part]

    attend_body(capacity, experts, target, *refs[:-4], bias_scr, lse_scr)


def attend_body(
    capacity,
    experts,
    target,
    lengths_ref,
    x_ref,
    dy_ref,
    routes_t_ref,
    mask_ref,
    norms_ref,
    wq_ref,
    wk_ref,
    wv_ref,
    wo_ref,
    wr_ref,
    a1_ref,
    q_ref,
    k_ref,
    v_ref,
    o_ref,
    x1_ref,
    a2_ref,
    lse_ref,
    info_ref,
    cols_ref,
    probs_ref,
    bias_scr,
    lse_scr,
):
    tokens, width = x_ref.shape
    chunk = 128
    gain_one, bias_one = norms_ref[0:1, :], norms_ref[1:2, :]
    gain_two, bias_two = norms_ref[2:3, :], norms_ref[3:4, :]

    @pl.loop(0, tokens // chunk)
    def _(i):
        rows = pl.ds(pl.multiple_of(i * chunk, chunk), chunk)
        unit_rows, _ = norm_rows(x_ref[rows, :].astype(SINGLE))
        a1_ref[rows, :] = (unit_rows * gain_one + bias_one).astype(HALF)
        here = lax.broadcasted_iota(jnp.int32, (chunk, 1), 0) + i * chunk
        there = lax.broadcasted_iota(jnp.int32, (1, tokens), 1)
        same = doc_of(here, lengths_ref) == doc_of(there, lengths_ref)
        keep = (mask_ref[...] == 1) | (there == here)
        visible = same & (there <= here) & keep
        bias_scr[rows, :] = jnp.where(visible, 0.0, HIDDEN)

    @pl.loop(0, tokens // TILE)
    def _(i):
        rows = pl.ds(pl.multiple_of(i * TILE, TILE), TILE)
        a1 = a1_ref[rows, :]
        q_ref[rows, :] = (mm(a1, wq_ref[...]).astype(HALF) * HEAD ** (-0.5)).astype(HALF)
        k_ref[rows, :] = mm(a1, wk_ref[...]).astype(HALF)
        v_ref[rows, :] = mm(a1, wv_ref[...]).astype(HALF)

    lse_scr[...] = jnp.zeros_like(lse_scr)

    @pl.loop(0, width // PAIR)
    def _(i):
        cols = pl.ds(pl.multiple_of(i * PAIR, PAIR), PAIR)
        low, masks = half_masks(TILE)
        lane = lax.broadcasted_iota(jnp.int32, (TILE, 128), 1)
        for part in range(tokens // TILE):
            rows = slice(part * TILE, (part + 1) * TILE)
            keys = (part + 1) * TILE
            q_t = q_ref[rows, cols]
            k_t = k_ref[0:keys, cols]
            v_t = v_ref[0:keys, cols]
            results = []
            for h in range(2):
                scores = mm(q_t * masks[h], k_t, NT) + bias_scr[rows, 0:keys]
                top = jnp.max(scores, -1, keepdims=True)
                expo = jnp.exp(scores - top)
                total = jnp.sum(expo, -1, keepdims=True)
                results.append(mm(expo.astype(HALF), v_t) * (1.0 / total))
                log_total = top + jnp.log(total)
                lse_scr[rows, :] = jnp.where(lane == 2 * i + h, log_total, lse_scr[rows, :])
            o_ref[rows, cols] = jnp.where(low, results[0], results[1]).astype(HALF)

    lse_ref[...] = jnp.transpose(lse_scr[...])[0 : lse_ref.shape[0], :]

    @pl.loop(0, tokens // TILE)
    def _(i):
        rows = pl.ds(pl.multiple_of(i * TILE, TILE), TILE)
        x1 = x_ref[rows, :].astype(SINGLE) + mm(o_ref[rows, :], wo_ref[...])
        x1_ref[rows, :] = x1
        unit_rows, _ = norm_rows(x1)
        a2_ref[rows, :] = (unit_rows * gain_two + bias_two).astype(HALF)

    rows16 = wr_ref.shape[0]
    logits = mm(wr_ref[...], a2_ref[...], NT)
    sub = lax.broadcasted_iota(jnp.int32, (rows16, tokens), 0)
    logits = jnp.where(sub < experts, logits, -1e30)
    expo = jnp.exp(logits - jnp.max(logits, 0, keepdims=True))
    probs = expo / jnp.sum(expo, 0, keepdims=True)
    probs_ref[...] = probs
    hots = route_hots(routes_t_ref, rows16, tokens)
    chosen = [jnp.sum(jnp.where(hot, probs, 0.0), 0, keepdims=True) for hot in hots]
    chosen_total = chosen[0] + chosen[1]
    gates = [one / chosen_total for one in chosen]
    upper = jnp.where(
        lax.broadcasted_iota(jnp.int32, (tokens, tokens), 0)
        < lax.broadcasted_iota(jnp.int32, (tokens, tokens), 1),
        1.0,
        0.0,
    ).astype(HALF)
    both = jnp.where(hots[0] | hots[1], 1.0, 0.0).astype(HALF)
    earlier = mm(both, upper)
    places = []
    for pick in range(2):
        slot = jnp.sum(jnp.where(hots[pick], earlier, 0.0), 0, keepdims=True)
        first = routes_t_ref[pick : pick + 1, :].astype(SINGLE) * capacity
        places.append(jnp.where(slot < capacity, first + slot, -1.0))
    info = jnp.concatenate(
        places + gates + [mask_ref[...].astype(SINGLE), chosen_total, chosen_total, chosen_total], 0
    )
    info_ref[...] = info
    cols_ref[...] = jnp.transpose(
        jnp.concatenate([info, jnp.zeros((128 - info.shape[0], tokens), SINGLE)], 0)
    )
    spots = [one.astype(jnp.int32) for one in places]
    for e in range(experts):
        slots = lax.broadcasted_iota(jnp.int32, (capacity, tokens), 0) + e * capacity
        hit = [slots == spots[pick] for pick in range(2)]
        place = jnp.where(hit[0] | hit[1], 1.0, 0.0).astype(HALF)
        weight = jnp.sum(
            jnp.where(hit[0], gates[0], 0.0) + jnp.where(hit[1], gates[1], 0.0), 1, keepdims=True
        )
        target(e, 0)[...] = mm(place, a2_ref[...]).astype(HALF)
        target(e, 1)[...] = (mm(place, dy_ref[...]) * weight).astype(HALF)


def expert_step(x_of, dy_of, total, w_in, w_out, in_dims, acc_scr, held, first, chunk):
    back_dims = NT if in_dims == NN else NN

    @pl.loop(0, total // chunk)
    def _(i):
        rows = pl.ds(pl.multiple_of(i * chunk, 16), chunk)
        pre = mm(x_of(i), w_in, in_dims)
        grad = mm(dy_of(i), w_out, NT)
        square = pre * pre
        tanh = jnp.tanh(GELU_C * pre * (1.0 + GELU_A * square))
        plus = 0.5 * (1.0 + tanh)
        hidden = (pre * plus).astype(HALF)
        slope = plus + 0.5 * pre * (1.0 - tanh * tanh) * (GELU_C * (1.0 + 3.0 * GELU_A * square))
        grad_pre = (grad * slope).astype(HALF)
        if held is not None:
            held[0, rows, :] = hidden
            held[1, rows, :] = grad_pre
        out = mm(hidden, w_out)
        back = mm(grad_pre, w_in, back_dims)
        if first is True:
            acc_scr[0, rows, :] = out
            acc_scr[1, rows, :] = back
        elif first is False:
            acc_scr[0, rows, :] += out
            acc_scr[1, rows, :] += back
        else:

            @pl.when(first)
            def _():
                acc_scr[0, rows, :] = out
                acc_scr[1, rows, :] = back

            @pl.when(jnp.logical_not(first))
            def _():
                acc_scr[0, rows, :] += out
                acc_scr[1, rows, :] += back


def frozen_kernel(
    r0_ref, r1_ref, win_ref, wout_ref, o0_ref, o1_ref, x_scr, dy_scr, acc_scr
):
    capacity = r0_ref.shape[2]
    step, last = pl.program_id(1), pl.num_programs(1) - 1

    @pl.when(step == 0)
    def _():
        for m, ref in enumerate((r0_ref, r1_ref)):
            x_scr[m * capacity : (m + 1) * capacity, :] = ref[0, 0]
            dy_scr[m * capacity : (m + 1) * capacity, :] = ref[0, 1]

    expert_step(
        lambda i: x_scr[...],
        lambda i: dy_scr[...],
        2 * capacity,
        win_ref[0],
        wout_ref[0],
        NN,
        acc_scr,
        None,
        step == 0,
        2 * capacity,
    )

    @pl.when(step == last)
    def _():
        for m, ref in enumerate((o0_ref, o1_ref)):
            for part in range(2):
                ref[0, part] = acc_scr[part, m * capacity : (m + 1) * capacity, :].astype(HALF)


def owned_kernel(
    r0_ref,
    r1_ref,
    w_ref,
    o0_ref,
    o1_ref,
    dw_ref,
    x_scr,
    dy_scr,
    xt_scr,
    dyt_scr,
    acc_scr,
    held_scr,
):
    sources, _, capacity, width = r0_ref.shape
    group, _, shard, _ = w_ref.shape
    step, last = pl.program_id(0), pl.num_programs(0) - 1
    rows_all = x_scr.shape[0]

    @pl.when(step == 0)
    def _():
        for m, ref in enumerate((r0_ref, r1_ref)):
            for s in range(sources):
                at = (m * sources + s) * capacity
                x_scr[at : at + capacity, :] = ref[s, 0]
                dy_scr[at : at + capacity, :] = ref[s, 1]
        for at in range(0, width, 128):
            xt_scr[at : at + 128, :] = jnp.transpose(x_scr[:, at : at + 128])
            dyt_scr[at : at + 128, :] = jnp.transpose(dy_scr[:, at : at + 128])

    w_in = w_ref[:, 0].reshape(group * shard, width)
    w_out = w_ref[:, 1].reshape(group * shard, width)
    chunk = 2 * capacity
    expert_step(
        lambda i: x_scr[pl.ds(pl.multiple_of(i * chunk, 16), chunk), :],
        lambda i: dy_scr[pl.ds(pl.multiple_of(i * chunk, 16), chunk), :],
        rows_all,
        w_in,
        w_out,
        NT,
        acc_scr,
        held_scr,
        step == 0,
        chunk,
    )

    @pl.loop(0, width // TILE)
    def _(i):
        rows = pl.ds(pl.multiple_of(i * TILE, TILE), TILE)
        for part, (left, right) in enumerate(((xt_scr, held_scr.at[1]), (dyt_scr, held_scr.at[0]))):
            total = mm(left[rows, :], right[...]).astype(HALF)
            for g in range(group):
                dw_ref[g, part, rows, :] = total[:, g * shard : (g + 1) * shard]

    @pl.when(step == last)
    def _():
        for m, ref in enumerate((o0_ref, o1_ref)):
            for s in range(sources):
                at = (m * sources + s) * capacity
                for part in range(2):
                    ref[s, part] = acc_scr[part, at : at + capacity, :].astype(HALF)


def back_kernel(capacity, experts, *refs):
    froz_ref, back_ref = refs[20:22]
    mixed_ref, xgrad_ref, dq_ref, dk_ref, dv_ref, db_ref, small_ref = refs[22:29]
    out_scr, dbuf_scr = refs[29:31]
    frozen = froz_ref.shape[0]
    for e in range(experts):
        source = froz_ref.at[e] if e < frozen else back_ref.at[e - frozen]
        out_scr[e * capacity : (e + 1) * capacity, :] = source[0]
        dbuf_scr[e * capacity : (e + 1) * capacity, :] = source[1]
    dx1_scr = refs[32]
    back_body(capacity, experts, None, None, *refs[:20], mixed_ref, dx1_scr, *refs[24:])
    finish_body(
        refs[1],
        refs[4],
        *refs[5:8],
        dx1_scr,
        xgrad_ref,
        dq_ref,
        dk_ref,
        dv_ref,
        small_ref,
        refs[9].shape[0],
        0,
        refs[1].shape[0] // TILE,
    )


def flat(ref):
    rows = ref[...]
    return rows if rows.ndim == 2 else rows.reshape(-1, rows.shape[-1])


def block_of(ref, e, rows):
    return ref[rows, :] if len(ref.shape) == 2 else ref[e]


def back_body(
    capacity,
    experts,
    middle,
    after_group,
    lengths_ref,
    x_ref,
    dy_ref,
    routes_t_ref,
    norms_ref,
    wq_ref,
    wk_ref,
    wv_ref,
    wo_ref,
    wr_ref,
    q_ref,
    k_ref,
    v_ref,
    o_ref,
    x1_ref,
    a2_ref,
    lse_ref,
    info_ref,
    cols_ref,
    probs_ref,
    mixed_ref,
    dx1_ref,
    dq_ref,
    dk_ref,
    dv_ref,
    db_ref,
    small_ref,
    out_scr,
    dbuf_scr,
    bias_scr,
    dx1_scr,
    do_scr,
    delta_scr,
):
    tokens, width = x_ref.shape
    gain_two = norms_ref[2:3, :]
    slots_all = experts * capacity

    spots = [info_ref[pick : pick + 1, :].astype(jnp.int32) for pick in range(2)]
    gates = [info_ref[2 + pick : 3 + pick, :] for pick in range(2)]
    chosen_total = info_ref[5:6, :]

    def gate_part(e, carry):
        rows = pl.ds(pl.multiple_of(e * capacity, 16), capacity)
        overlap = mm(block_of(out_scr, e, rows), dy_ref[...], NT)
        slots = lax.broadcasted_iota(jnp.int32, (capacity, tokens), 0) + e * capacity
        return tuple(
            carry[pick]
            + jnp.sum(jnp.where(slots == spots[pick], overlap, 0.0), 0, keepdims=True)
            for pick in range(2)
        )

    zero_row = jnp.zeros((1, tokens), SINGLE)
    gate_grads = lax.fori_loop(0, experts, gate_part, (zero_row, zero_row))
    rows16 = wr_ref.shape[0]
    hots = route_hots(routes_t_ref, rows16, tokens)
    weighted = gate_grads[0] * gates[0] + gate_grads[1] * gates[1]
    grad_probs = jnp.where(hots[0], (gate_grads[0] - weighted) / chosen_total, 0.0)
    grad_probs = grad_probs + jnp.where(hots[1], (gate_grads[1] - weighted) / chosen_total, 0.0)
    probs = probs_ref[...]
    grad_logits = probs * (grad_probs - jnp.sum(grad_probs * probs, 0, keepdims=True))
    logits_low = grad_logits.astype(HALF)
    small_ref[0:rows16, :] = mm(logits_low, a2_ref[...])
    small_ref[rows16:, :] = jnp.zeros_like(small_ref[rows16:, :])

    @pl.loop(0, tokens // TILE)
    def _(i):
        rows = pl.ds(pl.multiple_of(i * TILE, TILE), TILE)
        slots = lax.broadcasted_iota(jnp.int32, (TILE, slots_all), 1)
        hit = [slots == cols_ref[rows, pick : pick + 1].astype(jnp.int32) for pick in range(2)]
        gated = jnp.where(hit[0], cols_ref[rows, 2:3], 0.0)
        gated = jnp.where(hit[1], cols_ref[rows, 3:4], gated).astype(HALF)
        place = jnp.where(hit[0] | hit[1], 1.0, 0.0).astype(HALF)
        x1 = x1_ref[rows, :]
        mixed_ref[rows, :] = (x1 + mm(gated, flat(out_scr))).astype(HALF)
        dx1_scr[rows, :] = mm(place, flat(dbuf_scr))

    logits_col = jnp.transpose(
        jnp.concatenate([grad_logits, jnp.zeros((128 - rows16, tokens), SINGLE)], 0)
    )
    delta_scr[...] = logits_col.astype(HALF).astype(SINGLE)
    router = jnp.concatenate([wr_ref[...], jnp.zeros((128 - rows16, width), HALF)], 0)

    @pl.loop(0, tokens // TILE)
    def _(i):
        rows = pl.ds(pl.multiple_of(i * TILE, TILE), TILE)
        unit_rows, inverse = norm_rows(x1_ref[rows, :])
        grad = dx1_scr[rows, :] + mm(delta_scr[rows, :].astype(HALF), router)
        small_ref[rows16 : rows16 + 1, :] += jnp.sum(grad * unit_rows, 0, keepdims=True)
        small_ref[rows16 + 1 : rows16 + 2, :] += jnp.sum(grad, 0, keepdims=True)
        dx1 = dy_ref[rows, :].astype(SINGLE) + norm_back(grad, unit_rows, inverse, gain_two)
        dx1_ref[rows, :] = dx1
        branch = dx1.astype(HALF)
        db_ref[rows, :] = branch
        do_scr[rows, :] = mm(branch, wo_ref[...], NT).astype(HALF)

    if middle is not None:
        middle()

    @pl.loop(0, tokens // 128)
    def _(i):
        rows = pl.ds(pl.multiple_of(i * 128, 128), 128)
        key = lax.broadcasted_iota(jnp.int32, (128, 1), 0) + i * 128
        query = lax.broadcasted_iota(jnp.int32, (1, tokens), 1)
        same = doc_of(key, lengths_ref) == doc_of(query, lengths_ref)
        keep = (cols_ref[rows, 4:5] > 0.5) | (query == key)
        visible = same & (key <= query) & keep
        bias_scr[rows, :] = jnp.where(visible, 0.0, HIDDEN)

    def one_pair(i):
        cols = pl.ds(pl.multiple_of(i * PAIR, PAIR), PAIR)
        low, masks = half_masks(TILE)
        tiles = tokens // TILE
        half_sum = jnp.where(
            (lax.broadcasted_iota(jnp.int32, (8, PAIR), 1) // HEAD)
            == lax.broadcasted_iota(jnp.int32, (8, PAIR), 0),
            1.0,
            0.0,
        )
        overlap = do_scr[:, cols].astype(SINGLE) * o_ref[:, cols].astype(SINGLE)
        deltas = lax.dot_general(
            half_sum,
            overlap,
            NT,
            precision=lax.Precision.HIGHEST,
            preferred_element_type=SINGLE,
        )
        grad_q = [[None] * tiles for _ in range(2)]
        for part in range(tiles):
            keys = slice(part * TILE, (part + 1) * TILE)
            queries = slice(part * TILE, tokens)
            k_t, v_t = k_ref[keys, cols], v_ref[keys, cols]
            q_t, do_t = q_ref[queries, cols], do_scr[queries, cols]
            grad_k, grad_v = [], []
            for h in range(2):
                scores = mm(k_t * masks[h], q_t, NT) + bias_scr[keys, queries]
                log_total = lse_ref[pl.ds(2 * i + h, 1), queries]
                probs = jnp.exp(scores - log_total)
                grad_p = mm(v_t * masks[h], do_t, NT)
                grad_s = (probs * (grad_p - deltas[h : h + 1, queries])).astype(HALF)
                grad_v.append(mm(probs.astype(HALF), do_t))
                grad_k.append(mm(grad_s, q_t))
                step = mm(grad_s, k_t, TN)
                for t in range(part, tiles):
                    piece = step[(t - part) * TILE : (t - part + 1) * TILE, :]
                    grad_q[h][t] = piece if grad_q[h][t] is None else grad_q[h][t] + piece
            dv_ref[keys, cols] = jnp.where(low, grad_v[0], grad_v[1]).astype(HALF)
            dk_ref[keys, cols] = jnp.where(low, grad_k[0], grad_k[1]).astype(HALF)
        for t in range(tiles):
            both = jnp.where(low, grad_q[0][t], grad_q[1][t]) * HEAD ** (-0.5)
            dq_ref[t * TILE : (t + 1) * TILE, cols] = both.astype(HALF)

    if after_group is None:
        pl.loop(0, width // PAIR)(one_pair)
    else:
        for group in range(width // TILE):
            pl.loop(group * TILE // PAIR, (group + 1) * TILE // PAIR)(one_pair)
            after_group(group)


def finish_body(
    x_ref,
    norms_ref,
    wq_ref,
    wk_ref,
    wv_ref,
    dx1_ref,
    xgrad_ref,
    dq_ref,
    dk_ref,
    dv_ref,
    small_ref,
    rows16,
    first,
    last,
):
    gain_one = norms_ref[0:1, :]

    @pl.loop(first, last)
    def _(i):
        rows = pl.ds(pl.multiple_of(i * TILE, TILE), TILE)
        unit_rows, inverse = norm_rows(x_ref[rows, :].astype(SINGLE))
        grad = mm(dq_ref[rows, :], wq_ref[...], NT)
        grad = grad + mm(dk_ref[rows, :], wk_ref[...], NT)
        grad = grad + mm(dv_ref[rows, :], wv_ref[...], NT)
        small_ref[rows16 + 2 : rows16 + 3, :] += jnp.sum(grad * unit_rows, 0, keepdims=True)
        small_ref[rows16 + 3 : rows16 + 4, :] += jnp.sum(grad, 0, keepdims=True)
        part = norm_back(grad, unit_rows, inverse, gain_one)
        xgrad_ref[rows, :] = (dx1_ref[rows, :] + part).astype(HALF)


def weights_kernel(*refs):
    ins, dw_ref = refs[:-1], refs[-1]
    micro = len(ins) // 6
    width = dw_ref.shape[-1]

    @pl.loop(0, width // TILE)
    def _(i):
        cols = pl.ds(pl.multiple_of(i * TILE, TILE), TILE)
        for part in range(4):
            total = weight_grad(ins, micro, part, cols)
            dw_ref[part, cols, :] = total.astype(HALF)


def weight_grad(ins, micro, part, cols):
    total = None
    for m in range(micro):
        a1, o, dq, dk, dv, db = ins[6 * m : 6 * m + 6]
        left = o if part == 3 else a1
        right = (dq, dk, dv, db)[part]
        step = mm(left[:, cols], right[...], TN)
        total = step if total is None else total + step
    return total


def meet(peers):
    barrier = pltpu.get_barrier_semaphore()
    for peer in peers:
        pl.semaphore_signal(barrier, inc=1, device_id=peer, device_id_type=pl.DeviceIdType.MESH)
    return barrier


def remote(source, target, peer, send_sem, recv_sem, at):
    return pltpu.make_async_remote_copy(
        src_ref=source,
        dst_ref=target,
        send_sem=send_sem.at[at],
        recv_sem=recv_sem.at[at],
        device_id=peer,
        device_id_type=pl.DeviceIdType.MESH,
    )


def reduce_peers(z, x, y, c, zs, xs, cs):
    places = [(z, x, y, 1 - c), (z, 1 - x, y, c), (z, x, 1 - y, c)]
    places += [((z + step) % zs, x, y, c) for step in range(1, zs)]
    return [(zz * xs + xx, yy * cs + cc) for zz, xx, yy, cc in places]


class Reduction:
    def __init__(self, place, shape, lefts, rights, out_ref, pay, got, send_sem, recv_sem):
        self.place, self.shape = place, shape
        self.lefts, self.rights = lefts, rights
        self.out_ref, self.pay, self.got = out_ref, pay, got
        self.sems = send_sem, recv_sem
        self.rows = out_ref.shape[1]
        self.copies = [self.plan(k) for k in range(pay.shape[0])]

    def plan(self, k):
        z, x, y, c = self.place
        zs, xs, _, cs = self.shape
        pay, (first, second, third, fourth) = self.pay.at[k], [one.at[k] for one in self.got]

        def link(source, target, zz, xx, yy, cc, at):
            peer = (zz * xs + xx, yy * cs + cc)
            return remote(source, target, peer, *self.sems, 6 * k + at)

        start = link(pay.at[:, :, :, 1 - c], first, z, x, y, 1 - c, 0)
        if k % 2 == 0:
            two = link(pay.at[:, :, 1 - y, c], second, z, x, 1 - y, c, 1)
            three = link(pay.at[:, 1 - x, y, c], third, z, 1 - x, y, c, 2)
        else:
            two = link(pay.at[:, 1 - x, :, c], second, z, 1 - x, y, c, 1)
            three = link(pay.at[:, x, 1 - y, c], third, z, x, 1 - y, c, 2)
        four = []
        for step in range(1, zs):
            zz = (z + step) % zs
            four.append(link(pay.at[zz, x, y, c], fourth.at[step - 1], zz, x, y, c, 2 + step))
        return start, two, three, four

    def produce(self, k):
        zs, xs, ys, cs = self.shape
        rows = self.rows
        tile = 16 * rows
        width = self.lefts[0].shape[0]
        for j in range(width // tile):
            for part, (left, right) in enumerate(zip(self.lefts, self.rights)):
                total = mm(left[j * tile : (j + 1) * tile, :], right(k)).astype(HALF)
                for i in range(16):
                    n = 16 * j + i
                    at = (n // (ys * cs) // xs, n // (ys * cs) % xs, n % (ys * cs) // cs, n % cs)
                    for half in range(2):
                        spot = (2 * k + half,) + at + (slice(part * rows, (part + 1) * rows),)
                        self.pay[spot] = total[
                            i * rows : (i + 1) * rows, half * 128 : (half + 1) * 128
                        ]
        for half in range(2):
            self.copies[2 * k + half][0].start()

    def add(self, k, places):
        @pl.loop(0, self.shape[0])
        def _(i):
            for at, held in places(i):
                at = (k,) + at
                self.pay[at] = (self.pay[at].astype(SINGLE) + held[...].astype(SINGLE)).astype(
                    HALF
                )

    def second(self, block):
        for k in (2 * block, 2 * block + 1):
            self.second_half(k)

    def second_half(self, k):
        _, _, _, c = self.place
        _, xs, ys, _ = self.shape
        held = self.got[0].at[k]
        self.copies[k][0].wait()
        self.add(
            k,
            lambda i: [
                ((i, xx, yy, c), held.at[i, xx, yy]) for xx in range(xs) for yy in range(ys)
            ],
        )
        self.copies[k][1].start()

    def third(self, block):
        for k in (2 * block, 2 * block + 1):
            self.third_half(k)

    def third_half(self, k):
        _, x, y, c = self.place
        _, xs, ys, _ = self.shape
        held = self.got[1].at[k]
        self.copies[k][1].wait()
        if k % 2 == 0:
            self.add(k, lambda i: [((i, xx, y, c), held.at[i, xx]) for xx in range(xs)])
        else:
            self.add(k, lambda i: [((i, x, yy, c), held.at[i, yy]) for yy in range(ys)])
        self.copies[k][2].start()

    def fourth(self, block):
        for k in (2 * block, 2 * block + 1):
            self.fourth_half(k)

    def fourth_half(self, k):
        _, x, y, c = self.place
        held = self.got[2].at[k]
        self.copies[k][2].wait()
        self.add(k, lambda i: [((i, x, y, c), held.at[i])])
        for copy in self.copies[k][3]:
            copy.start()

    def final(self, block):
        for k in (2 * block, 2 * block + 1):
            self.final_half(k)

    def final_half(self, k):
        z, x, y, c = self.place
        held = self.got[3].at[k]
        for copy in self.copies[k][3]:
            copy.wait()
        total = self.pay[k, z, x, y, c].astype(SINGLE)
        for i in range(self.shape[0] - 1):
            total = total + held[i].astype(SINGLE)
        for part in range(4):
            self.out_ref[part, :, k * 128 : (k + 1) * 128] = total[
                part * self.rows : (part + 1) * self.rows
            ]


def front_kernel(
    capacity,
    experts,
    frozen,
    lengths_ref,
    routes_t_ref,
    mask_ref,
    norms_ref,
    wr_ref,
    tokens_ref,
    cot_ref,
    wq_any,
    wk_any,
    wv_any,
    wo_any,
    fin_any,
    fout_any,
    nin_any,
    nout_any,
    a1_any,
    q_any,
    k_any,
    v_any,
    o_any,
    x1_any,
    a2_any,
    lse_ref,
    info_ref,
    cols_ref,
    probs_ref,
    froz_any,
    ret_any,
    done_any,
    dw_any,
    core_any,
    near_any,
    own_any,
    all_w,
    local_w,
    stage,
    arrived,
    send_sem,
    recv_sem,
    own_sem,
):
    micro, tok, width = tokens_ref.shape
    zs, xs, cs = 4, 2, 2
    shard = nin_any.shape[2]
    dp, ex = lax.axis_index("dp"), lax.axis_index("expert")
    z, x, y, c = dp // xs, dp % xs, ex // cs, ex % cs
    me = y * xs + x
    owners = experts - frozen

    def device(zz, xx, yy, cc):
        return (zz * xs + xx, yy * cs + cc)

    def near(step):
        return z + 1 - 2 * (z % 2) if step == 1 else (zs - 1 - z if step == 3 else (z + 2) % zs)

    core = device(z, x, y, 1 - c)
    swapped = device(z, c, y, x)
    straight, distant = device(near(1), x, y, c), device(near(3), x, y, c)
    others = [(x + (d & 1)) % 2 + xs * ((y + (d >> 1)) % 2) for d in (3, 2, 1)]
    row_peers = [device(z, other % xs, other // xs, c) for other in others]
    fourth = device(z + (near(1) - z) * ((x + c + 1) % 2), c, y, x)
    peers = [core, straight, distant, fourth] + row_peers
    pl.semaphore_wait(meet(peers), len(peers))

    def link(source, target, peer, at):
        return remote(source, target, peer, send_sem, recv_sem, at)

    held_w = all_w.at[z * xs + c]
    exchange = link(local_w, all_w.at[dp], swapped, 0)
    spread = [link(held_w, held_w, straight, 1), link(held_w, held_w, distant, 2)]
    spread_own = [link(local_w, held_w, straight, 1), link(local_w, held_w, distant, 2)]
    keep_own = pltpu.make_async_copy(local_w, all_w.at[dp], own_sem.at[0])
    far = near(3) * xs + c
    onward = link(all_w.at[far], all_w.at[far], straight, 3)
    order = [z, near(1), near(3), near(2)]
    across = [
        link(all_w.at[zz * xs + c], all_w.at[zz * xs + c], core, 4 + i)
        for i, zz in enumerate(order)
    ]
    rows_out = [
        [
            link(
                stage.at[:, m * owners + other],
                arrived.at[:, m * owners + me],
                peer,
                8 + 3 * m + i,
            )
            for i, (other, peer) in enumerate(zip(others, row_peers))
        ]
        for m in range(micro)
    ]
    rows_own = [
        pltpu.make_async_copy(
            stage.at[:, m * owners + me], arrived.at[:, m * owners + me], own_sem.at[1 + m]
        )
        for m in range(micro)
    ]
    results_out = [
        link(stage.at[:, other], ret_any.at[:, me], peer, 14 + i)
        for i, (other, peer) in enumerate(zip(others, row_peers))
    ]
    results_own = pltpu.make_async_copy(stage.at[:, me], ret_any.at[:, me], own_sem.at[3])
    near_far = link(dw_any.at[near(3)], near_any, straight, 21)
    near_own = link(dw_any.at[near(1), 0], own_any, straight, 22)

    def first_half(
        w_scr,
        x_scr,
        dy_scr,
        a1_scr,
        q_scr,
        k_scr,
        v_scr,
        o_scr,
        x1_scr,
        a2_scr,
        bias_scr,
        lse_scr,
        froz_rows,
        win_scr,
        wout_scr,
        acc_scr,
        nin_scr,
        in_sem,
        out_sem,
        stream_sem,
    ):
        def load(source, target, at):
            copy = pltpu.make_async_copy(source, target, in_sem.at[at])
            copy.start()
            return copy

        nout_scr = x1_scr.at[1, pl.ds(0, shard)]
        new_loads = [load(nin_any.at[0], nin_scr, 0), load(nout_any.at[0], nout_scr, 1)]
        row_loads = [
            [
                load(tokens_ref.at[m], x_scr.at[m], 2 + 2 * m),
                load(cot_ref.at[m], dy_scr.at[m], 3 + 2 * m),
            ]
            for m in range(micro)
        ]
        weight_loads = [
            load(ref, w_scr.at[i], 2 + 2 * micro + i)
            for i, ref in enumerate((wq_any, wk_any, wv_any, wo_any))
        ]
        for copy in new_loads:
            copy.wait()
        local_w[0] = jnp.transpose(nin_scr[...]).astype(HALF)
        local_w[1] = nout_scr[...].astype(HALF)

        @pl.when(x != c)
        def _():
            exchange.start()

        @pl.when(x == c)
        def _():
            keep_own.start()
            spread_own[1].start()
            spread_own[0].start()

        blocks = fin_any.shape[2] // width

        def stream(step, slot):
            e, f = step // blocks, step % blocks
            at = pl.ds(pl.multiple_of(f * width, width), width)
            return (
                pltpu.make_async_copy(
                    fin_any.at[e, :, at], win_scr.at[slot], stream_sem.at[0, slot]
                ),
                pltpu.make_async_copy(
                    fout_any.at[e, at, :], wout_scr.at[slot], stream_sem.at[1, slot]
                ),
            )

        for copy in stream(0, 0):
            copy.start()
        for copy in weight_loads + row_loads[0]:
            copy.wait()
        saves = []
        for m in range(micro):
            if m:
                for copy in row_loads[m]:
                    copy.wait()

            def target(e, part, m=m):
                if e < frozen:
                    return froz_rows.at[part, e, m]
                return stage.at[part, m * owners + e - frozen]

            attend_body(
                capacity,
                experts,
                target,
                lengths_ref.at[m],
                x_scr.at[m],
                dy_scr.at[m],
                routes_t_ref.at[m],
                mask_ref.at[pl.ds(m, 1)],
                norms_ref,
                w_scr.at[0],
                w_scr.at[1],
                w_scr.at[2],
                w_scr.at[3],
                wr_ref,
                a1_scr.at[m],
                q_scr.at[m],
                k_scr.at[m],
                v_scr.at[m],
                o_scr.at[m],
                x1_scr.at[m],
                a2_scr.at[m],
                lse_ref.at[m],
                info_ref.at[m],
                cols_ref.at[m],
                probs_ref.at[m],
                bias_scr,
                lse_scr,
            )
            for copy in rows_out[m]:
                copy.start()
            rows_own[m].start()
            for i, (source, target_any) in enumerate(
                (
                    (a1_scr, a1_any),
                    (q_scr, q_any),
                    (k_scr, k_any),
                    (v_scr, v_any),
                    (o_scr, o_any),
                    (x1_scr, x1_any),
                    (a2_scr, a2_any),
                )
            ):
                copy = pltpu.make_async_copy(
                    source.at[m], target_any.at[m], out_sem.at[7 * m + i]
                )
                copy.start()
                saves.append(copy)
            if m == 0:

                @pl.when(x != c)
                def _():
                    exchange.wait_recv()
                    spread[1].start()
                    spread[0].start()

                @pl.when(x == c)
                def _():
                    keep_own.wait()

                across[0].start()


        steps = frozen * blocks

        @pl.loop(0, steps)
        def _(step):
            slot = step % 2
            e = step // blocks

            @pl.when(step + 1 < steps)
            def _():
                for copy in stream(step + 1, 1 - slot):
                    copy.start()

            for copy in stream(step, slot):
                copy.wait()
            expert_step(
                lambda rows: froz_rows[0, e].reshape(micro * capacity, width)[...],
                lambda rows: froz_rows[1, e].reshape(micro * capacity, width)[...],
                micro * capacity,
                win_scr[slot],
                wout_scr[slot],
                NN,
                acc_scr,
                None,
                step % blocks == 0,
                micro * capacity,
            )

            @pl.when(step % blocks == blocks - 1)
            def _():
                for m in range(micro):
                    for part in range(2):
                        froz_rows[part, e, m] = acc_scr[
                            part, m * capacity : (m + 1) * capacity, :
                        ].astype(HALF)

            @pl.when(step == steps // 2)
            def _():
                spread[1].wait_recv()
                onward.start()
                across[2].start()

            @pl.when(step == steps // 2 + 1)
            def _():
                spread[0].wait_recv()
                across[1].start()

        last = pltpu.make_async_copy(froz_rows, froz_any, out_sem.at[7 * micro])
        last.start()
        for copy in saves:
            copy.wait()
        last.wait()

    pl.run_scoped(
        first_half,
        pltpu.VMEM((4, width, width), HALF),
        pltpu.VMEM((micro, tok, width), HALF),
        pltpu.VMEM((micro, tok, width), HALF),
        pltpu.VMEM((micro, tok, width), HALF),
        pltpu.VMEM((micro, tok, width), HALF),
        pltpu.VMEM((micro, tok, width), HALF),
        pltpu.VMEM((micro, tok, width), HALF),
        pltpu.VMEM((micro, tok, width), HALF),
        pltpu.VMEM((micro, tok, width), SINGLE),
        pltpu.VMEM((micro, tok, width), HALF),
        pltpu.VMEM((tok, tok), SINGLE),
        pltpu.VMEM((tok, 128), SINGLE),
        pltpu.VMEM((2, frozen, micro, capacity, width), HALF),
        pltpu.VMEM((2, width, width), HALF),
        pltpu.VMEM((2, width, width), HALF),
        pltpu.VMEM((2, micro * capacity, width), SINGLE),
        pltpu.VMEM((width, shard), SINGLE),
        pltpu.SemaphoreType.DMA((2 + 2 * micro + 4,)),
        pltpu.SemaphoreType.DMA((7 * micro + 1,)),
        pltpu.SemaphoreType.DMA((2, 2)),
    )

    rows_one = owners * capacity
    rows_all = micro * rows_one

    def second_half(
        xt_scr, dyt_scr, acc_scr, held, current, dw_stage, core_scr, held_sem, dw_sem, core_sem
    ):
        def rows_of(part, m):
            def get(rows):
                return arrived[part, pl.ds(m * owners + 2 * rows, 2)].reshape(2 * capacity, width)

            return get

        def weights(zz):
            two = all_w.at[pl.ds(zz * xs, xs)]
            return (
                two[:, 0].reshape(xs * shard, width),
                two[:, 1].reshape(xs * shard, width),
            )

        def results(m):
            for copy in rows_out[m]:
                copy.wait_send()
            for other in range(owners):
                for part in range(2):
                    stage[part, m * owners + other] = acc_scr[
                        m, part, other * capacity : (other + 1) * capacity, :
                    ].astype(HALF)

        def first_step(i):
            across[i].wait_recv()
            w_in, w_out = weights(order[i])
            expert_step(
                rows_of(0, 0),
                rows_of(1, 0),
                rows_one,
                w_in,
                w_out,
                NT,
                acc_scr.at[0],
                held.at[:, i],
                i == 0,
                2 * capacity,
            )

        rows_own[0].wait()
        for copy in rows_out[0]:
            copy.wait_recv()
        for i in range(zs - 1):
            first_step(i)

        rows_own[1].wait()
        for copy in rows_out[1]:
            copy.wait_recv()
        for at in range(0, width, 128):
            for part, scr in enumerate((xt_scr, dyt_scr)):
                scr[at : at + 128, :] = jnp.transpose(
                    arrived[part, :, :, at : at + 128].reshape(rows_all, 128)
                )
        turn = [2, 1, 3, 0]
        halves = [
            link(dw_stage.at[i % 2, 1 - c], core_any.at[i], core, 17 + i) for i in range(zs)
        ]
        fetches = [
            pltpu.make_async_copy(core_any.at[i], core_scr, core_sem) for i in range(zs)
        ]
        writes = [
            pltpu.make_async_copy(
                dw_stage.at[i % 2, c], dw_any.at[order[turn[i]]], dw_sem.at[i % 2]
            )
            for i in range(zs)
        ]

        def add_core(i):
            fetches[i].wait()
            for part in range(2):

                @pl.loop(0, width // 128)
                def _(r):
                    rows = pl.ds(pl.multiple_of(r * 128, 128), 128)
                    dw_stage[i % 2, c, part, rows, :] = (
                        dw_stage[i % 2, c, part, rows, :].astype(SINGLE)
                        + core_scr[part, rows, :].astype(SINGLE)
                    ).astype(HALF)

            writes[i].start()

        for i in range(zs):
            slot = i % 2
            fetch = [
                pltpu.make_async_copy(
                    held.at[part, turn[i]], current.at[part, pl.ds(0, rows_one)], held_sem.at[part]
                )
                for part in range(2)
            ]
            for copy in fetch:
                copy.start()
            w_in, w_out = weights(order[turn[i]])
            expert_step(
                rows_of(0, 1),
                rows_of(1, 1),
                rows_one,
                w_in,
                w_out,
                NT,
                acc_scr.at[1],
                current.at[:, pl.ds(rows_one, rows_one)],
                i == 0,
                2 * capacity,
            )
            for copy in fetch:
                copy.wait()
            if i > 1:
                halves[i - 1].wait_recv()
                fetches[i - 1].start()
                halves[i - 2].wait_send()

            @pl.loop(0, width // TILE)
            def _(r):
                rows = pl.ds(pl.multiple_of(r * TILE, TILE), TILE)
                for part, left in enumerate((xt_scr, dyt_scr)):
                    total = mm(left[rows, :], current[1 - part]).astype(HALF)
                    for g in range(xs):
                        dw_stage[slot, g, part, rows, :] = total[:, g * shard : (g + 1) * shard]

            halves[i].start()
            if i > 1:
                add_core(i - 1)
            if i == 0:
                onward.wait_recv()
                across[3].start()
                halves[0].wait_recv()
                fetches[0].start()
                add_core(0)
                writes[0].wait()
                near_far.start()
                first_step(3)
                results(0)
                for copy in results_out:
                    copy.start()
                results_own.start()
            if i == 2:
                writes[1].wait()
                near_own.start()
        results(1)
        final = pltpu.make_async_copy(
            stage.at[:, pl.ds(owners, owners)], done_any, held_sem.at[0]
        )
        final.start()
        halves[zs - 1].wait_recv()
        fetches[zs - 1].start()
        add_core(zs - 1)
        halves[zs - 2].wait_send()
        halves[zs - 1].wait_send()
        writes[zs - 2].wait()
        writes[zs - 1].wait()
        final.wait()
        for copy in results_out:
            copy.wait_send()
        results_own.wait()

    pl.run_scoped(
        second_half,
        pltpu.VMEM((width, rows_all), HALF),
        pltpu.VMEM((width, rows_all), HALF),
        pltpu.VMEM((micro, 2, rows_one, width), SINGLE),
        pltpu.VMEM((2, zs, rows_one, xs * shard), HALF),
        pltpu.VMEM((2, rows_all, xs * shard), HALF),
        pltpu.VMEM((2, xs, 2, width, shard), HALF),
        pltpu.VMEM((2, width, shard), HALF),
        pltpu.SemaphoreType.DMA((2,)),
        pltpu.SemaphoreType.DMA((2,)),
        pltpu.SemaphoreType.DMA,
    )

    @pl.when(x != c)
    def _():
        exchange.wait_send()

    spread[0].wait_send()
    spread[1].wait_send()
    onward.wait_send()
    for copy in across:
        copy.wait_send()
    for copy in results_out:
        copy.wait_recv()
    near_far.wait()
    near_own.wait()


def tail_kernel(
    capacity,
    experts,
    frozen,
    lengths_ref,
    routes_t_ref,
    norms_ref,
    wr_ref,
    lse_ref,
    info_ref,
    cols_ref,
    probs_ref,
    tokens_ref,
    cot_ref,
    wq_any,
    wk_any,
    wv_any,
    wo_any,
    a1_any,
    q_any,
    k_any,
    v_any,
    o_any,
    x1_any,
    a2_any,
    froz_any,
    ret_any,
    done_any,
    dw_any,
    near_any,
    own_any,
    mixed_any,
    xgrad_any,
    shared_ref,
    tiny_ref,
    gin_any,
    gout_any,
    w_scr,
    rows_scr,
    x1_scr,
    a1t_scr,
    ot_scr,
    db_scr,
    comb,
    small_scr,
    bias_scr,
    dx1_scr,
    do_scr,
    delta_scr,
    part_w,
    near_scr,
    own_scr,
    land_own,
    land_far,
    land_side,
    gin_scr,
    gout_scr,
    pay,
    got,
    tiny,
    tiny_got,
    send_sem,
    recv_sem,
    red_send,
    red_recv,
    in_sem,
    out_sem,
):
    micro, tok, width = tokens_ref.shape
    zs, xs, ys, cs = 4, 2, 2, 2
    dp, ex = lax.axis_index("dp"), lax.axis_index("expert")
    z, x, y, c = dp // xs, dp % xs, ex // cs, ex % cs
    me = y * xs + x
    owners = experts - frozen

    def device(zz, xx, yy, cc):
        return (zz * xs + xx, yy * cs + cc)

    z1, z2 = z + 1 - 2 * (z % 2), (z + 2) % zs
    others = [(x + (d & 1)) % 2 + xs * ((y + (d >> 1)) % 2) for d in (3, 2, 1)]
    row_peers = [device(z, other % xs, other // xs, c) for other in others]
    core = device(z, x, y, 1 - c)
    straight = device(z1, x, y, c)
    swapped, crossed = device(z, c, y, x), device(z2, c, y, x)
    fourth = device(z + (z1 - z) * ((x + c + 1) % 2), c, y, x)
    peers = row_peers + [crossed, fourth] + reduce_peers(z, x, y, c, zs, xs, cs)
    pl.semaphore_wait(meet(peers), len(peers))

    def link(source, target, peer, at):
        return remote(source, target, peer, send_sem, recv_sem, at)

    results_out = [
        link(done_any.at[:, other], comb.at[1, :, frozen + me], peer, i)
        for i, (other, peer) in enumerate(zip(others, row_peers))
    ]
    near_own = link(dw_any.at[z1, 1], land_own, straight, 4)
    far_sum = [link(part_w.at[0, i], land_far.at[i], crossed, 5 + i) for i in range(2)]
    side_sum = link(part_w.at[1], land_side, swapped, 7)

    near_own.start()
    for copy in results_out:
        copy.start()

    def load(source, target, at):
        copy = pltpu.make_async_copy(source, target, in_sem.at[at])
        copy.start()
        return copy

    loads = []
    for m in range(micro):
        group = []
        for i, source in enumerate(
            (tokens_ref, cot_ref, q_any, k_any, v_any, o_any, a2_any, a1_any)
        ):
            group.append(load(source.at[m], rows_scr.at[i, m], 16 * m + i))
        group.append(load(x1_any.at[m], x1_scr.at[m], 16 * m + 8))
        group.append(load(froz_any.at[:, :, m], comb.at[m, :, pl.ds(0, frozen)], 16 * m + 9))
        if m == 0:
            group.append(load(ret_any, comb.at[0, :, pl.ds(frozen, owners)], 10))
            for i, source in enumerate((wq_any, wk_any, wv_any, wo_any)):
                group.append(load(source, w_scr.at[i], 32 + i))
            mine = [load(dw_any.at[z2], part_w.at[0], 14), load(near_any, near_scr, 15)]
            mine_last = [load(dw_any.at[z], part_w.at[1], 36), load(own_any, own_scr, 11)]
        else:
            group.append(load(done_any.at[:, me], comb.at[1, :, frozen + me], 16 * m + 10))
        loads.append(group)

    def add_rows(target, source):
        @pl.loop(0, width // 128)
        def _(i):
            rows = pl.ds(pl.multiple_of(i * 128, 128), 128)
            target[rows, :] = (
                target[rows, :].astype(SINGLE) + source[rows, :].astype(SINGLE)
            ).astype(HALF)

    def after_own():
        for copy in mine_last:
            copy.wait()
        add_rows(part_w.at[1, 0], own_scr)
        near_own.wait()
        add_rows(part_w.at[1, 1], land_own)

        @pl.when(x != c)
        def _():
            side_sum.start()

    for copy in mine:
        copy.wait()
    for i in range(2):
        add_rows(part_w.at[0, i], near_scr.at[i])
        far_sum[i].start()

    def right_of(i):
        def get(k):
            cols = slice(k * TILE, (k + 1) * TILE)
            rows = db_scr[:, :, cols] if i is None else rows_scr[i, :, :, cols]
            return rows.reshape(micro * tok, TILE)

        return get

    reduction = Reduction(
        (z, x, y, c),
        (zs, xs, ys, cs),
        (a1t_scr, a1t_scr, a1t_scr, ot_scr),
        [right_of(i) for i in (2, 3, 4, None)],
        shared_ref,
        pay,
        got,
        red_send,
        red_recv,
    )

    def after_group(group):
        reduction.produce(group)
        if group >= 1:
            reduction.second(group - 1)
        if group >= 2:
            reduction.third(group - 2)

    outs = []

    def back(m, middle, after):
        x_ref, dy_ref, q_ref, k_ref, v_ref, o_ref, a2_ref, _ = [
            rows_scr.at[i, m] for i in range(8)
        ]
        back_body(
            capacity,
            experts,
            middle,
            after,
            lengths_ref.at[m],
            x_ref,
            dy_ref,
            routes_t_ref.at[m],
            norms_ref,
            w_scr.at[0],
            w_scr.at[1],
            w_scr.at[2],
            w_scr.at[3],
            wr_ref,
            q_ref,
            k_ref,
            v_ref,
            o_ref,
            x1_scr.at[m],
            a2_ref,
            lse_ref.at[m],
            info_ref.at[m],
            cols_ref.at[m],
            probs_ref.at[m],
            a2_ref,
            x1_scr.at[m],
            q_ref,
            k_ref,
            v_ref,
            db_scr.at[m],
            small_scr.at[m],
            comb.at[m, 0],
            comb.at[m, 1],
            bias_scr,
            dx1_scr,
            do_scr,
            delta_scr,
        )
        copy = pltpu.make_async_copy(a2_ref, mixed_any.at[m], out_sem.at[2 * m])
        copy.start()
        outs.append(copy)

    def finish(m, first, last):
        x_ref = rows_scr.at[0, m]
        finish_body(
            x_ref,
            norms_ref,
            w_scr.at[0],
            w_scr.at[1],
            w_scr.at[2],
            x1_scr.at[m],
            x_ref,
            rows_scr.at[2, m],
            rows_scr.at[3, m],
            rows_scr.at[4, m],
            small_scr.at[m],
            wr_ref.shape[0],
            first,
            last,
        )
        if last == tok // TILE:
            copy = pltpu.make_async_copy(x_ref, xgrad_any.at[m], out_sem.at[2 * m + 1])
            copy.start()
            outs.append(copy)

    for copy in loads[0]:
        copy.wait()
    back(0, None, None)
    finish(0, 0, tok // TILE)
    for copy in loads[1]:
        copy.wait()
    for m in range(micro):
        for at in range(0, width, 128):
            tokens_at = slice(m * tok, (m + 1) * tok)
            a1t_scr[at : at + 128, tokens_at] = jnp.transpose(rows_scr[7, m, :, at : at + 128])
            ot_scr[at : at + 128, tokens_at] = jnp.transpose(rows_scr[5, m, :, at : at + 128])
    for copy in results_out:
        copy.wait()
    back(1, after_own, after_group)

    tiny_peers = reduce_peers(z, x, y, c, zs, xs, cs)

    def spread_tiny(at):
        copy = remote(
            tiny, tiny_got.at[at], tiny_peers[(0, 2, 1, 3, 4, 5)[at]], red_send, red_recv, 36 + at
        )
        copy.start()
        return copy

    def gather_tiny(copy, at):
        copy.wait()
        tiny[...] += tiny_got[at]

    finish(1, 0, 1)
    reduction.second(2)
    reduction.third(1)
    reduction.fourth(0)
    finish(1, 1, tok // TILE)
    tiny[...] = small_scr[0] + small_scr[1]
    tiny_copy = spread_tiny(0)
    reduction.third(2)
    reduction.fourth(1)
    gather_tiny(tiny_copy, 0)
    tiny_copy = spread_tiny(1)
    reduction.final(0)
    gather_tiny(tiny_copy, 1)
    tiny_copy = spread_tiny(2)
    reduction.fourth(2)
    gather_tiny(tiny_copy, 2)
    tiny_copies = [spread_tiny(3 + i) for i in range(zs - 1)]
    reduction.final(1)
    for copy in far_sum:
        copy.wait()

    @pl.when(x != c)
    def _():
        side_sum.wait()

    def total_of(part, rows):
        base = land_far[part, rows, :].astype(SINGLE)
        own = part_w[1, part, rows, :].astype(SINGLE)
        other = land_side[part, rows, :].astype(SINGLE)
        return base + jnp.where(x == c, own, other)

    for i in range(0, width, 128):
        gin_scr[i : i + 128, :] = total_of(0, slice(i, i + 128))
        gout_scr[:, i : i + 128] = jnp.transpose(total_of(1, slice(i, i + 128)))
    done = [
        pltpu.make_async_copy(gin_scr, gin_any.at[0], out_sem.at[2 * micro]),
        pltpu.make_async_copy(gout_scr, gout_any.at[0], out_sem.at[2 * micro + 1]),
    ]
    for copy in done:
        copy.start()
    reduction.final(2)
    for copy in outs:
        copy.wait()
    for copy in tiny_copies:
        copy.wait()
    total = tiny[...]
    for i in range(zs - 1):
        total = total + tiny_got[3 + i]
    tiny_ref[...] = total
    for copy in done:
        copy.wait()


def vmem(count):
    return [pl.BlockSpec(memory_space=pltpu.VMEM)] * count


def params(mib, **more):
    return pltpu.CompilerParams(vmem_limit_bytes=mib << 20, **more)


def general(
    tokens,
    routes,
    lengths,
    key_mask,
    gain_one,
    bias_one,
    w_query,
    w_key,
    w_value,
    w_output,
    gain_two,
    bias_two,
    w_router,
    frozen_in,
    frozen_out,
    new_in,
    new_out,
    cotangent,
):
    micro, tok, width = tokens.shape
    owners = lax.axis_size("expert")
    dp = lax.axis_size("dp")
    frozen, _, ff = frozen_in.shape
    experts = frozen + owners
    capacity = 10 * tok // (4 * experts) // 8 * 8
    shard = new_in.shape[2]
    slots_all = experts * capacity
    shape = jax.ShapeDtypeStruct
    smem = pl.BlockSpec(memory_space=pltpu.SMEM)

    local_w = jnp.stack([new_in[0].T.astype(HALF), new_out[0].astype(HALF)], 0)
    all_w = lax.all_gather(local_w, "dp", axis=0, tiled=False)

    routes_t = jnp.swapaxes(routes, 1, 2)
    norms = jnp.concatenate([gain_one, bias_one, gain_two, bias_two]).reshape(4, width)
    rows16 = 16
    router_t = jnp.pad(w_router.T, ((0, rows16 - experts), (0, 0)))

    saved, froz_sent, arrived = [], [], []
    for m in range(micro):
        outs = pl.pallas_call(
            functools.partial(attend_kernel, capacity, experts, frozen),
            out_shape=[shape((tok, width), HALF)] * 5
            + [
                shape((tok, width), SINGLE),
                shape((tok, width), HALF),
                shape((16, tok), SINGLE),
                shape((8, tok), SINGLE),
                shape((tok, 128), SINGLE),
                shape((rows16, tok), SINGLE),
                shape((frozen, 2, capacity, width), HALF),
                shape((owners, 2, capacity, width), HALF),
            ],
            in_specs=[smem] + vmem(10),
            out_specs=vmem(13),
            scratch_shapes=[pltpu.VMEM((tok, tok), SINGLE), pltpu.VMEM((tok, 128), SINGLE)],
            compiler_params=params(56),
            cost_estimate=pl.CostEstimate(
                flops=8_000_000_000, bytes_accessed=20_000_000, transcendentals=3_000_000
            ),
            name="attend",
        )(
            lengths[m, 0],
            tokens[m],
            cotangent[m],
            routes_t[m],
            key_mask[m][None, :],
            norms,
            w_query,
            w_key,
            w_value,
            w_output,
            router_t,
        )
        saved.append(outs[:11])
        froz_sent.append(outs[11])
        arrived.append(
            lax.all_to_all(outs[12], "expert", split_axis=0, concat_axis=0, tiled=True)
        )

    block = min(768, ff)
    rows_spec = pl.BlockSpec((1, 2, capacity, width), lambda e, f: (e, 0, 0, 0))
    froz_back = pl.pallas_call(
        frozen_kernel,
        grid=(frozen, ff // block),
        out_shape=[shape((frozen, 2, capacity, width), HALF)] * 2,
        in_specs=[
            rows_spec,
            rows_spec,
            pl.BlockSpec((1, width, block), lambda e, f: (e, 0, f)),
            pl.BlockSpec((1, block, width), lambda e, f: (e, f, 0)),
        ],
        out_specs=[rows_spec, rows_spec],
        scratch_shapes=[
            pltpu.VMEM((2 * capacity, width), HALF),
            pltpu.VMEM((2 * capacity, width), HALF),
            pltpu.VMEM((2, 2 * capacity, width), SINGLE),
        ],
        compiler_params=params(50),
        cost_estimate=pl.CostEstimate(
            flops=16_000_000_000, bytes_accessed=25_000_000, transcendentals=2_500_000
        ),
        name="frozen",
    )(froz_sent[0], froz_sent[1], frozen_in, frozen_out)

    rows_all = micro * owners * capacity
    group = max(1, 768 // shard)
    whole = pl.BlockSpec((owners, 2, capacity, width), lambda f: (0, 0, 0, 0))
    done0, done1, grads_w = pl.pallas_call(
        owned_kernel,
        grid=(dp // group,),
        out_shape=[shape((owners, 2, capacity, width), HALF)] * 2
        + [shape((dp, 2, width, shard), HALF)],
        in_specs=[whole, whole, pl.BlockSpec((group, 2, shard, width), lambda f: (f, 0, 0, 0))],
        out_specs=[whole, whole, pl.BlockSpec((group, 2, width, shard), lambda f: (f, 0, 0, 0))],
        scratch_shapes=[
            pltpu.VMEM((rows_all, width), HALF),
            pltpu.VMEM((rows_all, width), HALF),
            pltpu.VMEM((width, rows_all), HALF),
            pltpu.VMEM((width, rows_all), HALF),
            pltpu.VMEM((2, rows_all, width), SINGLE),
            pltpu.VMEM((2, rows_all, group * shard), HALF),
        ],
        compiler_params=params(60),
        cost_estimate=pl.CostEstimate(
            flops=47_000_000_000, bytes_accessed=35_000_000, transcendentals=5_000_000
        ),
        name="owned",
    )(arrived[0], arrived[1], all_w)

    returned = [
        lax.all_to_all(one, "expert", split_axis=0, concat_axis=0, tiled=True)
        for one in (done0, done1)
    ]
    summed_w = lax.psum_scatter(grads_w, "dp", scatter_dimension=0, tiled=True)[0]

    mixed_list, xgrad_list, small_list, weight_ins = [], [], [], []
    for m in range(micro):
        a1, q, k, v, o, x1, a2, lse, info, cols, probs = saved[m]
        mixed, xgrad, dq, dk, dv, db, small = pl.pallas_call(
            functools.partial(back_kernel, capacity, experts),
            out_shape=[shape((tok, width), HALF)] * 6 + [shape((rows16 + 8, width), SINGLE)],
            in_specs=[smem] + vmem(21),
            out_specs=vmem(7),
            scratch_shapes=[
                pltpu.VMEM((slots_all, width), HALF),
                pltpu.VMEM((slots_all, width), HALF),
                pltpu.VMEM((tok, tok), SINGLE),
                pltpu.VMEM((tok, width), SINGLE),
                pltpu.VMEM((tok, width), HALF),
                pltpu.VMEM((tok, 128), SINGLE),
            ],
            compiler_params=params(56),
            cost_estimate=pl.CostEstimate(
                flops=16_000_000_000, bytes_accessed=25_000_000, transcendentals=3_000_000
            ),
            name="back",
        )(
            lengths[m, 0],
            tokens[m],
            cotangent[m],
            routes_t[m],
            norms,
            w_query,
            w_key,
            w_value,
            w_output,
            router_t,
            q,
            k,
            v,
            o,
            x1,
            a2,
            lse,
            info,
            cols,
            probs,
            froz_back[m],
            returned[m],
        )
        mixed_list.append(mixed)
        xgrad_list.append(xgrad)
        small_list.append(small)
        weight_ins += [a1, o, dq, dk, dv, db]

    grads = pl.pallas_call(
        weights_kernel,
        out_shape=shape((4, width, width), HALF),
        in_specs=vmem(len(weight_ins)),
        out_specs=vmem(1)[0],
        compiler_params=params(50),
        name="weights",
    )(*weight_ins)
    shared = lax.psum_scatter(grads, ("dp", "expert"), scatter_dimension=1, tiled=True)
    shared = shared.astype(SINGLE)
    small = sum(small_list[1:], small_list[0])
    small = jnp.concatenate([small[:experts], small[rows16 : rows16 + 4]], 0).T
    small = lax.psum_scatter(small, ("dp", "expert"), scatter_dimension=0, tiled=True)
    return (
        jnp.stack(mixed_list, 0),
        jnp.stack(xgrad_list, 0),
        small[:, experts + 2],
        small[:, experts + 3],
        shared[0],
        shared[1],
        shared[2],
        shared[3],
        small[:, experts],
        small[:, experts + 1],
        small[:, :experts],
        summed_w[0].astype(SINGLE)[None],
        summed_w[1].astype(SINGLE).T[None],
    )


def fused(
    tokens,
    routes,
    lengths,
    key_mask,
    gain_one,
    bias_one,
    w_query,
    w_key,
    w_value,
    w_output,
    gain_two,
    bias_two,
    w_router,
    frozen_in,
    frozen_out,
    new_in,
    new_out,
    cotangent,
):
    micro, tok, width = tokens.shape
    owners = lax.axis_size("expert")
    dp = lax.axis_size("dp")
    frozen = frozen_in.shape[0]
    experts = frozen + owners
    capacity = 10 * tok // (4 * experts) // 8 * 8
    shard = new_in.shape[2]
    zs, xs, ys, cs = 4, 2, 2, 2
    shape = jax.ShapeDtypeStruct
    smem = pl.BlockSpec(memory_space=pltpu.SMEM)

    def anywhere(count):
        return [pl.BlockSpec(memory_space=pl.ANY)] * count

    routes_t = jnp.swapaxes(routes, 1, 2)
    norms = jnp.concatenate([gain_one, bias_one, gain_two, bias_two]).reshape(4, width)
    rows16 = 16
    router_t = jnp.pad(w_router.T, ((0, rows16 - experts), (0, 0)))
    dma = pltpu.SemaphoreType.DMA

    outs = pl.pallas_call(
        functools.partial(front_kernel, capacity, experts, frozen),
        out_shape=[shape((micro, tok, width), HALF)] * 5
        + [
            shape((micro, tok, width), SINGLE),
            shape((micro, tok, width), HALF),
            shape((micro, 16, tok), SINGLE),
            shape((micro, 8, tok), SINGLE),
            shape((micro, tok, 128), SINGLE),
            shape((micro, rows16, tok), SINGLE),
            shape((2, frozen, micro, capacity, width), HALF),
            shape((2, owners, capacity, width), HALF),
            shape((2, owners, capacity, width), HALF),
            shape((zs, 2, width, shard), HALF),
            shape((zs, 2, width, shard), HALF),
            shape((2, width, shard), HALF),
            shape((width, shard), HALF),
        ],
        in_specs=[smem] + vmem(4) + anywhere(10),
        out_specs=anywhere(7) + vmem(4) + anywhere(7),
        scratch_shapes=[
            pltpu.VMEM((dp, 2, shard, width), HALF),
            pltpu.VMEM((2, shard, width), HALF),
            pltpu.VMEM((2, micro * owners, capacity, width), HALF),
            pltpu.VMEM((2, micro * owners, capacity, width), HALF),
            dma((23,)),
            dma((23,)),
            dma((4,)),
        ],
        compiler_params=params(63, collective_id=1, has_side_effects=True),
        name="front",
    )(
        lengths[:, 0],
        routes_t,
        key_mask,
        norms,
        router_t,
        tokens,
        cotangent,
        w_query,
        w_key,
        w_value,
        w_output,
        frozen_in,
        frozen_out,
        new_in,
        new_out,
    )
    a1, q, k, v, o, x1, a2, lse, info, cols, probs, froz, ret, done, dw, _, near, own = outs
    rows = width // (dp * owners)
    blocks = width // 128
    landing = [(zs, xs, ys), (zs, 2), (zs,), (zs - 1,)]
    mixed, xgrad, shared, small, grad_in, grad_out = pl.pallas_call(
        functools.partial(tail_kernel, capacity, experts, frozen),
        out_shape=[
            shape((micro, tok, width), HALF),
            shape((micro, tok, width), HALF),
            shape((4, rows, width), SINGLE),
            shape((rows16 + 8, width), SINGLE),
            shape((1, width, shard), SINGLE),
            shape((1, shard, width), SINGLE),
        ],
        in_specs=[smem] + vmem(7) + anywhere(19),
        out_specs=anywhere(2) + vmem(2) + anywhere(2),
        scratch_shapes=[
            pltpu.VMEM((4, width, width), HALF),
            pltpu.VMEM((8, micro, tok, width), HALF),
            pltpu.VMEM((micro, tok, width), SINGLE),
            pltpu.VMEM((width, micro * tok), HALF),
            pltpu.VMEM((width, micro * tok), HALF),
            pltpu.VMEM((micro, tok, width), HALF),
            pltpu.VMEM((micro, 2, experts, capacity, width), HALF),
            pltpu.VMEM((micro, rows16 + 8, width), SINGLE),
            pltpu.VMEM((tok, tok), SINGLE),
            pltpu.VMEM((tok, width), SINGLE),
            pltpu.VMEM((tok, width), HALF),
            pltpu.VMEM((tok, 128), SINGLE),
            pltpu.VMEM((2, 2, width, shard), HALF),
            pltpu.VMEM((2, width, shard), HALF),
            pltpu.VMEM((width, shard), HALF),
            pltpu.VMEM((width, shard), HALF),
            pltpu.VMEM((2, width, shard), HALF),
            pltpu.VMEM((2, width, shard), HALF),
            pltpu.VMEM((width, shard), SINGLE),
            pltpu.VMEM((shard, width), SINGLE),
            pltpu.VMEM((blocks, zs, xs, ys, cs, 4 * rows, 128), HALF),
            [pltpu.VMEM((blocks,) + lead + (4 * rows, 128), HALF) for lead in landing],
            pltpu.VMEM((rows16 + 8, width), SINGLE),
            pltpu.VMEM((zs + 2, rows16 + 8, width), SINGLE),
            dma((8,)),
            dma((8,)),
            dma((42,)),
            dma((42,)),
            dma((37,)),
            dma((2 * micro + 2,)),
        ],
        compiler_params=params(63, collective_id=2, has_side_effects=True),
        name="tail",
    )(
        lengths[:, 0],
        routes_t,
        norms,
        router_t,
        lse,
        info,
        cols,
        probs,
        tokens,
        cotangent,
        w_query,
        w_key,
        w_value,
        w_output,
        a1,
        q,
        k,
        v,
        o,
        x1,
        a2,
        froz,
        ret,
        done,
        dw,
        near,
        own,
    )
    at = (lax.axis_index("dp") * owners + lax.axis_index("expert")) * rows
    small = lax.dynamic_slice_in_dim(small, at, rows, 1)
    return (
        mixed,
        xgrad,
        small[rows16 + 2],
        small[rows16 + 3],
        shared[0],
        shared[1],
        shared[2],
        shared[3],
        small[rows16],
        small[rows16 + 1],
        small[:experts].T,
        grad_in,
        grad_out,
    )


def solution(mesh):
    both = ("dp", "expert")
    small_slice = mesh.shape["dp"] == 8 and mesh.shape["expert"] == 4
    return jax.shard_map(
        fused if small_slice else general,
        mesh=mesh,
        in_specs=(
            P(None, both, None),
            P(None, both, None),
            P(None, both, None),
            P(None, both),
        )
        + (P(),) * 11
        + (P("expert", None, "dp"), P("expert", "dp", None), P(None, both, None)),
        out_specs=(P(None, both, None), P(None, both, None), P(both), P(both))
        + (P(both, None),) * 4
        + (P(both), P(both), P(both, None), P("expert", None, "dp"), P("expert", "dp", None)),
        check_vma=False,
    )
```

```python
import functools

import jax
import jax.numpy as jnp
from jax import lax
from jax.experimental import pallas as pl
from jax.experimental.pallas import tpu as pltpu
from jax.sharding import PartitionSpec as P

HEAD = 64
PAIR = 2 * HEAD
TILE = 256
EPS = 1e-05
HALF = jnp.bfloat16
SINGLE = jnp.float32
HIDDEN = -1000000000.0
GELU_C = 0.7978845608028654
GELU_A = 0.044715

NN = (((1,), (0,)), ((), ()))
NT = (((1,), (1,)), ((), ()))
TN = (((0,), (0,)), ((), ()))


def mm(a, b, dims=NN):
    return lax.dot_general(a, b, dims, preferred_element_type=SINGLE)


def norm_rows(values):
    center = values - jnp.mean(values, -1, keepdims=True)
    inverse = lax.rsqrt(jnp.mean(center * center, -1, keepdims=True) + EPS)
    return center * inverse, inverse


def norm_back(grad, unit_rows, inverse, gain):
    scaled = grad * gain
    return inverse * (
        scaled
        - jnp.mean(scaled, -1, keepdims=True)
        - unit_rows * jnp.mean(scaled * unit_rows, -1, keepdims=True)
    )


def doc_of(places, lengths_ref):
    doc = jnp.zeros(places.shape, jnp.int32)
    end = 0
    for i in range(lengths_ref.shape[0]):
        end = end + lengths_ref[i]
        doc = doc + jnp.where(places >= end, 1, 0)
    return doc


def half_masks(rows):
    lane = lax.broadcasted_iota(jnp.int32, (rows, PAIR), 1)
    first = jnp.where(lane < HEAD, 1.0, 0.0).astype(HALF)
    second = jnp.where(lane < HEAD, 0.0, 1.0).astype(HALF)
    return lane < HEAD, (first, second)


def route_hots(routes_t_ref, rows, tokens):
    sub = lax.broadcasted_iota(jnp.int32, (rows, tokens), 0)
    return [sub == routes_t_ref[pick : pick + 1, :] for pick in range(2)]


def attend_kernel(capacity, experts, frozen, *refs):
    froz_ref, send_ref, bias_scr, lse_scr = refs[-4:]

    def target(e, part):
        return froz_ref.at[e, part] if e < frozen else send_ref.at[e - frozen, part]

    attend_body(capacity, experts, target, *refs[:-4], bias_scr, lse_scr)


def attend_body(
    capacity,
    experts,
    target,
    lengths_ref,
    x_ref,
    dy_ref,
    routes_t_ref,
    mask_ref,
    norms_ref,
    wq_ref,
    wk_ref,
    wv_ref,
    wo_ref,
    wr_ref,
    a1_ref,
    q_ref,
    k_ref,
    v_ref,
    o_ref,
    x1_ref,
    a2_ref,
    lse_ref,
    info_ref,
    cols_ref,
    probs_ref,
    bias_scr,
    lse_scr,
):
    tokens, width = x_ref.shape
    chunk = 128
    gain_one, bias_one = norms_ref[0:1, :], norms_ref[1:2, :]
    gain_two, bias_two = norms_ref[2:3, :], norms_ref[3:4, :]

    @pl.loop(0, tokens // chunk)
    def _(i):
        rows = pl.ds(pl.multiple_of(i * chunk, chunk), chunk)
        unit_rows, _ = norm_rows(x_ref[rows, :].astype(SINGLE))
        a1_ref[rows, :] = (unit_rows * gain_one + bias_one).astype(HALF)
        here = lax.broadcasted_iota(jnp.int32, (chunk, 1), 0) + i * chunk
        there = lax.broadcasted_iota(jnp.int32, (1, tokens), 1)
        same = doc_of(here, lengths_ref) == doc_of(there, lengths_ref)
        keep = (mask_ref[...] == 1) | (there == here)
        visible = same & (there <= here) & keep
        bias_scr[rows, :] = jnp.where(visible, 0.0, HIDDEN)

    @pl.loop(0, tokens // TILE)
    def _(i):
        rows = pl.ds(pl.multiple_of(i * TILE, TILE), TILE)
        a1 = a1_ref[rows, :]
        q_ref[rows, :] = (mm(a1, wq_ref[...]).astype(HALF) * HEAD ** (-0.5)).astype(HALF)
        k_ref[rows, :] = mm(a1, wk_ref[...]).astype(HALF)
        v_ref[rows, :] = mm(a1, wv_ref[...]).astype(HALF)

    lse_scr[...] = jnp.zeros_like(lse_scr)

    @pl.loop(0, width // PAIR)
    def _(i):
        cols = pl.ds(pl.multiple_of(i * PAIR, PAIR), PAIR)
        low, masks = half_masks(TILE)
        lane = lax.broadcasted_iota(jnp.int32, (TILE, 128), 1)
        for part in range(tokens // TILE):
            rows = slice(part * TILE, (part + 1) * TILE)
            keys = (part + 1) * TILE
            q_t = q_ref[rows, cols]
            k_t = k_ref[0:keys, cols]
            v_t = jnp.concatenate([v_ref[0:keys, cols], jnp.ones((keys, PAIR), HALF)], 1)
            results = []
            for h in range(2):
                scores = mm(q_t * masks[h], k_t, NT) + bias_scr[rows, 0:keys]
                top = jnp.max(scores, -1, keepdims=True)
                expo = jnp.exp(scores - top).astype(HALF)
                both = mm(expo, v_t)
                total = both[:, PAIR:]
                results.append(both[:, :PAIR] * (1.0 / total))
                log_total = top + jnp.log(total)
                lse_scr[rows, :] = jnp.where(lane == 2 * i + h, log_total, lse_scr[rows, :])
            o_ref[rows, cols] = jnp.where(low, results[0], results[1]).astype(HALF)

    lse_ref[...] = jnp.transpose(lse_scr[...])[0 : lse_ref.shape[0], :]

    @pl.loop(0, tokens // TILE)
    def _(i):
        rows = pl.ds(pl.multiple_of(i * TILE, TILE), TILE)
        x1 = x_ref[rows, :].astype(SINGLE) + mm(o_ref[rows, :], wo_ref[...])
        x1_ref[rows, :] = x1
        unit_rows, _ = norm_rows(x1)
        a2_ref[rows, :] = (unit_rows * gain_two + bias_two).astype(HALF)

    rows16 = wr_ref.shape[0]
    logits = mm(wr_ref[...], a2_ref[...], NT)
    sub = lax.broadcasted_iota(jnp.int32, (rows16, tokens), 0)
    logits = jnp.where(sub < experts, logits, -1e30)
    expo = jnp.exp(logits - jnp.max(logits, 0, keepdims=True))
    probs = expo / jnp.sum(expo, 0, keepdims=True)
    probs_ref[...] = probs
    hots = route_hots(routes_t_ref, rows16, tokens)
    chosen = [jnp.sum(jnp.where(hot, probs, 0.0), 0, keepdims=True) for hot in hots]
    chosen_total = chosen[0] + chosen[1]
    gates = [one / chosen_total for one in chosen]
    upper = jnp.where(
        lax.broadcasted_iota(jnp.int32, (tokens, tokens), 0)
        < lax.broadcasted_iota(jnp.int32, (tokens, tokens), 1),
        1.0,
        0.0,
    ).astype(HALF)
    both = jnp.where(hots[0] | hots[1], 1.0, 0.0).astype(HALF)
    earlier = mm(both, upper)
    places = []
    for pick in range(2):
        slot = jnp.sum(jnp.where(hots[pick], earlier, 0.0), 0, keepdims=True)
        first = routes_t_ref[pick : pick + 1, :].astype(SINGLE) * capacity
        places.append(jnp.where(slot < capacity, first + slot, -1.0))
    info = jnp.concatenate(
        places + gates + [mask_ref[...].astype(SINGLE), chosen_total, chosen_total, chosen_total], 0
    )
    info_ref[...] = info
    cols_ref[...] = jnp.transpose(
        jnp.concatenate([info, jnp.zeros((128 - info.shape[0], tokens), SINGLE)], 0)
    )
    spots = [one.astype(jnp.int32) for one in places]
    for e in range(experts):
        slots = lax.broadcasted_iota(jnp.int32, (capacity, tokens), 0) + e * capacity
        hit = [slots == spots[pick] for pick in range(2)]
        place = jnp.where(hit[0] | hit[1], 1.0, 0.0).astype(HALF)
        weight = jnp.sum(
            jnp.where(hit[0], gates[0], 0.0) + jnp.where(hit[1], gates[1], 0.0), 1, keepdims=True
        )
        target(e, 0)[...] = mm(place, a2_ref[...]).astype(HALF)
        target(e, 1)[...] = (mm(place, dy_ref[...]) * weight).astype(HALF)


def expert_step(x_of, dy_of, total, w_in, w_out, in_dims, acc_scr, held, first, chunk):
    back_dims = NT if in_dims == NN else NN

    @pl.loop(0, total // chunk)
    def _(i):
        rows = pl.ds(pl.multiple_of(i * chunk, 16), chunk)
        pre = mm(x_of(i), w_in, in_dims)
        grad = mm(dy_of(i), w_out, NT)
        square = pre * pre
        plus = 0.5 + 0.5 * jnp.tanh(pre * (GELU_C + GELU_C * GELU_A * square))
        gelu = pre * plus
        hidden = gelu.astype(HALF)
        slope = plus + gelu * (1.0 - plus) * (2.0 * GELU_C + 6.0 * GELU_C * GELU_A * square)
        grad_pre = (grad * slope).astype(HALF)
        if held is not None:
            held[0, rows, :] = hidden
            held[1, rows, :] = grad_pre
        out = mm(hidden, w_out)
        back = mm(grad_pre, w_in, back_dims)
        if first is True:
            acc_scr[0, rows, :] = out
            acc_scr[1, rows, :] = back
        elif first is False:
            acc_scr[0, rows, :] += out
            acc_scr[1, rows, :] += back
        else:

            @pl.when(first)
            def _():
                acc_scr[0, rows, :] = out
                acc_scr[1, rows, :] = back

            @pl.when(jnp.logical_not(first))
            def _():
                acc_scr[0, rows, :] += out
                acc_scr[1, rows, :] += back


def frozen_kernel(
    r0_ref, r1_ref, win_ref, wout_ref, o0_ref, o1_ref, x_scr, dy_scr, acc_scr
):
    capacity = r0_ref.shape[2]
    step, last = pl.program_id(1), pl.num_programs(1) - 1

    @pl.when(step == 0)
    def _():
        for m, ref in enumerate((r0_ref, r1_ref)):
            x_scr[m * capacity : (m + 1) * capacity, :] = ref[0, 0]
            dy_scr[m * capacity : (m + 1) * capacity, :] = ref[0, 1]

    expert_step(
        lambda i: x_scr[...],
        lambda i: dy_scr[...],
        2 * capacity,
        win_ref[0],
        wout_ref[0],
        NN,
        acc_scr,
        None,
        step == 0,
        2 * capacity,
    )

    @pl.when(step == last)
    def _():
        for m, ref in enumerate((o0_ref, o1_ref)):
            for part in range(2):
                ref[0, part] = acc_scr[part, m * capacity : (m + 1) * capacity, :].astype(HALF)


def owned_kernel(
    r0_ref,
    r1_ref,
    w_ref,
    o0_ref,
    o1_ref,
    dw_ref,
    x_scr,
    dy_scr,
    xt_scr,
    dyt_scr,
    acc_scr,
    held_scr,
):
    sources, _, capacity, width = r0_ref.shape
    group, _, shard, _ = w_ref.shape
    step, last = pl.program_id(0), pl.num_programs(0) - 1
    rows_all = x_scr.shape[0]

    @pl.when(step == 0)
    def _():
        for m, ref in enumerate((r0_ref, r1_ref)):
            for s in range(sources):
                at = (m * sources + s) * capacity
                x_scr[at : at + capacity, :] = ref[s, 0]
                dy_scr[at : at + capacity, :] = ref[s, 1]
        for at in range(0, width, 128):
            xt_scr[at : at + 128, :] = jnp.transpose(x_scr[:, at : at + 128])
            dyt_scr[at : at + 128, :] = jnp.transpose(dy_scr[:, at : at + 128])

    w_in = w_ref[:, 0].reshape(group * shard, width)
    w_out = w_ref[:, 1].reshape(group * shard, width)
    chunk = 2 * capacity
    expert_step(
        lambda i: x_scr[pl.ds(pl.multiple_of(i * chunk, 16), chunk), :],
        lambda i: dy_scr[pl.ds(pl.multiple_of(i * chunk, 16), chunk), :],
        rows_all,
        w_in,
        w_out,
        NT,
        acc_scr,
        held_scr,
        step == 0,
        chunk,
    )

    @pl.loop(0, width // TILE)
    def _(i):
        rows = pl.ds(pl.multiple_of(i * TILE, TILE), TILE)
        for part, (left, right) in enumerate(((xt_scr, held_scr.at[1]), (dyt_scr, held_scr.at[0]))):
            total = mm(left[rows, :], right[...]).astype(HALF)
            for g in range(group):
                dw_ref[g, part, rows, :] = total[:, g * shard : (g + 1) * shard]

    @pl.when(step == last)
    def _():
        for m, ref in enumerate((o0_ref, o1_ref)):
            for s in range(sources):
                at = (m * sources + s) * capacity
                for part in range(2):
                    ref[s, part] = acc_scr[part, at : at + capacity, :].astype(HALF)


def back_kernel(capacity, experts, *refs):
    froz_ref, back_ref = refs[20:22]
    mixed_ref, xgrad_ref, dq_ref, dk_ref, dv_ref, db_ref, small_ref = refs[22:29]
    out_scr, dbuf_scr = refs[29:31]
    frozen = froz_ref.shape[0]
    for e in range(experts):
        source = froz_ref.at[e] if e < frozen else back_ref.at[e - frozen]
        out_scr[e * capacity : (e + 1) * capacity, :] = source[0]
        dbuf_scr[e * capacity : (e + 1) * capacity, :] = source[1]
    dx1_scr = refs[32]
    back_body(capacity, experts, None, None, *refs[:20], mixed_ref, dx1_scr, *refs[24:])
    finish_body(
        refs[1],
        refs[4],
        *refs[5:8],
        dx1_scr,
        xgrad_ref,
        dq_ref,
        dk_ref,
        dv_ref,
        small_ref,
        refs[9].shape[0],
        0,
        refs[1].shape[0] // TILE,
    )


def flat(ref):
    rows = ref[...]
    return rows if rows.ndim == 2 else rows.reshape(-1, rows.shape[-1])


def block_of(ref, e, rows):
    return ref[rows, :] if len(ref.shape) == 2 else ref[e]


def back_body(
    capacity,
    experts,
    middle,
    after_group,
    lengths_ref,
    x_ref,
    dy_ref,
    routes_t_ref,
    norms_ref,
    wq_ref,
    wk_ref,
    wv_ref,
    wo_ref,
    wr_ref,
    q_ref,
    k_ref,
    v_ref,
    o_ref,
    x1_ref,
    a2_ref,
    lse_ref,
    info_ref,
    cols_ref,
    probs_ref,
    mixed_ref,
    dx1_ref,
    dq_ref,
    dk_ref,
    dv_ref,
    db_ref,
    small_ref,
    out_scr,
    dbuf_scr,
    bias_scr,
    dx1_scr,
    do_scr,
    delta_scr,
):
    tokens, width = x_ref.shape
    gain_two = norms_ref[2:3, :]
    slots_all = experts * capacity

    spots = [info_ref[pick : pick + 1, :].astype(jnp.int32) for pick in range(2)]
    gates = [info_ref[2 + pick : 3 + pick, :] for pick in range(2)]
    chosen_total = info_ref[5:6, :]

    def gate_part(e, carry):
        rows = pl.ds(pl.multiple_of(e * capacity, 16), capacity)
        overlap = mm(block_of(out_scr, e, rows), dy_ref[...], NT)
        slots = lax.broadcasted_iota(jnp.int32, (capacity, tokens), 0) + e * capacity
        return tuple(
            carry[pick]
            + jnp.sum(jnp.where(slots == spots[pick], overlap, 0.0), 0, keepdims=True)
            for pick in range(2)
        )

    zero_row = jnp.zeros((1, tokens), SINGLE)
    gate_grads = lax.fori_loop(0, experts, gate_part, (zero_row, zero_row))
    rows16 = wr_ref.shape[0]
    hots = route_hots(routes_t_ref, rows16, tokens)
    weighted = gate_grads[0] * gates[0] + gate_grads[1] * gates[1]
    grad_probs = jnp.where(hots[0], (gate_grads[0] - weighted) / chosen_total, 0.0)
    grad_probs = grad_probs + jnp.where(hots[1], (gate_grads[1] - weighted) / chosen_total, 0.0)
    probs = probs_ref[...]
    grad_logits = probs * (grad_probs - jnp.sum(grad_probs * probs, 0, keepdims=True))
    logits_low = grad_logits.astype(HALF)
    small_ref[0:rows16, :] = mm(logits_low, a2_ref[...])
    small_ref[rows16:, :] = jnp.zeros_like(small_ref[rows16:, :])

    @pl.loop(0, tokens // TILE)
    def _(i):
        rows = pl.ds(pl.multiple_of(i * TILE, TILE), TILE)
        slots = lax.broadcasted_iota(jnp.int32, (TILE, slots_all), 1)
        hit = [slots == cols_ref[rows, pick : pick + 1].astype(jnp.int32) for pick in range(2)]
        gated = jnp.where(hit[0], cols_ref[rows, 2:3], 0.0)
        gated = jnp.where(hit[1], cols_ref[rows, 3:4], gated).astype(HALF)
        place = jnp.where(hit[0] | hit[1], 1.0, 0.0).astype(HALF)
        x1 = x1_ref[rows, :]
        mixed_ref[rows, :] = (x1 + mm(gated, flat(out_scr))).astype(HALF)
        dx1_scr[rows, :] = mm(place, flat(dbuf_scr))

    logits_col = jnp.transpose(
        jnp.concatenate([grad_logits, jnp.zeros((128 - rows16, tokens), SINGLE)], 0)
    )
    delta_scr[...] = logits_col.astype(HALF).astype(SINGLE)
    router = jnp.concatenate([wr_ref[...], jnp.zeros((128 - rows16, width), HALF)], 0)

    @pl.loop(0, tokens // TILE)
    def _(i):
        rows = pl.ds(pl.multiple_of(i * TILE, TILE), TILE)
        unit_rows, inverse = norm_rows(x1_ref[rows, :])
        grad = dx1_scr[rows, :] + mm(delta_scr[rows, :].astype(HALF), router)
        small_ref[rows16 : rows16 + 1, :] += jnp.sum(grad * unit_rows, 0, keepdims=True)
        small_ref[rows16 + 1 : rows16 + 2, :] += jnp.sum(grad, 0, keepdims=True)
        dx1 = dy_ref[rows, :].astype(SINGLE) + norm_back(grad, unit_rows, inverse, gain_two)
        dx1_ref[rows, :] = dx1
        branch = dx1.astype(HALF)
        db_ref[rows, :] = branch
        do_scr[rows, :] = mm(branch, wo_ref[...], NT).astype(HALF)

    if middle is not None:
        middle()

    @pl.loop(0, tokens // 128)
    def _(i):
        rows = pl.ds(pl.multiple_of(i * 128, 128), 128)
        key = lax.broadcasted_iota(jnp.int32, (128, 1), 0) + i * 128
        query = lax.broadcasted_iota(jnp.int32, (1, tokens), 1)
        same = doc_of(key, lengths_ref) == doc_of(query, lengths_ref)
        keep = (cols_ref[rows, 4:5] > 0.5) | (query == key)
        visible = same & (key <= query) & keep
        bias_scr[rows, :] = jnp.where(visible, 0.0, HIDDEN)

    def one_pair(i):
        cols = pl.ds(pl.multiple_of(i * PAIR, PAIR), PAIR)
        low, masks = half_masks(TILE)
        tiles = tokens // TILE
        half_sum = jnp.where(
            (lax.broadcasted_iota(jnp.int32, (8, PAIR), 1) // HEAD)
            == lax.broadcasted_iota(jnp.int32, (8, PAIR), 0),
            1.0,
            0.0,
        )
        overlap = do_scr[:, cols].astype(SINGLE) * o_ref[:, cols].astype(SINGLE)
        deltas = lax.dot_general(
            half_sum,
            overlap,
            NT,
            precision=lax.Precision.HIGHEST,
            preferred_element_type=SINGLE,
        )
        grad_q = [[None] * tiles for _ in range(2)]
        for part in range(tiles):
            keys = slice(part * TILE, (part + 1) * TILE)
            queries = slice(part * TILE, tokens)
            k_t, v_t = k_ref[keys, cols], v_ref[keys, cols]
            q_t, do_t = q_ref[queries, cols], do_scr[queries, cols]
            grad_k, grad_v = [], []
            for h in range(2):
                scores = mm(k_t * masks[h], q_t, NT) + bias_scr[keys, queries]
                log_total = lse_ref[pl.ds(2 * i + h, 1), queries]
                probs = jnp.exp(scores - log_total)
                grad_p = mm(v_t * masks[h], do_t, NT)
                grad_s = (probs * (grad_p - deltas[h : h + 1, queries])).astype(HALF)
                grad_v.append(mm(probs.astype(HALF), do_t))
                grad_k.append(mm(grad_s, q_t))
                step = mm(grad_s, k_t, TN)
                for t in range(part, tiles):
                    piece = step[(t - part) * TILE : (t - part + 1) * TILE, :]
                    grad_q[h][t] = piece if grad_q[h][t] is None else grad_q[h][t] + piece
            dv_ref[keys, cols] = jnp.where(low, grad_v[0], grad_v[1]).astype(HALF)
            dk_ref[keys, cols] = jnp.where(low, grad_k[0], grad_k[1]).astype(HALF)
        for t in range(tiles):
            both = jnp.where(low, grad_q[0][t], grad_q[1][t]) * HEAD ** (-0.5)
            dq_ref[t * TILE : (t + 1) * TILE, cols] = both.astype(HALF)

    if after_group is None:
        pl.loop(0, width // PAIR)(one_pair)
    else:
        for group in range(width // TILE):
            pl.loop(group * TILE // PAIR, (group + 1) * TILE // PAIR)(one_pair)
            after_group(group)


def finish_body(
    x_ref,
    norms_ref,
    wq_ref,
    wk_ref,
    wv_ref,
    dx1_ref,
    xgrad_ref,
    dq_ref,
    dk_ref,
    dv_ref,
    small_ref,
    rows16,
    first,
    last,
):
    gain_one = norms_ref[0:1, :]

    @pl.loop(first, last)
    def _(i):
        rows = pl.ds(pl.multiple_of(i * TILE, TILE), TILE)
        unit_rows, inverse = norm_rows(x_ref[rows, :].astype(SINGLE))
        grad = mm(dq_ref[rows, :], wq_ref[...], NT)
        grad = grad + mm(dk_ref[rows, :], wk_ref[...], NT)
        grad = grad + mm(dv_ref[rows, :], wv_ref[...], NT)
        small_ref[rows16 + 2 : rows16 + 3, :] += jnp.sum(grad * unit_rows, 0, keepdims=True)
        small_ref[rows16 + 3 : rows16 + 4, :] += jnp.sum(grad, 0, keepdims=True)
        part = norm_back(grad, unit_rows, inverse, gain_one)
        xgrad_ref[rows, :] = (dx1_ref[rows, :] + part).astype(HALF)


def weights_kernel(*refs):
    ins, dw_ref = refs[:-1], refs[-1]
    micro = len(ins) // 6
    width = dw_ref.shape[-1]

    @pl.loop(0, width // TILE)
    def _(i):
        cols = pl.ds(pl.multiple_of(i * TILE, TILE), TILE)
        for part in range(4):
            total = weight_grad(ins, micro, part, cols)
            dw_ref[part, cols, :] = total.astype(HALF)


def weight_grad(ins, micro, part, cols):
    total = None
    for m in range(micro):
        a1, o, dq, dk, dv, db = ins[6 * m : 6 * m + 6]
        left = o if part == 3 else a1
        right = (dq, dk, dv, db)[part]
        step = mm(left[:, cols], right[...], TN)
        total = step if total is None else total + step
    return total


def meet(peers):
    barrier = pltpu.get_barrier_semaphore()
    for peer in peers:
        pl.semaphore_signal(barrier, inc=1, device_id=peer, device_id_type=pl.DeviceIdType.MESH)
    return barrier


def remote(source, target, peer, send_sem, recv_sem, at):
    return pltpu.make_async_remote_copy(
        src_ref=source,
        dst_ref=target,
        send_sem=send_sem.at[at],
        recv_sem=recv_sem.at[at],
        device_id=peer,
        device_id_type=pl.DeviceIdType.MESH,
    )


def reduce_peers(z, x, y, c, zs, xs, cs):
    places = [(z, x, y, 1 - c), (z, 1 - x, y, c), (z, x, 1 - y, c)]
    places += [((z + step) % zs, x, y, c) for step in range(1, zs)]
    return [(zz * xs + xx, yy * cs + cc) for zz, xx, yy, cc in places]


class Reduction:
    def __init__(self, place, shape, lefts, rights, out_ref, pay, got, send_sem, recv_sem):
        self.place, self.shape = place, shape
        self.lefts, self.rights = lefts, rights
        self.out_ref, self.pay, self.got = out_ref, pay, got
        self.sems = send_sem, recv_sem
        self.rows = out_ref.shape[1]
        self.copies = [self.plan(k) for k in range(pay.shape[0])]

    def plan(self, k):
        z, x, y, c = self.place
        zs, xs, _, cs = self.shape
        pay, (first, second, third, fourth) = self.pay.at[k], [one.at[k] for one in self.got]

        def link(source, target, zz, xx, yy, cc, at):
            peer = (zz * xs + xx, yy * cs + cc)
            return remote(source, target, peer, *self.sems, 6 * k + at)

        start = link(pay.at[:, :, :, 1 - c], first, z, x, y, 1 - c, 0)
        if k % 2 == 0:
            two = link(pay.at[:, :, 1 - y, c], second, z, x, 1 - y, c, 1)
            three = link(pay.at[:, 1 - x, y, c], third, z, 1 - x, y, c, 2)
        else:
            two = link(pay.at[:, 1 - x, :, c], second, z, 1 - x, y, c, 1)
            three = link(pay.at[:, x, 1 - y, c], third, z, x, 1 - y, c, 2)
        four = []
        for step in range(1, zs):
            zz = (z + step) % zs
            four.append(link(pay.at[zz, x, y, c], fourth.at[step - 1], zz, x, y, c, 2 + step))
        return start, two, three, four

    def produce(self, k):
        zs, xs, ys, cs = self.shape
        rows = self.rows
        tile = 16 * rows
        width = self.lefts[0].shape[0]
        for j in range(width // tile):
            for part, (left, right) in enumerate(zip(self.lefts, self.rights)):
                total = mm(left[j * tile : (j + 1) * tile, :], right(k)).astype(HALF)
                for i in range(16):
                    n = 16 * j + i
                    at = (n // (ys * cs) // xs, n // (ys * cs) % xs, n % (ys * cs) // cs, n % cs)
                    for half in range(2):
                        spot = (2 * k + half,) + at + (slice(part * rows, (part + 1) * rows),)
                        self.pay[spot] = total[
                            i * rows : (i + 1) * rows, half * 128 : (half + 1) * 128
                        ]
        for half in range(2):
            self.copies[2 * k + half][0].start()

    def add(self, k, places):
        @pl.loop(0, self.shape[0])
        def _(i):
            for at, held in places(i):
                at = (k,) + at
                self.pay[at] = (self.pay[at].astype(SINGLE) + held[...].astype(SINGLE)).astype(
                    HALF
                )

    def second(self, block):
        for k in (2 * block, 2 * block + 1):
            self.second_half(k)

    def second_half(self, k):
        _, _, _, c = self.place
        _, xs, ys, _ = self.shape
        held = self.got[0].at[k]
        self.copies[k][0].wait()
        self.add(
            k,
            lambda i: [
                ((i, xx, yy, c), held.at[i, xx, yy]) for xx in range(xs) for yy in range(ys)
            ],
        )
        self.copies[k][1].start()

    def third(self, block):
        for k in (2 * block, 2 * block + 1):
            self.third_half(k)

    def third_half(self, k):
        _, x, y, c = self.place
        _, xs, ys, _ = self.shape
        held = self.got[1].at[k]
        self.copies[k][1].wait()
        if k % 2 == 0:
            self.add(k, lambda i: [((i, xx, y, c), held.at[i, xx]) for xx in range(xs)])
        else:
            self.add(k, lambda i: [((i, x, yy, c), held.at[i, yy]) for yy in range(ys)])
        self.copies[k][2].start()

    def fourth(self, block):
        for k in (2 * block, 2 * block + 1):
            self.fourth_half(k)

    def fourth_half(self, k):
        _, x, y, c = self.place
        held = self.got[2].at[k]
        self.copies[k][2].wait()
        self.add(k, lambda i: [((i, x, y, c), held.at[i])])
        for copy in self.copies[k][3]:
            copy.start()

    def final(self, block):
        for k in (2 * block, 2 * block + 1):
            self.final_half(k)

    def final_half(self, k):
        z, x, y, c = self.place
        held = self.got[3].at[k]
        for copy in self.copies[k][3]:
            copy.wait()
        total = self.pay[k, z, x, y, c].astype(SINGLE)
        for i in range(self.shape[0] - 1):
            total = total + held[i].astype(SINGLE)
        for part in range(4):
            self.out_ref[part, :, k * 128 : (k + 1) * 128] = total[
                part * self.rows : (part + 1) * self.rows
            ]


def front_kernel(
    capacity,
    experts,
    frozen,
    lengths_ref,
    routes_t_ref,
    mask_ref,
    norms_ref,
    wr_ref,
    tokens_ref,
    cot_ref,
    wq_any,
    wk_any,
    wv_any,
    wo_any,
    fin_any,
    fout_any,
    nin_any,
    nout_any,
    a1_any,
    q_any,
    k_any,
    v_any,
    o_any,
    x1_any,
    a2_any,
    lse_ref,
    info_ref,
    cols_ref,
    probs_ref,
    froz_any,
    ret_any,
    done_any,
    dw_any,
    core_any,
    near_any,
    first_any,
    own_any,
    all_w,
    local_w,
    stage,
    arrived,
    send_sem,
    recv_sem,
    own_sem,
):
    micro, tok, width = tokens_ref.shape
    zs, xs, cs = 4, 2, 2
    shard = nin_any.shape[2]
    dp, ex = lax.axis_index("dp"), lax.axis_index("expert")
    z, x, y, c = dp // xs, dp % xs, ex // cs, ex % cs
    me = y * xs + x
    owners = experts - frozen

    def device(zz, xx, yy, cc):
        return (zz * xs + xx, yy * cs + cc)

    def near(step):
        return z + 1 - 2 * (z % 2) if step == 1 else (zs - 1 - z if step == 3 else (z + 2) % zs)

    core = device(z, x, y, 1 - c)
    swapped = device(z, c, y, x)
    straight, distant = device(near(1), x, y, c), device(near(3), x, y, c)
    others = [(x + (d & 1)) % 2 + xs * ((y + (d >> 1)) % 2) for d in (3, 2, 1)]
    row_peers = [device(z, other % xs, other // xs, c) for other in others]
    fourth = device(z + (near(1) - z) * ((x + c + 1) % 2), c, y, x)
    peers = [core, straight, distant, fourth] + row_peers
    pl.semaphore_wait(meet(peers), len(peers))

    def link(source, target, peer, at):
        return remote(source, target, peer, send_sem, recv_sem, at)

    held_w = all_w.at[z * xs + c]
    exchange = link(local_w, all_w.at[dp], swapped, 0)
    spread = [link(held_w, held_w, straight, 1), link(held_w, held_w, distant, 2)]
    spread_own = [link(local_w, held_w, straight, 1), link(local_w, held_w, distant, 2)]
    keep_own = pltpu.make_async_copy(local_w, all_w.at[dp], own_sem.at[0])
    far = near(3) * xs + c
    onward = link(all_w.at[far], all_w.at[far], straight, 3)
    order = [z, near(1), near(3), near(2)]
    across = [
        link(all_w.at[zz * xs + c], all_w.at[zz * xs + c], core, 4 + i)
        for i, zz in enumerate(order)
    ]
    rows_out = [
        [
            link(
                stage.at[:, m * owners + other],
                arrived.at[:, m * owners + me],
                peer,
                8 + 3 * m + i,
            )
            for i, (other, peer) in enumerate(zip(others, row_peers))
        ]
        for m in range(micro)
    ]
    rows_own = [
        pltpu.make_async_copy(
            stage.at[:, m * owners + me], arrived.at[:, m * owners + me], own_sem.at[1 + m]
        )
        for m in range(micro)
    ]
    results_out = [
        link(stage.at[:, other], ret_any.at[:, me], peer, 14 + i)
        for i, (other, peer) in enumerate(zip(others, row_peers))
    ]
    results_own = pltpu.make_async_copy(stage.at[:, me], ret_any.at[:, me], own_sem.at[3])
    near_far = link(dw_any.at[near(3)], near_any, straight, 21)
    near_own = link(dw_any.at[near(1), 0], first_any, straight, 22)

    def first_half(
        w_scr,
        x_scr,
        dy_scr,
        a1_scr,
        q_scr,
        k_scr,
        v_scr,
        o_scr,
        x1_scr,
        a2_scr,
        bias_scr,
        lse_scr,
        froz_rows,
        win_scr,
        wout_scr,
        acc_scr,
        nin_scr,
        in_sem,
        out_sem,
        stream_sem,
    ):
        def load(source, target, at):
            copy = pltpu.make_async_copy(source, target, in_sem.at[at])
            copy.start()
            return copy

        nout_scr = x1_scr.at[1, pl.ds(0, shard)]
        new_loads = [load(nin_any.at[0], nin_scr, 0), load(nout_any.at[0], nout_scr, 1)]
        row_loads = [
            [
                load(tokens_ref.at[m], x_scr.at[m], 2 + 2 * m),
                load(cot_ref.at[m], dy_scr.at[m], 3 + 2 * m),
            ]
            for m in range(micro)
        ]
        weight_loads = [
            load(ref, w_scr.at[i], 2 + 2 * micro + i)
            for i, ref in enumerate((wq_any, wk_any, wv_any, wo_any))
        ]
        for copy in new_loads:
            copy.wait()
        local_w[0] = jnp.transpose(nin_scr[...]).astype(HALF)
        local_w[1] = nout_scr[...].astype(HALF)

        @pl.when(x != c)
        def _():
            exchange.start()

        @pl.when(x == c)
        def _():
            keep_own.start()
            spread_own[1].start()
            spread_own[0].start()

        blocks = fin_any.shape[2] // width

        def stream(step, slot):
            e, f = step // blocks, step % blocks
            at = pl.ds(pl.multiple_of(f * width, width), width)
            return (
                pltpu.make_async_copy(
                    fin_any.at[e, :, at], win_scr.at[slot], stream_sem.at[0, slot]
                ),
                pltpu.make_async_copy(
                    fout_any.at[e, at, :], wout_scr.at[slot], stream_sem.at[1, slot]
                ),
            )

        for copy in stream(0, 0):
            copy.start()
        for copy in weight_loads + row_loads[0]:
            copy.wait()
        saves = []
        for m in range(micro):
            if m:
                for copy in row_loads[m]:
                    copy.wait()

            def target(e, part, m=m):
                if e < frozen:
                    return froz_rows.at[part, e, m]
                return stage.at[part, m * owners + e - frozen]

            attend_body(
                capacity,
                experts,
                target,
                lengths_ref.at[m],
                x_scr.at[m],
                dy_scr.at[m],
                routes_t_ref.at[m],
                mask_ref.at[pl.ds(m, 1)],
                norms_ref,
                w_scr.at[0],
                w_scr.at[1],
                w_scr.at[2],
                w_scr.at[3],
                wr_ref,
                a1_scr.at[m],
                q_scr.at[m],
                k_scr.at[m],
                v_scr.at[m],
                o_scr.at[m],
                x1_scr.at[m],
                a2_scr.at[m],
                lse_ref.at[m],
                info_ref.at[m],
                cols_ref.at[m],
                probs_ref.at[m],
                bias_scr,
                lse_scr,
            )
            for copy in rows_out[m]:
                copy.start()
            rows_own[m].start()
            for i, (source, target_any) in enumerate(
                (
                    (a1_scr, a1_any),
                    (q_scr, q_any),
                    (k_scr, k_any),
                    (v_scr, v_any),
                    (o_scr, o_any),
                    (x1_scr, x1_any),
                    (a2_scr, a2_any),
                )
            ):
                copy = pltpu.make_async_copy(
                    source.at[m], target_any.at[m], out_sem.at[7 * m + i]
                )
                copy.start()
                saves.append(copy)
            if m == 0:

                @pl.when(x != c)
                def _():
                    exchange.wait_recv()
                    spread[1].start()
                    spread[0].start()

                @pl.when(x == c)
                def _():
                    keep_own.wait()

                across[0].start()


        steps = frozen * blocks

        @pl.loop(0, steps)
        def _(step):
            slot = step % 2
            e = step // blocks

            @pl.when(step + 1 < steps)
            def _():
                for copy in stream(step + 1, 1 - slot):
                    copy.start()

            for copy in stream(step, slot):
                copy.wait()
            expert_step(
                lambda rows: froz_rows[0, e].reshape(micro * capacity, width)[...],
                lambda rows: froz_rows[1, e].reshape(micro * capacity, width)[...],
                micro * capacity,
                win_scr[slot],
                wout_scr[slot],
                NN,
                acc_scr,
                None,
                step % blocks == 0,
                micro * capacity,
            )

            @pl.when(step % blocks == blocks - 1)
            def _():
                for m in range(micro):
                    for part in range(2):
                        froz_rows[part, e, m] = acc_scr[
                            part, m * capacity : (m + 1) * capacity, :
                        ].astype(HALF)

            @pl.when(step == steps // 2)
            def _():
                spread[1].wait_recv()
                onward.start()
                across[2].start()

            @pl.when(step == steps // 2 + 1)
            def _():
                spread[0].wait_recv()
                across[1].start()

        last = pltpu.make_async_copy(froz_rows, froz_any, out_sem.at[7 * micro])
        last.start()
        for copy in saves:
            copy.wait()
        last.wait()

    pl.run_scoped(
        first_half,
        pltpu.VMEM((4, width, width), HALF),
        pltpu.VMEM((micro, tok, width), HALF),
        pltpu.VMEM((micro, tok, width), HALF),
        pltpu.VMEM((micro, tok, width), HALF),
        pltpu.VMEM((micro, tok, width), HALF),
        pltpu.VMEM((micro, tok, width), HALF),
        pltpu.VMEM((micro, tok, width), HALF),
        pltpu.VMEM((micro, tok, width), HALF),
        pltpu.VMEM((micro, tok, width), SINGLE),
        pltpu.VMEM((micro, tok, width), HALF),
        pltpu.VMEM((tok, tok), SINGLE),
        pltpu.VMEM((tok, 128), SINGLE),
        pltpu.VMEM((2, frozen, micro, capacity, width), HALF),
        pltpu.VMEM((2, width, width), HALF),
        pltpu.VMEM((2, width, width), HALF),
        pltpu.VMEM((2, micro * capacity, width), SINGLE),
        pltpu.VMEM((width, shard), SINGLE),
        pltpu.SemaphoreType.DMA((2 + 2 * micro + 4,)),
        pltpu.SemaphoreType.DMA((7 * micro + 1,)),
        pltpu.SemaphoreType.DMA((2, 2)),
    )

    rows_one = owners * capacity
    rows_all = micro * rows_one

    def second_half(
        xt_scr, dyt_scr, acc_scr, held, current, dw_stage, core_scr, held_sem, dw_sem, core_sem
    ):
        def rows_of(part, m):
            def get(rows):
                return arrived[part, pl.ds(m * owners, owners)].reshape(rows_one, width)

            return get

        def weights(zz):
            two = all_w.at[pl.ds(zz * xs, xs)]
            return (
                two[:, 0].reshape(xs * shard, width),
                two[:, 1].reshape(xs * shard, width),
            )

        def results(m):
            for copy in rows_out[m]:
                copy.wait_send()
            for other in range(owners):
                for part in range(2):
                    stage[part, m * owners + other] = acc_scr[
                        m, part, other * capacity : (other + 1) * capacity, :
                    ].astype(HALF)

        def first_step(i):
            across[i].wait_recv()
            w_in, w_out = weights(order[i])
            expert_step(
                rows_of(0, 0),
                rows_of(1, 0),
                rows_one,
                w_in,
                w_out,
                NT,
                acc_scr.at[0],
                held.at[:, i],
                i == 0,
                rows_one,
            )

        rows_own[0].wait()
        for copy in rows_out[0]:
            copy.wait_recv()
        for i in range(zs - 1):
            first_step(i)

        rows_own[1].wait()
        for copy in rows_out[1]:
            copy.wait_recv()
        for at in range(0, width, 128):
            for part, scr in enumerate((xt_scr, dyt_scr)):
                scr[at : at + 128, :] = jnp.transpose(
                    arrived[part, :, :, at : at + 128].reshape(rows_all, 128)
                )
        turn = [2, 1, 3, 0]
        halves = [
            link(dw_stage.at[i % 2, 1 - c], core_any.at[i], core, 17 + i) for i in range(zs - 1)
        ]
        fetches = [
            pltpu.make_async_copy(core_any.at[i], core_scr, core_sem) for i in range(zs - 1)
        ]
        writes = [
            pltpu.make_async_copy(
                dw_stage.at[i % 2, c], dw_any.at[order[turn[i]]], dw_sem.at[i % 2]
            )
            for i in range(zs)
        ]

        def add_core(i):
            fetches[i].wait()
            for part in range(2):

                @pl.loop(0, width // 128)
                def _(r):
                    rows = pl.ds(pl.multiple_of(r * 128, 128), 128)
                    dw_stage[i % 2, c, part, rows, :] = (
                        dw_stage[i % 2, c, part, rows, :].astype(SINGLE)
                        + core_scr[part, rows, :].astype(SINGLE)
                    ).astype(HALF)

            writes[i].start()

        for i in range(zs):
            slot = i % 2
            fetch = [
                pltpu.make_async_copy(
                    held.at[part, turn[i]], current.at[part, pl.ds(0, rows_one)], held_sem.at[part]
                )
                for part in range(2)
            ]
            for copy in fetch:
                copy.start()
            w_in, w_out = weights(order[turn[i]])
            expert_step(
                rows_of(0, 1),
                rows_of(1, 1),
                rows_one,
                w_in,
                w_out,
                NT,
                acc_scr.at[1],
                current.at[:, pl.ds(rows_one, rows_one)],
                i == 0,
                rows_one,
            )
            for copy in fetch:
                copy.wait()
            if i > 1:
                halves[i - 1].wait_recv()
                fetches[i - 1].start()
                halves[i - 2].wait_send()
            if i == 2:
                add_core(1)
                writes[1].wait()
                near_own.start()

            @pl.loop(0, width // TILE)
            def _(r):
                rows = pl.ds(pl.multiple_of(r * TILE, TILE), TILE)
                for part, left in enumerate((xt_scr, dyt_scr)):
                    total = mm(left[rows, :], current[1 - part]).astype(HALF)
                    for g in range(xs):
                        dw_stage[slot, g, part, rows, :] = total[:, g * shard : (g + 1) * shard]

            if i < zs - 1:
                halves[i].start()
            if i > 2:
                add_core(i - 1)
            if i == 0:
                onward.wait_recv()
                across[3].start()
                halves[0].wait_recv()
                fetches[0].start()
                add_core(0)
                writes[0].wait()
                near_far.start()
                first_step(3)
                results(0)
                for copy in results_out:
                    copy.start()
                results_own.start()
        results(1)
        final = pltpu.make_async_copy(
            stage.at[:, pl.ds(owners, owners)], done_any, held_sem.at[0]
        )
        final.start()
        writes[zs - 1].start()
        other_half = pltpu.make_async_copy(
            dw_stage.at[(zs - 1) % 2, 1 - c], own_any, held_sem.at[1]
        )
        other_half.start()
        halves[zs - 2].wait_send()
        writes[zs - 2].wait()
        writes[zs - 1].wait()
        other_half.wait()
        final.wait()
        for copy in results_out:
            copy.wait_send()
        results_own.wait()

    pl.run_scoped(
        second_half,
        pltpu.VMEM((width, rows_all), HALF),
        pltpu.VMEM((width, rows_all), HALF),
        pltpu.VMEM((micro, 2, rows_one, width), SINGLE),
        pltpu.VMEM((2, zs, rows_one, xs * shard), HALF),
        pltpu.VMEM((2, rows_all, xs * shard), HALF),
        pltpu.VMEM((2, xs, 2, width, shard), HALF),
        pltpu.VMEM((2, width, shard), HALF),
        pltpu.SemaphoreType.DMA((2,)),
        pltpu.SemaphoreType.DMA((2,)),
        pltpu.SemaphoreType.DMA,
    )

    @pl.when(x != c)
    def _():
        exchange.wait_send()

    spread[0].wait_send()
    spread[1].wait_send()
    onward.wait_send()
    for copy in across:
        copy.wait_send()
    for copy in results_out:
        copy.wait_recv()
    near_far.wait()
    near_own.wait()


def tail_kernel(
    capacity,
    experts,
    frozen,
    lengths_ref,
    routes_t_ref,
    norms_ref,
    wr_ref,
    lse_ref,
    info_ref,
    cols_ref,
    probs_ref,
    tokens_ref,
    cot_ref,
    wq_any,
    wk_any,
    wv_any,
    wo_any,
    a1_any,
    q_any,
    k_any,
    v_any,
    o_any,
    x1_any,
    a2_any,
    froz_any,
    ret_any,
    done_any,
    dw_any,
    near_any,
    first_any,
    own_any,
    mixed_any,
    xgrad_any,
    shared_ref,
    tiny_ref,
    gin_any,
    gout_any,
    w_scr,
    rows_scr,
    x1_scr,
    a1t_scr,
    ot_scr,
    db_scr,
    comb,
    small_scr,
    bias_scr,
    dx1_scr,
    do_scr,
    delta_scr,
    part_w,
    near_scr,
    land_core,
    land_own,
    land_far,
    land_side,
    gin_scr,
    gout_scr,
    pay,
    got,
    tiny,
    tiny_got,
    send_sem,
    recv_sem,
    red_send,
    red_recv,
    in_sem,
    out_sem,
):
    micro, tok, width = tokens_ref.shape
    zs, xs, ys, cs = 4, 2, 2, 2
    dp, ex = lax.axis_index("dp"), lax.axis_index("expert")
    z, x, y, c = dp // xs, dp % xs, ex // cs, ex % cs
    me = y * xs + x
    owners = experts - frozen

    def device(zz, xx, yy, cc):
        return (zz * xs + xx, yy * cs + cc)

    z1, z2 = z + 1 - 2 * (z % 2), (z + 2) % zs
    others = [(x + (d & 1)) % 2 + xs * ((y + (d >> 1)) % 2) for d in (3, 2, 1)]
    row_peers = [device(z, other % xs, other // xs, c) for other in others]
    core = device(z, x, y, 1 - c)
    straight = device(z1, x, y, c)
    swapped, crossed = device(z, c, y, x), device(z2, c, y, x)
    fourth = device(z + (z1 - z) * ((x + c + 1) % 2), c, y, x)
    peers = row_peers + [crossed, fourth] + reduce_peers(z, x, y, c, zs, xs, cs)
    pl.semaphore_wait(meet(peers), len(peers))

    def link(source, target, peer, at):
        return remote(source, target, peer, send_sem, recv_sem, at)

    results_out = [
        link(done_any.at[:, other], comb.at[1, :, frozen + me], peer, i)
        for i, (other, peer) in enumerate(zip(others, row_peers))
    ]
    last_half = link(own_any, land_core, core, 3)
    near_own = link(dw_any.at[z1, 1], land_own.at[1], straight, 4)
    far_sum = [link(part_w.at[0, i], land_far.at[i], crossed, 5 + i) for i in range(2)]
    side_sum = link(part_w.at[1], land_side, swapped, 7)

    for copy in results_out:
        copy.start()

    def load(source, target, at):
        copy = pltpu.make_async_copy(source, target, in_sem.at[at])
        copy.start()
        return copy

    sources = (tokens_ref, cot_ref, q_any, k_any, v_any, o_any, a2_any, a1_any)
    weights = (wq_any, wk_any, wv_any, wo_any)

    def load_rows(m, which):
        return [load(sources[i].at[m], rows_scr.at[i, m], 16 * m + i) for i in which]

    def load_blocks(m):
        return [
            load(x1_any.at[m], x1_scr.at[m], 16 * m + 8),
            load(froz_any.at[:, :, m], comb.at[m, :, pl.ds(0, frozen)], 16 * m + 9),
        ]

    mine = [load(dw_any.at[z2], part_w.at[0], 14), load(near_any, near_scr, 15)]
    loads = [load(ret_any, comb.at[0, :, pl.ds(frozen, owners)], 10)]
    loads += load_blocks(0) + load_rows(0, (1, 6)) + [load(wo_any, w_scr.at[3], 35)]
    later = load_rows(0, (2, 3, 4, 5, 0, 7))
    later += [load(weights[i], w_scr.at[i], 32 + i) for i in range(3)]
    near_own.start()
    last_half.start()

    def load_last():
        last = load_rows(1, range(8)) + load_blocks(1)
        last.append(load(done_any.at[:, me], comb.at[1, :, frozen + me], 26))
        last.append(load(dw_any.at[z], part_w.at[1], 36))
        last.append(load(first_any, land_own.at[0], 11))
        return last

    def add_rows(target, source):
        @pl.loop(0, width // 128)
        def _(i):
            rows = pl.ds(pl.multiple_of(i * 128, 128), 128)
            target[rows, :] = (
                target[rows, :].astype(SINGLE) + source[rows, :].astype(SINGLE)
            ).astype(HALF)

    def after_own():
        last_half.wait()
        for i in range(2):
            add_rows(part_w.at[1, i], land_core.at[i])
        near_own.wait()
        for i in range(2):
            add_rows(part_w.at[1, i], land_own.at[i])

        @pl.when(x != c)
        def _():
            side_sum.start()

    last_loads = []

    for copy in mine:
        copy.wait()
    for i in range(2):
        add_rows(part_w.at[0, i], near_scr.at[i])
        far_sum[i].start()

    def first_middle():
        for copy in later:
            copy.wait()
        last_loads.extend(load_last())

    def right_of(i):
        def get(k):
            cols = slice(k * TILE, (k + 1) * TILE)
            rows = db_scr[:, :, cols] if i is None else rows_scr[i, :, :, cols]
            return rows.reshape(micro * tok, TILE)

        return get

    reduction = Reduction(
        (z, x, y, c),
        (zs, xs, ys, cs),
        (a1t_scr, a1t_scr, a1t_scr, ot_scr),
        [right_of(i) for i in (2, 3, 4, None)],
        shared_ref,
        pay,
        got,
        red_send,
        red_recv,
    )

    def after_group(group):
        reduction.produce(group)
        if group >= 1:
            reduction.second(group - 1)
        if group >= 2:
            reduction.third(group - 2)

    outs = []

    def back(m, middle, after):
        x_ref, dy_ref, q_ref, k_ref, v_ref, o_ref, a2_ref, _ = [
            rows_scr.at[i, m] for i in range(8)
        ]
        back_body(
            capacity,
            experts,
            middle,
            after,
            lengths_ref.at[m],
            x_ref,
            dy_ref,
            routes_t_ref.at[m],
            norms_ref,
            w_scr.at[0],
            w_scr.at[1],
            w_scr.at[2],
            w_scr.at[3],
            wr_ref,
            q_ref,
            k_ref,
            v_ref,
            o_ref,
            x1_scr.at[m],
            a2_ref,
            lse_ref.at[m],
            info_ref.at[m],
            cols_ref.at[m],
            probs_ref.at[m],
            a2_ref,
            x1_scr.at[m],
            q_ref,
            k_ref,
            v_ref,
            db_scr.at[m],
            small_scr.at[m],
            comb.at[m, 0],
            comb.at[m, 1],
            bias_scr,
            dx1_scr,
            do_scr,
            delta_scr,
        )
        copy = pltpu.make_async_copy(a2_ref, mixed_any.at[m], out_sem.at[2 * m])
        copy.start()
        outs.append(copy)

    def finish(m, first, last):
        x_ref = rows_scr.at[0, m]
        finish_body(
            x_ref,
            norms_ref,
            w_scr.at[0],
            w_scr.at[1],
            w_scr.at[2],
            x1_scr.at[m],
            x_ref,
            rows_scr.at[2, m],
            rows_scr.at[3, m],
            rows_scr.at[4, m],
            small_scr.at[m],
            wr_ref.shape[0],
            first,
            last,
        )
        if last == tok // TILE:
            copy = pltpu.make_async_copy(x_ref, xgrad_any.at[m], out_sem.at[2 * m + 1])
            copy.start()
            outs.append(copy)

    for copy in loads:
        copy.wait()
    back(0, first_middle, None)
    finish(0, 0, tok // TILE)
    for copy in last_loads:
        copy.wait()
    for m in range(micro):
        for at in range(0, width, 128):
            tokens_at = slice(m * tok, (m + 1) * tok)
            a1t_scr[at : at + 128, tokens_at] = jnp.transpose(rows_scr[7, m, :, at : at + 128])
            ot_scr[at : at + 128, tokens_at] = jnp.transpose(rows_scr[5, m, :, at : at + 128])
    for copy in results_out:
        copy.wait()
    back(1, after_own, after_group)

    tiny_peers = reduce_peers(z, x, y, c, zs, xs, cs)

    def spread_tiny(at):
        copy = remote(
            tiny, tiny_got.at[at], tiny_peers[(0, 2, 1, 3, 4, 5)[at]], red_send, red_recv, 36 + at
        )
        copy.start()
        return copy

    def gather_tiny(copy, at):
        copy.wait()
        tiny[...] += tiny_got[at]

    finish(1, 0, 1)
    reduction.second(2)
    reduction.third(1)
    reduction.fourth(0)
    finish(1, 1, tok // TILE)
    tiny[...] = small_scr[0] + small_scr[1]
    tiny_copy = spread_tiny(0)
    reduction.third(2)
    reduction.fourth(1)
    gather_tiny(tiny_copy, 0)
    tiny_copy = spread_tiny(1)
    reduction.final(0)
    gather_tiny(tiny_copy, 1)
    tiny_copy = spread_tiny(2)
    reduction.fourth(2)
    gather_tiny(tiny_copy, 2)
    tiny_copies = [spread_tiny(3 + i) for i in range(zs - 1)]
    reduction.final(1)
    for copy in far_sum:
        copy.wait()

    @pl.when(x != c)
    def _():
        side_sum.wait()

    def total_of(part, rows):
        base = land_far[part, rows, :].astype(SINGLE)
        own = part_w[1, part, rows, :].astype(SINGLE)
        other = land_side[part, rows, :].astype(SINGLE)
        return base + jnp.where(x == c, own, other)

    for i in range(0, width, 128):
        gin_scr[i : i + 128, :] = total_of(0, slice(i, i + 128)).astype(HALF)
        gout_scr[:, i : i + 128] = jnp.transpose(total_of(1, slice(i, i + 128)).astype(HALF))
    done = [
        pltpu.make_async_copy(gin_scr, gin_any.at[0], out_sem.at[2 * micro]),
        pltpu.make_async_copy(gout_scr, gout_any.at[0], out_sem.at[2 * micro + 1]),
    ]
    for copy in done:
        copy.start()
    reduction.final(2)
    for copy in outs:
        copy.wait()
    for copy in tiny_copies:
        copy.wait()
    total = tiny[...]
    for i in range(zs - 1):
        total = total + tiny_got[3 + i]
    tiny_ref[...] = total
    for copy in done:
        copy.wait()


def vmem(count):
    return [pl.BlockSpec(memory_space=pltpu.VMEM)] * count


def params(mib, **more):
    return pltpu.CompilerParams(vmem_limit_bytes=mib << 20, **more)


def general(
    tokens,
    routes,
    lengths,
    key_mask,
    gain_one,
    bias_one,
    w_query,
    w_key,
    w_value,
    w_output,
    gain_two,
    bias_two,
    w_router,
    frozen_in,
    frozen_out,
    new_in,
    new_out,
    cotangent,
):
    micro, tok, width = tokens.shape
    owners = lax.axis_size("expert")
    dp = lax.axis_size("dp")
    frozen, _, ff = frozen_in.shape
    experts = frozen + owners
    capacity = 10 * tok // (4 * experts) // 8 * 8
    shard = new_in.shape[2]
    slots_all = experts * capacity
    shape = jax.ShapeDtypeStruct
    smem = pl.BlockSpec(memory_space=pltpu.SMEM)

    local_w = jnp.stack([new_in[0].T.astype(HALF), new_out[0].astype(HALF)], 0)
    all_w = lax.all_gather(local_w, "dp", axis=0, tiled=False)

    routes_t = jnp.swapaxes(routes, 1, 2)
    norms = jnp.concatenate([gain_one, bias_one, gain_two, bias_two]).reshape(4, width)
    rows16 = 16
    router_t = jnp.pad(w_router.T, ((0, rows16 - experts), (0, 0)))

    saved, froz_sent, arrived = [], [], []
    for m in range(micro):
        outs = pl.pallas_call(
            functools.partial(attend_kernel, capacity, experts, frozen),
            out_shape=[shape((tok, width), HALF)] * 5
            + [
                shape((tok, width), SINGLE),
                shape((tok, width), HALF),
                shape((16, tok), SINGLE),
                shape((8, tok), SINGLE),
                shape((tok, 128), SINGLE),
                shape((rows16, tok), SINGLE),
                shape((frozen, 2, capacity, width), HALF),
                shape((owners, 2, capacity, width), HALF),
            ],
            in_specs=[smem] + vmem(10),
            out_specs=vmem(13),
            scratch_shapes=[pltpu.VMEM((tok, tok), SINGLE), pltpu.VMEM((tok, 128), SINGLE)],
            compiler_params=params(56),
            cost_estimate=pl.CostEstimate(
                flops=8_000_000_000, bytes_accessed=20_000_000, transcendentals=3_000_000
            ),
            name="attend",
        )(
            lengths[m, 0],
            tokens[m],
            cotangent[m],
            routes_t[m],
            key_mask[m][None, :],
            norms,
            w_query,
            w_key,
            w_value,
            w_output,
            router_t,
        )
        saved.append(outs[:11])
        froz_sent.append(outs[11])
        arrived.append(
            lax.all_to_all(outs[12], "expert", split_axis=0, concat_axis=0, tiled=True)
        )

    block = min(768, ff)
    rows_spec = pl.BlockSpec((1, 2, capacity, width), lambda e, f: (e, 0, 0, 0))
    froz_back = pl.pallas_call(
        frozen_kernel,
        grid=(frozen, ff // block),
        out_shape=[shape((frozen, 2, capacity, width), HALF)] * 2,
        in_specs=[
            rows_spec,
            rows_spec,
            pl.BlockSpec((1, width, block), lambda e, f: (e, 0, f)),
            pl.BlockSpec((1, block, width), lambda e, f: (e, f, 0)),
        ],
        out_specs=[rows_spec, rows_spec],
        scratch_shapes=[
            pltpu.VMEM((2 * capacity, width), HALF),
            pltpu.VMEM((2 * capacity, width), HALF),
            pltpu.VMEM((2, 2 * capacity, width), SINGLE),
        ],
        compiler_params=params(50),
        cost_estimate=pl.CostEstimate(
            flops=16_000_000_000, bytes_accessed=25_000_000, transcendentals=2_500_000
        ),
        name="frozen",
    )(froz_sent[0], froz_sent[1], frozen_in, frozen_out)

    rows_all = micro * owners * capacity
    group = max(1, 768 // shard)
    whole = pl.BlockSpec((owners, 2, capacity, width), lambda f: (0, 0, 0, 0))
    done0, done1, grads_w = pl.pallas_call(
        owned_kernel,
        grid=(dp // group,),
        out_shape=[shape((owners, 2, capacity, width), HALF)] * 2
        + [shape((dp, 2, width, shard), HALF)],
        in_specs=[whole, whole, pl.BlockSpec((group, 2, shard, width), lambda f: (f, 0, 0, 0))],
        out_specs=[whole, whole, pl.BlockSpec((group, 2, width, shard), lambda f: (f, 0, 0, 0))],
        scratch_shapes=[
            pltpu.VMEM((rows_all, width), HALF),
            pltpu.VMEM((rows_all, width), HALF),
            pltpu.VMEM((width, rows_all), HALF),
            pltpu.VMEM((width, rows_all), HALF),
            pltpu.VMEM((2, rows_all, width), SINGLE),
            pltpu.VMEM((2, rows_all, group * shard), HALF),
        ],
        compiler_params=params(60),
        cost_estimate=pl.CostEstimate(
            flops=47_000_000_000, bytes_accessed=35_000_000, transcendentals=5_000_000
        ),
        name="owned",
    )(arrived[0], arrived[1], all_w)

    returned = [
        lax.all_to_all(one, "expert", split_axis=0, concat_axis=0, tiled=True)
        for one in (done0, done1)
    ]
    summed_w = lax.psum_scatter(grads_w, "dp", scatter_dimension=0, tiled=True)[0]

    mixed_list, xgrad_list, small_list, weight_ins = [], [], [], []
    for m in range(micro):
        a1, q, k, v, o, x1, a2, lse, info, cols, probs = saved[m]
        mixed, xgrad, dq, dk, dv, db, small = pl.pallas_call(
            functools.partial(back_kernel, capacity, experts),
            out_shape=[shape((tok, width), HALF)] * 6 + [shape((rows16 + 8, width), SINGLE)],
            in_specs=[smem] + vmem(21),
            out_specs=vmem(7),
            scratch_shapes=[
                pltpu.VMEM((slots_all, width), HALF),
                pltpu.VMEM((slots_all, width), HALF),
                pltpu.VMEM((tok, tok), SINGLE),
                pltpu.VMEM((tok, width), SINGLE),
                pltpu.VMEM((tok, width), HALF),
                pltpu.VMEM((tok, 128), SINGLE),
            ],
            compiler_params=params(56),
            cost_estimate=pl.CostEstimate(
                flops=16_000_000_000, bytes_accessed=25_000_000, transcendentals=3_000_000
            ),
            name="back",
        )(
            lengths[m, 0],
            tokens[m],
            cotangent[m],
            routes_t[m],
            norms,
            w_query,
            w_key,
            w_value,
            w_output,
            router_t,
            q,
            k,
            v,
            o,
            x1,
            a2,
            lse,
            info,
            cols,
            probs,
            froz_back[m],
            returned[m],
        )
        mixed_list.append(mixed)
        xgrad_list.append(xgrad)
        small_list.append(small)
        weight_ins += [a1, o, dq, dk, dv, db]

    grads = pl.pallas_call(
        weights_kernel,
        out_shape=shape((4, width, width), HALF),
        in_specs=vmem(len(weight_ins)),
        out_specs=vmem(1)[0],
        compiler_params=params(50),
        name="weights",
    )(*weight_ins)
    shared = lax.psum_scatter(grads, ("dp", "expert"), scatter_dimension=1, tiled=True)
    shared = shared.astype(SINGLE)
    small = sum(small_list[1:], small_list[0])
    small = jnp.concatenate([small[:experts], small[rows16 : rows16 + 4]], 0).T
    small = lax.psum_scatter(small, ("dp", "expert"), scatter_dimension=0, tiled=True)
    return (
        jnp.stack(mixed_list, 0),
        jnp.stack(xgrad_list, 0),
        small[:, experts + 2],
        small[:, experts + 3],
        shared[0],
        shared[1],
        shared[2],
        shared[3],
        small[:, experts],
        small[:, experts + 1],
        small[:, :experts],
        summed_w[0].astype(SINGLE)[None],
        summed_w[1].astype(SINGLE).T[None],
    )


def fused(
    tokens,
    routes,
    lengths,
    key_mask,
    gain_one,
    bias_one,
    w_query,
    w_key,
    w_value,
    w_output,
    gain_two,
    bias_two,
    w_router,
    frozen_in,
    frozen_out,
    new_in,
    new_out,
    cotangent,
):
    micro, tok, width = tokens.shape
    owners = lax.axis_size("expert")
    dp = lax.axis_size("dp")
    frozen = frozen_in.shape[0]
    experts = frozen + owners
    capacity = 10 * tok // (4 * experts) // 8 * 8
    shard = new_in.shape[2]
    zs, xs, ys, cs = 4, 2, 2, 2
    shape = jax.ShapeDtypeStruct
    smem = pl.BlockSpec(memory_space=pltpu.SMEM)

    def anywhere(count):
        return [pl.BlockSpec(memory_space=pl.ANY)] * count

    routes_t = jnp.swapaxes(routes, 1, 2)
    norms = jnp.concatenate([gain_one, bias_one, gain_two, bias_two]).reshape(4, width)
    rows16 = 16
    router_t = jnp.pad(w_router.T, ((0, rows16 - experts), (0, 0)))
    dma = pltpu.SemaphoreType.DMA

    outs = pl.pallas_call(
        functools.partial(front_kernel, capacity, experts, frozen),
        out_shape=[shape((micro, tok, width), HALF)] * 5
        + [
            shape((micro, tok, width), SINGLE),
            shape((micro, tok, width), HALF),
            shape((micro, 16, tok), SINGLE),
            shape((micro, 8, tok), SINGLE),
            shape((micro, tok, 128), SINGLE),
            shape((micro, rows16, tok), SINGLE),
            shape((2, frozen, micro, capacity, width), HALF),
            shape((2, owners, capacity, width), HALF),
            shape((2, owners, capacity, width), HALF),
            shape((zs, 2, width, shard), HALF),
            shape((zs, 2, width, shard), HALF),
            shape((2, width, shard), HALF),
            shape((width, shard), HALF),
            shape((2, width, shard), HALF),
        ],
        in_specs=[smem] + vmem(4) + anywhere(10),
        out_specs=anywhere(7) + vmem(4) + anywhere(8),
        scratch_shapes=[
            pltpu.VMEM((dp, 2, shard, width), HALF),
            pltpu.VMEM((2, shard, width), HALF),
            pltpu.VMEM((2, micro * owners, capacity, width), HALF),
            pltpu.VMEM((2, micro * owners, capacity, width), HALF),
            dma((23,)),
            dma((23,)),
            dma((4,)),
        ],
        compiler_params=params(63, collective_id=1, has_side_effects=True),
        name="front",
    )(
        lengths[:, 0],
        routes_t,
        key_mask,
        norms,
        router_t,
        tokens,
        cotangent,
        w_query,
        w_key,
        w_value,
        w_output,
        frozen_in,
        frozen_out,
        new_in,
        new_out,
    )
    a1, q, k, v, o, x1, a2, lse, info, cols, probs, froz, ret, done, dw, _, near, first, own = outs
    rows = width // (dp * owners)
    blocks = width // 128
    landing = [(zs, xs, ys), (zs, 2), (zs,), (zs - 1,)]
    mixed, xgrad, shared, small, grad_in, grad_out = pl.pallas_call(
        functools.partial(tail_kernel, capacity, experts, frozen),
        out_shape=[
            shape((micro, tok, width), HALF),
            shape((micro, tok, width), HALF),
            shape((4, rows, width), SINGLE),
            shape((rows16 + 8, width), SINGLE),
            shape((1, width, shard), HALF),
            shape((1, shard, width), HALF),
        ],
        in_specs=[smem] + vmem(7) + anywhere(20),
        out_specs=anywhere(2) + vmem(2) + anywhere(2),
        scratch_shapes=[
            pltpu.VMEM((4, width, width), HALF),
            pltpu.VMEM((8, micro, tok, width), HALF),
            pltpu.VMEM((micro, tok, width), SINGLE),
            pltpu.VMEM((width, micro * tok), HALF),
            pltpu.VMEM((width, micro * tok), HALF),
            pltpu.VMEM((micro, tok, width), HALF),
            pltpu.VMEM((micro, 2, experts, capacity, width), HALF),
            pltpu.VMEM((micro, rows16 + 8, width), SINGLE),
            pltpu.VMEM((tok, tok), SINGLE),
            pltpu.VMEM((tok, width), SINGLE),
            pltpu.VMEM((tok, width), HALF),
            pltpu.VMEM((tok, 128), SINGLE),
            pltpu.VMEM((2, 2, width, shard), HALF),
            pltpu.VMEM((2, width, shard), HALF),
            pltpu.VMEM((2, width, shard), HALF),
            pltpu.VMEM((2, width, shard), HALF),
            pltpu.VMEM((2, width, shard), HALF),
            pltpu.VMEM((2, width, shard), HALF),
            pltpu.VMEM((width, shard), HALF),
            pltpu.VMEM((shard, width), HALF),
            pltpu.VMEM((blocks, zs, xs, ys, cs, 4 * rows, 128), HALF),
            [pltpu.VMEM((blocks,) + lead + (4 * rows, 128), HALF) for lead in landing],
            pltpu.VMEM((rows16 + 8, width), SINGLE),
            pltpu.VMEM((zs + 2, rows16 + 8, width), SINGLE),
            dma((8,)),
            dma((8,)),
            dma((42,)),
            dma((42,)),
            dma((37,)),
            dma((2 * micro + 2,)),
        ],
        compiler_params=params(63, collective_id=2, has_side_effects=True),
        name="tail",
    )(
        lengths[:, 0],
        routes_t,
        norms,
        router_t,
        lse,
        info,
        cols,
        probs,
        tokens,
        cotangent,
        w_query,
        w_key,
        w_value,
        w_output,
        a1,
        q,
        k,
        v,
        o,
        x1,
        a2,
        froz,
        ret,
        done,
        dw,
        near,
        first,
        own,
    )
    at = (lax.axis_index("dp") * owners + lax.axis_index("expert")) * rows
    small = lax.dynamic_slice_in_dim(small, at, rows, 1)
    return (
        mixed,
        xgrad,
        small[rows16 + 2],
        small[rows16 + 3],
        shared[0],
        shared[1],
        shared[2],
        shared[3],
        small[rows16],
        small[rows16 + 1],
        small[:experts].T,
        grad_in.astype(SINGLE),
        grad_out.astype(SINGLE),
    )


def solution(mesh):
    both = ("dp", "expert")
    small_slice = mesh.shape["dp"] == 8 and mesh.shape["expert"] == 4
    return jax.shard_map(
        fused if small_slice else general,
        mesh=mesh,
        in_specs=(
            P(None, both, None),
            P(None, both, None),
            P(None, both, None),
            P(None, both),
        )
        + (P(),) * 11
        + (P("expert", None, "dp"), P("expert", "dp", None), P(None, both, None)),
        out_specs=(P(None, both, None), P(None, both, None), P(both), P(both))
        + (P(both, None),) * 4
        + (P(both), P(both), P(both, None), P("expert", None, "dp"), P("expert", "dp", None)),
        check_vma=False,
    )
```

```python
import functools

import jax
import jax.numpy as jnp
from jax import lax
from jax.experimental import pallas as pl
from jax.experimental.pallas import tpu as pltpu
from jax.sharding import PartitionSpec as P

HEAD = 64
PAIR = 2 * HEAD
TILE = 256
EPS = 1e-05
HALF = jnp.bfloat16
SINGLE = jnp.float32
HIDDEN = -1000000000.0
GELU_C = 0.7978845608028654
GELU_A = 0.044715

NN = (((1,), (0,)), ((), ()))
NT = (((1,), (1,)), ((), ()))
TN = (((0,), (0,)), ((), ()))


def mm(a, b, dims=NN):
    return lax.dot_general(a, b, dims, preferred_element_type=SINGLE)


def norm_rows(values):
    center = values - jnp.mean(values, -1, keepdims=True)
    inverse = lax.rsqrt(jnp.mean(center * center, -1, keepdims=True) + EPS)
    return center * inverse, inverse


def norm_back(grad, unit_rows, inverse, gain):
    scaled = grad * gain
    return inverse * (
        scaled
        - jnp.mean(scaled, -1, keepdims=True)
        - unit_rows * jnp.mean(scaled * unit_rows, -1, keepdims=True)
    )


def doc_of(places, lengths_ref):
    doc = jnp.zeros(places.shape, jnp.int32)
    end = 0
    for i in range(lengths_ref.shape[0]):
        end = end + lengths_ref[i]
        doc = doc + jnp.where(places >= end, 1, 0)
    return doc


def half_masks(rows):
    lane = lax.broadcasted_iota(jnp.int32, (rows, PAIR), 1)
    first = jnp.where(lane < HEAD, 1.0, 0.0).astype(HALF)
    second = jnp.where(lane < HEAD, 0.0, 1.0).astype(HALF)
    return lane < HEAD, (first, second)


def route_hots(routes_t_ref, rows, tokens):
    sub = lax.broadcasted_iota(jnp.int32, (rows, tokens), 0)
    return [sub == routes_t_ref[pick : pick + 1, :] for pick in range(2)]


def attend_kernel(capacity, experts, frozen, *refs):
    froz_ref, send_ref, bias_scr, lse_scr = refs[-4:]

    def target(e, part):
        return froz_ref.at[e, part] if e < frozen else send_ref.at[e - frozen, part]

    attend_body(capacity, experts, target, *refs[:-4], bias_scr, lse_scr)


def attend_body(
    capacity,
    experts,
    target,
    lengths_ref,
    x_ref,
    dy_ref,
    routes_t_ref,
    mask_ref,
    norms_ref,
    wq_ref,
    wk_ref,
    wv_ref,
    wo_ref,
    wr_ref,
    a1_ref,
    q_ref,
    k_ref,
    v_ref,
    o_ref,
    x1_ref,
    a2_ref,
    lse_ref,
    info_ref,
    cols_ref,
    probs_ref,
    bias_scr,
    lse_scr,
):
    tokens, width = x_ref.shape
    chunk = 128
    gain_one, bias_one = norms_ref[0:1, :], norms_ref[1:2, :]
    gain_two, bias_two = norms_ref[2:3, :], norms_ref[3:4, :]

    @pl.loop(0, tokens // chunk)
    def _(i):
        rows = pl.ds(pl.multiple_of(i * chunk, chunk), chunk)
        unit_rows, _ = norm_rows(x_ref[rows, :].astype(SINGLE))
        a1_ref[rows, :] = (unit_rows * gain_one + bias_one).astype(HALF)
        here = lax.broadcasted_iota(jnp.int32, (chunk, 1), 0) + i * chunk
        there = lax.broadcasted_iota(jnp.int32, (1, tokens), 1)
        same = doc_of(here, lengths_ref) == doc_of(there, lengths_ref)
        keep = (mask_ref[...] == 1) | (there == here)
        visible = same & (there <= here) & keep
        bias_scr[rows, :] = jnp.where(visible, 0.0, HIDDEN)

    @pl.loop(0, tokens // TILE)
    def _(i):
        rows = pl.ds(pl.multiple_of(i * TILE, TILE), TILE)
        a1 = a1_ref[rows, :]
        q_ref[rows, :] = (mm(a1, wq_ref[...]).astype(HALF) * HEAD ** (-0.5)).astype(HALF)
        k_ref[rows, :] = mm(a1, wk_ref[...]).astype(HALF)
        v_ref[rows, :] = mm(a1, wv_ref[...]).astype(HALF)

    lse_scr[...] = jnp.zeros_like(lse_scr)

    @pl.loop(0, width // PAIR, unroll=2)
    def _(i):
        cols = pl.ds(pl.multiple_of(i * PAIR, PAIR), PAIR)
        low, masks = half_masks(TILE)
        lane = lax.broadcasted_iota(jnp.int32, (TILE, 128), 1)
        for part in range(tokens // TILE):
            rows = slice(part * TILE, (part + 1) * TILE)
            keys = (part + 1) * TILE
            q_t = q_ref[rows, cols]
            k_t = k_ref[0:keys, cols]
            v_t = jnp.concatenate([v_ref[0:keys, cols], jnp.ones((keys, PAIR), HALF)], 1)
            results = []
            for h in range(2):
                scores = mm(q_t * masks[h], k_t, NT) + bias_scr[rows, 0:keys]
                top = jnp.max(scores, -1, keepdims=True)
                expo = jnp.exp(scores - top).astype(HALF)
                both = mm(expo, v_t)
                total = both[:, PAIR:]
                results.append(both[:, :PAIR] * (1.0 / total))
                log_total = top + jnp.log(total)
                lse_scr[rows, :] = jnp.where(lane == 2 * i + h, log_total, lse_scr[rows, :])
            o_ref[rows, cols] = jnp.where(low, results[0], results[1]).astype(HALF)

    lse_ref[...] = jnp.transpose(lse_scr[...])[0 : lse_ref.shape[0], :]

    @pl.loop(0, tokens // TILE)
    def _(i):
        rows = pl.ds(pl.multiple_of(i * TILE, TILE), TILE)
        x1 = x_ref[rows, :].astype(SINGLE) + mm(o_ref[rows, :], wo_ref[...])
        x1_ref[rows, :] = x1
        unit_rows, _ = norm_rows(x1)
        a2_ref[rows, :] = (unit_rows * gain_two + bias_two).astype(HALF)

    rows16 = wr_ref.shape[0]
    logits = mm(wr_ref[...], a2_ref[...], NT)
    sub = lax.broadcasted_iota(jnp.int32, (rows16, tokens), 0)
    logits = jnp.where(sub < experts, logits, -1e30)
    expo = jnp.exp(logits - jnp.max(logits, 0, keepdims=True))
    probs = expo / jnp.sum(expo, 0, keepdims=True)
    probs_ref[...] = probs
    hots = route_hots(routes_t_ref, rows16, tokens)
    chosen = [jnp.sum(jnp.where(hot, probs, 0.0), 0, keepdims=True) for hot in hots]
    chosen_total = chosen[0] + chosen[1]
    gates = [one / chosen_total for one in chosen]
    upper = jnp.where(
        lax.broadcasted_iota(jnp.int32, (tokens, tokens), 0)
        < lax.broadcasted_iota(jnp.int32, (tokens, tokens), 1),
        1.0,
        0.0,
    ).astype(HALF)
    both = jnp.where(hots[0] | hots[1], 1.0, 0.0).astype(HALF)
    earlier = mm(both, upper)
    places = []
    for pick in range(2):
        slot = jnp.sum(jnp.where(hots[pick], earlier, 0.0), 0, keepdims=True)
        first = routes_t_ref[pick : pick + 1, :].astype(SINGLE) * capacity
        places.append(jnp.where(slot < capacity, first + slot, -1.0))
    info = jnp.concatenate(
        places + gates + [mask_ref[...].astype(SINGLE), chosen_total, chosen_total, chosen_total], 0
    )
    info_ref[...] = info
    cols_ref[...] = jnp.transpose(
        jnp.concatenate([info, jnp.zeros((128 - info.shape[0], tokens), SINGLE)], 0)
    )
    spots = [one.astype(jnp.int32) for one in places]
    for e in range(experts):
        slots = lax.broadcasted_iota(jnp.int32, (capacity, tokens), 0) + e * capacity
        hit = [slots == spots[pick] for pick in range(2)]
        place = jnp.where(hit[0] | hit[1], 1.0, 0.0).astype(HALF)
        weight = jnp.sum(
            jnp.where(hit[0], gates[0], 0.0) + jnp.where(hit[1], gates[1], 0.0), 1, keepdims=True
        )
        target(e, 0)[...] = mm(place, a2_ref[...]).astype(HALF)
        target(e, 1)[...] = (mm(place, dy_ref[...]) * weight).astype(HALF)


def expert_step(x_of, dy_of, total, w_in, w_out, in_dims, acc_scr, held, first, chunk):
    back_dims = NT if in_dims == NN else NN

    @pl.loop(0, total // chunk)
    def _(i):
        rows = pl.ds(pl.multiple_of(i * chunk, 16), chunk)
        pre = mm(x_of(i), w_in, in_dims)
        grad = mm(dy_of(i), w_out, NT)
        square = pre * pre
        plus = 0.5 + 0.5 * jnp.tanh(pre * (GELU_C + GELU_C * GELU_A * square))
        gelu = pre * plus
        hidden = gelu.astype(HALF)
        slope = plus + gelu * (1.0 - plus) * (2.0 * GELU_C + 6.0 * GELU_C * GELU_A * square)
        grad_pre = (grad * slope).astype(HALF)
        if held is not None:
            held[0, rows, :] = hidden
            held[1, rows, :] = grad_pre
        out = mm(hidden, w_out)
        back = mm(grad_pre, w_in, back_dims)
        if first is True:
            acc_scr[0, rows, :] = out
            acc_scr[1, rows, :] = back
        elif first is False:
            acc_scr[0, rows, :] += out
            acc_scr[1, rows, :] += back
        else:

            @pl.when(first)
            def _():
                acc_scr[0, rows, :] = out
                acc_scr[1, rows, :] = back

            @pl.when(jnp.logical_not(first))
            def _():
                acc_scr[0, rows, :] += out
                acc_scr[1, rows, :] += back


def frozen_kernel(
    r0_ref, r1_ref, win_ref, wout_ref, o0_ref, o1_ref, x_scr, dy_scr, acc_scr
):
    capacity = r0_ref.shape[2]
    step, last = pl.program_id(1), pl.num_programs(1) - 1

    @pl.when(step == 0)
    def _():
        for m, ref in enumerate((r0_ref, r1_ref)):
            x_scr[m * capacity : (m + 1) * capacity, :] = ref[0, 0]
            dy_scr[m * capacity : (m + 1) * capacity, :] = ref[0, 1]

    expert_step(
        lambda i: x_scr[...],
        lambda i: dy_scr[...],
        2 * capacity,
        win_ref[0],
        wout_ref[0],
        NN,
        acc_scr,
        None,
        step == 0,
        2 * capacity,
    )

    @pl.when(step == last)
    def _():
        for m, ref in enumerate((o0_ref, o1_ref)):
            for part in range(2):
                ref[0, part] = acc_scr[part, m * capacity : (m + 1) * capacity, :].astype(HALF)


def owned_kernel(
    r0_ref,
    r1_ref,
    w_ref,
    o0_ref,
    o1_ref,
    dw_ref,
    x_scr,
    dy_scr,
    xt_scr,
    dyt_scr,
    acc_scr,
    held_scr,
):
    sources, _, capacity, width = r0_ref.shape
    group, _, shard, _ = w_ref.shape
    step, last = pl.program_id(0), pl.num_programs(0) - 1
    rows_all = x_scr.shape[0]

    @pl.when(step == 0)
    def _():
        for m, ref in enumerate((r0_ref, r1_ref)):
            for s in range(sources):
                at = (m * sources + s) * capacity
                x_scr[at : at + capacity, :] = ref[s, 0]
                dy_scr[at : at + capacity, :] = ref[s, 1]
        for at in range(0, width, 128):
            xt_scr[at : at + 128, :] = jnp.transpose(x_scr[:, at : at + 128])
            dyt_scr[at : at + 128, :] = jnp.transpose(dy_scr[:, at : at + 128])

    w_in = w_ref[:, 0].reshape(group * shard, width)
    w_out = w_ref[:, 1].reshape(group * shard, width)
    chunk = 2 * capacity
    expert_step(
        lambda i: x_scr[pl.ds(pl.multiple_of(i * chunk, 16), chunk), :],
        lambda i: dy_scr[pl.ds(pl.multiple_of(i * chunk, 16), chunk), :],
        rows_all,
        w_in,
        w_out,
        NT,
        acc_scr,
        held_scr,
        step == 0,
        chunk,
    )

    @pl.loop(0, width // TILE)
    def _(i):
        rows = pl.ds(pl.multiple_of(i * TILE, TILE), TILE)
        for part, (left, right) in enumerate(((xt_scr, held_scr.at[1]), (dyt_scr, held_scr.at[0]))):
            total = mm(left[rows, :], right[...]).astype(HALF)
            for g in range(group):
                dw_ref[g, part, rows, :] = total[:, g * shard : (g + 1) * shard]

    @pl.when(step == last)
    def _():
        for m, ref in enumerate((o0_ref, o1_ref)):
            for s in range(sources):
                at = (m * sources + s) * capacity
                for part in range(2):
                    ref[s, part] = acc_scr[part, at : at + capacity, :].astype(HALF)


def back_kernel(capacity, experts, *refs):
    froz_ref, back_ref = refs[20:22]
    mixed_ref, xgrad_ref, dq_ref, dk_ref, dv_ref, db_ref, small_ref = refs[22:29]
    out_scr, dbuf_scr = refs[29:31]
    frozen = froz_ref.shape[0]
    for e in range(experts):
        source = froz_ref.at[e] if e < frozen else back_ref.at[e - frozen]
        out_scr[e * capacity : (e + 1) * capacity, :] = source[0]
        dbuf_scr[e * capacity : (e + 1) * capacity, :] = source[1]
    dx1_scr = refs[32]
    back_body(capacity, experts, None, None, *refs[:20], mixed_ref, dx1_scr, *refs[24:])
    finish_body(
        refs[1],
        refs[4],
        *refs[5:8],
        dx1_scr,
        xgrad_ref,
        dq_ref,
        dk_ref,
        dv_ref,
        small_ref,
        refs[9].shape[0],
        0,
        refs[1].shape[0] // TILE,
    )


def flat(ref):
    rows = ref[...]
    return rows if rows.ndim == 2 else rows.reshape(-1, rows.shape[-1])


def block_of(ref, e, rows):
    return ref[rows, :] if len(ref.shape) == 2 else ref[e]


def back_body(
    capacity,
    experts,
    middle,
    after_group,
    lengths_ref,
    x_ref,
    dy_ref,
    routes_t_ref,
    norms_ref,
    wq_ref,
    wk_ref,
    wv_ref,
    wo_ref,
    wr_ref,
    q_ref,
    k_ref,
    v_ref,
    o_ref,
    x1_ref,
    a2_ref,
    lse_ref,
    info_ref,
    cols_ref,
    probs_ref,
    mixed_ref,
    dx1_ref,
    dq_ref,
    dk_ref,
    dv_ref,
    db_ref,
    small_ref,
    out_scr,
    dbuf_scr,
    bias_scr,
    dx1_scr,
    do_scr,
    delta_scr,
):
    tokens, width = x_ref.shape
    gain_two = norms_ref[2:3, :]
    slots_all = experts * capacity

    spots = [info_ref[pick : pick + 1, :].astype(jnp.int32) for pick in range(2)]
    gates = [info_ref[2 + pick : 3 + pick, :] for pick in range(2)]
    chosen_total = info_ref[5:6, :]

    def gate_part(e, carry):
        rows = pl.ds(pl.multiple_of(e * capacity, 16), capacity)
        overlap = mm(block_of(out_scr, e, rows), dy_ref[...], NT)
        slots = lax.broadcasted_iota(jnp.int32, (capacity, tokens), 0) + e * capacity
        return tuple(
            carry[pick]
            + jnp.sum(jnp.where(slots == spots[pick], overlap, 0.0), 0, keepdims=True)
            for pick in range(2)
        )

    zero_row = jnp.zeros((1, tokens), SINGLE)
    gate_grads = lax.fori_loop(0, experts, gate_part, (zero_row, zero_row))
    rows16 = wr_ref.shape[0]
    hots = route_hots(routes_t_ref, rows16, tokens)
    weighted = gate_grads[0] * gates[0] + gate_grads[1] * gates[1]
    grad_probs = jnp.where(hots[0], (gate_grads[0] - weighted) / chosen_total, 0.0)
    grad_probs = grad_probs + jnp.where(hots[1], (gate_grads[1] - weighted) / chosen_total, 0.0)
    probs = probs_ref[...]
    grad_logits = probs * (grad_probs - jnp.sum(grad_probs * probs, 0, keepdims=True))
    logits_low = grad_logits.astype(HALF)
    small_ref[0:rows16, :] = mm(logits_low, a2_ref[...])
    small_ref[rows16:, :] = jnp.zeros_like(small_ref[rows16:, :])

    @pl.loop(0, tokens // TILE)
    def _(i):
        rows = pl.ds(pl.multiple_of(i * TILE, TILE), TILE)
        slots = lax.broadcasted_iota(jnp.int32, (TILE, slots_all), 1)
        hit = [slots == cols_ref[rows, pick : pick + 1].astype(jnp.int32) for pick in range(2)]
        place = jnp.where(hit[0] | hit[1], 1.0, 0.0).astype(HALF)
        if mixed_ref is not None:
            gated = jnp.where(hit[0], cols_ref[rows, 2:3], 0.0)
            gated = jnp.where(hit[1], cols_ref[rows, 3:4], gated).astype(HALF)
            mixed_ref[rows, :] = (x1_ref[rows, :] + mm(gated, flat(out_scr))).astype(HALF)
        dx1_scr[rows, :] = mm(place, flat(dbuf_scr))

    logits_col = jnp.transpose(
        jnp.concatenate([grad_logits, jnp.zeros((128 - rows16, tokens), SINGLE)], 0)
    )
    delta_scr[...] = logits_col.astype(HALF).astype(SINGLE)
    router = jnp.concatenate([wr_ref[...], jnp.zeros((128 - rows16, width), HALF)], 0)

    @pl.loop(0, tokens // TILE)
    def _(i):
        rows = pl.ds(pl.multiple_of(i * TILE, TILE), TILE)
        unit_rows, inverse = norm_rows(x1_ref[rows, :])
        grad = dx1_scr[rows, :] + mm(delta_scr[rows, :].astype(HALF), router)
        small_ref[rows16 : rows16 + 1, :] += jnp.sum(grad * unit_rows, 0, keepdims=True)
        small_ref[rows16 + 1 : rows16 + 2, :] += jnp.sum(grad, 0, keepdims=True)
        dx1 = dy_ref[rows, :].astype(SINGLE) + norm_back(grad, unit_rows, inverse, gain_two)
        dx1_ref[rows, :] = dx1
        branch = dx1.astype(HALF)
        db_ref[rows, :] = branch
        do_scr[rows, :] = mm(branch, wo_ref[...], NT).astype(HALF)

    if middle is not None:
        middle()

    @pl.loop(0, tokens // 128)
    def _(i):
        rows = pl.ds(pl.multiple_of(i * 128, 128), 128)
        key = lax.broadcasted_iota(jnp.int32, (128, 1), 0) + i * 128
        query = lax.broadcasted_iota(jnp.int32, (1, tokens), 1)
        same = doc_of(key, lengths_ref) == doc_of(query, lengths_ref)
        keep = (cols_ref[rows, 4:5] > 0.5) | (query == key)
        visible = same & (key <= query) & keep
        bias_scr[rows, :] = jnp.where(visible, 0.0, HIDDEN)

    def one_pair(i):
        cols = pl.ds(pl.multiple_of(i * PAIR, PAIR), PAIR)
        low, masks = half_masks(TILE)
        tiles = tokens // TILE
        half_sum = jnp.where(
            (lax.broadcasted_iota(jnp.int32, (8, PAIR), 1) // HEAD)
            == lax.broadcasted_iota(jnp.int32, (8, PAIR), 0),
            1.0,
            0.0,
        )
        overlap = do_scr[:, cols].astype(SINGLE) * o_ref[:, cols].astype(SINGLE)
        deltas = lax.dot_general(
            half_sum,
            overlap,
            NT,
            precision=lax.Precision.HIGHEST,
            preferred_element_type=SINGLE,
        )
        grad_q = [[None] * tiles for _ in range(2)]
        for part in range(tiles):
            keys = slice(part * TILE, (part + 1) * TILE)
            queries = slice(part * TILE, tokens)
            k_t, v_t = k_ref[keys, cols], v_ref[keys, cols]
            q_t, do_t = q_ref[queries, cols], do_scr[queries, cols]
            grad_k, grad_v = [], []
            for h in range(2):
                scores = mm(k_t * masks[h], q_t, NT) + bias_scr[keys, queries]
                log_total = lse_ref[pl.ds(2 * i + h, 1), queries]
                probs = jnp.exp(scores - log_total)
                grad_p = mm(v_t * masks[h], do_t, NT)
                grad_s = (probs * (grad_p - deltas[h : h + 1, queries])).astype(HALF)
                grad_v.append(mm(probs.astype(HALF), do_t))
                grad_k.append(mm(grad_s, q_t))
                step = mm(grad_s, k_t, TN)
                for t in range(part, tiles):
                    piece = step[(t - part) * TILE : (t - part + 1) * TILE, :]
                    grad_q[h][t] = piece if grad_q[h][t] is None else grad_q[h][t] + piece
            dv_ref[keys, cols] = jnp.where(low, grad_v[0], grad_v[1]).astype(HALF)
            dk_ref[keys, cols] = jnp.where(low, grad_k[0], grad_k[1]).astype(HALF)
        for t in range(tiles):
            both = jnp.where(low, grad_q[0][t], grad_q[1][t]) * HEAD ** (-0.5)
            dq_ref[t * TILE : (t + 1) * TILE, cols] = both.astype(HALF)

    if after_group is None:
        pl.loop(0, width // PAIR, unroll=2)(one_pair)
    else:
        for group in range(width // TILE):
            pl.loop(group * TILE // PAIR, (group + 1) * TILE // PAIR, unroll=2)(one_pair)
            after_group(group)


def mixed_body(slots_all, x1_ref, cols_ref, out_scr, mixed_ref):
    @pl.loop(0, x1_ref.shape[0] // TILE)
    def _(i):
        rows = pl.ds(pl.multiple_of(i * TILE, TILE), TILE)
        slots = lax.broadcasted_iota(jnp.int32, (TILE, slots_all), 1)
        gated = jnp.zeros((TILE, slots_all), SINGLE)
        for pick in range(2):
            hit = slots == cols_ref[rows, pick : pick + 1].astype(jnp.int32)
            gated = jnp.where(hit, cols_ref[rows, 2 + pick : 3 + pick], gated)
        gated = gated.astype(HALF)
        mixed_ref[rows, :] = (x1_ref[rows, :] + mm(gated, flat(out_scr))).astype(HALF)


def finish_body(
    x_ref,
    norms_ref,
    wq_ref,
    wk_ref,
    wv_ref,
    dx1_ref,
    xgrad_ref,
    dq_ref,
    dk_ref,
    dv_ref,
    small_ref,
    rows16,
    first,
    last,
):
    gain_one = norms_ref[0:1, :]

    @pl.loop(first, last)
    def _(i):
        rows = pl.ds(pl.multiple_of(i * TILE, TILE), TILE)
        unit_rows, inverse = norm_rows(x_ref[rows, :].astype(SINGLE))
        grad = mm(dq_ref[rows, :], wq_ref[...], NT)
        grad = grad + mm(dk_ref[rows, :], wk_ref[...], NT)
        grad = grad + mm(dv_ref[rows, :], wv_ref[...], NT)
        small_ref[rows16 + 2 : rows16 + 3, :] += jnp.sum(grad * unit_rows, 0, keepdims=True)
        small_ref[rows16 + 3 : rows16 + 4, :] += jnp.sum(grad, 0, keepdims=True)
        part = norm_back(grad, unit_rows, inverse, gain_one)
        xgrad_ref[rows, :] = (dx1_ref[rows, :] + part).astype(HALF)


def weights_kernel(*refs):
    ins, dw_ref = refs[:-1], refs[-1]
    micro = len(ins) // 6
    width = dw_ref.shape[-1]

    @pl.loop(0, width // TILE)
    def _(i):
        cols = pl.ds(pl.multiple_of(i * TILE, TILE), TILE)
        for part in range(4):
            total = weight_grad(ins, micro, part, cols)
            dw_ref[part, cols, :] = total.astype(HALF)


def weight_grad(ins, micro, part, cols):
    total = None
    for m in range(micro):
        a1, o, dq, dk, dv, db = ins[6 * m : 6 * m + 6]
        left = o if part == 3 else a1
        right = (dq, dk, dv, db)[part]
        step = mm(left[:, cols], right[...], TN)
        total = step if total is None else total + step
    return total


def meet(peers):
    barrier = pltpu.get_barrier_semaphore()
    for peer in peers:
        pl.semaphore_signal(barrier, inc=1, device_id=peer, device_id_type=pl.DeviceIdType.MESH)
    return barrier


def remote(source, target, peer, send_sem, recv_sem, at):
    return pltpu.make_async_remote_copy(
        src_ref=source,
        dst_ref=target,
        send_sem=send_sem.at[at],
        recv_sem=recv_sem.at[at],
        device_id=peer,
        device_id_type=pl.DeviceIdType.MESH,
    )


def reduce_peers(z, x, y, c, zs, xs, cs):
    places = [(z, x, y, 1 - c), (z, 1 - x, y, c), (z, x, 1 - y, c)]
    places += [((z + step) % zs, x, y, c) for step in range(1, zs)]
    return [(zz * xs + xx, yy * cs + cc) for zz, xx, yy, cc in places]


class Reduction:
    def __init__(self, place, shape, lefts, rights, out_ref, pay, got, send_sem, recv_sem):
        self.place, self.shape = place, shape
        self.lefts, self.rights = lefts, rights
        self.out_ref, self.pay, self.got = out_ref, pay, got
        self.sems = send_sem, recv_sem
        self.rows = out_ref.shape[1]
        self.copies = [self.plan(k) for k in range(pay.shape[0])]

    def plan(self, k):
        z, x, y, c = self.place
        zs, xs, _, cs = self.shape
        pay, (first, second, third, fourth) = self.pay.at[k], [one.at[k] for one in self.got]

        def link(source, target, zz, xx, yy, cc, at):
            peer = (zz * xs + xx, yy * cs + cc)
            return remote(source, target, peer, *self.sems, 6 * k + at)

        start = link(pay.at[:, :, :, 1 - c], first, z, x, y, 1 - c, 0)
        if k % 2 == 0:
            two = link(pay.at[:, :, 1 - y, c], second, z, x, 1 - y, c, 1)
            three = link(pay.at[:, 1 - x, y, c], third, z, 1 - x, y, c, 2)
        else:
            two = link(pay.at[:, 1 - x, :, c], second, z, 1 - x, y, c, 1)
            three = link(pay.at[:, x, 1 - y, c], third, z, x, 1 - y, c, 2)
        four = []
        for step in range(1, zs):
            zz = (z + step) % zs
            four.append(link(pay.at[zz, x, y, c], fourth.at[step - 1], zz, x, y, c, 2 + step))
        return start, two, three, four

    def produce(self, k):
        zs, xs, ys, cs = self.shape
        rows = self.rows
        tile = 16 * rows
        width = self.lefts[0].shape[0]
        for j in range(width // tile):
            for part, (left, right) in enumerate(zip(self.lefts, self.rights)):
                total = mm(left[j * tile : (j + 1) * tile, :], right(k)).astype(HALF)
                for i in range(16):
                    n = 16 * j + i
                    at = (n // (ys * cs) // xs, n // (ys * cs) % xs, n % (ys * cs) // cs, n % cs)
                    for half in range(2):
                        spot = (2 * k + half,) + at + (slice(part * rows, (part + 1) * rows),)
                        self.pay[spot] = total[
                            i * rows : (i + 1) * rows, half * 128 : (half + 1) * 128
                        ]
        for half in range(2):
            self.copies[2 * k + half][0].start()

    def add(self, k, places):
        @pl.loop(0, self.shape[0])
        def _(i):
            for at, held in places(i):
                at = (k,) + at
                self.pay[at] = (self.pay[at].astype(SINGLE) + held[...].astype(SINGLE)).astype(
                    HALF
                )

    def second(self, block):
        for k in (2 * block, 2 * block + 1):
            self.second_half(k)

    def second_half(self, k):
        _, _, _, c = self.place
        _, xs, ys, _ = self.shape
        held = self.got[0].at[k]
        self.copies[k][0].wait()
        self.add(
            k,
            lambda i: [
                ((i, xx, yy, c), held.at[i, xx, yy]) for xx in range(xs) for yy in range(ys)
            ],
        )
        self.copies[k][1].start()

    def third(self, block):
        for k in (2 * block, 2 * block + 1):
            self.third_half(k)

    def third_half(self, k):
        _, x, y, c = self.place
        _, xs, ys, _ = self.shape
        held = self.got[1].at[k]
        self.copies[k][1].wait()
        if k % 2 == 0:
            self.add(k, lambda i: [((i, xx, y, c), held.at[i, xx]) for xx in range(xs)])
        else:
            self.add(k, lambda i: [((i, x, yy, c), held.at[i, yy]) for yy in range(ys)])
        self.copies[k][2].start()

    def fourth(self, block):
        for k in (2 * block, 2 * block + 1):
            self.fourth_half(k)

    def fourth_half(self, k):
        _, x, y, c = self.place
        held = self.got[2].at[k]
        self.copies[k][2].wait()
        self.add(k, lambda i: [((i, x, y, c), held.at[i])])
        for copy in self.copies[k][3]:
            copy.start()

    def final(self, block):
        for k in (2 * block, 2 * block + 1):
            self.final_half(k)

    def final_half(self, k):
        z, x, y, c = self.place
        held = self.got[3].at[k]
        for copy in self.copies[k][3]:
            copy.wait()
        total = self.pay[k, z, x, y, c].astype(SINGLE)
        for i in range(self.shape[0] - 1):
            total = total + held[i].astype(SINGLE)
        for part in range(4):
            self.out_ref[part, :, k * 128 : (k + 1) * 128] = total[
                part * self.rows : (part + 1) * self.rows
            ]


def front_kernel(
    capacity,
    experts,
    frozen,
    lengths_ref,
    routes_t_ref,
    mask_ref,
    norms_ref,
    wr_ref,
    tokens_ref,
    cot_ref,
    wq_any,
    wk_any,
    wv_any,
    wo_any,
    fin_any,
    fout_any,
    nin_any,
    nout_any,
    a1_any,
    q_any,
    k_any,
    v_any,
    o_any,
    x1_any,
    a2_any,
    lse_ref,
    info_ref,
    cols_ref,
    probs_ref,
    froz_any,
    ret_any,
    done_any,
    dw_any,
    core_any,
    near_any,
    first_any,
    own_any,
    all_w,
    local_w,
    stage,
    arrived,
    send_sem,
    recv_sem,
    own_sem,
):
    micro, tok, width = tokens_ref.shape
    zs, xs, cs = 4, 2, 2
    shard = nin_any.shape[2]
    dp, ex = lax.axis_index("dp"), lax.axis_index("expert")
    z, x, y, c = dp // xs, dp % xs, ex // cs, ex % cs
    me = y * xs + x
    owners = experts - frozen

    def device(zz, xx, yy, cc):
        return (zz * xs + xx, yy * cs + cc)

    def near(step):
        return z + 1 - 2 * (z % 2) if step == 1 else (zs - 1 - z if step == 3 else (z + 2) % zs)

    core = device(z, x, y, 1 - c)
    swapped = device(z, c, y, x)
    straight, distant = device(near(1), x, y, c), device(near(3), x, y, c)
    others = [(x + (d & 1)) % 2 + xs * ((y + (d >> 1)) % 2) for d in (3, 2, 1)]
    row_peers = [device(z, other % xs, other // xs, c) for other in others]
    fourth = device(z + (near(1) - z) * ((x + c + 1) % 2), c, y, x)
    peers = [core, straight, distant, fourth] + row_peers
    pl.semaphore_wait(meet(peers), len(peers))

    def link(source, target, peer, at):
        return remote(source, target, peer, send_sem, recv_sem, at)

    held_w = all_w.at[z * xs + c]
    exchange = link(local_w, all_w.at[dp], swapped, 0)
    spread = [link(held_w, held_w, straight, 1), link(held_w, held_w, distant, 2)]
    spread_own = [link(local_w, held_w, straight, 1), link(local_w, held_w, distant, 2)]
    keep_own = pltpu.make_async_copy(local_w, all_w.at[dp], own_sem.at[0])
    far = near(3) * xs + c
    onward = link(all_w.at[far], all_w.at[far], straight, 3)
    order = [z, near(1), near(3), near(2)]
    across = [
        link(all_w.at[zz * xs + c], all_w.at[zz * xs + c], core, 4 + i)
        for i, zz in enumerate(order)
    ]
    rows_out = [
        [
            link(
                stage.at[:, m * owners + other],
                arrived.at[:, m * owners + me],
                peer,
                8 + 3 * m + i,
            )
            for i, (other, peer) in enumerate(zip(others, row_peers))
        ]
        for m in range(micro)
    ]
    rows_own = [
        pltpu.make_async_copy(
            stage.at[:, m * owners + me], arrived.at[:, m * owners + me], own_sem.at[1 + m]
        )
        for m in range(micro)
    ]
    results_out = [
        link(stage.at[:, other], ret_any.at[:, me], peer, 14 + i)
        for i, (other, peer) in enumerate(zip(others, row_peers))
    ]
    results_own = pltpu.make_async_copy(stage.at[:, me], ret_any.at[:, me], own_sem.at[3])
    near_far = link(dw_any.at[near(3)], near_any, straight, 21)
    near_own = link(dw_any.at[near(1), 0], first_any, straight, 22)

    def first_half(
        w_scr,
        x_scr,
        dy_scr,
        a1_scr,
        q_scr,
        k_scr,
        v_scr,
        o_scr,
        x1_scr,
        a2_scr,
        bias_scr,
        lse_scr,
        froz_rows,
        win_scr,
        wout_scr,
        acc_scr,
        nin_scr,
        in_sem,
        out_sem,
        stream_sem,
    ):
        def load(source, target, at):
            copy = pltpu.make_async_copy(source, target, in_sem.at[at])
            copy.start()
            return copy

        nout_scr = x1_scr.at[1, pl.ds(0, shard)]
        new_loads = [load(nin_any.at[0], nin_scr, 0), load(nout_any.at[0], nout_scr, 1)]
        row_loads = [
            [
                load(tokens_ref.at[m], x_scr.at[m], 2 + 2 * m),
                load(cot_ref.at[m], dy_scr.at[m], 3 + 2 * m),
            ]
            for m in range(micro)
        ]
        weight_loads = [
            load(ref, w_scr.at[i], 2 + 2 * micro + i)
            for i, ref in enumerate((wq_any, wk_any, wv_any, wo_any))
        ]
        for copy in new_loads:
            copy.wait()
        local_w[0] = jnp.transpose(nin_scr[...]).astype(HALF)
        local_w[1] = nout_scr[...].astype(HALF)

        @pl.when(x != c)
        def _():
            exchange.start()

        @pl.when(x == c)
        def _():
            keep_own.start()
            spread_own[1].start()
            spread_own[0].start()

        blocks = fin_any.shape[2] // width

        def stream(step, slot):
            e, f = step // blocks, step % blocks
            at = pl.ds(pl.multiple_of(f * width, width), width)
            return (
                pltpu.make_async_copy(
                    fin_any.at[e, :, at], win_scr.at[slot], stream_sem.at[0, slot]
                ),
                pltpu.make_async_copy(
                    fout_any.at[e, at, :], wout_scr.at[slot], stream_sem.at[1, slot]
                ),
            )

        for copy in stream(0, 0):
            copy.start()
        for copy in weight_loads + row_loads[0]:
            copy.wait()
        saves = []
        for m in range(micro):
            if m:
                for copy in row_loads[m]:
                    copy.wait()

            def target(e, part, m=m):
                if e < frozen:
                    return froz_rows.at[part, e, m]
                return stage.at[part, m * owners + e - frozen]

            attend_body(
                capacity,
                experts,
                target,
                lengths_ref.at[m],
                x_scr.at[m],
                dy_scr.at[m],
                routes_t_ref.at[m],
                mask_ref.at[pl.ds(m, 1)],
                norms_ref,
                w_scr.at[0],
                w_scr.at[1],
                w_scr.at[2],
                w_scr.at[3],
                wr_ref,
                a1_scr.at[m],
                q_scr.at[m],
                k_scr.at[m],
                v_scr.at[m],
                o_scr.at[m],
                x1_scr.at[m],
                a2_scr.at[m],
                lse_ref.at[m],
                info_ref.at[m],
                cols_ref.at[m],
                probs_ref.at[m],
                bias_scr,
                lse_scr,
            )
            for copy in rows_out[m]:
                copy.start()
            rows_own[m].start()
            for i, (source, target_any) in enumerate(
                (
                    (a1_scr, a1_any),
                    (q_scr, q_any),
                    (k_scr, k_any),
                    (v_scr, v_any),
                    (o_scr, o_any),
                    (x1_scr, x1_any),
                    (a2_scr, a2_any),
                )
            ):
                copy = pltpu.make_async_copy(
                    source.at[m], target_any.at[m], out_sem.at[7 * m + i]
                )
                copy.start()
                saves.append(copy)
            if m == 0:

                @pl.when(x != c)
                def _():
                    exchange.wait_recv()
                    spread[1].start()
                    spread[0].start()

                @pl.when(x == c)
                def _():
                    keep_own.wait()

                across[0].start()


        steps = frozen * blocks

        @pl.loop(0, steps)
        def _(step):
            slot = step % 2
            e = step // blocks

            @pl.when(step + 1 < steps)
            def _():
                for copy in stream(step + 1, 1 - slot):
                    copy.start()

            for copy in stream(step, slot):
                copy.wait()
            expert_step(
                lambda rows: froz_rows[0, e].reshape(micro * capacity, width)[...],
                lambda rows: froz_rows[1, e].reshape(micro * capacity, width)[...],
                micro * capacity,
                win_scr[slot],
                wout_scr[slot],
                NN,
                acc_scr,
                None,
                step % blocks == 0,
                micro * capacity,
            )

            @pl.when(step % blocks == blocks - 1)
            def _():
                for m in range(micro):
                    for part in range(2):
                        froz_rows[part, e, m] = acc_scr[
                            part, m * capacity : (m + 1) * capacity, :
                        ].astype(HALF)

            @pl.when(step == steps // 2)
            def _():
                spread[1].wait_recv()
                onward.start()
                across[2].start()

            @pl.when(step == steps // 2 + 1)
            def _():
                spread[0].wait_recv()
                across[1].start()

        last = pltpu.make_async_copy(froz_rows, froz_any, out_sem.at[7 * micro])
        last.start()
        for copy in saves:
            copy.wait()
        last.wait()

    pl.run_scoped(
        first_half,
        pltpu.VMEM((4, width, width), HALF),
        pltpu.VMEM((micro, tok, width), HALF),
        pltpu.VMEM((micro, tok, width), HALF),
        pltpu.VMEM((micro, tok, width), HALF),
        pltpu.VMEM((micro, tok, width), HALF),
        pltpu.VMEM((micro, tok, width), HALF),
        pltpu.VMEM((micro, tok, width), HALF),
        pltpu.VMEM((micro, tok, width), HALF),
        pltpu.VMEM((micro, tok, width), SINGLE),
        pltpu.VMEM((micro, tok, width), HALF),
        pltpu.VMEM((tok, tok), SINGLE),
        pltpu.VMEM((tok, 128), SINGLE),
        pltpu.VMEM((2, frozen, micro, capacity, width), HALF),
        pltpu.VMEM((2, width, width), HALF),
        pltpu.VMEM((2, width, width), HALF),
        pltpu.VMEM((2, micro * capacity, width), SINGLE),
        pltpu.VMEM((width, shard), SINGLE),
        pltpu.SemaphoreType.DMA((2 + 2 * micro + 4,)),
        pltpu.SemaphoreType.DMA((7 * micro + 1,)),
        pltpu.SemaphoreType.DMA((2, 2)),
    )

    rows_one = owners * capacity
    rows_all = micro * rows_one

    def second_half(
        xt_scr, dyt_scr, acc_scr, held, current, dw_stage, core_scr, held_sem, dw_sem, core_sem
    ):
        def rows_of(part, m):
            def get(rows):
                return arrived[part, pl.ds(m * owners, owners)].reshape(rows_one, width)

            return get

        def weights(zz):
            two = all_w.at[pl.ds(zz * xs, xs)]
            return (
                two[:, 0].reshape(xs * shard, width),
                two[:, 1].reshape(xs * shard, width),
            )

        def results(m):
            for copy in rows_out[m]:
                copy.wait_send()
            for other in range(owners):
                for part in range(2):
                    stage[part, m * owners + other] = acc_scr[
                        m, part, other * capacity : (other + 1) * capacity, :
                    ].astype(HALF)

        def first_step(i):
            across[i].wait_recv()
            w_in, w_out = weights(order[i])
            expert_step(
                rows_of(0, 0),
                rows_of(1, 0),
                rows_one,
                w_in,
                w_out,
                NT,
                acc_scr.at[0],
                held.at[:, i],
                i == 0,
                rows_one,
            )

        rows_own[0].wait()
        for copy in rows_out[0]:
            copy.wait_recv()
        first_step(0)
        first_step(2)

        rows_own[1].wait()
        for copy in rows_out[1]:
            copy.wait_recv()
        for at in range(0, width, 128):
            for part, scr in enumerate((xt_scr, dyt_scr)):
                scr[at : at + 128, :] = jnp.transpose(
                    arrived[part, :, :, at : at + 128].reshape(rows_all, 128)
                )
        turn = [2, 1, 3, 0]
        halves = [
            link(dw_stage.at[i % 2, 1 - c], core_any.at[i], core, 17 + i) for i in range(zs - 1)
        ]
        fetches = [
            pltpu.make_async_copy(core_any.at[i], core_scr, core_sem) for i in range(zs - 1)
        ]
        writes = [
            pltpu.make_async_copy(
                dw_stage.at[i % 2, c], dw_any.at[order[turn[i]]], dw_sem.at[i % 2]
            )
            for i in range(zs)
        ]

        def add_core(i):
            fetches[i].wait()
            for part in range(2):

                @pl.loop(0, width // 128)
                def _(r):
                    rows = pl.ds(pl.multiple_of(r * 128, 128), 128)
                    dw_stage[i % 2, c, part, rows, :] = (
                        dw_stage[i % 2, c, part, rows, :].astype(SINGLE)
                        + core_scr[part, rows, :].astype(SINGLE)
                    ).astype(HALF)

            writes[i].start()

        for i in range(zs):
            slot = i % 2
            fetch = [
                pltpu.make_async_copy(
                    held.at[part, turn[i]], current.at[part, pl.ds(0, rows_one)], held_sem.at[part]
                )
                for part in range(2)
            ]
            for copy in fetch:
                copy.start()
            w_in, w_out = weights(order[turn[i]])
            expert_step(
                rows_of(0, 1),
                rows_of(1, 1),
                rows_one,
                w_in,
                w_out,
                NT,
                acc_scr.at[1],
                current.at[:, pl.ds(rows_one, rows_one)],
                i == 0,
                rows_one,
            )
            for copy in fetch:
                copy.wait()
            if i > 1:
                halves[i - 1].wait_recv()
                fetches[i - 1].start()
                halves[i - 2].wait_send()
            if i == 2:
                add_core(1)
                writes[1].wait()
                near_own.start()

            @pl.loop(0, width // TILE)
            def _(r):
                rows = pl.ds(pl.multiple_of(r * TILE, TILE), TILE)
                for part, left in enumerate((xt_scr, dyt_scr)):
                    total = mm(left[rows, :], current[1 - part]).astype(HALF)
                    for g in range(xs):
                        dw_stage[slot, g, part, rows, :] = total[:, g * shard : (g + 1) * shard]

            if i < zs - 1:
                halves[i].start()
            if i > 2:
                add_core(i - 1)
            if i == 0:
                first_step(1)
                onward.wait_recv()
                across[3].start()
                halves[0].wait_recv()
                fetches[0].start()
                add_core(0)
                writes[0].wait()
                near_far.start()
                first_step(3)
                results(0)
                for copy in results_out:
                    copy.start()
                results_own.start()
        results(1)
        final = pltpu.make_async_copy(
            stage.at[:, pl.ds(owners, owners)], done_any, held_sem.at[0]
        )
        final.start()
        writes[zs - 1].start()
        other_half = pltpu.make_async_copy(
            dw_stage.at[(zs - 1) % 2, 1 - c], own_any, held_sem.at[1]
        )
        other_half.start()
        halves[zs - 2].wait_send()
        writes[zs - 2].wait()
        writes[zs - 1].wait()
        other_half.wait()
        final.wait()
        for copy in results_out:
            copy.wait_send()
        results_own.wait()

    pl.run_scoped(
        second_half,
        pltpu.VMEM((width, rows_all), HALF),
        pltpu.VMEM((width, rows_all), HALF),
        pltpu.VMEM((micro, 2, rows_one, width), SINGLE),
        pltpu.VMEM((2, zs, rows_one, xs * shard), HALF),
        pltpu.VMEM((2, rows_all, xs * shard), HALF),
        pltpu.VMEM((2, xs, 2, width, shard), HALF),
        pltpu.VMEM((2, width, shard), HALF),
        pltpu.SemaphoreType.DMA((2,)),
        pltpu.SemaphoreType.DMA((2,)),
        pltpu.SemaphoreType.DMA,
    )

    @pl.when(x != c)
    def _():
        exchange.wait_send()

    spread[0].wait_send()
    spread[1].wait_send()
    onward.wait_send()
    for copy in across:
        copy.wait_send()
    for copy in results_out:
        copy.wait_recv()
    near_far.wait()
    near_own.wait()


def tail_kernel(
    capacity,
    experts,
    frozen,
    lengths_ref,
    routes_t_ref,
    norms_ref,
    wr_ref,
    lse_ref,
    info_ref,
    cols_ref,
    probs_ref,
    tokens_ref,
    cot_ref,
    wq_any,
    wk_any,
    wv_any,
    wo_any,
    a1_any,
    q_any,
    k_any,
    v_any,
    o_any,
    x1_any,
    a2_any,
    froz_any,
    ret_any,
    done_any,
    dw_any,
    near_any,
    first_any,
    own_any,
    mixed_any,
    xgrad_any,
    shared_ref,
    tiny_ref,
    gin_any,
    gout_any,
    w_scr,
    rows_scr,
    x1_scr,
    a1t_scr,
    ot_scr,
    db_scr,
    comb,
    small_scr,
    bias_scr,
    dx1_scr,
    do_scr,
    delta_scr,
    part_w,
    near_scr,
    land_core,
    land_own,
    land_far,
    land_side,
    gin_scr,
    gout_scr,
    pay,
    got,
    tiny,
    tiny_got,
    send_sem,
    recv_sem,
    red_send,
    red_recv,
    in_sem,
    out_sem,
):
    micro, tok, width = tokens_ref.shape
    zs, xs, ys, cs = 4, 2, 2, 2
    dp, ex = lax.axis_index("dp"), lax.axis_index("expert")
    z, x, y, c = dp // xs, dp % xs, ex // cs, ex % cs
    me = y * xs + x
    owners = experts - frozen

    def device(zz, xx, yy, cc):
        return (zz * xs + xx, yy * cs + cc)

    z1, z2 = z + 1 - 2 * (z % 2), (z + 2) % zs
    others = [(x + (d & 1)) % 2 + xs * ((y + (d >> 1)) % 2) for d in (3, 2, 1)]
    row_peers = [device(z, other % xs, other // xs, c) for other in others]
    core = device(z, x, y, 1 - c)
    straight = device(z1, x, y, c)
    swapped, crossed = device(z, c, y, x), device(z2, c, y, x)
    fourth = device(z + (z1 - z) * ((x + c + 1) % 2), c, y, x)
    peers = row_peers + [crossed, fourth] + reduce_peers(z, x, y, c, zs, xs, cs)
    pl.semaphore_wait(meet(peers), len(peers))

    def link(source, target, peer, at):
        return remote(source, target, peer, send_sem, recv_sem, at)

    results_out = [
        link(done_any.at[:, other], comb.at[1, :, frozen + me], peer, i)
        for i, (other, peer) in enumerate(zip(others, row_peers))
    ]
    last_half = link(own_any, land_core, core, 3)
    near_own = link(dw_any.at[z1, 1], land_own.at[1], straight, 4)
    far_sum = [link(part_w.at[0, i], land_far.at[i], crossed, 5 + i) for i in range(2)]
    side_sum = link(part_w.at[1], land_side, swapped, 7)

    for copy in results_out:
        copy.start()

    def load(source, target, at):
        copy = pltpu.make_async_copy(source, target, in_sem.at[at])
        copy.start()
        return copy

    sources = (tokens_ref, cot_ref, q_any, k_any, v_any, o_any, a2_any, a1_any)
    weights = (wq_any, wk_any, wv_any, wo_any)

    def load_rows(m, which):
        return [load(sources[i].at[m], rows_scr.at[i, m], 16 * m + i) for i in which]

    def load_blocks(m):
        return [
            load(x1_any.at[m], x1_scr.at[m], 16 * m + 8),
            load(froz_any.at[:, :, m], comb.at[m, :, pl.ds(0, frozen)], 16 * m + 9),
        ]

    mine = [load(dw_any.at[z2], part_w.at[0], 14), load(near_any, near_scr, 15)]
    loads = [load(ret_any, comb.at[0, :, pl.ds(frozen, owners)], 10)]
    loads += load_blocks(0) + load_rows(0, (1, 6)) + [load(wo_any, w_scr.at[3], 35)]
    later = load_rows(0, (2, 3, 4, 5, 0, 7))
    later += [load(weights[i], w_scr.at[i], 32 + i) for i in range(3)]
    near_own.start()
    last_half.start()

    def load_last():
        last = load_rows(1, range(8)) + load_blocks(1)
        last.append(load(done_any.at[:, me], comb.at[1, :, frozen + me], 26))
        last.append(load(dw_any.at[z], part_w.at[1], 36))
        last.append(load(first_any, land_own.at[0], 11))
        return last

    def add_rows(target, source):
        @pl.loop(0, width // 128)
        def _(i):
            rows = pl.ds(pl.multiple_of(i * 128, 128), 128)
            target[rows, :] = (
                target[rows, :].astype(SINGLE) + source[rows, :].astype(SINGLE)
            ).astype(HALF)

    def after_own():
        last_half.wait()
        for i in range(2):
            add_rows(part_w.at[1, i], land_core.at[i])
        near_own.wait()
        for i in range(2):
            add_rows(part_w.at[1, i], land_own.at[i])

        @pl.when(x != c)
        def _():
            side_sum.start()

    last_loads = []

    for copy in mine:
        copy.wait()
    for i in range(2):
        add_rows(part_w.at[0, i], near_scr.at[i])
        far_sum[i].start()

    def first_middle():
        for copy in later:
            copy.wait()
        last_loads.extend(load_last())

    def right_of(i):
        def get(k):
            cols = slice(k * TILE, (k + 1) * TILE)
            rows = db_scr[:, :, cols] if i is None else rows_scr[i, :, :, cols]
            return rows.reshape(micro * tok, TILE)

        return get

    reduction = Reduction(
        (z, x, y, c),
        (zs, xs, ys, cs),
        (a1t_scr, a1t_scr, a1t_scr, ot_scr),
        [right_of(i) for i in (2, 3, 4, None)],
        shared_ref,
        pay,
        got,
        red_send,
        red_recv,
    )

    def after_group(group):
        reduction.produce(group)
        if group >= 1:
            reduction.second(group - 1)
        if group >= 2:
            reduction.third(group - 2)

    outs = []

    def back(m, middle, after):
        x_ref, dy_ref, q_ref, k_ref, v_ref, o_ref, a2_ref, _ = [
            rows_scr.at[i, m] for i in range(8)
        ]
        back_body(
            capacity,
            experts,
            middle,
            after,
            lengths_ref.at[m],
            x_ref,
            dy_ref,
            routes_t_ref.at[m],
            norms_ref,
            w_scr.at[0],
            w_scr.at[1],
            w_scr.at[2],
            w_scr.at[3],
            wr_ref,
            q_ref,
            k_ref,
            v_ref,
            o_ref,
            x1_scr.at[m],
            a2_ref,
            lse_ref.at[m],
            info_ref.at[m],
            cols_ref.at[m],
            probs_ref.at[m],
            a2_ref if m == 0 else None,
            x1_scr.at[m] if m == 0 else dx1_scr,
            q_ref,
            k_ref,
            v_ref,
            db_scr.at[m],
            small_scr.at[m],
            comb.at[m, 0],
            comb.at[m, 1],
            bias_scr,
            dx1_scr,
            do_scr,
            delta_scr,
        )
        if m == 0:
            mixed_out(m)

    def mixed_out(m):
        copy = pltpu.make_async_copy(rows_scr.at[6, m], mixed_any.at[m], out_sem.at[2 * m])
        copy.start()
        outs.append(copy)

    def finish(m, first, last):
        x_ref = rows_scr.at[0, m]
        finish_body(
            x_ref,
            norms_ref,
            w_scr.at[0],
            w_scr.at[1],
            w_scr.at[2],
            x1_scr.at[m] if m == 0 else dx1_scr,
            x_ref,
            rows_scr.at[2, m],
            rows_scr.at[3, m],
            rows_scr.at[4, m],
            small_scr.at[m],
            wr_ref.shape[0],
            first,
            last,
        )
        if last == tok // TILE:
            copy = pltpu.make_async_copy(x_ref, xgrad_any.at[m], out_sem.at[2 * m + 1])
            copy.start()
            outs.append(copy)

    for copy in loads:
        copy.wait()
    back(0, first_middle, None)
    finish(0, 0, tok // TILE)
    for copy in last_loads:
        copy.wait()
    for m in range(micro):
        for at in range(0, width, 128):
            tokens_at = slice(m * tok, (m + 1) * tok)
            a1t_scr[at : at + 128, tokens_at] = jnp.transpose(rows_scr[7, m, :, at : at + 128])
            ot_scr[at : at + 128, tokens_at] = jnp.transpose(rows_scr[5, m, :, at : at + 128])
    for copy in results_out:
        copy.wait()
    back(1, after_own, after_group)

    tiny_peers = reduce_peers(z, x, y, c, zs, xs, cs)

    def spread_tiny(at):
        copy = remote(
            tiny, tiny_got.at[at], tiny_peers[(0, 2, 1, 3, 4, 5)[at]], red_send, red_recv, 36 + at
        )
        copy.start()
        return copy

    def gather_tiny(copy, at):
        copy.wait()
        tiny[...] += tiny_got[at]

    finish(1, 0, 1)
    reduction.second(2)
    reduction.third(1)
    reduction.fourth(0)
    finish(1, 1, tok // TILE)
    tiny[...] = small_scr[0] + small_scr[1]
    tiny_copy = spread_tiny(0)
    reduction.third(2)
    reduction.fourth(1)
    mixed_body(experts * capacity, x1_scr.at[1], cols_ref.at[1], comb.at[1, 0], rows_scr.at[6, 1])
    mixed_out(1)
    gather_tiny(tiny_copy, 0)
    tiny_copy = spread_tiny(1)
    reduction.final(0)
    gather_tiny(tiny_copy, 1)
    tiny_copy = spread_tiny(2)
    reduction.fourth(2)
    gather_tiny(tiny_copy, 2)
    tiny_copies = [spread_tiny(3 + i) for i in range(zs - 1)]
    reduction.final(1)
    for copy in far_sum:
        copy.wait()

    @pl.when(x != c)
    def _():
        side_sum.wait()

    def total_of(part, rows):
        base = land_far[part, rows, :].astype(SINGLE)
        own = part_w[1, part, rows, :].astype(SINGLE)
        other = land_side[part, rows, :].astype(SINGLE)
        return base + jnp.where(x == c, own, other)

    for i in range(0, width, 128):
        gin_scr[i : i + 128, :] = total_of(0, slice(i, i + 128)).astype(HALF)
        gout_scr[:, i : i + 128] = jnp.transpose(total_of(1, slice(i, i + 128)).astype(HALF))
    done = [
        pltpu.make_async_copy(gin_scr, gin_any.at[0], out_sem.at[2 * micro]),
        pltpu.make_async_copy(gout_scr, gout_any.at[0], out_sem.at[2 * micro + 1]),
    ]
    for copy in done:
        copy.start()
    reduction.final(2)
    for copy in outs:
        copy.wait()
    for copy in tiny_copies:
        copy.wait()
    total = tiny[...]
    for i in range(zs - 1):
        total = total + tiny_got[3 + i]
    tiny_ref[...] = total
    for copy in done:
        copy.wait()


def vmem(count):
    return [pl.BlockSpec(memory_space=pltpu.VMEM)] * count


def params(mib, **more):
    return pltpu.CompilerParams(vmem_limit_bytes=mib << 20, **more)


def general(
    tokens,
    routes,
    lengths,
    key_mask,
    gain_one,
    bias_one,
    w_query,
    w_key,
    w_value,
    w_output,
    gain_two,
    bias_two,
    w_router,
    frozen_in,
    frozen_out,
    new_in,
    new_out,
    cotangent,
):
    micro, tok, width = tokens.shape
    owners = lax.axis_size("expert")
    dp = lax.axis_size("dp")
    frozen, _, ff = frozen_in.shape
    experts = frozen + owners
    capacity = 10 * tok // (4 * experts) // 8 * 8
    shard = new_in.shape[2]
    slots_all = experts * capacity
    shape = jax.ShapeDtypeStruct
    smem = pl.BlockSpec(memory_space=pltpu.SMEM)

    local_w = jnp.stack([new_in[0].T.astype(HALF), new_out[0].astype(HALF)], 0)
    all_w = lax.all_gather(local_w, "dp", axis=0, tiled=False)

    routes_t = jnp.swapaxes(routes, 1, 2)
    norms = jnp.concatenate([gain_one, bias_one, gain_two, bias_two]).reshape(4, width)
    rows16 = 16
    router_t = jnp.pad(w_router.T, ((0, rows16 - experts), (0, 0)))

    saved, froz_sent, arrived = [], [], []
    for m in range(micro):
        outs = pl.pallas_call(
            functools.partial(attend_kernel, capacity, experts, frozen),
            out_shape=[shape((tok, width), HALF)] * 5
            + [
                shape((tok, width), SINGLE),
                shape((tok, width), HALF),
                shape((16, tok), SINGLE),
                shape((8, tok), SINGLE),
                shape((tok, 128), SINGLE),
                shape((rows16, tok), SINGLE),
                shape((frozen, 2, capacity, width), HALF),
                shape((owners, 2, capacity, width), HALF),
            ],
            in_specs=[smem] + vmem(10),
            out_specs=vmem(13),
            scratch_shapes=[pltpu.VMEM((tok, tok), SINGLE), pltpu.VMEM((tok, 128), SINGLE)],
            compiler_params=params(56),
            cost_estimate=pl.CostEstimate(
                flops=8_000_000_000, bytes_accessed=20_000_000, transcendentals=3_000_000
            ),
            name="attend",
        )(
            lengths[m, 0],
            tokens[m],
            cotangent[m],
            routes_t[m],
            key_mask[m][None, :],
            norms,
            w_query,
            w_key,
            w_value,
            w_output,
            router_t,
        )
        saved.append(outs[:11])
        froz_sent.append(outs[11])
        arrived.append(
            lax.all_to_all(outs[12], "expert", split_axis=0, concat_axis=0, tiled=True)
        )

    block = min(768, ff)
    rows_spec = pl.BlockSpec((1, 2, capacity, width), lambda e, f: (e, 0, 0, 0))
    froz_back = pl.pallas_call(
        frozen_kernel,
        grid=(frozen, ff // block),
        out_shape=[shape((frozen, 2, capacity, width), HALF)] * 2,
        in_specs=[
            rows_spec,
            rows_spec,
            pl.BlockSpec((1, width, block), lambda e, f: (e, 0, f)),
            pl.BlockSpec((1, block, width), lambda e, f: (e, f, 0)),
        ],
        out_specs=[rows_spec, rows_spec],
        scratch_shapes=[
            pltpu.VMEM((2 * capacity, width), HALF),
            pltpu.VMEM((2 * capacity, width), HALF),
            pltpu.VMEM((2, 2 * capacity, width), SINGLE),
        ],
        compiler_params=params(50),
        cost_estimate=pl.CostEstimate(
            flops=16_000_000_000, bytes_accessed=25_000_000, transcendentals=2_500_000
        ),
        name="frozen",
    )(froz_sent[0], froz_sent[1], frozen_in, frozen_out)

    rows_all = micro * owners * capacity
    group = max(1, 768 // shard)
    whole = pl.BlockSpec((owners, 2, capacity, width), lambda f: (0, 0, 0, 0))
    done0, done1, grads_w = pl.pallas_call(
        owned_kernel,
        grid=(dp // group,),
        out_shape=[shape((owners, 2, capacity, width), HALF)] * 2
        + [shape((dp, 2, width, shard), HALF)],
        in_specs=[whole, whole, pl.BlockSpec((group, 2, shard, width), lambda f: (f, 0, 0, 0))],
        out_specs=[whole, whole, pl.BlockSpec((group, 2, width, shard), lambda f: (f, 0, 0, 0))],
        scratch_shapes=[
            pltpu.VMEM((rows_all, width), HALF),
            pltpu.VMEM((rows_all, width), HALF),
            pltpu.VMEM((width, rows_all), HALF),
            pltpu.VMEM((width, rows_all), HALF),
            pltpu.VMEM((2, rows_all, width), SINGLE),
            pltpu.VMEM((2, rows_all, group * shard), HALF),
        ],
        compiler_params=params(60),
        cost_estimate=pl.CostEstimate(
            flops=47_000_000_000, bytes_accessed=35_000_000, transcendentals=5_000_000
        ),
        name="owned",
    )(arrived[0], arrived[1], all_w)

    returned = [
        lax.all_to_all(one, "expert", split_axis=0, concat_axis=0, tiled=True)
        for one in (done0, done1)
    ]
    summed_w = lax.psum_scatter(grads_w, "dp", scatter_dimension=0, tiled=True)[0]

    mixed_list, xgrad_list, small_list, weight_ins = [], [], [], []
    for m in range(micro):
        a1, q, k, v, o, x1, a2, lse, info, cols, probs = saved[m]
        mixed, xgrad, dq, dk, dv, db, small = pl.pallas_call(
            functools.partial(back_kernel, capacity, experts),
            out_shape=[shape((tok, width), HALF)] * 6 + [shape((rows16 + 8, width), SINGLE)],
            in_specs=[smem] + vmem(21),
            out_specs=vmem(7),
            scratch_shapes=[
                pltpu.VMEM((slots_all, width), HALF),
                pltpu.VMEM((slots_all, width), HALF),
                pltpu.VMEM((tok, tok), SINGLE),
                pltpu.VMEM((tok, width), SINGLE),
                pltpu.VMEM((tok, width), HALF),
                pltpu.VMEM((tok, 128), SINGLE),
            ],
            compiler_params=params(56),
            cost_estimate=pl.CostEstimate(
                flops=16_000_000_000, bytes_accessed=25_000_000, transcendentals=3_000_000
            ),
            name="back",
        )(
            lengths[m, 0],
            tokens[m],
            cotangent[m],
            routes_t[m],
            norms,
            w_query,
            w_key,
            w_value,
            w_output,
            router_t,
            q,
            k,
            v,
            o,
            x1,
            a2,
            lse,
            info,
            cols,
            probs,
            froz_back[m],
            returned[m],
        )
        mixed_list.append(mixed)
        xgrad_list.append(xgrad)
        small_list.append(small)
        weight_ins += [a1, o, dq, dk, dv, db]

    grads = pl.pallas_call(
        weights_kernel,
        out_shape=shape((4, width, width), HALF),
        in_specs=vmem(len(weight_ins)),
        out_specs=vmem(1)[0],
        compiler_params=params(50),
        name="weights",
    )(*weight_ins)
    shared = lax.psum_scatter(grads, ("dp", "expert"), scatter_dimension=1, tiled=True)
    shared = shared.astype(SINGLE)
    small = sum(small_list[1:], small_list[0])
    small = jnp.concatenate([small[:experts], small[rows16 : rows16 + 4]], 0).T
    small = lax.psum_scatter(small, ("dp", "expert"), scatter_dimension=0, tiled=True)
    return (
        jnp.stack(mixed_list, 0),
        jnp.stack(xgrad_list, 0),
        small[:, experts + 2],
        small[:, experts + 3],
        shared[0],
        shared[1],
        shared[2],
        shared[3],
        small[:, experts],
        small[:, experts + 1],
        small[:, :experts],
        summed_w[0].astype(SINGLE)[None],
        summed_w[1].astype(SINGLE).T[None],
    )


def fused(
    tokens,
    routes,
    lengths,
    key_mask,
    gain_one,
    bias_one,
    w_query,
    w_key,
    w_value,
    w_output,
    gain_two,
    bias_two,
    w_router,
    frozen_in,
    frozen_out,
    new_in,
    new_out,
    cotangent,
):
    micro, tok, width = tokens.shape
    owners = lax.axis_size("expert")
    dp = lax.axis_size("dp")
    frozen = frozen_in.shape[0]
    experts = frozen + owners
    capacity = 10 * tok // (4 * experts) // 8 * 8
    shard = new_in.shape[2]
    zs, xs, ys, cs = 4, 2, 2, 2
    shape = jax.ShapeDtypeStruct
    smem = pl.BlockSpec(memory_space=pltpu.SMEM)

    def anywhere(count):
        return [pl.BlockSpec(memory_space=pl.ANY)] * count

    routes_t = jnp.swapaxes(routes, 1, 2)
    norms = jnp.concatenate([gain_one, bias_one, gain_two, bias_two]).reshape(4, width)
    rows16 = 16
    router_t = jnp.pad(w_router.T, ((0, rows16 - experts), (0, 0)))
    dma = pltpu.SemaphoreType.DMA

    outs = pl.pallas_call(
        functools.partial(front_kernel, capacity, experts, frozen),
        out_shape=[shape((micro, tok, width), HALF)] * 5
        + [
            shape((micro, tok, width), SINGLE),
            shape((micro, tok, width), HALF),
            shape((micro, 16, tok), SINGLE),
            shape((micro, 8, tok), SINGLE),
            shape((micro, tok, 128), SINGLE),
            shape((micro, rows16, tok), SINGLE),
            shape((2, frozen, micro, capacity, width), HALF),
            shape((2, owners, capacity, width), HALF),
            shape((2, owners, capacity, width), HALF),
            shape((zs, 2, width, shard), HALF),
            shape((zs, 2, width, shard), HALF),
            shape((2, width, shard), HALF),
            shape((width, shard), HALF),
            shape((2, width, shard), HALF),
        ],
        in_specs=[smem] + vmem(4) + anywhere(10),
        out_specs=anywhere(7) + vmem(4) + anywhere(8),
        scratch_shapes=[
            pltpu.VMEM((dp, 2, shard, width), HALF),
            pltpu.VMEM((2, shard, width), HALF),
            pltpu.VMEM((2, micro * owners, capacity, width), HALF),
            pltpu.VMEM((2, micro * owners, capacity, width), HALF),
            dma((23,)),
            dma((23,)),
            dma((4,)),
        ],
        compiler_params=params(63, collective_id=1, has_side_effects=True),
        name="front",
    )(
        lengths[:, 0],
        routes_t,
        key_mask,
        norms,
        router_t,
        tokens,
        cotangent,
        w_query,
        w_key,
        w_value,
        w_output,
        frozen_in,
        frozen_out,
        new_in,
        new_out,
    )
    a1, q, k, v, o, x1, a2, lse, info, cols, probs, froz, ret, done, dw, _, near, first, own = outs
    rows = width // (dp * owners)
    blocks = width // 128
    landing = [(zs, xs, ys), (zs, 2), (zs,), (zs - 1,)]
    mixed, xgrad, shared, small, grad_in, grad_out = pl.pallas_call(
        functools.partial(tail_kernel, capacity, experts, frozen),
        out_shape=[
            shape((micro, tok, width), HALF),
            shape((micro, tok, width), HALF),
            shape((4, rows, width), SINGLE),
            shape((rows16 + 8, width), SINGLE),
            shape((1, width, shard), HALF),
            shape((1, shard, width), HALF),
        ],
        in_specs=[smem] + vmem(7) + anywhere(20),
        out_specs=anywhere(2) + vmem(2) + anywhere(2),
        scratch_shapes=[
            pltpu.VMEM((4, width, width), HALF),
            pltpu.VMEM((8, micro, tok, width), HALF),
            pltpu.VMEM((micro, tok, width), SINGLE),
            pltpu.VMEM((width, micro * tok), HALF),
            pltpu.VMEM((width, micro * tok), HALF),
            pltpu.VMEM((micro, tok, width), HALF),
            pltpu.VMEM((micro, 2, experts, capacity, width), HALF),
            pltpu.VMEM((micro, rows16 + 8, width), SINGLE),
            pltpu.VMEM((tok, tok), SINGLE),
            pltpu.VMEM((tok, width), SINGLE),
            pltpu.VMEM((tok, width), HALF),
            pltpu.VMEM((tok, 128), SINGLE),
            pltpu.VMEM((2, 2, width, shard), HALF),
            pltpu.VMEM((2, width, shard), HALF),
            pltpu.VMEM((2, width, shard), HALF),
            pltpu.VMEM((2, width, shard), HALF),
            pltpu.VMEM((2, width, shard), HALF),
            pltpu.VMEM((2, width, shard), HALF),
            pltpu.VMEM((width, shard), HALF),
            pltpu.VMEM((shard, width), HALF),
            pltpu.VMEM((blocks, zs, xs, ys, cs, 4 * rows, 128), HALF),
            [pltpu.VMEM((blocks,) + lead + (4 * rows, 128), HALF) for lead in landing],
            pltpu.VMEM((rows16 + 8, width), SINGLE),
            pltpu.VMEM((zs + 2, rows16 + 8, width), SINGLE),
            dma((8,)),
            dma((8,)),
            dma((42,)),
            dma((42,)),
            dma((37,)),
            dma((2 * micro + 2,)),
        ],
        compiler_params=params(63, collective_id=2, has_side_effects=True),
        name="tail",
    )(
        lengths[:, 0],
        routes_t,
        norms,
        router_t,
        lse,
        info,
        cols,
        probs,
        tokens,
        cotangent,
        w_query,
        w_key,
        w_value,
        w_output,
        a1,
        q,
        k,
        v,
        o,
        x1,
        a2,
        froz,
        ret,
        done,
        dw,
        near,
        first,
        own,
    )
    at = (lax.axis_index("dp") * owners + lax.axis_index("expert")) * rows
    small = lax.dynamic_slice_in_dim(small, at, rows, 1)
    return (
        mixed,
        xgrad,
        small[rows16 + 2],
        small[rows16 + 3],
        shared[0],
        shared[1],
        shared[2],
        shared[3],
        small[rows16],
        small[rows16 + 1],
        small[:experts].T,
        grad_in.astype(SINGLE),
        grad_out.astype(SINGLE),
    )


def solution(mesh):
    both = ("dp", "expert")
    small_slice = mesh.shape["dp"] == 8 and mesh.shape["expert"] == 4
    return jax.shard_map(
        fused if small_slice else general,
        mesh=mesh,
        in_specs=(
            P(None, both, None),
            P(None, both, None),
            P(None, both, None),
            P(None, both),
        )
        + (P(),) * 11
        + (P("expert", None, "dp"), P("expert", "dp", None), P(None, both, None)),
        out_specs=(P(None, both, None), P(None, both, None), P(both), P(both))
        + (P(both, None),) * 4
        + (P(both), P(both), P(both, None), P("expert", None, "dp"), P("expert", "dp", None)),
        check_vma=False,
    )
```
